32 devices in a mesh: dp: 4 (over z), expert: 8 (over y, x, core).
Axes of the slice: x: 2, y: 2, z: 4, core: 2. Of those that a mesh axis runs over, the one named last changes fastest.
Arguments:
- tokens: bfloat16 [512, 64, 512], P(('dp', 'expert')), may hold values from -8 to 8
- lengths: int32 [512], P(('dp', 'expert')), may hold values from 16 to 64
- tasks: int32 [512], P(('dp', 'expert')), may hold values from 0 to 29
- routes: int32 [30, 2], replicated, may hold values from 0 to 7, all different within a row
- gate_table: float32 [30, 8], replicated, may hold values from -4 to 4
- ln1_gain: float32 [512], replicated, may hold values from 0.1 to 1.9
- ln1_bias: float32 [512], replicated, may hold values from -1.5 to 1.5
- ln2_gain: float32 [512], replicated, may hold values from 0.1 to 1.9
- ln2_bias: float32 [512], replicated, may hold values from -1.5 to 1.5
- w_query: bfloat16 [512, 512], replicated, may hold values from -0.25 to 0.25
- w_key: bfloat16 [512, 512], replicated, may hold values from -0.25 to 0.25
- w_value: bfloat16 [512, 512], replicated, may hold values from -0.25 to 0.25
- w_out: bfloat16 [512, 512], replicated, may hold values from -1 to 1
- w_in: bfloat16 [8, 512, 2048], P('expert'), may hold values from -0.25 to 0.25
- w_back: bfloat16 [8, 2048, 512], P('expert'), may hold values from -0.1875 to 0.1875
- cotangent: bfloat16 [512, 64, 512], P(('dp', 'expert')), may hold values from -6 to 6
Outputs:
- output: bfloat16 [512, 64, 512], P(('dp', 'expert'))
- input_grad: bfloat16 [512, 64, 512], P(('dp', 'expert'))
- gate_grad: float32 [30, 8], replicated
- ln1_gain_grad: float32 [512], replicated
- ln1_bias_grad: float32 [512], replicated
- ln2_gain_grad: float32 [512], replicated
- ln2_bias_grad: float32 [512], replicated
- query_grad: float32 [512, 512], replicated
- key_grad: float32 [512, 512], replicated
- value_grad: float32 [512, 512], replicated
- out_grad: float32 [512, 512], replicated
- in_grad: float32 [8, 512, 2048], P('expert', 'dp')
- back_grad: float32 [8, 2048, 512], P('expert', 'dp')
- rms: float32 [3], replicated
The draws below stay inside these ranges and needn't reach their ends.
Inputs may be any that keep to these rules, and one draw needn't show every extreme that they name: `routes`: each task names two different experts; every expert is named by some task.
All inputs are finite; a program needn't handle non-finite values.
Results may differ from the reference program's by a relative error of at most 0.012.
The reference program's roundings to bfloat16 on the way count: a program that leaves them out, or rounds other values in their place, can miss the bound.
Values may be sent and summed in bfloat16 or wider, within the bound.
A program may use at most 192 MiB of HBM per device.

```python
import math
import jax
import jax.numpy as jnp
import numpy as np
from jax import lax

D = 512
HEADS = 8
FF = 2048
TASKS = 30
S_DEV = 16
SLOT = 64
HEAD = 64
EXPERTS = 8
SENTS = 512
CAP = 8


def draw_tokens(key, part):
    key = jax.random.fold_in(key, 11)
    entries = jnp.clip(jax.random.normal(key, (SENTS, SLOT, D), jnp.float32), -4.0, 4.0)
    low_end = 0.6
    high_end = 1.8
    place = jnp.arange(SENTS).astype(jnp.float32) / jnp.float32(max(SENTS - 1, 1))
    factor = low_end + (high_end - low_end) * place
    return (entries * factor[:, None, None]).astype(jnp.bfloat16)


def place_ends(values, stream_key, least, high):
    longest = values.shape.index(max(values.shape))
    spots = []
    for shift in (0, 1):
        where = [jax.random.randint(jax.random.fold_in(stream_key, axis), (), 0, length) for axis, length in enumerate(values.shape)]
        where[longest] = (where[longest] + shift) % values.shape[longest]
        spots.append(tuple(where))
    return values.at[spots[0]].set(least).at[spots[1]].set(high)


def block_levels(stream_key, shape, pieces, least, high):
    def one(position, parts):
        heights = jax.random.uniform(jax.random.fold_in(jax.random.fold_in(stream_key, 6), position), (parts,), jnp.float32, least / len(pieces), high / len(pieces))
        return jnp.repeat(jnp.exp(heights), shape[position] // parts).reshape((-1,) + (1,) * (len(shape) - position - 1))

    factor_of = one(*pieces[0])
    for cut in pieces[1:]:
        factor_of = factor_of * one(*cut)
    return factor_of


def rank_table(amount, lean):
    portions = [(1 << 20) // math.isqrt(rank ** lean) + 1 for rank in range(1, amount + 1)]
    width = 1 + sum(portions) // (1 << 30)
    return np.cumsum(np.array([max(1, weight // width) for weight in portions]))


def skewed_ids(rng, dims, number_of, lean):
    grid = rank_table(number_of, lean)
    lot = jax.random.randint(jax.random.fold_in(rng, 1), dims, 0, int(grid[number_of - 1]))
    standing = jnp.searchsorted(jnp.asarray(grid, jnp.int32), lot, side="right")
    return jax.random.permutation(jax.random.fold_in(rng, 2), number_of)[standing].astype(jnp.int32)


def distinct(key, rows, number_of, top, lift):
    sequence = jax.random.permutation(jax.random.fold_in(key, 1), number_of)
    favour = sequence
    for power in range(3):
        favour = favour * favour // number_of
    favour = favour * lift // number_of
    lots = jax.random.randint(jax.random.fold_in(key, 2), (rows, number_of), 0, 4096) + favour
    holders = jax.random.permutation(jax.random.fold_in(key, 3), rows)[jnp.arange(number_of) % rows]
    lots = jnp.where(jnp.arange(rows)[:, None] == holders[None, :], 1 << 14, lots)
    score = lots * number_of + jnp.arange(number_of)
    return lax.top_k(score.astype(jnp.int32), top)[1].astype(jnp.int32)


def noise(rng, extent, spread, reach, cuts=(), held_as=jnp.bfloat16):
    values = spread * jax.random.normal(rng, extent, jnp.float32)
    if cuts:
        values = values * block_levels(rng, extent, cuts, -0.22, 0.18)
    return jnp.clip(values, -reach, reach).astype(held_as)


def setup_inputs(seed: int = 0) -> dict:
    seeds = jax.random.split(jax.random.key(seed), 17)
    tokens = draw_tokens(jax.random.fold_in(seeds[16], 71), 0)
    lengths = place_ends(jax.random.randint(seeds[1], (SENTS,), SLOT // 4, SLOT + 1), jax.random.fold_in(seeds[1], 1), SLOT // 4, SLOT).astype(jnp.int32)
    tasks = place_ends(skewed_ids(seeds[2], (SENTS,), TASKS, 2), jax.random.fold_in(seeds[2], 3), 0, TASKS - 1).astype(jnp.int32)
    routes = distinct(seeds[3], TASKS, EXPERTS, 2, 4096)
    gate_table = noise(seeds[4], (TASKS, EXPERTS), 0.7, 4.0, (), jnp.float32)
    ln1_gain = jnp.clip(1.0 + 0.18 * jax.random.normal(seeds[5], (D,), jnp.float32), 0.1, 1.9)
    ln1_bias = noise(seeds[6], (D,), 0.3, 1.5, (), jnp.float32)
    ln2_gain = jnp.clip(1.0 + 0.18 * jax.random.normal(seeds[7], (D,), jnp.float32), 0.1, 1.9)
    ln2_bias = noise(seeds[8], (D,), 0.3, 1.5, (), jnp.float32)
    w_query = noise(seeds[9], (D, D), D ** -0.5, 0.25)
    w_key = noise(seeds[10], (D, D), D ** -0.5, 0.25)
    w_value = noise(seeds[11], (D, D), D ** -0.5, 0.25)
    w_out = noise(seeds[12], (D, D), (D // 16) ** -0.5, 1.0)
    w_in = noise(seeds[13], (EXPERTS, D, FF), D ** -0.5, 0.25, ((0, 8),))
    w_back = noise(seeds[14], (EXPERTS, FF, D), (FF // 2) ** -0.5, 0.1875, ((0, 8),))
    cotangent = noise(seeds[15], (SENTS, SLOT, D), 1.0, 6.0, ((0, 32),))
    return {"tokens": tokens, "lengths": lengths, "tasks": tasks, "routes": routes, "gate_table": gate_table, "ln1_gain": ln1_gain, "ln1_bias": ln1_bias, "ln2_gain": ln2_gain, "ln2_bias": ln2_bias, "w_query": w_query, "w_key": w_key, "w_value": w_value, "w_out": w_out, "w_in": w_in, "w_back": w_back, "cotangent": cotangent}


@jax.custom_vjp
def lower_forward(value_rows):
    return lax.optimization_barrier(value_rows.astype(jnp.bfloat16)).astype(jnp.float32)

@jax.custom_vjp
def lower_backward(value_rows):
    return value_rows

def low_keep(value_rows):
    return (lower_forward(value_rows), None)

def low_pass(kept, grad):
    return (grad,)

def back_keep(value_rows):
    return (value_rows, None)

def back_low(kept, grad):
    return (lower_forward(grad),)
lower_forward.defvjp(low_keep, low_pass)
lower_backward.defvjp(back_keep, back_low)
TOP_PRECISION = lax.Precision.HIGHEST

def normalize(value):
    centered = value - lax.optimization_barrier(jnp.mean(value, axis=-1, keepdims=True))
    variance = lax.optimization_barrier(jnp.mean(centered * centered, axis=-1, keepdims=True))
    return centered * lax.rsqrt(variance + 1e-05)

def expert_apply(packed):
    inputs, first, second = packed
    hidden = jnp.einsum('bcld,df->bclf', inputs, first, precision=TOP_PRECISION)
    hidden = lower_backward(hidden)
    active = lower_forward(jax.nn.gelu(hidden))
    result = jnp.einsum('bclf,fd->bcld', active, second, precision=TOP_PRECISION)
    return lower_forward(lower_backward(result))

def reference(tokens, lengths, tasks, routes, gate_table, ln1_gain, ln1_bias, ln2_gain, ln2_bias, w_query, w_key, w_value, w_out, w_in, w_back, cotangent):
    sents = tokens.shape[0]
    blocks = sents // S_DEV
    chosen = routes[tasks]
    flat = chosen.reshape(blocks, 2 * S_DEV)
    order = jnp.arange(2 * S_DEV)
    earlier = (flat[:, :, None] == flat[:, None, :]) & (order[None, None, :] < order[None, :, None])
    rank = lax.optimization_barrier(jnp.sum(earlier.astype(jnp.int32), axis=2))
    expert_ids = jnp.arange(EXPERTS).astype(jnp.int32)
    slot_ids = jnp.arange(CAP).astype(jnp.int32)
    dispatch = ((flat[:, None, None, :] == expert_ids[None, :, None, None]) & (rank[:, None, None, :] == slot_ids[None, None, :, None])).astype(jnp.float32)
    valid = (jnp.arange(SLOT)[None, :] < lengths[:, None]).astype(jnp.float32)
    keymask = valid[:, None, None, :] > 0.5
    scale = 1.0 / jnp.sqrt(jnp.float32(HEAD))

    def forward(x, table, g1, b1, g2, b2, query_matrix, key_matrix, value_matrix, output_matrix, w1, w2):
        attention_probs = lower_forward(normalize(x) * g1 + b1)
        query_rows = lower_forward(lower_backward(jnp.einsum('tjy,ya->tja', attention_probs, query_matrix, precision=TOP_PRECISION)))
        key_rows = lower_forward(lower_backward(jnp.einsum('tjy,ya->tja', attention_probs, key_matrix, precision=TOP_PRECISION)))
        value_rows = lower_forward(lower_backward(jnp.einsum('tjy,ya->tja', attention_probs, value_matrix, precision=TOP_PRECISION)))
        qh = query_rows.reshape(sents, SLOT, HEADS, HEAD)
        kh = key_rows.reshape(sents, SLOT, HEADS, HEAD)
        vh = value_rows.reshape(sents, SLOT, HEADS, HEAD)
        scores = lower_backward(jnp.einsum('sqhd,skhd->shqk', qh, kh, precision=TOP_PRECISION) * scale)
        scores = jnp.where(keymask, scores, -1000000000.0)
        prob = lower_forward(jax.nn.softmax(scores, axis=-1))
        context_rows = jnp.einsum('shqk,skhd->sqhd', prob, vh, precision=TOP_PRECISION).reshape(sents, SLOT, D)
        context_rows = lower_forward(lower_backward(context_rows))
        attention_block = lower_backward(jnp.einsum('tjy,ya->tja', context_rows, output_matrix, precision=TOP_PRECISION))
        h = x + attention_block
        m = lower_forward(normalize(h) * g2 + b2)
        copies = jnp.broadcast_to(m[:, None], (sents, 2, SLOT, D)).reshape(blocks, 2 * S_DEV, SLOT, D)
        sent = lower_backward(jnp.einsum('becn,bnld->ebcld', dispatch, copies, precision=TOP_PRECISION))
        results = lax.map(jax.checkpoint(expert_apply), (sent, w1, w2))
        backward_rule = jnp.einsum('becn,ebcld->bnld', dispatch, results, precision=TOP_PRECISION).reshape(sents, 2, SLOT, D)
        logits = table[tasks[:, None], chosen]
        gate_values = jax.nn.softmax(logits, axis=-1)
        expert_mixture = jnp.einsum('jb,jbwo->jwo', gate_values, backward_rule, precision=TOP_PRECISION)
        total = valid[:, :, None] * (h + expert_mixture)
        return (total, (attention_block, expert_mixture))
    primals = (tokens.astype(jnp.float32), gate_table, ln1_gain, ln1_bias, ln2_gain, ln2_bias, w_query.astype(jnp.float32), w_key.astype(jnp.float32), w_value.astype(jnp.float32), w_out.astype(jnp.float32), w_in.astype(jnp.float32), w_back.astype(jnp.float32))
    total, pull, extra = jax.vjp(forward, *primals, has_aux=True)
    attention_block, expert_mixture = extra
    grads = pull(cotangent.astype(jnp.float32))
    mask3 = valid[:, :, None]
    count = jnp.sum(valid) * D
    sums = jnp.stack([jnp.sum(total * total), jnp.sum(mask3 * attention_block * attention_block), jnp.sum(mask3 * expert_mixture * expert_mixture)])
    rms = jnp.sqrt(sums / count)
    return (total.astype(jnp.bfloat16), grads[0].astype(jnp.bfloat16), grads[1], grads[2], grads[3], grads[4], grads[5], grads[6], grads[7], grads[8], grads[9], grads[10], grads[11], rms)
```

```python
import functools

import jax
import jax.numpy as jnp
from jax import lax
from jax.experimental import pallas as pl
from jax.experimental.pallas import tpu as pltpu
from jax.sharding import PartitionSpec as P

HEADS = 8


def normalize(value):
    centered = value - jnp.mean(value, axis=-1, keepdims=True)
    variance = jnp.mean(centered * centered, axis=-1, keepdims=True)
    inverse = lax.rsqrt(variance + 1e-05)
    return (centered * inverse, inverse)


def project(left, right):
    return jnp.dot(left, right, preferred_element_type=jnp.float32)


def expert_forward(incoming, first, second):
    pre_act = project(incoming, first)
    active = jax.nn.gelu(pre_act).astype(jnp.bfloat16)
    produced = project(active, second).astype(jnp.bfloat16)
    return (pre_act, active, produced)


def expert_backward(incoming, pre_act, active, grad_in, first, second):
    dactive = project(grad_in, second.T)
    back_local = project(active.T, grad_in)
    gelu_pull = jax.vjp(jax.nn.gelu, pre_act)[1]
    dpre = gelu_pull(dactive)[0].astype(jnp.bfloat16)
    in_local = project(incoming.T, dpre)
    dincoming = project(dpre, first.T).astype(jnp.bfloat16)
    return (in_local, back_local, dincoming)


BF = jnp.bfloat16
F32 = jnp.float32
VM = pltpu.VMEM


def mm(a, b, ca=1, cb=0):
    return lax.dot_general(a, b, (((ca,), (cb,)), ((), ())), preferred_element_type=F32)


def block_diagonal(group, slot, head):
    shape = (group * slot, group * head)
    rows = lax.broadcasted_iota(jnp.int32, shape, 0) // slot
    cols = lax.broadcasted_iota(jnp.int32, shape, 1) // head
    return rows == cols


def spread(part, mask, group):
    return jnp.where(mask, jnp.concatenate([part] * group, axis=0), jnp.zeros((), part.dtype))


def fold(product, mask, slot, group):
    kept = jnp.where(mask, product, 0.0)
    total = kept[0:slot]
    for one in range(1, group):
        total = total + kept[one * slot : (one + 1) * slot]
    return total


def attend(query, keyed, valued, length, mask, slot, group, scale):
    scores = mm(keyed, spread(query, mask, group), 1, 1) * scale
    place = lax.broadcasted_iota(jnp.int32, scores.shape, 0)
    scores = jnp.where(place < length, scores, -1000000000.0)
    raised = jnp.exp(scores - jnp.max(scores, axis=0, keepdims=True))
    prob = raised / jnp.sum(raised, axis=0, keepdims=True)
    context = fold(mm(prob.astype(BF), valued, 0, 0), mask, slot, group)
    return prob, context


def attention_forward_kernel(
    heads, len_ref, x_ref, wq, wk, wv, wo, g1, b1, g2, b2,
    act_o, q_o, k_o, v_o, ctx_o, p_o, h_o, m_o, st_o,
):
    count, slot, width = x_ref.shape
    head = width // heads
    group = max(1, min(heads, 256 // head))
    span = group * head
    step = pl.program_id(0)
    scale = head ** -0.5
    mask = block_diagonal(group, slot, head)
    x = x_ref[...].astype(F32).reshape(count * slot, width)
    normed, _ = normalize(x)
    act = (normed * g1[...] + b1[...]).astype(BF)
    act_o[...] = act
    q_o[...] = mm(act, wq[...]).astype(BF)
    k_o[...] = mm(act, wk[...]).astype(BF)
    v_o[...] = mm(act, wv[...]).astype(BF)
    for s in range(count):
        length = len_ref[step * count + s]
        rows = slice(s * slot, (s + 1) * slot)
        for part in range(heads // group):
            cols = slice(part * span, (part + 1) * span)
            prob, context = attend(
                q_o[rows, cols], k_o[rows, cols], v_o[rows, cols], length, mask, slot, group, scale
            )
            p_o[s, part] = prob
            ctx_o[rows, cols] = context.astype(BF)
    attn = mm(ctx_o[...], wo[...])
    hidden = x + attn
    h_o[...] = hidden
    normed2, _ = normalize(hidden)
    m_o[...] = (normed2 * g2[...] + b2[...]).astype(BF).reshape(count, slot, width)
    place = lax.broadcasted_iota(jnp.int32, (slot, width), 0)
    total = jnp.zeros((1, width), F32)
    for s in range(count):
        length = len_ref[step * count + s]
        part = attn[s * slot : (s + 1) * slot]
        total = total + jnp.sum(jnp.where(place < length, part * part, 0.0), axis=0, keepdims=True)

    @pl.when(step == 0)
    def _():
        st_o[...] = jnp.zeros_like(st_o)

    st_o[...] += total


def attention_forward(tokens, lengths, wq, wk, wv, wo, g1, b1, g2, b2, heads):
    sents, slot, width = tokens.shape
    count = 4 if sents % 4 == 0 else 1
    rows = count * slot
    head = width // heads
    group = max(1, min(heads, 256 // head))
    whole = lambda *shape: pl.BlockSpec(shape, lambda i: (0,) * len(shape))
    flat = pl.BlockSpec((rows, width), lambda i: (i, 0))
    cube = pl.BlockSpec((count, slot, width), lambda i: (i, 0, 0))
    probs = pl.BlockSpec((count, heads // group, slot, group * slot), lambda i: (i, 0, 0, 0))
    shape = jax.ShapeDtypeStruct
    total = sents * slot
    return pl.pallas_call(
        functools.partial(attention_forward_kernel, heads),
        grid=(sents // count,),
        in_specs=[pl.BlockSpec(memory_space=pltpu.SMEM), cube]
        + [whole(width, width)] * 4
        + [whole(1, width)] * 4,
        out_specs=[flat] * 5 + [probs, flat, cube, whole(1, width)],
        out_shape=[shape((total, width), BF)] * 5
        + [
            shape((sents, heads // group, slot, group * slot), F32),
            shape((total, width), F32),
            shape((sents, slot, width), BF),
            shape((1, width), F32),
        ],
        compiler_params=pltpu.CompilerParams(
            dimension_semantics=("arbitrary",), vmem_limit_bytes=56 * 2**20
        ),
        cost_estimate=pl.CostEstimate(
            flops=8 * total * width * width + 4 * total * slot * width,
            bytes_accessed=16 * total * width,
            transcendentals=total * slot * heads,
        ),
    )(lengths, tokens, wq, wk, wv, wo, g1[None], b1[None], g2[None], b2[None])


def row_sum(value, width):
    return jnp.sum(value, axis=0, keepdims=True)


def layer_norm_pull(grad, normed, inverse, gain):
    scaled = grad * gain
    inner = scaled - jnp.mean(scaled, axis=-1, keepdims=True)
    inner = inner - normed * jnp.mean(scaled * normed, axis=-1, keepdims=True)
    return inverse * inner


def attention_pull(dcontext, query, keyed, valued, prob, mask, slot, group, scale):
    low = prob.astype(BF)
    dspread = spread(dcontext, mask, group)
    dprob = mm(valued, dspread, 1, 1)
    inner = jnp.sum(dprob * prob, axis=0, keepdims=True)
    dscores = (prob * (dprob - inner)).astype(BF)
    dquery = fold(mm(dscores, keyed, 0, 0), mask, slot, group) * scale
    dkeyed = mm(dscores, spread(query, mask, group)) * scale
    dvalued = mm(low, dspread)
    return dquery.astype(BF), dkeyed.astype(BF), dvalued.astype(BF)


def attention_backward_chunk(
    heads, length_of, x_ref, cot_ref, dm_ref, h_ref, act, q, k, v, ctx, p_ref,
    wq, wk, wv, wo, g1, g2, ig_o, dq_s, dk_s, dv_s, dctx_s, gq, gk, gv, go, norms,
):
    count, slot, width = x_ref.shape
    head = width // heads
    group = max(1, min(heads, 256 // head))
    span = group * head
    scale = head ** -0.5
    mask = block_diagonal(group, slot, head)
    place = lax.broadcasted_iota(jnp.int32, (slot, width), 0)
    flat = lambda value: value.astype(F32).reshape(count * slot, width)
    normed2, inverse2 = normalize(h_ref[...])
    dm = flat(dm_ref[...])
    cot = cot_ref[...].astype(F32)
    gt = jnp.concatenate(
        [jnp.where(place < length_of(s), cot[s], 0.0) for s in range(count)], axis=0
    )
    dhidden = gt + layer_norm_pull(dm, normed2, inverse2, g2[...])
    norms[2:3] += row_sum(dm * normed2, width)
    norms[3:4] += row_sum(dm, width)
    dattn = dhidden.astype(BF)
    go[...] += mm(ctx[...], dattn, 0, 0)
    dctx_s[...] = mm(dattn, wo[...], 1, 1).astype(BF)
    for s in range(count):
        rows = slice(s * slot, (s + 1) * slot)
        for part in range(heads // group):
            cols = slice(part * span, (part + 1) * span)
            dq_s[rows, cols], dk_s[rows, cols], dv_s[rows, cols] = attention_pull(
                dctx_s[rows, cols], q[rows, cols], k[rows, cols], v[rows, cols],
                p_ref[s, part], mask, slot, group, scale,
            )
    dq, dk, dv = dq_s[...], dk_s[...], dv_s[...]
    gq[...] += mm(act[...], dq, 0, 0)
    gk[...] += mm(act[...], dk, 0, 0)
    gv[...] += mm(act[...], dv, 0, 0)
    dact = mm(dq, wq[...], 1, 1) + mm(dk, wk[...], 1, 1) + mm(dv, wv[...], 1, 1)
    normed1, inverse1 = normalize(flat(x_ref[...]))
    norms[0:1] += row_sum(dact * normed1, width)
    norms[1:2] += row_sum(dact, width)
    dx = dhidden + layer_norm_pull(dact, normed1, inverse1, g1[...])
    ig_o[...] = dx.astype(BF).reshape(count, slot, width)


def attention_backward_kernel(
    heads, len_ref, x_ref, cot_ref, dm_ref, h_ref, act, q, k, v, ctx, p_ref,
    wq, wk, wv, wo, g1, g2, ig_o, gq, gk, gv, go, norms, dq_s, dk_s, dv_s, dctx_s,
):
    step = pl.program_id(0)
    count = x_ref.shape[0]

    @pl.when(step == 0)
    def _():
        for total in (gq, gk, gv, go, norms):
            total[...] = jnp.zeros_like(total)

    attention_backward_chunk(
        heads, lambda s: len_ref[step * count + s], x_ref, cot_ref, dm_ref, h_ref,
        act, q, k, v, ctx, p_ref, wq, wk, wv, wo, g1, g2, ig_o,
        dq_s, dk_s, dv_s, dctx_s, gq, gk, gv, go, norms,
    )


def attention_backward(
    lengths, tokens, cot, dm, hidden, act, q, k, v, ctx, prob, wq, wk, wv, wo, g1, g2, heads
):
    sents, slot, width = tokens.shape
    count = 4 if sents % 4 == 0 else 1
    rows = count * slot
    head = width // heads
    group = max(1, min(heads, 256 // head))
    whole = lambda *shape: pl.BlockSpec(shape, lambda i: (0,) * len(shape))
    flat = pl.BlockSpec((rows, width), lambda i: (i, 0))
    cube = pl.BlockSpec((count, slot, width), lambda i: (i, 0, 0))
    probs = pl.BlockSpec((count, heads // group, slot, group * slot), lambda i: (i, 0, 0, 0))
    shape = jax.ShapeDtypeStruct
    total = sents * slot
    return pl.pallas_call(
        functools.partial(attention_backward_kernel, heads),
        grid=(sents // count,),
        in_specs=[pl.BlockSpec(memory_space=pltpu.SMEM), cube, cube, cube]
        + [flat] * 6 + [probs]
        + [whole(width, width)] * 4
        + [whole(1, width)] * 2,
        out_specs=[cube] + [whole(width, width)] * 4 + [whole(8, width)],
        out_shape=[shape((sents, slot, width), BF)]
        + [shape((width, width), F32)] * 4
        + [shape((8, width), F32)],
        scratch_shapes=[VM((rows, width), BF)] * 4,
        compiler_params=pltpu.CompilerParams(
            dimension_semantics=("arbitrary",), vmem_limit_bytes=56 * 2**20
        ),
        cost_estimate=pl.CostEstimate(
            flops=16 * total * width * width + 10 * total * slot * width,
            bytes_accessed=24 * total * width,
            transcendentals=0,
        ),
    )(lengths, tokens, cot, dm, hidden, act, q, k, v, ctx, prob, wq, wk, wv, wo, g1[None], g2[None])


def local(
    tokens,
    lengths,
    tasks,
    routes,
    gate_table,
    ln1_gain,
    ln1_bias,
    ln2_gain,
    ln2_bias,
    w_query,
    w_key,
    w_value,
    w_out,
    w_in,
    w_back,
    cotangent,
):
    sents, slot, width = tokens.shape
    heads = HEADS
    experts = gate_table.shape[1]
    ntasks = routes.shape[0]
    capacity = max(1, 4 * sents // experts)
    task_hot = (tasks[:, None] == jnp.arange(ntasks)[None, :]).astype(jnp.int32)
    chosen = jnp.sum(task_hot[:, :, None] * routes[None, :, :], axis=1)
    flat = chosen.reshape(-1)
    order = jnp.arange(2 * sents)
    earlier = (flat[:, None] == flat[None, :]) & (order[None, :] < order[:, None])
    rank = jnp.sum(earlier.astype(jnp.int32), axis=1)
    slot_id = flat * capacity + rank
    placed = rank < capacity
    dispatch = (
        (jnp.arange(experts * capacity)[:, None] == slot_id[None, :]) & placed[None, :]
    ).astype(jnp.bfloat16)
    collect = dispatch.T
    expert_hot = (chosen[:, :, None] == jnp.arange(experts)[None, None, :]).astype(jnp.float32)
    valid = (jnp.arange(slot)[None, :] < lengths[:, None]).astype(jnp.float32)
    mask3 = valid[:, :, None]
    act, query, keyed, valued, context, prob, hidden, mixed, attn_sum = attention_forward(
        tokens, lengths, w_query, w_key, w_value, w_out,
        ln1_gain, ln1_bias, ln2_gain, ln2_bias, heads,
    )
    hidden_res = hidden.reshape(sents, slot, width)
    table_rows = jnp.dot(task_hot.astype(jnp.float32), gate_table, precision=lax.Precision.HIGHEST)
    picked = jnp.sum(expert_hot * table_rows[:, None, :], axis=-1)
    gate_values = jax.nn.softmax(picked, axis=-1)
    grad_total = cotangent.astype(jnp.float32) * mask3
    copies = jnp.broadcast_to(mixed[:, None], (sents, 2, slot, width)).reshape(
        2 * sents, slot * width
    )
    outgoing = (
        project(dispatch, copies).astype(jnp.bfloat16).reshape(experts, capacity, slot, width)
    )
    dycopy = (
        (gate_values[:, :, None, None] * grad_total[:, None])
        .astype(jnp.bfloat16)
        .reshape(2 * sents, slot * width)
    )
    grad_out = (
        project(dispatch, dycopy).astype(jnp.bfloat16).reshape(experts, capacity, slot, width)
    )
    incoming = lax.all_to_all(outgoing, "expert", split_axis=0, concat_axis=0, tiled=True).reshape(
        -1, width
    )
    pre_act, active, produced = expert_forward(incoming, w_in[0], w_back[0])
    returned = lax.all_to_all(
        produced.reshape(experts, capacity, slot, width),
        "expert",
        split_axis=0,
        concat_axis=0,
        tiled=True,
    )
    grad_in = lax.all_to_all(grad_out, "expert", split_axis=0, concat_axis=0, tiled=True).reshape(
        -1, width
    )
    in_local, back_local, dincoming = expert_backward(
        incoming, pre_act, active, grad_in, w_in[0], w_back[0]
    )
    grad_back = lax.all_to_all(
        dincoming.reshape(experts, capacity, slot, width),
        "expert",
        split_axis=0,
        concat_axis=0,
        tiled=True,
    )
    ycopy = project(collect, returned.reshape(experts * capacity, slot * width)).reshape(
        sents, 2, slot, width
    )
    expert_mixture = jnp.sum(gate_values[:, :, None, None] * ycopy, axis=1)
    total = mask3 * (hidden_res + expert_mixture)
    output = total.astype(jnp.bfloat16)
    stats_local = jnp.stack(
        [
            jnp.sum(total * total),
            jnp.sum(attn_sum),
            jnp.sum(mask3 * expert_mixture * expert_mixture),
            jnp.sum(valid),
        ]
    )
    stat_totals = lax.psum(stats_local, ("dp", "expert"))
    gate_dot = jnp.sum(ycopy * grad_total[:, None], axis=(2, 3))
    dpicked = gate_values * (gate_dot - jnp.sum(gate_values * gate_dot, axis=-1, keepdims=True))
    dlogits = jnp.sum(expert_hot * dpicked[:, :, None], axis=1)
    table_grad = jnp.dot(task_hot.T.astype(jnp.float32), dlogits, precision=lax.Precision.HIGHEST)
    dmixed = project(collect, grad_back.reshape(experts * capacity, slot * width)).reshape(
        sents, 2, slot, width
    )
    dmixed = jnp.sum(dmixed, axis=1)
    input_grad, wq_grad, wk_grad, wv_grad, wout_grad, norms = attention_backward(
        lengths, tokens, cotangent, dmixed, hidden, act, query, keyed, valued, context, prob,
        w_query, w_key, w_value, w_out, ln1_gain, ln2_gain, heads,
    )
    gain1_grad, bias1_grad, gain2_grad, bias2_grad = norms[0], norms[1], norms[2], norms[3]
    members = (
        wq_grad,
        wk_grad,
        wv_grad,
        wout_grad,
        gain1_grad,
        bias1_grad,
        gain2_grad,
        bias2_grad,
        table_grad,
    )
    members = members + ()
    summed = lax.psum(members, ("dp", "expert"))
    rms = jnp.sqrt(stat_totals[0:3] / (stat_totals[3] * width))
    in_share, back_share = (
        lax.psum_scatter(
            in_local.astype(jnp.bfloat16), "dp", scatter_dimension=0, tiled=True
        ).astype(jnp.float32),
        lax.psum_scatter(
            back_local.astype(jnp.bfloat16), "dp", scatter_dimension=0, tiled=True
        ).astype(jnp.float32),
    )
    return (
        output,
        input_grad,
        summed[8],
        summed[4],
        summed[5],
        summed[6],
        summed[7],
        summed[0],
        summed[1],
        summed[2],
        summed[3],
        in_share[None],
        back_share[None],
        rms,
    )


def solution(mesh):
    in_specs = (
        P(("dp", "expert"), None, None),
        P(("dp", "expert")),
        P(("dp", "expert")),
        P(),
        P(),
        P(),
        P(),
        P(),
        P(),
        P(),
        P(),
        P(),
        P(),
        P("expert", None, None),
        P("expert", None, None),
        P(("dp", "expert"), None, None),
    )
    out_specs = (
        P(("dp", "expert"), None, None),
        P(("dp", "expert"), None, None),
        P(),
        P(),
        P(),
        P(),
        P(),
        P(),
        P(),
        P(),
        P(),
        P("expert", "dp", None),
        P("expert", "dp", None),
        P(),
    )
    return jax.shard_map(local, mesh=mesh, in_specs=in_specs, out_specs=out_specs, check_vma=False)
```

```python
import functools

import jax
import jax.numpy as jnp
from jax import lax
from jax.experimental import pallas as pl
from jax.experimental.pallas import tpu as pltpu
from jax.sharding import PartitionSpec as P

HEADS = 8


def normalize(value):
    centered = value - jnp.mean(value, axis=-1, keepdims=True)
    variance = jnp.mean(centered * centered, axis=-1, keepdims=True)
    inverse = lax.rsqrt(variance + 1e-05)
    return (centered * inverse, inverse)


def project(left, right):
    return jnp.dot(left, right, preferred_element_type=jnp.float32)


def expert_forward(incoming, first, second):
    pre_act = project(incoming, first)
    active = jax.nn.gelu(pre_act).astype(jnp.bfloat16)
    produced = project(active, second).astype(jnp.bfloat16)
    return (pre_act, active, produced)


def expert_backward(incoming, pre_act, active, grad_in, first, second):
    dactive = project(grad_in, second.T)
    back_local = project(active.T, grad_in)
    gelu_pull = jax.vjp(jax.nn.gelu, pre_act)[1]
    dpre = gelu_pull(dactive)[0].astype(jnp.bfloat16)
    in_local = project(incoming.T, dpre)
    dincoming = project(dpre, first.T).astype(jnp.bfloat16)
    return (in_local, back_local, dincoming)


BF = jnp.bfloat16
F32 = jnp.float32
VM = pltpu.VMEM


def mm(a, b, ca=1, cb=0):
    return lax.dot_general(a, b, (((ca,), (cb,)), ((), ())), preferred_element_type=F32)


def block_diagonal(group, slot, head):
    shape = (group * slot, group * head)
    rows = lax.broadcasted_iota(jnp.int32, shape, 0) // slot
    cols = lax.broadcasted_iota(jnp.int32, shape, 1) // head
    return rows == cols


def spread(part, mask, group):
    return jnp.where(mask, jnp.concatenate([part] * group, axis=0), jnp.zeros((), part.dtype))


def fold(product, mask, slot, group):
    kept = jnp.where(mask, product, 0.0)
    total = kept[0:slot]
    for one in range(1, group):
        total = total + kept[one * slot : (one + 1) * slot]
    return total


def attend(query, keyed, valued, length, mask, slot, group, scale):
    scores = mm(keyed, spread(query, mask, group), 1, 1) * scale
    place = lax.broadcasted_iota(jnp.int32, scores.shape, 0)
    scores = jnp.where(place < length, scores, -1000000000.0)
    raised = jnp.exp(scores - jnp.max(scores, axis=0, keepdims=True))
    prob = raised / jnp.sum(raised, axis=0, keepdims=True)
    context = fold(mm(prob.astype(BF), valued, 0, 0), mask, slot, group)
    return prob, context


def attention_forward_kernel(
    heads, len_ref, x_ref, wq, wk, wv, wo, g1, b1, g2, b2,
    act_o, q_o, k_o, v_o, ctx_o, p_o, h_o, m_o, st_o,
):
    count, slot, width = x_ref.shape
    head = width // heads
    group = max(1, min(heads, 256 // head))
    span = group * head
    step = pl.program_id(0)
    scale = head ** -0.5
    mask = block_diagonal(group, slot, head)
    x = x_ref[...].astype(F32).reshape(count * slot, width)
    normed, _ = normalize(x)
    act = (normed * g1[...] + b1[...]).astype(BF)
    act_o[...] = act
    q_o[...] = mm(act, wq[...]).astype(BF)
    k_o[...] = mm(act, wk[...]).astype(BF)
    v_o[...] = mm(act, wv[...]).astype(BF)
    for s in range(count):
        length = len_ref[step * count + s]
        rows = slice(s * slot, (s + 1) * slot)
        for part in range(heads // group):
            cols = slice(part * span, (part + 1) * span)
            prob, context = attend(
                q_o[rows, cols], k_o[rows, cols], v_o[rows, cols], length, mask, slot, group, scale
            )
            p_o[s, part] = prob
            ctx_o[rows, cols] = context.astype(BF)
    attn = mm(ctx_o[...], wo[...])
    hidden = x + attn
    h_o[...] = hidden
    normed2, _ = normalize(hidden)
    m_o[...] = (normed2 * g2[...] + b2[...]).astype(BF).reshape(count, slot, width)
    place = lax.broadcasted_iota(jnp.int32, (slot, width), 0)
    total = jnp.zeros((1, width), F32)
    for s in range(count):
        length = len_ref[step * count + s]
        part = attn[s * slot : (s + 1) * slot]
        total = total + jnp.sum(jnp.where(place < length, part * part, 0.0), axis=0, keepdims=True)

    @pl.when(step == 0)
    def _():
        st_o[...] = jnp.zeros_like(st_o)

    st_o[...] += total


def attention_forward(tokens, lengths, wq, wk, wv, wo, g1, b1, g2, b2, heads):
    sents, slot, width = tokens.shape
    count = 4 if sents % 4 == 0 else 1
    rows = count * slot
    head = width // heads
    group = max(1, min(heads, 256 // head))
    whole = lambda *shape: pl.BlockSpec(shape, lambda i: (0,) * len(shape))
    flat = pl.BlockSpec((rows, width), lambda i: (i, 0))
    cube = pl.BlockSpec((count, slot, width), lambda i: (i, 0, 0))
    probs = pl.BlockSpec((count, heads // group, slot, group * slot), lambda i: (i, 0, 0, 0))
    shape = jax.ShapeDtypeStruct
    total = sents * slot
    return pl.pallas_call(
        functools.partial(attention_forward_kernel, heads),
        grid=(sents // count,),
        in_specs=[pl.BlockSpec(memory_space=pltpu.SMEM), cube]
        + [whole(width, width)] * 4
        + [whole(1, width)] * 4,
        out_specs=[flat] * 5 + [probs, flat, cube, whole(1, width)],
        out_shape=[shape((total, width), BF)] * 5
        + [
            shape((sents, heads // group, slot, group * slot), F32),
            shape((total, width), F32),
            shape((sents, slot, width), BF),
            shape((1, width), F32),
        ],
        compiler_params=pltpu.CompilerParams(
            dimension_semantics=("arbitrary",), vmem_limit_bytes=56 * 2**20
        ),
        cost_estimate=pl.CostEstimate(
            flops=8 * total * width * width + 4 * total * slot * width,
            bytes_accessed=16 * total * width,
            transcendentals=total * slot * heads,
        ),
    )(lengths, tokens, wq, wk, wv, wo, g1[None], b1[None], g2[None], b2[None])


def row_sum(value, width):
    return jnp.sum(value, axis=0, keepdims=True)


def layer_norm_pull(grad, normed, inverse, gain):
    scaled = grad * gain
    inner = scaled - jnp.mean(scaled, axis=-1, keepdims=True)
    inner = inner - normed * jnp.mean(scaled * normed, axis=-1, keepdims=True)
    return inverse * inner


def attention_pull(dcontext, query, keyed, valued, prob, mask, slot, group, scale):
    low = prob.astype(BF)
    dspread = spread(dcontext, mask, group)
    dprob = mm(valued, dspread, 1, 1)
    inner = jnp.sum(dprob * prob, axis=0, keepdims=True)
    dscores = (prob * (dprob - inner)).astype(BF)
    dquery = fold(mm(dscores, keyed, 0, 0), mask, slot, group) * scale
    dkeyed = mm(dscores, spread(query, mask, group)) * scale
    dvalued = mm(low, dspread)
    return dquery.astype(BF), dkeyed.astype(BF), dvalued.astype(BF)


def attention_backward_chunk(
    heads, length_of, x_ref, cot_ref, dm_ref, h_ref, act, q, k, v, ctx, p_ref,
    wq, wk, wv, wo, g1, g2, ig_o, dq_s, dk_s, dv_s, dctx_s, gq, gk, gv, go, norms,
):
    count, slot, width = x_ref.shape
    head = width // heads
    group = max(1, min(heads, 256 // head))
    span = group * head
    scale = head ** -0.5
    mask = block_diagonal(group, slot, head)
    place = lax.broadcasted_iota(jnp.int32, (slot, width), 0)
    flat = lambda value: value.astype(F32).reshape(count * slot, width)
    normed2, inverse2 = normalize(h_ref[...])
    dm = flat(dm_ref[...])
    cot = cot_ref[...].astype(F32)
    gt = jnp.concatenate(
        [jnp.where(place < length_of(s), cot[s], 0.0) for s in range(count)], axis=0
    )
    dhidden = gt + layer_norm_pull(dm, normed2, inverse2, g2[...])
    norms[2:3] += row_sum(dm * normed2, width)
    norms[3:4] += row_sum(dm, width)
    dattn = dhidden.astype(BF)
    go[...] += mm(ctx[...], dattn, 0, 0)
    dctx_s[...] = mm(dattn, wo[...], 1, 1).astype(BF)
    for s in range(count):
        rows = slice(s * slot, (s + 1) * slot)
        for part in range(heads // group):
            cols = slice(part * span, (part + 1) * span)
            dq_s[rows, cols], dk_s[rows, cols], dv_s[rows, cols] = attention_pull(
                dctx_s[rows, cols], q[rows, cols], k[rows, cols], v[rows, cols],
                p_ref[s, part], mask, slot, group, scale,
            )
    dq, dk, dv = dq_s[...], dk_s[...], dv_s[...]
    gq[...] += mm(act[...], dq, 0, 0)
    gk[...] += mm(act[...], dk, 0, 0)
    gv[...] += mm(act[...], dv, 0, 0)
    dact = mm(dq, wq[...], 1, 1) + mm(dk, wk[...], 1, 1) + mm(dv, wv[...], 1, 1)
    normed1, inverse1 = normalize(flat(x_ref[...]))
    norms[0:1] += row_sum(dact * normed1, width)
    norms[1:2] += row_sum(dact, width)
    dx = dhidden + layer_norm_pull(dact, normed1, inverse1, g1[...])
    ig_o[...] = dx.astype(BF).reshape(count, slot, width)


def attention_backward_kernel(
    heads, len_ref, x_ref, cot_ref, dm_ref, h_ref, act, q, k, v, ctx, p_ref,
    wq, wk, wv, wo, g1, g2, ig_o, gq, gk, gv, go, norms, dq_s, dk_s, dv_s, dctx_s,
):
    step = pl.program_id(0)
    count = x_ref.shape[0]

    @pl.when(step == 0)
    def _():
        for total in (gq, gk, gv, go, norms):
            total[...] = jnp.zeros_like(total)

    attention_backward_chunk(
        heads, lambda s: len_ref[step * count + s], x_ref, cot_ref, dm_ref, h_ref,
        act, q, k, v, ctx, p_ref, wq, wk, wv, wo, g1, g2, ig_o,
        dq_s, dk_s, dv_s, dctx_s, gq, gk, gv, go, norms,
    )


def attention_backward(
    lengths, tokens, cot, dm, hidden, act, q, k, v, ctx, prob, wq, wk, wv, wo, g1, g2, heads
):
    sents, slot, width = tokens.shape
    count = 4 if sents % 4 == 0 else 1
    rows = count * slot
    head = width // heads
    group = max(1, min(heads, 256 // head))
    whole = lambda *shape: pl.BlockSpec(shape, lambda i: (0,) * len(shape))
    flat = pl.BlockSpec((rows, width), lambda i: (i, 0))
    cube = pl.BlockSpec((count, slot, width), lambda i: (i, 0, 0))
    probs = pl.BlockSpec((count, heads // group, slot, group * slot), lambda i: (i, 0, 0, 0))
    shape = jax.ShapeDtypeStruct
    total = sents * slot
    return pl.pallas_call(
        functools.partial(attention_backward_kernel, heads),
        grid=(sents // count,),
        in_specs=[pl.BlockSpec(memory_space=pltpu.SMEM), cube, cube, cube]
        + [flat] * 6 + [probs]
        + [whole(width, width)] * 4
        + [whole(1, width)] * 2,
        out_specs=[cube] + [whole(width, width)] * 4 + [whole(8, width)],
        out_shape=[shape((sents, slot, width), BF)]
        + [shape((width, width), F32)] * 4
        + [shape((8, width), F32)],
        scratch_shapes=[VM((rows, width), BF)] * 4,
        compiler_params=pltpu.CompilerParams(
            dimension_semantics=("arbitrary",), vmem_limit_bytes=56 * 2**20
        ),
        cost_estimate=pl.CostEstimate(
            flops=16 * total * width * width + 10 * total * slot * width,
            bytes_accessed=24 * total * width,
            transcendentals=0,
        ),
    )(lengths, tokens, cot, dm, hidden, act, q, k, v, ctx, prob, wq, wk, wv, wo, g1[None], g2[None])


MESH_ID = pl.DeviceIdType.MESH
CORE, NEAR, FAR = 1, 2, 4


def plane_peer(relation):
    me = lax.axis_index("expert")
    bits = []
    for bit in (CORE, NEAR, FAR):
        value = (me // bit) % 2
        bits.append((1 - value if relation & bit else value) * bit)
    return bits[0] + bits[1] + bits[2]


def remote(src, dst, sends, recvs, index, relation):
    return pltpu.make_async_remote_copy(
        src_ref=src,
        dst_ref=dst,
        send_sem=sends.at[index],
        recv_sem=recvs.at[index],
        device_id=(lax.axis_index("dp"), plane_peer(relation)),
        device_id_type=MESH_ID,
    )


def plane_barrier():
    barrier = pltpu.get_barrier_semaphore()
    for relation in range(1, 8):
        pl.semaphore_signal(
            barrier,
            inc=1,
            device_id=(lax.axis_index("dp"), plane_peer(relation)),
            device_id_type=MESH_ID,
        )
    pl.semaphore_wait(barrier, 7)


def gather_copies(own, held, sends, recvs, base):
    half = own.shape[0] // 2
    low, high = pl.ds(0, half), pl.ds(half, half)
    plan = [
        (own.at[low], held[2].at[low], NEAR),
        (own.at[high], held[4].at[high], FAR),
        (own, held[1], CORE),
        (own.at[high], held[2].at[high], NEAR),
        (own.at[low], held[4].at[low], FAR),
        (held[2].at[low], held[6].at[low], FAR),
        (held[4].at[high], held[6].at[high], NEAR),
        (held[2], held[3], CORE),
        (held[4], held[5], CORE),
        (held[6], held[7], CORE),
    ]
    return [
        remote(src, dst, sends, recvs, base + place, relation)
        for place, (src, dst, relation) in enumerate(plan)
    ]


def return_copies(parts, cores, sides, sends, recvs, base):
    half = parts[0].shape[0] // 2
    low, high = pl.ds(0, half), pl.ds(half, half)
    plan = [
        (parts[1], cores[0], CORE),
        (parts[3], cores[2], CORE),
        (parts[5], cores[4], CORE),
        (parts[7], cores[6], CORE),
        (parts[2].at[low], sides[0], NEAR),
        (parts[6].at[low], sides[1], NEAR),
        (parts[4].at[high], sides[2], FAR),
        (parts[6].at[high], sides[3], FAR),
        (parts[4].at[low], sides[4], FAR),
        (parts[2].at[high], sides[5], NEAR),
    ]
    return [
        remote(src, dst, sends, recvs, base + place, relation)
        for place, (src, dst, relation) in enumerate(plan)
    ]


def add_into(target, start, other, count):
    def one(i, carry):
        total = target[start + i].astype(F32) + other[i].astype(F32)
        target[start + i] = total.astype(BF)
        return carry

    lax.fori_loop(0, count, one, 0)


def return_finish(parts, sides, back, out):
    half = out.shape[0] // 2
    back[4].wait_recv()
    add_into(parts[0], 0, sides[0], half)
    back[5].wait_recv()
    add_into(parts[4], 0, sides[1], half)
    back[8].start()
    back[6].wait_recv()
    add_into(parts[0], half, sides[2], half)
    back[7].wait_recv()
    add_into(parts[2], half, sides[3], half)
    back[9].start()
    back[8].wait_recv()
    add_into(parts[0], 0, sides[4], half)
    back[9].wait_recv()
    add_into(parts[0], half, sides[5], half)

    def one(i, carry):
        out[i] = parts[0][i]
        return carry

    lax.fori_loop(0, out.shape[0], one, 0)
    for copy in back:
        copy.wait_send()


GELU_A = 0.7978845608028654
GELU_B = 0.044715


def expert_kernel(
    cap, tab, gates, m, cot, win, wback, dm_o, py_o, gin_o, gback_o, dg_o, *scratch
):
    sents, slot, width = m.shape
    hidden = win.shape[1]
    held_m = dict(zip(range(1, 8), scratch[0:7]))
    held_c = dict(zip(range(1, 8), scratch[7:14]))
    parts = dict(zip(range(8), scratch[14:22]))
    cores = dict(zip((0, 2, 4, 6), scratch[22:26]))
    sides = scratch[26:32]
    xs, gs, dys, zs, dus, ys, dms, stage, dg_s, accb, acci, sends, recvs, local = scratch[32:]
    me = lax.axis_index("expert")
    tile = min(512, hidden)
    entries = 2 * cap + sents

    plane_barrier()
    to_m = gather_copies(m, held_m, sends, recvs, 0)
    to_c = gather_copies(cot, held_c, sends, recvs, 10)
    back = return_copies(parts, cores, sides, sends, recvs, 20)
    gates_back = {
        r: remote(dg_s.at[r], dg_o.at[r], sends, recvs, 30 + r, r) for r in range(1, 8)
    }
    for place in (0, 1, 2):
        to_m[place].start()
        to_c[place].start()
    for place in (3, 4):
        to_m[place].start()
        to_c[place].start()
    accb[...] = jnp.zeros_like(accb)
    acci[...] = jnp.zeros_like(acci)
    place = lax.broadcasted_iota(jnp.int32, (slot, width), 0)
    held_m[0], held_c[0] = m, cot

    def arrive(*indices):
        for index in indices:
            to_m[index].wait_recv()
            to_c[index].wait_recv()

    def forward(*indices):
        for index in indices:
            to_m[index].start()
            to_c[index].start()

    def before(r):
        if r == 1:
            arrive(2)
        if r == 2:
            arrive(0, 1)
            forward(5, 6)
            arrive(3)
            forward(7)
            arrive(4)
            forward(8)
        if r == 3:
            arrive(7)
        if r == 5:
            arrive(8)
        if r == 6:
            arrive(5, 6)
            forward(9)
        if r == 7:
            arrive(9)
        source = plane_peer(r)

        def fetch(j, carry):
            index = tab[source, me * entries + j]
            length = tab[source, me * entries + cap + j]
            gate = gates[source, me * cap + j]
            xs[j] = held_m[r][index]
            gt = jnp.where(place < length, held_c[r][index].astype(F32), 0.0)
            gs[j] = gt.astype(BF)
            dys[j] = (gt * gate).astype(BF)
            return carry

        lax.fori_loop(0, cap, fetch, 0)

    def after(r):
        source = plane_peer(r)
        if r >= 2:
            pltpu.make_async_copy(stage.at[r % 2], py_o.at[r - 2], local.at[r % 2]).wait()

        def give(i, carry):
            index = tab[source, me * entries + 2 * cap + i]
            there = jnp.maximum(index, 0)
            gate = gates[source, me * cap + there]
            hit = (index >= 0).astype(F32)
            parts[r][i] = (dms[there].astype(F32) * hit).astype(BF)
            stage[r % 2, i] = (ys[there].astype(F32) * (hit * gate)).astype(BF)
            return carry

        lax.fori_loop(0, sents, give, 0)
        pltpu.make_async_copy(stage.at[r % 2], py_o.at[r], local.at[r % 2]).start()

        def dots(j, carry):
            product = ys[j].astype(F32) * gs[j].astype(F32)
            total = jnp.sum(jnp.sum(product, axis=0, keepdims=True), axis=1, keepdims=True)
            if r == 0:
                dg_o[0, pl.ds(j, 1)] = jnp.broadcast_to(total, (1, 128))
            else:
                dg_s[r, pl.ds(j, 1)] = jnp.broadcast_to(total, (1, 128))
            return carry

        lax.fori_loop(0, cap, dots, 0)
        if r > 0:
            gates_back[r].start()
        if r % 2 == 1:
            back[r // 2].start()
        if r == 4:
            back[1].wait_recv()
            add_into(parts[2], 0, cores[2], sents)
            back[4].start()
        if r == 6:
            back[2].wait_recv()
            add_into(parts[4], 0, cores[4], sents)
            back[6].start()
        if r == 7:
            back[3].wait_recv()
            add_into(parts[6], 0, cores[6], sents)
            back[5].start()
            back[7].start()
            back[0].wait_recv()
            add_into(parts[0], 0, cores[0], sents)

    def chunk(t, carry):
        for r in range(8):
            pl.when(t == r)(functools.partial(before, r))
        x = xs[...].reshape(cap * slot, width)
        dy = dys[...].reshape(cap * slot, width)

        def inner(f, carry):
            cols = pl.ds(pl.multiple_of(f * tile, tile), tile)
            u = mm(x, win[:, cols])
            square = u * u
            th = jnp.tanh(u * (GELU_A + GELU_A * GELU_B * square))
            cdf = 0.5 + 0.5 * th
            slope = cdf + (0.5 * u) * (1.0 - th * th) * (GELU_A + 3 * GELU_A * GELU_B * square)
            z = (u * cdf).astype(BF)
            zs[:, cols] = z
            dz = mm(dy, wback[cols, :], 1, 1)
            du = (dz * slope).astype(BF)
            dus[:, cols] = du
            accb[cols, :] += mm(z, dy, 0, 0)
            acci[:, cols] += mm(x, du, 0, 0)
            return carry

        lax.fori_loop(0, hidden // tile, inner, 0)
        ys[...] = mm(zs[...], wback[...]).astype(BF).reshape(cap, slot, width)
        dms[...] = mm(dus[...], win[...], 1, 1).astype(BF).reshape(cap, slot, width)
        for r in range(8):
            pl.when(t == r)(functools.partial(after, r))
        return carry

    lax.fori_loop(0, 8, chunk, 0)
    gin_o[...] = acci[...].astype(BF)
    gback_o[...] = accb[...].astype(BF)
    return_finish(parts, sides, back, dm_o)
    for r in range(1, 8):
        gates_back[r].wait()
    for index in range(10):
        to_m[index].wait_send()
        to_c[index].wait_send()
    for r in (6, 7):
        pltpu.make_async_copy(stage.at[r % 2], py_o.at[r], local.at[r % 2]).wait()


def expert_exchange(tab, gates, m, cot, win, wback, cap):
    sents, slot, width = m.shape
    hidden = win.shape[1]
    vm = pl.BlockSpec(memory_space=VM)
    sm = pl.BlockSpec(memory_space=pltpu.SMEM)
    shape = jax.ShapeDtypeStruct
    cube = (sents, slot, width)
    rows = cap * slot
    return pl.pallas_call(
        functools.partial(expert_kernel, cap),
        in_specs=[sm, sm, vm, vm, vm, vm],
        out_specs=[vm, pl.BlockSpec(memory_space=pl.ANY), vm, vm, vm],
        out_shape=[
            shape(cube, BF),
            shape((8,) + cube, BF),
            shape((width, hidden), BF),
            shape((hidden, width), BF),
            shape((8, cap, 128), F32),
        ],
        scratch_shapes=[VM(cube, BF)] * (14 + 8 + 4)
        + [VM((sents // 2, slot, width), BF)] * 6
        + [VM((cap, slot, width), BF)] * 3
        + [VM((rows, hidden), BF)] * 2
        + [VM((cap, slot, width), BF)] * 2
        + [VM((2,) + cube, BF), VM((8, cap, 128), F32)]
        + [VM((hidden, width), F32), VM((width, hidden), F32)]
        + [
            pltpu.SemaphoreType.DMA((38,)),
            pltpu.SemaphoreType.DMA((38,)),
            pltpu.SemaphoreType.DMA((2,)),
        ],
        compiler_params=pltpu.CompilerParams(
            collective_id=1, has_side_effects=True, vmem_limit_bytes=63 * 2**20
        ),
        cost_estimate=pl.CostEstimate(
            flops=12 * 8 * rows * width * hidden, bytes_accessed=40 * 2**20, transcendentals=0
        ),
    )(tab, gates, m, cot, win, wback)


def combine_kernel(py, out, *scratch):
    parts = dict(zip(range(8), scratch[0:8]))
    cores = dict(zip((0, 2, 4, 6), scratch[8:12]))
    sides = scratch[12:18]
    sends, recvs, local = scratch[18:]
    sents = out.shape[0]
    loads = [pltpu.make_async_copy(py.at[r], parts[r], local.at[r]) for r in range(8)]
    for load in loads:
        load.start()
    plane_barrier()
    back = return_copies(parts, cores, sides, sends, recvs, 0)
    for r in (1, 3, 5, 7):
        loads[r].wait()
        back[r // 2].start()
    for r, starts in ((6, (5, 7)), (2, (4,)), (4, (6,)), (0, ())):
        loads[r].wait()
        back[r // 2].wait_recv()
        add_into(parts[r], 0, cores[r], sents)
        for index in starts:
            back[index].start()
    return_finish(parts, sides, back, out)


def combine_exchange(py):
    cube = py.shape[1:]
    return pl.pallas_call(
        combine_kernel,
        in_specs=[pl.BlockSpec(memory_space=pl.ANY)],
        out_specs=pl.BlockSpec(memory_space=VM),
        out_shape=jax.ShapeDtypeStruct(cube, BF),
        scratch_shapes=[VM(cube, BF)] * 12
        + [VM((cube[0] // 2,) + cube[1:], BF)] * 6
        + [
            pltpu.SemaphoreType.DMA((10,)),
            pltpu.SemaphoreType.DMA((10,)),
            pltpu.SemaphoreType.DMA((8,)),
        ],
        compiler_params=pltpu.CompilerParams(
            collective_id=2, has_side_effects=True, vmem_limit_bytes=40 * 2**20
        ),
        cost_estimate=pl.CostEstimate(flops=0, bytes_accessed=16 * 2**20, transcendentals=0),
    )(py)


def local(
    tokens,
    lengths,
    tasks,
    routes,
    gate_table,
    ln1_gain,
    ln1_bias,
    ln2_gain,
    ln2_bias,
    w_query,
    w_key,
    w_value,
    w_out,
    w_in,
    w_back,
    cotangent,
):
    sents, slot, width = tokens.shape
    heads = HEADS
    experts = gate_table.shape[1]
    ntasks = routes.shape[0]
    capacity = max(1, 4 * sents // experts)
    task_hot = (tasks[:, None] == jnp.arange(ntasks)[None, :]).astype(jnp.int32)
    chosen = jnp.sum(task_hot[:, :, None] * routes[None, :, :], axis=1)
    flat = chosen.reshape(-1)
    order = jnp.arange(2 * sents)
    earlier = (flat[:, None] == flat[None, :]) & (order[None, :] < order[:, None])
    rank = jnp.sum(earlier.astype(jnp.int32), axis=1)
    slot_id = flat * capacity + rank
    placed = rank < capacity
    dispatch = (
        (jnp.arange(experts * capacity)[:, None] == slot_id[None, :]) & placed[None, :]
    ).astype(jnp.bfloat16)
    collect = dispatch.T
    expert_hot = (chosen[:, :, None] == jnp.arange(experts)[None, None, :]).astype(jnp.float32)
    valid = (jnp.arange(slot)[None, :] < lengths[:, None]).astype(jnp.float32)
    mask3 = valid[:, :, None]
    act, query, keyed, valued, context, prob, hidden, mixed, attn_sum = attention_forward(
        tokens, lengths, w_query, w_key, w_value, w_out,
        ln1_gain, ln1_bias, ln2_gain, ln2_bias, heads,
    )
    hidden_res = hidden.reshape(sents, slot, width)
    table_rows = jnp.dot(task_hot.astype(jnp.float32), gate_table, precision=lax.Precision.HIGHEST)
    picked = jnp.sum(expert_hot * table_rows[:, None, :], axis=-1)
    gate_values = jax.nn.softmax(picked, axis=-1)
    grad_total = cotangent.astype(jnp.float32) * mask3
    copies = jnp.broadcast_to(mixed[:, None], (sents, 2, slot, width)).reshape(
        2 * sents, slot * width
    )
    outgoing = (
        project(dispatch, copies).astype(jnp.bfloat16).reshape(experts, capacity, slot, width)
    )
    dycopy = (
        (gate_values[:, :, None, None] * grad_total[:, None])
        .astype(jnp.bfloat16)
        .reshape(2 * sents, slot * width)
    )
    grad_out = (
        project(dispatch, dycopy).astype(jnp.bfloat16).reshape(experts, capacity, slot, width)
    )
    incoming = lax.all_to_all(outgoing, "expert", split_axis=0, concat_axis=0, tiled=True).reshape(
        -1, width
    )
    pre_act, active, produced = expert_forward(incoming, w_in[0], w_back[0])
    returned = lax.all_to_all(
        produced.reshape(experts, capacity, slot, width),
        "expert",
        split_axis=0,
        concat_axis=0,
        tiled=True,
    )
    grad_in = lax.all_to_all(grad_out, "expert", split_axis=0, concat_axis=0, tiled=True).reshape(
        -1, width
    )
    in_local, back_local, dincoming = expert_backward(
        incoming, pre_act, active, grad_in, w_in[0], w_back[0]
    )
    grad_back = lax.all_to_all(
        dincoming.reshape(experts, capacity, slot, width),
        "expert",
        split_axis=0,
        concat_axis=0,
        tiled=True,
    )
    ycopy = project(collect, returned.reshape(experts * capacity, slot * width)).reshape(
        sents, 2, slot, width
    )
    expert_mixture = jnp.sum(gate_values[:, :, None, None] * ycopy, axis=1)
    total = mask3 * (hidden_res + expert_mixture)
    output = total.astype(jnp.bfloat16)
    stats_local = jnp.stack(
        [
            jnp.sum(total * total),
            jnp.sum(attn_sum),
            jnp.sum(mask3 * expert_mixture * expert_mixture),
            jnp.sum(valid),
        ]
    )
    stat_totals = lax.psum(stats_local, ("dp", "expert"))
    gate_dot = jnp.sum(ycopy * grad_total[:, None], axis=(2, 3))
    dpicked = gate_values * (gate_dot - jnp.sum(gate_values * gate_dot, axis=-1, keepdims=True))
    dlogits = jnp.sum(expert_hot * dpicked[:, :, None], axis=1)
    table_grad = jnp.dot(task_hot.T.astype(jnp.float32), dlogits, precision=lax.Precision.HIGHEST)
    dmixed = project(collect, grad_back.reshape(experts * capacity, slot * width)).reshape(
        sents, 2, slot, width
    )
    dmixed = jnp.sum(dmixed, axis=1)
    input_grad, wq_grad, wk_grad, wv_grad, wout_grad, norms = attention_backward(
        lengths, tokens, cotangent, dmixed, hidden, act, query, keyed, valued, context, prob,
        w_query, w_key, w_value, w_out, ln1_gain, ln2_gain, heads,
    )
    gain1_grad, bias1_grad, gain2_grad, bias2_grad = norms[0], norms[1], norms[2], norms[3]
    members = (
        wq_grad,
        wk_grad,
        wv_grad,
        wout_grad,
        gain1_grad,
        bias1_grad,
        gain2_grad,
        bias2_grad,
        table_grad,
    )
    members = members + ()
    summed = lax.psum(members, ("dp", "expert"))
    rms = jnp.sqrt(stat_totals[0:3] / (stat_totals[3] * width))
    in_share, back_share = (
        lax.psum_scatter(
            in_local.astype(jnp.bfloat16), "dp", scatter_dimension=0, tiled=True
        ).astype(jnp.float32),
        lax.psum_scatter(
            back_local.astype(jnp.bfloat16), "dp", scatter_dimension=0, tiled=True
        ).astype(jnp.float32),
    )
    return (
        output,
        input_grad,
        summed[8],
        summed[4],
        summed[5],
        summed[6],
        summed[7],
        summed[0],
        summed[1],
        summed[2],
        summed[3],
        in_share[None],
        back_share[None],
        rms,
    )


def local_plane(
    tokens,
    lengths,
    tasks,
    routes,
    gate_table,
    ln1_gain,
    ln1_bias,
    ln2_gain,
    ln2_bias,
    w_query,
    w_key,
    w_value,
    w_out,
    w_in,
    w_back,
    cotangent,
):
    sents, slot, width = tokens.shape
    heads = HEADS
    experts = gate_table.shape[1]
    ntasks = routes.shape[0]
    capacity = max(1, 4 * sents // experts)
    task_hot = (tasks[:, None] == jnp.arange(ntasks)[None, :]).astype(jnp.int32)
    chosen = jnp.sum(task_hot[:, :, None] * routes[None, :, :], axis=1)
    flat = chosen.reshape(-1)
    order = jnp.arange(2 * sents)
    earlier = (flat[:, None] == flat[None, :]) & (order[None, :] < order[:, None])
    rank = jnp.sum(earlier.astype(jnp.int32), axis=1)
    slot_id = flat * capacity + rank
    placed = rank < capacity
    expert_hot = (chosen[:, :, None] == jnp.arange(experts)[None, None, :]).astype(jnp.float32)
    valid = (jnp.arange(slot)[None, :] < lengths[:, None]).astype(jnp.float32)
    mask3 = valid[:, :, None]
    act, query, keyed, valued, context, prob, hidden, mixed, attn_sum = attention_forward(
        tokens, lengths, w_query, w_key, w_value, w_out,
        ln1_gain, ln1_bias, ln2_gain, ln2_bias, heads,
    )
    hidden_res = hidden.reshape(sents, slot, width)
    table_rows = jnp.dot(task_hot.astype(jnp.float32), gate_table, precision=lax.Precision.HIGHEST)
    picked = jnp.sum(expert_hot * table_rows[:, None, :], axis=-1)
    gate_values = jax.nn.softmax(picked, axis=-1)
    hits = (
        (jnp.arange(experts * capacity)[:, None] == slot_id[None, :]) & placed[None, :]
    ).astype(jnp.float32)
    per_copy = jnp.stack(
        [
            (order // 2).astype(jnp.float32),
            jnp.repeat(lengths, 2).astype(jnp.float32),
            gate_values.reshape(-1),
        ]
    )
    per_slot = jnp.sum(hits[None] * per_copy[:, None, :], axis=-1).reshape(3, experts, capacity)
    taken = (flat[None, :] == jnp.arange(experts)[:, None]) & placed[None, :]
    ranks = jnp.sum(
        (taken * (rank + 1)[None, :]).reshape(experts, sents, 2), axis=-1
    ).astype(jnp.float32)
    sent_table = jnp.concatenate([per_slot[0], per_slot[1], ranks - 1.0, per_slot[2]], axis=1)
    table = lax.all_gather(sent_table, "expert")
    entries = 2 * capacity + sents
    places = table[:, :, :entries].astype(jnp.int32).reshape(experts, -1)
    gate_slots = table[:, :, entries:].reshape(experts, -1)
    dmixed, parts_back, in_local, back_local, slot_dots = expert_exchange(
        places, gate_slots, mixed, cotangent, w_in[0], w_back[0], capacity
    )
    expert_mixture = combine_exchange(parts_back).astype(jnp.float32)
    total = mask3 * (hidden_res + expert_mixture)
    output = total.astype(jnp.bfloat16)
    stats_local = jnp.stack(
        [
            jnp.sum(total * total),
            jnp.sum(attn_sum),
            jnp.sum(mask3 * expert_mixture * expert_mixture),
            jnp.sum(valid),
        ]
    )
    stat_totals = lax.psum(stats_local, ("dp", "expert"))
    me = lax.axis_index("expert")
    dots_here = jnp.take(slot_dots[:, :, 0], me ^ jnp.arange(experts), axis=0).reshape(-1)
    gate_dot = jnp.sum(hits * dots_here[:, None], axis=0).reshape(sents, 2)
    dpicked = gate_values * (gate_dot - jnp.sum(gate_values * gate_dot, axis=-1, keepdims=True))
    dlogits = jnp.sum(expert_hot * dpicked[:, :, None], axis=1)
    table_grad = jnp.dot(task_hot.T.astype(jnp.float32), dlogits, precision=lax.Precision.HIGHEST)
    input_grad, wq_grad, wk_grad, wv_grad, wout_grad, norms = attention_backward(
        lengths, tokens, cotangent, dmixed, hidden, act, query, keyed, valued, context, prob,
        w_query, w_key, w_value, w_out, ln1_gain, ln2_gain, heads,
    )
    gain1_grad, bias1_grad, gain2_grad, bias2_grad = norms[0], norms[1], norms[2], norms[3]
    members = (
        wq_grad,
        wk_grad,
        wv_grad,
        wout_grad,
        gain1_grad,
        bias1_grad,
        gain2_grad,
        bias2_grad,
        table_grad,
    )
    members = members + ()
    summed = lax.psum(members, ("dp", "expert"))
    rms = jnp.sqrt(stat_totals[0:3] / (stat_totals[3] * width))
    in_share, back_share = (
        lax.psum_scatter(
            in_local, "dp", scatter_dimension=0, tiled=True
        ).astype(jnp.float32),
        lax.psum_scatter(
            back_local, "dp", scatter_dimension=0, tiled=True
        ).astype(jnp.float32),
    )
    return (
        output,
        input_grad,
        summed[8],
        summed[4],
        summed[5],
        summed[6],
        summed[7],
        summed[0],
        summed[1],
        summed[2],
        summed[3],
        in_share[None],
        back_share[None],
        rms,
    )


def solution(mesh):
    in_specs = (
        P(("dp", "expert"), None, None),
        P(("dp", "expert")),
        P(("dp", "expert")),
        P(),
        P(),
        P(),
        P(),
        P(),
        P(),
        P(),
        P(),
        P(),
        P(),
        P("expert", None, None),
        P("expert", None, None),
        P(("dp", "expert"), None, None),
    )
    out_specs = (
        P(("dp", "expert"), None, None),
        P(("dp", "expert"), None, None),
        P(),
        P(),
        P(),
        P(),
        P(),
        P(),
        P(),
        P(),
        P(),
        P("expert", "dp", None),
        P("expert", "dp", None),
        P(),
    )
    plane = dict(mesh.shape)["expert"]
    body = local_plane if plane == 2 * 2 * 2 else local
    return jax.shard_map(body, mesh=mesh, in_specs=in_specs, out_specs=out_specs, check_vma=False)
```

```python
import functools

import jax
import jax.numpy as jnp
from jax import lax
from jax.experimental import pallas as pl
from jax.experimental.pallas import tpu as pltpu
from jax.sharding import PartitionSpec as P

HEADS = 8


def normalize(value):
    centered = value - jnp.mean(value, axis=-1, keepdims=True)
    variance = jnp.mean(centered * centered, axis=-1, keepdims=True)
    inverse = lax.rsqrt(variance + 1e-05)
    return (centered * inverse, inverse)


def project(left, right):
    return jnp.dot(left, right, preferred_element_type=jnp.float32)


def expert_forward(incoming, first, second):
    pre_act = project(incoming, first)
    active = jax.nn.gelu(pre_act).astype(jnp.bfloat16)
    produced = project(active, second).astype(jnp.bfloat16)
    return (pre_act, active, produced)


def expert_backward(incoming, pre_act, active, grad_in, first, second):
    dactive = project(grad_in, second.T)
    back_local = project(active.T, grad_in)
    gelu_pull = jax.vjp(jax.nn.gelu, pre_act)[1]
    dpre = gelu_pull(dactive)[0].astype(jnp.bfloat16)
    in_local = project(incoming.T, dpre)
    dincoming = project(dpre, first.T).astype(jnp.bfloat16)
    return (in_local, back_local, dincoming)


BF = jnp.bfloat16
F32 = jnp.float32
VM = pltpu.VMEM


def mm(a, b, ca=1, cb=0):
    return lax.dot_general(a, b, (((ca,), (cb,)), ((), ())), preferred_element_type=F32)


def block_diagonal(group, slot, head):
    shape = (group * slot, group * head)
    rows = lax.broadcasted_iota(jnp.int32, shape, 0) // slot
    cols = lax.broadcasted_iota(jnp.int32, shape, 1) // head
    return rows == cols


def spread(part, mask, group):
    return jnp.where(mask, jnp.concatenate([part] * group, axis=0), jnp.zeros((), part.dtype))


def fold(product, mask, slot, group):
    kept = jnp.where(mask, product, 0.0)
    total = kept[0:slot]
    for one in range(1, group):
        total = total + kept[one * slot : (one + 1) * slot]
    return total


def attend(query, keyed, valued, length, mask, slot, group, scale):
    scores = mm(keyed, spread(query, mask, group), 1, 1) * scale
    place = lax.broadcasted_iota(jnp.int32, scores.shape, 0)
    scores = jnp.where(place < length, scores, -1000000000.0)
    raised = jnp.exp(scores - jnp.max(scores, axis=0, keepdims=True))
    prob = raised / jnp.sum(raised, axis=0, keepdims=True)
    context = fold(mm(prob.astype(BF), valued, 0, 0), mask, slot, group)
    return prob, context


def attention_forward_kernel(
    heads, len_ref, x_ref, wq, wk, wv, wo, g1, b1, g2, b2,
    act_o, q_o, k_o, v_o, ctx_o, p_o, h_o, m_o, st_o,
):
    count, slot, width = x_ref.shape
    head = width // heads
    group = max(1, min(heads, 256 // head))
    span = group * head
    step = pl.program_id(0)
    scale = head ** -0.5
    mask = block_diagonal(group, slot, head)
    x = x_ref[...].astype(F32).reshape(count * slot, width)
    normed, _ = normalize(x)
    act = (normed * g1[...] + b1[...]).astype(BF)
    act_o[...] = act
    q_o[...] = mm(act, wq[...]).astype(BF)
    k_o[...] = mm(act, wk[...]).astype(BF)
    v_o[...] = mm(act, wv[...]).astype(BF)
    for s in range(count):
        length = len_ref[step * count + s]
        rows = slice(s * slot, (s + 1) * slot)
        for part in range(heads // group):
            cols = slice(part * span, (part + 1) * span)
            prob, context = attend(
                q_o[rows, cols], k_o[rows, cols], v_o[rows, cols], length, mask, slot, group, scale
            )
            p_o[s, part] = prob
            ctx_o[rows, cols] = context.astype(BF)
    attn = mm(ctx_o[...], wo[...])
    hidden = x + attn
    h_o[...] = hidden
    normed2, _ = normalize(hidden)
    m_o[...] = (normed2 * g2[...] + b2[...]).astype(BF).reshape(count, slot, width)
    place = lax.broadcasted_iota(jnp.int32, (slot, width), 0)
    total = jnp.zeros((1, width), F32)
    for s in range(count):
        length = len_ref[step * count + s]
        part = attn[s * slot : (s + 1) * slot]
        total = total + jnp.sum(jnp.where(place < length, part * part, 0.0), axis=0, keepdims=True)

    @pl.when(step == 0)
    def _():
        st_o[...] = jnp.zeros_like(st_o)

    st_o[...] += total


def attention_forward(tokens, lengths, wq, wk, wv, wo, g1, b1, g2, b2, heads):
    sents, slot, width = tokens.shape
    count = 4 if sents % 4 == 0 else 1
    rows = count * slot
    head = width // heads
    group = max(1, min(heads, 256 // head))
    whole = lambda *shape: pl.BlockSpec(shape, lambda i: (0,) * len(shape))
    flat = pl.BlockSpec((rows, width), lambda i: (i, 0))
    cube = pl.BlockSpec((count, slot, width), lambda i: (i, 0, 0))
    probs = pl.BlockSpec((count, heads // group, slot, group * slot), lambda i: (i, 0, 0, 0))
    shape = jax.ShapeDtypeStruct
    total = sents * slot
    return pl.pallas_call(
        functools.partial(attention_forward_kernel, heads),
        grid=(sents // count,),
        in_specs=[pl.BlockSpec(memory_space=pltpu.SMEM), cube]
        + [whole(width, width)] * 4
        + [whole(1, width)] * 4,
        out_specs=[flat] * 5 + [probs, flat, cube, whole(1, width)],
        out_shape=[shape((total, width), BF)] * 5
        + [
            shape((sents, heads // group, slot, group * slot), F32),
            shape((total, width), F32),
            shape((sents, slot, width), BF),
            shape((1, width), F32),
        ],
        compiler_params=pltpu.CompilerParams(
            dimension_semantics=("arbitrary",), vmem_limit_bytes=56 * 2**20
        ),
        cost_estimate=pl.CostEstimate(
            flops=8 * total * width * width + 4 * total * slot * width,
            bytes_accessed=16 * total * width,
            transcendentals=total * slot * heads,
        ),
    )(lengths, tokens, wq, wk, wv, wo, g1[None], b1[None], g2[None], b2[None])


def row_sum(value, width):
    return jnp.sum(value, axis=0, keepdims=True)


def layer_norm_pull(grad, normed, inverse, gain):
    scaled = grad * gain
    inner = scaled - jnp.mean(scaled, axis=-1, keepdims=True)
    inner = inner - normed * jnp.mean(scaled * normed, axis=-1, keepdims=True)
    return inverse * inner


def attention_pull(dcontext, query, keyed, valued, prob, mask, slot, group, scale):
    low = prob.astype(BF)
    dspread = spread(dcontext, mask, group)
    dprob = mm(valued, dspread, 1, 1)
    inner = jnp.sum(dprob * prob, axis=0, keepdims=True)
    dscores = (prob * (dprob - inner)).astype(BF)
    dquery = fold(mm(dscores, keyed, 0, 0), mask, slot, group) * scale
    dkeyed = mm(dscores, spread(query, mask, group)) * scale
    dvalued = mm(low, dspread)
    return dquery.astype(BF), dkeyed.astype(BF), dvalued.astype(BF)


def attention_backward_chunk(
    heads, length_of, x_ref, cot_ref, dm_ref, h_ref, act, q, k, v, ctx, p_ref,
    wq, wk, wv, wo, g1, g2, ig_o, dq_s, dk_s, dv_s, dctx_s, gq, gk, gv, go, norms,
):
    count, slot, width = x_ref.shape
    head = width // heads
    group = max(1, min(heads, 256 // head))
    span = group * head
    scale = head ** -0.5
    mask = block_diagonal(group, slot, head)
    place = lax.broadcasted_iota(jnp.int32, (slot, width), 0)
    flat = lambda value: value.astype(F32).reshape(count * slot, width)
    normed2, inverse2 = normalize(h_ref[...])
    dm = flat(dm_ref[...])
    cot = cot_ref[...].astype(F32)
    gt = jnp.concatenate(
        [jnp.where(place < length_of(s), cot[s], 0.0) for s in range(count)], axis=0
    )
    dhidden = gt + layer_norm_pull(dm, normed2, inverse2, g2[...])
    norms[2:3] += row_sum(dm * normed2, width)
    norms[3:4] += row_sum(dm, width)
    dattn = dhidden.astype(BF)
    go[...] += mm(ctx[...], dattn, 0, 0)
    dctx_s[...] = mm(dattn, wo[...], 1, 1).astype(BF)
    for s in range(count):
        rows = slice(s * slot, (s + 1) * slot)
        for part in range(heads // group):
            cols = slice(part * span, (part + 1) * span)
            dq_s[rows, cols], dk_s[rows, cols], dv_s[rows, cols] = attention_pull(
                dctx_s[rows, cols], q[rows, cols], k[rows, cols], v[rows, cols],
                p_ref[s, part], mask, slot, group, scale,
            )
    dq, dk, dv = dq_s[...], dk_s[...], dv_s[...]
    gq[...] += mm(act[...], dq, 0, 0)
    gk[...] += mm(act[...], dk, 0, 0)
    gv[...] += mm(act[...], dv, 0, 0)
    dact = mm(dq, wq[...], 1, 1) + mm(dk, wk[...], 1, 1) + mm(dv, wv[...], 1, 1)
    normed1, inverse1 = normalize(flat(x_ref[...]))
    norms[0:1] += row_sum(dact * normed1, width)
    norms[1:2] += row_sum(dact, width)
    dx = dhidden + layer_norm_pull(dact, normed1, inverse1, g1[...])
    ig_o[...] = dx.astype(BF).reshape(count, slot, width)


def attention_backward_kernel(
    heads, len_ref, x_ref, cot_ref, dm_ref, h_ref, act, q, k, v, ctx, p_ref,
    wq, wk, wv, wo, g1, g2, ig_o, gq, gk, gv, go, norms, dq_s, dk_s, dv_s, dctx_s,
):
    step = pl.program_id(0)
    count = x_ref.shape[0]

    @pl.when(step == 0)
    def _():
        for total in (gq, gk, gv, go, norms):
            total[...] = jnp.zeros_like(total)

    attention_backward_chunk(
        heads, lambda s: len_ref[step * count + s], x_ref, cot_ref, dm_ref, h_ref,
        act, q, k, v, ctx, p_ref, wq, wk, wv, wo, g1, g2, ig_o,
        dq_s, dk_s, dv_s, dctx_s, gq, gk, gv, go, norms,
    )


def attention_backward(
    lengths, tokens, cot, dm, hidden, act, q, k, v, ctx, prob, wq, wk, wv, wo, g1, g2, heads
):
    sents, slot, width = tokens.shape
    count = 4 if sents % 4 == 0 else 1
    rows = count * slot
    head = width // heads
    group = max(1, min(heads, 256 // head))
    whole = lambda *shape: pl.BlockSpec(shape, lambda i: (0,) * len(shape))
    flat = pl.BlockSpec((rows, width), lambda i: (i, 0))
    cube = pl.BlockSpec((count, slot, width), lambda i: (i, 0, 0))
    probs = pl.BlockSpec((count, heads // group, slot, group * slot), lambda i: (i, 0, 0, 0))
    shape = jax.ShapeDtypeStruct
    total = sents * slot
    return pl.pallas_call(
        functools.partial(attention_backward_kernel, heads),
        grid=(sents // count,),
        in_specs=[pl.BlockSpec(memory_space=pltpu.SMEM), cube, cube, cube]
        + [flat] * 6 + [probs]
        + [whole(width, width)] * 4
        + [whole(1, width)] * 2,
        out_specs=[cube] + [whole(width, width)] * 4 + [whole(8, width)],
        out_shape=[shape((sents, slot, width), BF)]
        + [shape((width, width), F32)] * 4
        + [shape((8, width), F32)],
        scratch_shapes=[VM((rows, width), BF)] * 4,
        compiler_params=pltpu.CompilerParams(
            dimension_semantics=("arbitrary",), vmem_limit_bytes=56 * 2**20
        ),
        cost_estimate=pl.CostEstimate(
            flops=16 * total * width * width + 10 * total * slot * width,
            bytes_accessed=24 * total * width,
            transcendentals=0,
        ),
    )(lengths, tokens, cot, dm, hidden, act, q, k, v, ctx, prob, wq, wk, wv, wo, g1[None], g2[None])


MESH_ID = pl.DeviceIdType.MESH
CORE, NEAR, FAR = 1, 2, 4


def plane_peer(relation):
    me = lax.axis_index("expert")
    bits = []
    for bit in (CORE, NEAR, FAR):
        value = (me // bit) % 2
        bits.append((1 - value if relation & bit else value) * bit)
    return bits[0] + bits[1] + bits[2]


def remote(src, dst, sends, recvs, index, relation):
    return pltpu.make_async_remote_copy(
        src_ref=src,
        dst_ref=dst,
        send_sem=sends.at[index],
        recv_sem=recvs.at[index],
        device_id=(lax.axis_index("dp"), plane_peer(relation)),
        device_id_type=MESH_ID,
    )


def plane_barrier():
    barrier = pltpu.get_barrier_semaphore()
    for relation in range(1, 8):
        pl.semaphore_signal(
            barrier,
            inc=1,
            device_id=(lax.axis_index("dp"), plane_peer(relation)),
            device_id_type=MESH_ID,
        )
    pl.semaphore_wait(barrier, 7)


def gather_copies(own, held, sends, recvs, base):
    half = own.shape[0] // 2
    low, high = pl.ds(0, half), pl.ds(half, half)
    plan = [
        (own.at[low], held[2].at[low], NEAR),
        (own.at[high], held[4].at[high], FAR),
        (own, held[1], CORE),
        (own.at[high], held[2].at[high], NEAR),
        (own.at[low], held[4].at[low], FAR),
        (held[2].at[low], held[6].at[low], FAR),
        (held[4].at[high], held[6].at[high], NEAR),
        (held[2], held[3], CORE),
        (held[4], held[5], CORE),
        (held[6], held[7], CORE),
    ]
    return [
        remote(src, dst, sends, recvs, base + place, relation)
        for place, (src, dst, relation) in enumerate(plan)
    ]


def return_copies(parts, cores, sides, sends, recvs, base):
    half = parts[0].shape[0] // 2
    low, high = pl.ds(0, half), pl.ds(half, half)
    plan = [
        (parts[1], cores[0], CORE),
        (parts[3], cores[2], CORE),
        (parts[5], cores[4], CORE),
        (parts[7], cores[6], CORE),
        (parts[2].at[low], sides[0], NEAR),
        (parts[6].at[low], sides[1], NEAR),
        (parts[4].at[high], sides[2], FAR),
        (parts[6].at[high], sides[3], FAR),
        (parts[4].at[low], sides[4], FAR),
        (parts[2].at[high], sides[5], NEAR),
    ]
    return [
        remote(src, dst, sends, recvs, base + place, relation)
        for place, (src, dst, relation) in enumerate(plan)
    ]


def add_into(target, start, other, count):
    def one(i, carry):
        total = target[start + i].astype(F32) + other[i].astype(F32)
        target[start + i] = total.astype(BF)
        return carry

    lax.fori_loop(0, count, one, 0)


def return_finish(parts, sides, back, out):
    half = out.shape[0] // 2
    back[4].wait_recv()
    add_into(parts[0], 0, sides[0], half)
    back[5].wait_recv()
    add_into(parts[4], 0, sides[1], half)
    back[8].start()
    back[6].wait_recv()
    add_into(parts[0], half, sides[2], half)
    back[7].wait_recv()
    add_into(parts[2], half, sides[3], half)
    back[9].start()
    back[8].wait_recv()
    add_into(parts[0], 0, sides[4], half)
    back[9].wait_recv()
    add_into(parts[0], half, sides[5], half)

    def one(i, carry):
        out[i] = parts[0][i]
        return carry

    lax.fori_loop(0, out.shape[0], one, 0)
    for copy in back:
        copy.wait_send()


GELU_A = 0.7978845608028654
GELU_B = 0.044715


def expert_kernel(
    cap, tab, gates, m, cot, win, wback, dm_o, py_o, gin_o, gback_o, dg_o, *scratch
):
    sents, slot, width = m.shape
    hidden = win.shape[1]
    held_m = dict(zip(range(1, 8), scratch[0:7]))
    held_c = dict(zip(range(1, 8), scratch[7:14]))
    parts = dict(zip(range(8), scratch[14:22]))
    cores = dict(zip((0, 2, 4, 6), scratch[22:26]))
    sides = scratch[26:32]
    xs, gs, dys, zs, dus, ys, dms, stage, dg_s, accb, acci, sends, recvs, local = scratch[32:]
    me = lax.axis_index("expert")
    tile = min(512, hidden)
    entries = 2 * cap + sents

    plane_barrier()
    to_m = gather_copies(m, held_m, sends, recvs, 0)
    to_c = gather_copies(cot, held_c, sends, recvs, 10)
    back = return_copies(parts, cores, sides, sends, recvs, 20)
    gates_back = {
        r: remote(dg_s.at[r], dg_o.at[r], sends, recvs, 30 + r, r) for r in range(1, 8)
    }
    for place in (0, 1, 2):
        to_m[place].start()
        to_c[place].start()
    for place in (3, 4):
        to_m[place].start()
        to_c[place].start()
    accb[...] = jnp.zeros_like(accb)
    acci[...] = jnp.zeros_like(acci)
    place = lax.broadcasted_iota(jnp.int32, (slot, width), 0)
    held_m[0], held_c[0] = m, cot

    def arrive(*indices):
        for index in indices:
            to_m[index].wait_recv()
            to_c[index].wait_recv()

    def forward(*indices):
        for index in indices:
            to_m[index].start()
            to_c[index].start()

    def before(r):
        if r == 1:
            arrive(2)
        if r == 2:
            arrive(0, 1)
            forward(5, 6)
            arrive(3)
            forward(7)
            arrive(4)
            forward(8)
        if r == 3:
            arrive(7)
        if r == 5:
            arrive(8)
        if r == 6:
            arrive(5, 6)
            forward(9)
        if r == 7:
            arrive(9)
        source = plane_peer(r)

        def fetch(j, carry):
            index = tab[source, me * entries + j]
            length = tab[source, me * entries + cap + j]
            gate = gates[source, me * cap + j]
            xs[j] = held_m[r][index]
            gt = jnp.where(place < length, held_c[r][index].astype(F32), 0.0)
            gs[j] = gt.astype(BF)
            dys[j] = (gt * gate).astype(BF)
            return carry

        lax.fori_loop(0, cap, fetch, 0)

    def after(r):
        source = plane_peer(r)
        if r >= 2:
            pltpu.make_async_copy(stage.at[r % 2], py_o.at[r - 2], local.at[r % 2]).wait()

        def give(i, carry):
            index = tab[source, me * entries + 2 * cap + i]
            there = jnp.maximum(index, 0)
            gate = gates[source, me * cap + there]
            hit = (index >= 0).astype(F32)
            parts[r][i] = (dms[there].astype(F32) * hit).astype(BF)
            stage[r % 2, i] = (ys[there].astype(F32) * (hit * gate)).astype(BF)
            return carry

        lax.fori_loop(0, sents, give, 0)
        pltpu.make_async_copy(stage.at[r % 2], py_o.at[r], local.at[r % 2]).start()

        def dots(j, carry):
            product = ys[j].astype(F32) * gs[j].astype(F32)
            total = jnp.sum(jnp.sum(product, axis=0, keepdims=True), axis=1, keepdims=True)
            if r == 0:
                dg_o[0, pl.ds(j, 1)] = jnp.broadcast_to(total, (1, 128))
            else:
                dg_s[r, pl.ds(j, 1)] = jnp.broadcast_to(total, (1, 128))
            return carry

        lax.fori_loop(0, cap, dots, 0)
        if r > 0:
            gates_back[r].start()
        if r % 2 == 1:
            back[r // 2].start()
        if r == 4:
            back[1].wait_recv()
            add_into(parts[2], 0, cores[2], sents)
            back[4].start()
        if r == 6:
            back[2].wait_recv()
            add_into(parts[4], 0, cores[4], sents)
            back[6].start()
        if r == 7:
            back[3].wait_recv()
            add_into(parts[6], 0, cores[6], sents)
            back[5].start()
            back[7].start()
            back[0].wait_recv()
            add_into(parts[0], 0, cores[0], sents)

    def chunk(t, carry):
        for r in range(8):
            pl.when(t == r)(functools.partial(before, r))
        x = xs[...].reshape(cap * slot, width)
        dy = dys[...].reshape(cap * slot, width)

        def inner(f, carry):
            cols = pl.ds(pl.multiple_of(f * tile, tile), tile)
            u = mm(x, win[:, cols])
            square = u * u
            th = jnp.tanh(u * (GELU_A + GELU_A * GELU_B * square))
            cdf = 0.5 + 0.5 * th
            slope = cdf + (0.5 * u) * (1.0 - th * th) * (GELU_A + 3 * GELU_A * GELU_B * square)
            z = (u * cdf).astype(BF)
            zs[:, cols] = z
            dz = mm(dy, wback[cols, :], 1, 1)
            du = (dz * slope).astype(BF)
            dus[:, cols] = du
            accb[cols, :] += mm(z, dy, 0, 0)
            acci[:, cols] += mm(x, du, 0, 0)
            return carry

        lax.fori_loop(0, hidden // tile, inner, 0)
        ys[...] = mm(zs[...], wback[...]).astype(BF).reshape(cap, slot, width)
        dms[...] = mm(dus[...], win[...], 1, 1).astype(BF).reshape(cap, slot, width)
        for r in range(8):
            pl.when(t == r)(functools.partial(after, r))
        return carry

    lax.fori_loop(0, 8, chunk, 0)
    gin_o[...] = acci[...].astype(BF)
    gback_o[...] = accb[...].astype(BF)
    return_finish(parts, sides, back, dm_o)
    for r in range(1, 8):
        gates_back[r].wait()
    for index in range(10):
        to_m[index].wait_send()
        to_c[index].wait_send()
    for r in (6, 7):
        pltpu.make_async_copy(stage.at[r % 2], py_o.at[r], local.at[r % 2]).wait()


def expert_exchange(tab, gates, m, cot, win, wback, cap):
    sents, slot, width = m.shape
    hidden = win.shape[1]
    vm = pl.BlockSpec(memory_space=VM)
    sm = pl.BlockSpec(memory_space=pltpu.SMEM)
    shape = jax.ShapeDtypeStruct
    cube = (sents, slot, width)
    rows = cap * slot
    return pl.pallas_call(
        functools.partial(expert_kernel, cap),
        in_specs=[sm, sm, vm, vm, vm, vm],
        out_specs=[vm, pl.BlockSpec(memory_space=pl.ANY), vm, vm, vm],
        out_shape=[
            shape(cube, BF),
            shape((8,) + cube, BF),
            shape((width, hidden), BF),
            shape((hidden, width), BF),
            shape((8, cap, 128), F32),
        ],
        scratch_shapes=[VM(cube, BF)] * (14 + 8 + 4)
        + [VM((sents // 2, slot, width), BF)] * 6
        + [VM((cap, slot, width), BF)] * 3
        + [VM((rows, hidden), BF)] * 2
        + [VM((cap, slot, width), BF)] * 2
        + [VM((2,) + cube, BF), VM((8, cap, 128), F32)]
        + [VM((hidden, width), F32), VM((width, hidden), F32)]
        + [
            pltpu.SemaphoreType.DMA((38,)),
            pltpu.SemaphoreType.DMA((38,)),
            pltpu.SemaphoreType.DMA((2,)),
        ],
        compiler_params=pltpu.CompilerParams(
            collective_id=1, has_side_effects=True, vmem_limit_bytes=63 * 2**20
        ),
        cost_estimate=pl.CostEstimate(
            flops=12 * 8 * rows * width * hidden, bytes_accessed=40 * 2**20, transcendentals=0
        ),
    )(tab, gates, m, cot, win, wback)


def line_peer(offset, depth):
    return lax.rem(lax.axis_index("dp") + offset, depth)


def along(src, dst, sends, recvs, index, offset, depth):
    return pltpu.make_async_remote_copy(
        src_ref=src,
        dst_ref=dst,
        send_sem=sends.at[index],
        recv_sem=recvs.at[index],
        device_id=(line_peer(offset, depth), lax.axis_index("expert")),
        device_id_type=MESH_ID,
    )


class Reduction:
    def __init__(self, depth, value, wide, core_r, plane_r, line_s, line_r, final, sems, base):
        self.depth, self.value, self.wide, self.final = depth, value, wide, final
        self.core_r, self.plane_r, self.line_s, self.line_r = core_r, plane_r, line_s, line_r
        sends, recvs = sems
        me = lax.axis_index("expert")
        z = lax.axis_index("dp")
        core = me % 2
        self.half = value.shape[0] // 2
        self.quarter = self.half // 4
        self.share = self.quarter // depth
        self.mine = core * self.half
        self.other = (1 - core) * self.half
        self.block = self.mine + (me // 2) * self.quarter
        self.own = self.block + z * self.share
        self.to_core = remote(wide, core_r, sends, recvs, base, CORE)
        self.to_plane = []
        self.from_plane = []
        for place, relation in enumerate((2, 4, 6)):
            rows = pl.ds((plane_peer(relation) // 2) * self.quarter, self.quarter)
            self.to_plane.append(
                remote(wide.at[rows], plane_r.at[place], sends, recvs, base + 1 + place, relation)
            )
        self.to_line = []
        for offset in range(1, depth):
            rows = pl.ds(line_peer(offset, depth) * self.share, self.share)
            self.to_line.append(
                along(
                    line_s.at[rows], line_r.at[offset - 1], sends, recvs, base + 3 + offset,
                    offset, depth,
                )
            )
        after = base + 3 + depth
        rows = final.at[pl.ds(self.own, self.share)]
        self.back_line = [
            along(rows, rows, sends, recvs, after + offset - 1, offset, depth)
            for offset in range(1, depth)
        ]
        after = after + depth - 1
        rows = final.at[pl.ds(self.block, self.quarter)]
        self.back_plane = [
            remote(rows, rows, sends, recvs, after + place, relation)
            for place, relation in enumerate((2, 4, 6))
        ]
        rows = final.at[pl.ds(self.mine, self.half)]
        self.back_core = remote(rows, rows, sends, recvs, after + 3, CORE)

    @staticmethod
    def semaphores(depth):
        return 2 * depth + 6

    def send_core(self):
        self.wide[...] = self.value[pl.ds(self.other, self.half), :].astype(BF)
        self.to_core.start()

    def send_plane(self):
        self.to_core.wait()
        rows = pl.ds(self.mine, self.half)
        total = self.value[rows, :] + self.core_r[...].astype(F32)
        self.value[rows, :] = total
        self.wide[...] = total.astype(BF)
        for copy in self.to_plane:
            copy.start()

    def send_line(self):
        for copy in self.to_plane:
            copy.wait()
        rows = pl.ds(self.block, self.quarter)
        total = self.value[rows, :]
        for place in range(3):
            total = total + self.plane_r[place].astype(F32)
        self.value[rows, :] = total
        self.line_s[...] = total.astype(BF)
        for copy in self.to_line:
            copy.start()

    def send_back_line(self):
        for copy in self.to_line:
            copy.wait()
        rows = pl.ds(self.own, self.share)
        total = self.value[rows, :]
        for offset in range(1, self.depth):
            total = total + self.line_r[offset - 1].astype(F32)
        self.final[rows, :] = total.astype(BF)
        for copy in self.back_line:
            copy.start()

    def send_back_plane(self):
        for copy in self.back_line:
            copy.wait()
        for copy in self.back_plane:
            copy.start()

    def send_back_core(self):
        for copy in self.back_plane:
            copy.wait()
        self.back_core.start()

    def finish(self):
        self.back_core.wait()


def backward_kernel(
    heads, depth, len_ref, x_ref, cot_ref, dm_ref, h_ref, act, q, k, v, ctx, p_ref,
    wq, wk, wv, wo, g1, g2, small_in, py, gin, gback,
    ig_o, out_o, fin_o, fin_0, fin_1, gin_o, gback_o, small_o, *scratch
):
    sents, slot, width = x_ref.shape
    total_rows = sents * slot
    head = width // heads
    group = max(1, min(heads, 256 // head))
    span = group * head
    scale = head ** -0.5
    count = 4 if sents % 4 == 0 else 1
    rows_per = count * slot
    z = lax.axis_index("dp")
    parts = {0: scratch[0], 2: scratch[1], 4: scratch[2], 6: scratch[3]}
    cores = dict(zip((0, 2, 4, 6), scratch[4:8]))
    sides = scratch[8:14]
    dh_s, da_s, dctx_s, dq_s, dk_s, dv_s = scratch[14:20]
    red = scratch[20:38]
    line_in, line_back, extra_in, extra_back = scratch[38:42]
    small, small_core, small_plane, small_line = scratch[42:46]
    gin_s, gback_s = scratch[46:48]
    sends, recvs, local = scratch[48:]
    sems = (sends, recvs)
    grad_loads = [
        pltpu.make_async_copy(gin, gin_s, local.at[4]),
        pltpu.make_async_copy(gback, gback_s, local.at[5]),
    ]
    for load in grad_loads:
        load.start()

    loads = {
        r: pltpu.make_async_copy(py.at[r], parts[r], local.at[r // 2]) for r in (0, 2, 4, 6)
    }
    for r in (6, 2, 4, 0):
        loads[r].start()
    barrier = pltpu.get_barrier_semaphore()
    for relation in range(1, 8):
        pl.semaphore_signal(
            barrier, inc=1, device_id=(z, plane_peer(relation)), device_id_type=MESH_ID
        )
    for offset in range(1, depth):
        pl.semaphore_signal(
            barrier,
            inc=1,
            device_id=(line_peer(offset, depth), lax.axis_index("expert")),
            device_id_type=MESH_ID,
        )
    pl.semaphore_wait(barrier, 6 + depth)

    all_parts = dict(parts)
    for r in (1, 3, 5, 7):
        all_parts[r] = py.at[r]
    back = return_copies(all_parts, cores, sides, sends, recvs, 0)
    for r in (7, 3, 5, 1):
        back[r // 2].start()

    base = 10
    in_rows = gin.shape[0] // depth
    back_rows = gback.shape[0] // depth

    def line_piece(s, array, right, last):
        offset = 1 if right else depth - 1
        index = base + (0 if right else 2 * depth) + 2 * s + array
        share, source = ((in_rows, gin_s), (back_rows, gback_s))[array]
        into = (line_in, line_back)[array].at[s]
        if last and not right:
            into = (extra_in, extra_back)[array]
        here = source.at[pl.ds(s * share, share)]
        return along(here, into, sends, recvs, index, offset, depth)

    def add_piece(s, array):
        share, source = ((in_rows, gin_s), (back_rows, gback_s))[array]
        other = (line_in, line_back)[array]
        here = pl.ds(s * share, share)
        source[here, :] = (source[here, :].astype(F32) + other[s].astype(F32)).astype(BF)

    def pieces(right):
        order = range(depth - 1, 0, -1) if right else range(depth - 1)
        return [(s, array) for s in order for array in (0, 1)]

    def start_piece(s, array, right):
        if right:
            line_piece(s, array, True, False).start()
            return
        near = z == s + 1

        @pl.when(near)
        def _():
            line_piece(s, array, False, True).start()

        @pl.when(jnp.logical_not(near))
        def _():
            line_piece(s, array, False, False).start()

    def line_service(t, ahead=1):
        for right in (True, False):
            every = pieces(right)
            edge = 0 if right else depth - 1
            opening = range(0, 1 + ahead) if t == 0 else range(t + ahead, t + ahead + 1)

            @pl.when(z == edge)
            def _():
                for number in opening:
                    if number < len(every):
                        start_piece(*every[number], right)

            for number, (s, array) in enumerate(every):
                hops = t - number
                away = s if right else depth - 1 - s
                if 0 < hops < away:

                    @pl.when(z == (hops if right else depth - 1 - hops))
                    def _():
                        line_piece(s, array, right, False).wait_recv()
                        add_piece(s, array)
                        start_piece(s, array, right)

    def line_end():
        for s in range(depth):

            @pl.when(z == s)
            def _():
                here = pl.ds(s * in_rows, in_rows)
                there = pl.ds(s * back_rows, back_rows)
                gin_o[...] = gin_s[here, :].astype(F32)
                gback_o[...] = gback_s[there, :].astype(F32)
                if s > 0:
                    for array in (0, 1):
                        line_piece(s, array, True, True).wait_recv()
                    gin_o[...] += line_in[s].astype(F32)
                    gback_o[...] += line_back[s].astype(F32)
                if s < depth - 1:
                    for array in (0, 1):
                        line_piece(s, array, False, True).wait_recv()
                    gin_o[...] += extra_in[...].astype(F32)
                    gback_o[...] += extra_back[...].astype(F32)

        for s in range(depth):
            for array in (0, 1):

                @pl.when(z < s)
                def _():
                    line_piece(s, array, True, False).wait_send()

                @pl.when(z > s)
                def _():
                    line_piece(s, array, False, False).wait_send()

    for load in grad_loads:
        load.wait()
    line_service(0)

    base_red = base + 4 * depth
    per = Reduction.semaphores(depth)
    reds = []
    for place, final in enumerate((fin_o, fin_0, fin_1)):
        value, wide, core_r, plane_r, line_s, line_r = red[6 * place : 6 * place + 6]
        reds.append(
            Reduction(
                depth, value, wide, core_r, plane_r, line_s, line_r, final, sems,
                base_red + place * per,
            )
        )
    red_o, red_0, red_1 = reds

    small[...] = small_in[...]
    chunk_place = lax.broadcasted_iota(jnp.int32, (slot, width), 0)

    def masked(ref, c):
        return jnp.concatenate(
            [
                jnp.where(
                    chunk_place < len_ref[c * count + s], ref[c * count + s].astype(F32), 0.0
                )
                for s in range(count)
            ],
            axis=0,
        )

    def flat(ref, c):
        block = ref[pl.ds(c * count, count)]
        return block.astype(F32).reshape(rows_per, width)

    def first(c, carry):
        rows = pl.ds(pl.multiple_of(c * rows_per, rows_per), rows_per)
        normed2, inverse2 = normalize(h_ref[rows, :])
        dm = flat(dm_ref, c)
        dhidden = masked(cot_ref, c) + layer_norm_pull(dm, normed2, inverse2, g2[...])
        small[2:3] += row_sum(dm * normed2, width)
        small[3:4] += row_sum(dm, width)
        dh_s[rows, :] = dhidden
        dattn = dhidden.astype(BF)
        da_s[rows, :] = dattn
        dctx_s[rows, :] = mm(dattn, wo[...], 1, 1).astype(BF)
        return carry

    lax.fori_loop(0, sents // count, first, 0)
    red_o.value[...] = mm(ctx[...], da_s[...], 0, 0)
    red_o.send_core()
    mask = block_diagonal(group, slot, head)

    def pull(part, into):
        cols = slice(part * span, (part + 1) * span)

        def one(c, carry):
            for s in range(count):
                at = c * count + s
                rows = pl.ds(pl.multiple_of(at * slot, slot), slot)
                dq_s[rows, cols], dk_s[rows, cols], dv_s[rows, cols] = attention_pull(
                    dctx_s[rows, cols], q[rows, cols], k[rows, cols], v[rows, cols],
                    p_ref[at, part], mask, slot, group, scale,
                )
            return carry

        lax.fori_loop(0, sents // count, one, 0)
        into.value[0:width, :] = mm(act[...], dq_s[:, cols], 0, 0)
        into.value[width : 2 * width, :] = mm(act[...], dk_s[:, cols], 0, 0)
        into.value[2 * width : 3 * width, :] = mm(act[...], dv_s[:, cols], 0, 0)
        into.send_core()

    def returned(r, starts):
        loads[r].wait()
        back[r // 2].wait_recv()
        add_into(parts[r], 0, cores[r], sents)
        for index in starts:
            back[index].start()

    pull(0, red_0)
    red_o.send_plane()
    line_service(1)
    returned(6, (5, 7))
    pull(1, red_1)
    red_0.send_plane()
    red_o.send_line()
    line_service(2)
    returned(2, ())
    returned(4, ())
    returned(0, ())

    def last(c, carry):
        rows = pl.ds(pl.multiple_of(c * rows_per, rows_per), rows_per)
        dact = (
            mm(dq_s[rows, :], wq[...], 1, 1)
            + mm(dk_s[rows, :], wk[...], 1, 1)
            + mm(dv_s[rows, :], wv[...], 1, 1)
        )
        normed1, inverse1 = normalize(flat(x_ref, c))
        small[0:1] += row_sum(dact * normed1, width)
        small[1:2] += row_sum(dact, width)
        dx = dh_s[rows, :] + layer_norm_pull(dact, normed1, inverse1, g1[...])
        ig_o[pl.ds(c * count, count)] = dx.astype(BF).reshape(count, slot, width)
        return carry

    lax.fori_loop(0, sents // count, last, 0)
    red_1.send_plane()
    back[4].start()
    back[6].start()
    red_o.send_back_line()
    red_0.send_line()
    line_service(3)
    red_o.send_back_plane()
    red_0.send_back_line()
    red_1.send_line()
    half = sents // 2
    back[5].wait_recv()
    add_into(parts[4], 0, sides[1], half)
    back[7].wait_recv()
    add_into(parts[2], half, sides[3], half)
    line_service(4)
    red_o.send_back_core()
    red_0.send_back_plane()
    red_1.send_back_line()
    back[8].start()
    back[9].start()
    red_1.send_back_plane()
    red_0.send_back_core()
    back[4].wait_recv()
    add_into(parts[0], 0, sides[0], half)
    back[6].wait_recv()
    add_into(parts[0], half, sides[2], half)
    line_service(5)
    red_1.send_back_core()
    back[8].wait_recv()
    back[9].wait_recv()

    def outcome(low, side):
        def one(i, carry):
            at = low + i
            valid = chunk_place < len_ref[at]
            moe = jnp.where(valid, parts[0][at].astype(F32) + side[i].astype(F32), 0.0)
            rows = pl.ds(pl.multiple_of(at * slot, slot), slot)
            total = jnp.where(valid, h_ref[rows, :], 0.0) + moe
            out_o[at] = total.astype(BF)
            small[5:6] += row_sum(total * total, width)
            small[6:7] += row_sum(moe * moe, width)
            return carry

        lax.fori_loop(0, half, one, 0)

    outcome(0, sides[4])
    outcome(half, sides[5])

    base_small = base_red + 3 * per
    me = lax.axis_index("expert")
    to_core = remote(small, small_core, sends, recvs, base_small, CORE)
    to_core.start()
    to_core.wait()
    spot = me // 2
    small_plane[spot] = small[...] + small_core[...]
    to_plane = [
        remote(
            small_plane.at[spot], small_plane.at[spot], sends, recvs, base_small + 1 + place,
            relation,
        )
        for place, relation in enumerate((2, 4, 6))
    ]
    for copy in to_plane:
        copy.start()
    for copy in to_plane:
        copy.wait()
    total = small_plane[0]
    for place in range(1, 4):
        total = total + small_plane[place]
    small_line[z] = total
    to_line = [
        along(
            small_line.at[z], small_line.at[z], sends, recvs, base_small + 3 + offset, offset,
            depth,
        )
        for offset in range(1, depth)
    ]
    for copy in to_line:
        copy.start()
    for copy in to_line:
        copy.wait()
    total = small_line[0]
    for place in range(1, depth):
        total = total + small_line[place]
    small_o[...] = total
    for one in reds:
        one.finish()
    line_end()
    for copy in back:
        copy.wait_send()


def backward_exchange(
    depth, lengths, tokens, cot, dm, hidden, act, q, k, v, ctx, prob, wq, wk, wv, wo, g1, g2,
    small, py, gin, gback, heads,
):
    sents, slot, width = tokens.shape
    total = sents * slot
    vm = pl.BlockSpec(memory_space=VM)
    shape = jax.ShapeDtypeStruct
    cube = (sents, slot, width)
    head = width // heads
    span = max(1, min(heads, 256 // head)) * head
    pieces = [(width, width), (3 * width, span), (3 * width, width - span)]
    red = []
    for rows, cols in pieces:
        red += [
            VM((rows, cols), F32),
            VM((rows // 2, cols), BF),
            VM((rows // 2, cols), BF),
            VM((3, rows // 8, cols), BF),
            VM((rows // 8, cols), BF),
            VM((depth - 1, rows // 8 // depth, cols), BF),
        ]
    in_share = (gin.shape[0] // depth, gin.shape[1])
    back_share = (gback.shape[0] // depth, gback.shape[1])
    semaphores = 10 + 4 * depth + 3 * Reduction.semaphores(depth) + 4 + depth
    return pl.pallas_call(
        functools.partial(backward_kernel, heads, depth),
        in_specs=[pl.BlockSpec(memory_space=pltpu.SMEM)]
        + [vm] * 17
        + [pl.BlockSpec(memory_space=pl.ANY), pl.BlockSpec(memory_space=pl.ANY)]
        + [pl.BlockSpec(memory_space=pl.ANY)],
        out_specs=[vm] * 8,
        out_shape=[shape(cube, BF), shape(cube, BF)]
        + [shape(piece, BF) for piece in pieces]
        + [shape(in_share, F32), shape(back_share, F32), shape(small.shape, F32)],
        scratch_shapes=[VM(cube, BF)] * 8
        + [VM((sents // 2, slot, width), BF)] * 6
        + [VM((total, width), F32)]
        + [VM((total, width), BF)] * 5
        + red
        + [VM((depth,) + in_share, BF), VM((depth,) + back_share, BF)]
        + [VM(in_share, BF), VM(back_share, BF)]
        + [VM(small.shape, F32)] * 2
        + [VM((4,) + small.shape, F32), VM((depth,) + small.shape, F32)]
        + [VM(gin.shape, BF), VM(gback.shape, BF)]
        + [
            pltpu.SemaphoreType.DMA((semaphores,)),
            pltpu.SemaphoreType.DMA((semaphores,)),
            pltpu.SemaphoreType.DMA((6,)),
        ],
        compiler_params=pltpu.CompilerParams(
            collective_id=2, has_side_effects=True, vmem_limit_bytes=63 * 2**20
        ),
        cost_estimate=pl.CostEstimate(
            flops=16 * total * width * width, bytes_accessed=40 * 2**20, transcendentals=0
        ),
    )(
        lengths, tokens, cot, dm, hidden, act, q, k, v, ctx, prob, wq, wk, wv, wo,
        g1[None], g2[None], small, py, gin, gback,
    )


def local(
    tokens,
    lengths,
    tasks,
    routes,
    gate_table,
    ln1_gain,
    ln1_bias,
    ln2_gain,
    ln2_bias,
    w_query,
    w_key,
    w_value,
    w_out,
    w_in,
    w_back,
    cotangent,
):
    sents, slot, width = tokens.shape
    heads = HEADS
    experts = gate_table.shape[1]
    ntasks = routes.shape[0]
    capacity = max(1, 4 * sents // experts)
    task_hot = (tasks[:, None] == jnp.arange(ntasks)[None, :]).astype(jnp.int32)
    chosen = jnp.sum(task_hot[:, :, None] * routes[None, :, :], axis=1)
    flat = chosen.reshape(-1)
    order = jnp.arange(2 * sents)
    earlier = (flat[:, None] == flat[None, :]) & (order[None, :] < order[:, None])
    rank = jnp.sum(earlier.astype(jnp.int32), axis=1)
    slot_id = flat * capacity + rank
    placed = rank < capacity
    dispatch = (
        (jnp.arange(experts * capacity)[:, None] == slot_id[None, :]) & placed[None, :]
    ).astype(jnp.bfloat16)
    collect = dispatch.T
    expert_hot = (chosen[:, :, None] == jnp.arange(experts)[None, None, :]).astype(jnp.float32)
    valid = (jnp.arange(slot)[None, :] < lengths[:, None]).astype(jnp.float32)
    mask3 = valid[:, :, None]
    act, query, keyed, valued, context, prob, hidden, mixed, attn_sum = attention_forward(
        tokens, lengths, w_query, w_key, w_value, w_out,
        ln1_gain, ln1_bias, ln2_gain, ln2_bias, heads,
    )
    hidden_res = hidden.reshape(sents, slot, width)
    table_rows = jnp.dot(task_hot.astype(jnp.float32), gate_table, precision=lax.Precision.HIGHEST)
    picked = jnp.sum(expert_hot * table_rows[:, None, :], axis=-1)
    gate_values = jax.nn.softmax(picked, axis=-1)
    grad_total = cotangent.astype(jnp.float32) * mask3
    copies = jnp.broadcast_to(mixed[:, None], (sents, 2, slot, width)).reshape(
        2 * sents, slot * width
    )
    outgoing = (
        project(dispatch, copies).astype(jnp.bfloat16).reshape(experts, capacity, slot, width)
    )
    dycopy = (
        (gate_values[:, :, None, None] * grad_total[:, None])
        .astype(jnp.bfloat16)
        .reshape(2 * sents, slot * width)
    )
    grad_out = (
        project(dispatch, dycopy).astype(jnp.bfloat16).reshape(experts, capacity, slot, width)
    )
    incoming = lax.all_to_all(outgoing, "expert", split_axis=0, concat_axis=0, tiled=True).reshape(
        -1, width
    )
    pre_act, active, produced = expert_forward(incoming, w_in[0], w_back[0])
    returned = lax.all_to_all(
        produced.reshape(experts, capacity, slot, width),
        "expert",
        split_axis=0,
        concat_axis=0,
        tiled=True,
    )
    grad_in = lax.all_to_all(grad_out, "expert", split_axis=0, concat_axis=0, tiled=True).reshape(
        -1, width
    )
    in_local, back_local, dincoming = expert_backward(
        incoming, pre_act, active, grad_in, w_in[0], w_back[0]
    )
    grad_back = lax.all_to_all(
        dincoming.reshape(experts, capacity, slot, width),
        "expert",
        split_axis=0,
        concat_axis=0,
        tiled=True,
    )
    ycopy = project(collect, returned.reshape(experts * capacity, slot * width)).reshape(
        sents, 2, slot, width
    )
    expert_mixture = jnp.sum(gate_values[:, :, None, None] * ycopy, axis=1)
    total = mask3 * (hidden_res + expert_mixture)
    output = total.astype(jnp.bfloat16)
    stats_local = jnp.stack(
        [
            jnp.sum(total * total),
            jnp.sum(attn_sum),
            jnp.sum(mask3 * expert_mixture * expert_mixture),
            jnp.sum(valid),
        ]
    )
    stat_totals = lax.psum(stats_local, ("dp", "expert"))
    gate_dot = jnp.sum(ycopy * grad_total[:, None], axis=(2, 3))
    dpicked = gate_values * (gate_dot - jnp.sum(gate_values * gate_dot, axis=-1, keepdims=True))
    dlogits = jnp.sum(expert_hot * dpicked[:, :, None], axis=1)
    table_grad = jnp.dot(task_hot.T.astype(jnp.float32), dlogits, precision=lax.Precision.HIGHEST)
    dmixed = project(collect, grad_back.reshape(experts * capacity, slot * width)).reshape(
        sents, 2, slot, width
    )
    dmixed = jnp.sum(dmixed, axis=1)
    input_grad, wq_grad, wk_grad, wv_grad, wout_grad, norms = attention_backward(
        lengths, tokens, cotangent, dmixed, hidden, act, query, keyed, valued, context, prob,
        w_query, w_key, w_value, w_out, ln1_gain, ln2_gain, heads,
    )
    gain1_grad, bias1_grad, gain2_grad, bias2_grad = norms[0], norms[1], norms[2], norms[3]
    members = (
        wq_grad,
        wk_grad,
        wv_grad,
        wout_grad,
        gain1_grad,
        bias1_grad,
        gain2_grad,
        bias2_grad,
        table_grad,
    )
    members = members + ()
    summed = lax.psum(members, ("dp", "expert"))
    rms = jnp.sqrt(stat_totals[0:3] / (stat_totals[3] * width))
    in_share, back_share = (
        lax.psum_scatter(
            in_local.astype(jnp.bfloat16), "dp", scatter_dimension=0, tiled=True
        ).astype(jnp.float32),
        lax.psum_scatter(
            back_local.astype(jnp.bfloat16), "dp", scatter_dimension=0, tiled=True
        ).astype(jnp.float32),
    )
    return (
        output,
        input_grad,
        summed[8],
        summed[4],
        summed[5],
        summed[6],
        summed[7],
        summed[0],
        summed[1],
        summed[2],
        summed[3],
        in_share[None],
        back_share[None],
        rms,
    )


def local_plane(
    depth,
    tokens,
    lengths,
    tasks,
    routes,
    gate_table,
    ln1_gain,
    ln1_bias,
    ln2_gain,
    ln2_bias,
    w_query,
    w_key,
    w_value,
    w_out,
    w_in,
    w_back,
    cotangent,
):
    sents, slot, width = tokens.shape
    heads = HEADS
    experts = gate_table.shape[1]
    ntasks = routes.shape[0]
    capacity = max(1, 4 * sents // experts)
    task_hot = (tasks[:, None] == jnp.arange(ntasks)[None, :]).astype(jnp.int32)
    chosen = jnp.sum(task_hot[:, :, None] * routes[None, :, :], axis=1)
    flat = chosen.reshape(-1)
    order = jnp.arange(2 * sents)
    earlier = (flat[:, None] == flat[None, :]) & (order[None, :] < order[:, None])
    rank = jnp.sum(earlier.astype(jnp.int32), axis=1)
    slot_id = flat * capacity + rank
    placed = rank < capacity
    expert_hot = (chosen[:, :, None] == jnp.arange(experts)[None, None, :]).astype(jnp.float32)
    valid = (jnp.arange(slot)[None, :] < lengths[:, None]).astype(jnp.float32)
    act, query, keyed, valued, context, prob, hidden, mixed, attn_sum = attention_forward(
        tokens, lengths, w_query, w_key, w_value, w_out,
        ln1_gain, ln1_bias, ln2_gain, ln2_bias, heads,
    )
    table_rows = jnp.dot(task_hot.astype(jnp.float32), gate_table, precision=lax.Precision.HIGHEST)
    picked = jnp.sum(expert_hot * table_rows[:, None, :], axis=-1)
    gate_values = jax.nn.softmax(picked, axis=-1)
    hits = (
        (jnp.arange(experts * capacity)[:, None] == slot_id[None, :]) & placed[None, :]
    ).astype(jnp.float32)
    per_copy = jnp.stack(
        [
            (order // 2).astype(jnp.float32),
            jnp.repeat(lengths, 2).astype(jnp.float32),
            gate_values.reshape(-1),
        ]
    )
    per_slot = jnp.sum(hits[None] * per_copy[:, None, :], axis=-1).reshape(3, experts, capacity)
    taken = (flat[None, :] == jnp.arange(experts)[:, None]) & placed[None, :]
    ranks = jnp.sum(
        (taken * (rank + 1)[None, :]).reshape(experts, sents, 2), axis=-1
    ).astype(jnp.float32)
    sent_table = jnp.concatenate([per_slot[0], per_slot[1], ranks - 1.0, per_slot[2]], axis=1)
    table = lax.all_gather(sent_table, "expert")
    entries = 2 * capacity + sents
    places = table[:, :, :entries].astype(jnp.int32).reshape(experts, -1)
    gate_slots = table[:, :, entries:].reshape(experts, -1)
    dmixed, parts_back, in_local, back_local, slot_dots = expert_exchange(
        places, gate_slots, mixed, cotangent, w_in[0], w_back[0], capacity
    )
    me = lax.axis_index("expert")
    dots_here = jnp.take(slot_dots[:, :, 0], me ^ jnp.arange(experts), axis=0).reshape(-1)
    gate_dot = jnp.sum(hits * dots_here[:, None], axis=0).reshape(sents, 2)
    dpicked = gate_values * (gate_dot - jnp.sum(gate_values * gate_dot, axis=-1, keepdims=True))
    dlogits = jnp.sum(expert_hot * dpicked[:, :, None], axis=1)
    table_grad = jnp.dot(task_hot.T.astype(jnp.float32), dlogits, precision=lax.Precision.HIGHEST)
    row = lambda value: jnp.pad(value.reshape(-1), (0, width - value.size))[None]
    empty = jnp.zeros((4, width), jnp.float32)
    small = jnp.concatenate(
        [empty, attn_sum, empty[:2], row(jnp.sum(valid)), row(table_grad), empty, empty[:3]]
    )
    input_grad, output, sum_o, sum_0, sum_1, in_share, back_share, small = backward_exchange(
        depth, lengths, tokens, cotangent, dmixed, hidden, act, query, keyed, valued, context,
        prob, w_query, w_key, w_value, w_out, ln1_gain, ln2_gain,
        small, parts_back, in_local, back_local, heads,
    )
    sides = jnp.concatenate([sum_0, sum_1], axis=1).astype(jnp.float32)
    wide = lambda place: sides[place * width : (place + 1) * width]
    sums = jnp.sum(small[4:8], axis=1)
    rms = jnp.sqrt(jnp.stack([sums[1], sums[0], sums[2]]) / (sums[3] * width))
    return (
        output,
        input_grad,
        small[8, : table_grad.size].reshape(table_grad.shape),
        small[0],
        small[1],
        small[2],
        small[3],
        wide(0),
        wide(1),
        wide(2),
        sum_o.astype(jnp.float32),
        in_share[None],
        back_share[None],
        rms,
    )


def solution(mesh):
    in_specs = (
        P(("dp", "expert"), None, None),
        P(("dp", "expert")),
        P(("dp", "expert")),
        P(),
        P(),
        P(),
        P(),
        P(),
        P(),
        P(),
        P(),
        P(),
        P(),
        P("expert", None, None),
        P("expert", None, None),
        P(("dp", "expert"), None, None),
    )
    out_specs = (
        P(("dp", "expert"), None, None),
        P(("dp", "expert"), None, None),
        P(),
        P(),
        P(),
        P(),
        P(),
        P(),
        P(),
        P(),
        P(),
        P("expert", "dp", None),
        P("expert", "dp", None),
        P(),
    )
    plane = dict(mesh.shape)["expert"]
    depth = dict(mesh.shape)["dp"]
    body = functools.partial(local_plane, depth) if plane == 2 * 2 * 2 else local
    return jax.shard_map(body, mesh=mesh, in_specs=in_specs, out_specs=out_specs, check_vma=False)
```

```python
import functools

import jax
import jax.numpy as jnp
from jax import lax
from jax.experimental import pallas as pl
from jax.experimental.pallas import tpu as pltpu
from jax.sharding import PartitionSpec as P

HEADS = 8


def normalize(value):
    centered = value - jnp.mean(value, axis=-1, keepdims=True)
    variance = jnp.mean(centered * centered, axis=-1, keepdims=True)
    inverse = lax.rsqrt(variance + 1e-05)
    return (centered * inverse, inverse)


def norm_backward(grad, normed, inverse, gain):
    scaled = grad * gain
    inner = scaled - jnp.mean(scaled, axis=-1, keepdims=True)
    inner = inner - normed * jnp.mean(scaled * normed, axis=-1, keepdims=True)
    return (inverse * inner, jnp.sum(grad * normed, axis=(0, 1)), jnp.sum(grad, axis=(0, 1)))


def project(left, right):
    return jnp.dot(left, right, preferred_element_type=jnp.float32)


def expert_forward(incoming, first, second):
    pre_act = project(incoming, first)
    active = jax.nn.gelu(pre_act).astype(jnp.bfloat16)
    produced = project(active, second).astype(jnp.bfloat16)
    return (pre_act, active, produced)


def expert_backward(incoming, pre_act, active, grad_in, first, second):
    dactive = project(grad_in, second.T)
    back_local = project(active.T, grad_in)
    gelu_pull = jax.vjp(jax.nn.gelu, pre_act)[1]
    dpre = gelu_pull(dactive)[0].astype(jnp.bfloat16)
    in_local = project(incoming.T, dpre)
    dincoming = project(dpre, first.T).astype(jnp.bfloat16)
    return (in_local, back_local, dincoming)


BF = jnp.bfloat16
F32 = jnp.float32
VM = pltpu.VMEM


def mm(a, b, ca=1, cb=0):
    return lax.dot_general(a, b, (((ca,), (cb,)), ((), ())), preferred_element_type=F32)


def block_diagonal(group, slot, head):
    shape = (group * slot, group * head)
    rows = lax.broadcasted_iota(jnp.int32, shape, 0) // slot
    cols = lax.broadcasted_iota(jnp.int32, shape, 1) // head
    return rows == cols


def spread(part, mask, group):
    return jnp.where(mask, jnp.concatenate([part] * group, axis=0), jnp.zeros((), part.dtype))


def fold(product, mask, slot, group):
    kept = jnp.where(mask, product, 0.0)
    total = kept[0:slot]
    for one in range(1, group):
        total = total + kept[one * slot : (one + 1) * slot]
    return total


def attend(query, keyed, valued, length, mask, slot, group, scale):
    scores = mm(keyed, spread(query, mask, group), 1, 1) * scale
    place = lax.broadcasted_iota(jnp.int32, scores.shape, 0)
    scores = jnp.where(place < length, scores, -1000000000.0)
    raised = jnp.exp(scores - jnp.max(scores, axis=0, keepdims=True))
    prob = raised / jnp.sum(raised, axis=0, keepdims=True)
    context = fold(mm(prob.astype(BF), valued, 0, 0), mask, slot, group)
    return prob, context


def route_tables(cap, tasks, lengths, routes, gate_table):
    sents = tasks.shape[1]
    ntasks, experts = gate_table.shape
    iota = lambda rows, cols, axis: lax.broadcasted_iota(jnp.int32, (rows, cols), axis)
    hot = (iota(ntasks, sents, 0) == tasks).astype(F32)
    first = jnp.sum(hot * routes[:, 0:1].astype(F32), axis=0, keepdims=True)
    second = jnp.sum(hot * routes[:, 1:2].astype(F32), axis=0, keepdims=True)
    expert = iota(experts, sents, 0).astype(F32)
    is_first, is_second = expert == first, expert == second
    hit = jnp.logical_or(is_first, is_second)
    before = (iota(sents, sents, 0) < iota(sents, sents, 1)).astype(BF)
    rank = mm(hit.astype(F32).astype(BF), before)
    place = jnp.where(hit, jnp.where(rank < cap, rank, -1.0), -1.0)
    logits = lax.dot_general(
        gate_table, hot, (((0,), (0,)), ((), ())), precision=lax.Precision.HIGHEST,
        preferred_element_type=F32,
    )
    one = jnp.sum(jnp.where(is_first, logits, 0.0), axis=0, keepdims=True)
    two = jnp.sum(jnp.where(is_second, logits, 0.0), axis=0, keepdims=True)
    peak = jnp.maximum(one, two)
    one, two = jnp.exp(one - peak), jnp.exp(two - peak)
    gate = jnp.where(is_first, one / (one + two), 0.0)
    gate = gate + jnp.where(is_second, two / (one + two), 0.0)
    lane = iota(experts, 128, 1)
    index = iota(experts, sents, 1).astype(F32)
    table = jnp.zeros((experts, 128), F32)
    gates = jnp.zeros((experts, 128), F32)
    for j in range(cap):
        here = place == float(j)
        pick = lambda value: jnp.sum(jnp.where(here, value, 0.0), axis=1, keepdims=True)
        table = jnp.where(lane == j, pick(index), table)
        table = jnp.where(lane == cap + j, pick(lengths.astype(F32)), table)
        gates = jnp.where(lane == j, pick(gate), gates)
    shift = (iota(sents, 128, 1) == iota(sents, 128, 0) + 2 * cap).astype(BF)
    spots = mm((place + 1.0).astype(BF), shift)
    inside = jnp.logical_and(lane >= 2 * cap, lane < 2 * cap + sents)
    table = jnp.where(inside, spots - 1.0, table)
    return table.astype(jnp.int32), gates, hit.astype(F32), place, gate


def attention_forward_kernel(
    heads, cap, len_ref, x_ref, wq, wk, wv, wo, g1, b1, g2, b2, tasks, lengths, routes,
    gate_table, cot,
    act_o, q_o, k_o, v_o, ctx_o, p_o, h_o, m_o, st_o, plan_o, tab_o, gates_o, near_o, far_o,
    core_o, tab_s, gates_s, sends, recvs, local,
):
    count, slot, width = x_ref.shape
    head = width // heads
    group = max(1, min(heads, 256 // head))
    span = group * head
    step = pl.program_id(0)
    scale = head ** -0.5
    mask = block_diagonal(group, slot, head)
    experts = gate_table.shape[1]
    me = lax.axis_index("expert")
    half = cot.shape[0] // 2
    copies = [
        remote(cot.at[pl.ds(0, half)], near_o, sends, recvs, 0, NEAR),
        remote(cot.at[pl.ds(half, half)], far_o, sends, recvs, 1, FAR),
        remote(cot, core_o, sends, recvs, 2, CORE),
    ]
    for relation in range(1, 8):
        there = plane_peer(relation)
        copies += [
            remote(tab_s.at[there], tab_o.at[me], sends, recvs, 1 + 2 * relation, relation),
            remote(gates_s.at[there], gates_o.at[me], sends, recvs, 2 + 2 * relation, relation),
        ]
    own = [
        pltpu.make_async_copy(tab_s.at[me], tab_o.at[me], local.at[0]),
        pltpu.make_async_copy(gates_s.at[me], gates_o.at[me], local.at[1]),
    ]

    @pl.when(step == 0)
    def _():
        plane_barrier()
        for copy in copies[0:3]:
            copy.start()
        table, gates, hit, place, gate = route_tables(
            cap, tasks[...], lengths[...], routes[...], gate_table[...]
        )
        for e in range(experts):
            tab_s[e] = jnp.broadcast_to(table[e : e + 1], (8, 128))
            gates_s[e] = jnp.broadcast_to(gates[e : e + 1], (8, 128))
        for copy in copies[3:]:
            copy.start()
        for copy in own:
            copy.start()
        plan_o[0:experts] = hit
        plan_o[experts : 2 * experts] = place
        plan_o[2 * experts : 3 * experts] = gate
        st_o[...] = jnp.zeros_like(st_o)

    x = x_ref[...].astype(F32).reshape(count * slot, width)
    normed, _ = normalize(x)
    act = (normed * g1[...] + b1[...]).astype(BF)
    act_o[...] = act
    q_o[...] = mm(act, wq[...]).astype(BF)
    k_o[...] = mm(act, wk[...]).astype(BF)
    v_o[...] = mm(act, wv[...]).astype(BF)
    for s in range(count):
        length = len_ref[step * count + s]
        rows = slice(s * slot, (s + 1) * slot)
        for part in range(heads // group):
            cols = slice(part * span, (part + 1) * span)
            prob, context = attend(
                q_o[rows, cols], k_o[rows, cols], v_o[rows, cols], length, mask, slot, group, scale
            )
            p_o[s, part] = prob
            ctx_o[rows, cols] = context.astype(BF)
    attn = mm(ctx_o[...], wo[...])
    hidden = x + attn
    h_o[...] = hidden
    normed2, _ = normalize(hidden)
    m_o[...] = (normed2 * g2[...] + b2[...]).astype(BF).reshape(count, slot, width)
    place = lax.broadcasted_iota(jnp.int32, (slot, width), 0)
    total = jnp.zeros((1, width), F32)
    for s in range(count):
        length = len_ref[step * count + s]
        part = attn[s * slot : (s + 1) * slot]
        total = total + jnp.sum(jnp.where(place < length, part * part, 0.0), axis=0, keepdims=True)
    st_o[...] += total

    @pl.when(step == pl.num_programs(0) - 1)
    def _():
        for copy in copies + own:
            copy.wait()


def attention_forward(
    tokens, lengths, wq, wk, wv, wo, g1, b1, g2, b2, tasks, routes, gate_table, cot, heads, cap
):
    sents, slot, width = tokens.shape
    experts = gate_table.shape[1]
    count = 4 if sents % 4 == 0 else 1
    rows = count * slot
    head = width // heads
    group = max(1, min(heads, 256 // head))
    whole = lambda *shape: pl.BlockSpec(shape, lambda i: (0,) * len(shape))
    flat = pl.BlockSpec((rows, width), lambda i: (i, 0))
    cube = pl.BlockSpec((count, slot, width), lambda i: (i, 0, 0))
    probs = pl.BlockSpec((count, heads // group, slot, group * slot), lambda i: (i, 0, 0, 0))
    anywhere = pl.BlockSpec(memory_space=pl.ANY)
    shape = jax.ShapeDtypeStruct
    total = sents * slot
    half = (sents // 2, slot, width)
    return pl.pallas_call(
        functools.partial(attention_forward_kernel, heads, cap),
        grid=(sents // count,),
        in_specs=[pl.BlockSpec(memory_space=pltpu.SMEM), cube]
        + [whole(width, width)] * 4
        + [whole(1, width)] * 4
        + [whole(1, sents)] * 2
        + [whole(*routes.shape), whole(*gate_table.shape), anywhere],
        out_specs=[flat] * 5
        + [probs, flat, cube, whole(1, width), whole(3 * experts, sents)]
        + [anywhere] * 5,
        out_shape=[shape((total, width), BF)] * 5
        + [
            shape((sents, heads // group, slot, group * slot), F32),
            shape((total, width), F32),
            shape((sents, slot, width), BF),
            shape((1, width), F32),
            shape((3 * experts, sents), F32),
            shape((experts, 8, 128), jnp.int32),
            shape((experts, 8, 128), F32),
            shape(half, BF),
            shape(half, BF),
            shape(tokens.shape, BF),
        ],
        scratch_shapes=[
            VM((experts, 8, 128), jnp.int32),
            VM((experts, 8, 128), F32),
            pltpu.SemaphoreType.DMA((17,)),
            pltpu.SemaphoreType.DMA((17,)),
            pltpu.SemaphoreType.DMA((2,)),
        ],
        compiler_params=pltpu.CompilerParams(
            dimension_semantics=("arbitrary",), vmem_limit_bytes=56 * 2**20,
            collective_id=0, has_side_effects=True,
        ),
        cost_estimate=pl.CostEstimate(
            flops=8 * total * width * width + 4 * total * slot * width,
            bytes_accessed=16 * total * width,
            transcendentals=total * slot * heads,
        ),
    )(
        lengths, tokens, wq, wk, wv, wo, g1[None], b1[None], g2[None], b2[None],
        tasks[None], lengths[None], routes, gate_table, cot,
    )


def row_sum(value, width):
    return jnp.sum(value, axis=0, keepdims=True)


def layer_norm_pull(grad, normed, inverse, gain):
    scaled = grad * gain
    inner = scaled - jnp.mean(scaled, axis=-1, keepdims=True)
    inner = inner - normed * jnp.mean(scaled * normed, axis=-1, keepdims=True)
    return inverse * inner


def attention_pull(dcontext, query, keyed, valued, prob, mask, slot, group, scale):
    low = prob.astype(BF)
    dspread = spread(dcontext, mask, group)
    dprob = mm(valued, dspread, 1, 1)
    inner = jnp.sum(dprob * prob, axis=0, keepdims=True)
    dscores = (prob * (dprob - inner)).astype(BF)
    dquery = fold(mm(dscores, keyed, 0, 0), mask, slot, group) * scale
    dkeyed = mm(dscores, spread(query, mask, group)) * scale
    dvalued = mm(low, dspread)
    return dquery.astype(BF), dkeyed.astype(BF), dvalued.astype(BF)


MESH_ID = pl.DeviceIdType.MESH
CORE, NEAR, FAR = 1, 2, 4


def plane_peer(relation):
    me = lax.axis_index("expert")
    bits = []
    for bit in (CORE, NEAR, FAR):
        value = (me // bit) % 2
        bits.append((1 - value if relation & bit else value) * bit)
    return bits[0] + bits[1] + bits[2]


def remote(src, dst, sends, recvs, index, relation):
    return pltpu.make_async_remote_copy(
        src_ref=src,
        dst_ref=dst,
        send_sem=sends.at[index],
        recv_sem=recvs.at[index],
        device_id=(lax.axis_index("dp"), plane_peer(relation)),
        device_id_type=MESH_ID,
    )


def plane_barrier():
    barrier = pltpu.get_barrier_semaphore()
    for relation in range(1, 8):
        pl.semaphore_signal(
            barrier,
            inc=1,
            device_id=(lax.axis_index("dp"), plane_peer(relation)),
            device_id_type=MESH_ID,
        )
    pl.semaphore_wait(barrier, 7)


def gather_copies(own, held, sends, recvs, base):
    half = own.shape[0] // 2
    low, high = pl.ds(0, half), pl.ds(half, half)
    plan = [
        (own.at[low], held[2].at[low], NEAR),
        (own.at[high], held[4].at[high], FAR),
        (own, held[1], CORE),
        (own.at[high], held[2].at[high], NEAR),
        (own.at[low], held[4].at[low], FAR),
        (held[2].at[low], held[6].at[low], FAR),
        (held[4].at[high], held[6].at[high], NEAR),
        (held[2], held[3], CORE),
        (held[4], held[5], CORE),
        (held[6], held[7], CORE),
    ]
    return [
        remote(src, dst, sends, recvs, base + place, relation)
        for place, (src, dst, relation) in enumerate(plan)
    ]


def return_copies(parts, cores, sides, sends, recvs, base):
    half = parts[0].shape[0] // 2
    low, high = pl.ds(0, half), pl.ds(half, half)
    plan = [
        (parts[1], cores[0], CORE),
        (parts[3], cores[2], CORE),
        (parts[5], cores[4], CORE),
        (parts[7], cores[6], CORE),
        (parts[2].at[low], sides[0], NEAR),
        (parts[6].at[low], sides[1], NEAR),
        (parts[4].at[high], sides[2], FAR),
        (parts[6].at[high], sides[3], FAR),
        (parts[4].at[low], sides[4], FAR),
        (parts[2].at[high], sides[5], NEAR),
    ]
    return [
        remote(src, dst, sends, recvs, base + place, relation)
        for place, (src, dst, relation) in enumerate(plan)
    ]


def add_into(target, start, other, count):
    def one(i, carry):
        total = target[start + i].astype(F32) + other[i].astype(F32)
        target[start + i] = total.astype(BF)
        return carry

    lax.fori_loop(0, count, one, 0)


def return_finish(parts, sides, back, out):
    half = out.shape[0] // 2
    back[4].wait_recv()
    add_into(parts[0], 0, sides[0], half)
    back[5].wait_recv()
    add_into(parts[4], 0, sides[1], half)
    back[8].start()
    back[6].wait_recv()
    add_into(parts[0], half, sides[2], half)
    back[7].wait_recv()
    add_into(parts[2], half, sides[3], half)
    back[9].start()
    back[8].wait_recv()
    add_into(parts[0], 0, sides[4], half)
    back[9].wait_recv()
    add_into(parts[0], half, sides[5], half)

    def one(i, carry):
        out[i] = parts[0][i]
        return carry

    lax.fori_loop(0, out.shape[0], one, 0)
    for copy in back:
        copy.wait_send()


GELU_A = 0.7978845608028654
GELU_B = 0.044715


def expert_kernel(
    cap, tab, gates, m_in, cot_in, near_in, far_in, core_in, win_in, wback_in,
    dm_o, py_o, gin_o, gback_o, dg_o, *scratch
):
    sents, slot, width = m_in.shape
    hidden = win_in.shape[1]
    half = sents // 2
    held_m = dict(zip(range(8), scratch[0:8]))
    held_c = dict(zip(range(8), scratch[8:16]))
    parts = dict(zip(range(8), scratch[16:24]))
    cores = dict(zip((0, 2, 4, 6), scratch[24:28]))
    sides = scratch[28:34]
    win, wback = scratch[34:36]
    xs, gs, dys, zs, dus, ys, dms, stage, dg_s, accb, acci, sends, recvs, local = scratch[36:]
    me = lax.axis_index("expert")
    tile = min(1024, hidden)
    low, high = pl.ds(0, half), pl.ds(half, half)
    loads = [
        pltpu.make_async_copy(src, dst, local.at[2 + place])
        for place, (src, dst) in enumerate(
            [
                (m_in, held_m[0]),
                (cot_in, held_c[0]),
                (win_in, win),
                (wback_in, wback),
                (core_in, held_c[1]),
                (near_in, held_c[2].at[low]),
                (far_in, held_c[4].at[high]),
            ]
        )
    ]
    for load in loads:
        load.start()

    plane_barrier()
    to_m = gather_copies(m_in, held_m, sends, recvs, 0)
    to_c = gather_copies(cot_in, held_c, sends, recvs, 10)
    back = return_copies(parts, cores, sides, sends, recvs, 20)
    gates_back = {
        r: remote(dg_s.at[r], dg_o.at[me], sends, recvs, 30 + r, r) for r in range(1, 8)
    }
    for place in (0, 1, 2, 3, 4):
        to_m[place].start()
    for place in (3, 4):
        to_c[place].start()
    accb[...] = jnp.zeros_like(accb)
    acci[...] = jnp.zeros_like(acci)
    place = lax.broadcasted_iota(jnp.int32, (slot, width), 0)
    for load in loads[0:4]:
        load.wait()

    def arrive(*indices):
        for index in indices:
            to_m[index].wait_recv()
            if index > 2:
                to_c[index].wait_recv()

    def forward(*indices):
        for index in indices:
            to_m[index].start()
            to_c[index].start()

    def before(r):
        if r == 1:
            arrive(2)
            loads[4].wait()
        if r == 2:
            loads[5].wait()
            loads[6].wait()
            arrive(0, 1)
            forward(5, 6)
            arrive(3)
            forward(7)
            arrive(4)
            forward(8)
        if r == 3:
            arrive(7)
        if r == 5:
            arrive(8)
        if r == 6:
            arrive(5, 6)
            forward(9)
        if r == 7:
            arrive(9)
        source = plane_peer(r)

        def fetch(j, carry):
            index = tab[source, 0, j]
            length = tab[source, 0, cap + j]
            gate = gates[source, 0, j]
            xs[j] = held_m[r][index]
            gt = jnp.where(place < length, held_c[r][index].astype(F32), 0.0)
            gs[j] = gt.astype(BF)
            dys[j] = (gt * gate).astype(BF)
            return carry

        lax.fori_loop(0, cap, fetch, 0, unroll=2)

    def after(r):
        source = plane_peer(r)
        if r >= 2:
            pltpu.make_async_copy(stage.at[r % 2], py_o.at[r - 2], local.at[r % 2]).wait()

        def give(i, carry):
            index = tab[source, 0, 2 * cap + i]
            there = jnp.maximum(index, 0)
            gate = gates[source, 0, there]
            hit = (index >= 0).astype(F32)
            parts[r][i] = (dms[there].astype(F32) * hit).astype(BF)
            stage[r % 2, i] = (ys[there].astype(F32) * (hit * gate)).astype(BF)
            return carry

        lax.fori_loop(0, sents, give, 0, unroll=2)
        pltpu.make_async_copy(stage.at[r % 2], py_o.at[r], local.at[r % 2]).start()

        def dots(j, carry):
            product = ys[j].astype(F32) * gs[j].astype(F32)
            total = jnp.sum(jnp.sum(product, axis=0, keepdims=True), axis=1, keepdims=True)
            if r == 0:
                dg_o[me, pl.ds(j, 1)] = jnp.broadcast_to(total, (1, 128))
            else:
                dg_s[r, pl.ds(j, 1)] = jnp.broadcast_to(total, (1, 128))
            return carry

        lax.fori_loop(0, cap, dots, 0, unroll=4)
        if r > 0:
            gates_back[r].start()
        if r % 2 == 1:
            back[r // 2].start()
        if r == 4:
            back[1].wait_recv()
            add_into(parts[2], 0, cores[2], sents)
            back[4].start()
        if r == 6:
            back[2].wait_recv()
            add_into(parts[4], 0, cores[4], sents)
            back[6].start()
        if r == 7:
            back[3].wait_recv()
            add_into(parts[6], 0, cores[6], sents)
            back[5].start()
            back[7].start()
            back[0].wait_recv()
            add_into(parts[0], 0, cores[0], sents)

    def chunk(t, carry):
        for r in range(8):
            pl.when(t == r)(functools.partial(before, r))
        x = xs[...].reshape(cap * slot, width)
        dy = dys[...].reshape(cap * slot, width)

        def inner(f, carry):
            cols = pl.ds(pl.multiple_of(f * tile, tile), tile)
            u = mm(x, win[:, cols])
            square = u * u
            th = jnp.tanh(u * (GELU_A + GELU_A * GELU_B * square))
            cdf = 0.5 + 0.5 * th
            slope = cdf + (0.5 * u) * (1.0 - th * th) * (GELU_A + 3 * GELU_A * GELU_B * square)
            z = (u * cdf).astype(BF)
            zs[:, cols] = z
            dz = mm(dy, wback[cols, :], 1, 1)
            du = (dz * slope).astype(BF)
            dus[:, cols] = du
            accb[cols, :] += mm(z, dy, 0, 0)
            acci[:, cols] += mm(x, du, 0, 0)
            return carry

        lax.fori_loop(0, hidden // tile, inner, 0)
        ys[...] = mm(zs[...], wback[...]).astype(BF).reshape(cap, slot, width)
        dms[...] = mm(dus[...], win[...], 1, 1).astype(BF).reshape(cap, slot, width)
        for r in range(8):
            pl.when(t == r)(functools.partial(after, r))
        return carry

    lax.fori_loop(0, 8, chunk, 0)
    win[...] = acci[...].astype(BF)
    wback[...] = accb[...].astype(BF)
    stores = [
        pltpu.make_async_copy(win, gin_o, local.at[4]),
        pltpu.make_async_copy(wback, gback_o, local.at[5]),
    ]
    for store in stores:
        store.start()
    return_finish(parts, sides, back, dm_o)
    for store in stores:
        store.wait()
    for r in range(1, 8):
        gates_back[r].wait()
    for index in range(10):
        to_m[index].wait_send()
        if index > 2:
            to_c[index].wait_send()
    for r in (6, 7):
        pltpu.make_async_copy(stage.at[r % 2], py_o.at[r], local.at[r % 2]).wait()


def expert_exchange(tab, gates, m, cot, near, far, core, win, wback, cap):
    sents, slot, width = m.shape
    hidden = win.shape[1]
    vm = pl.BlockSpec(memory_space=VM)
    sm = pl.BlockSpec(memory_space=pltpu.SMEM)
    anywhere = pl.BlockSpec(memory_space=pl.ANY)
    shape = jax.ShapeDtypeStruct
    cube = (sents, slot, width)
    rows = cap * slot
    return pl.pallas_call(
        functools.partial(expert_kernel, cap),
        in_specs=[sm, sm] + [anywhere] * 7,
        out_specs=[vm, anywhere, anywhere, anywhere, vm],
        out_shape=[
            shape(cube, BF),
            shape((8,) + cube, BF),
            shape((width, hidden), BF),
            shape((hidden, width), BF),
            shape((8, cap, 128), F32),
        ],
        scratch_shapes=[VM(cube, BF)] * (16 + 8 + 4)
        + [VM((sents // 2, slot, width), BF)] * 6
        + [VM((width, hidden), BF), VM((hidden, width), BF)]
        + [VM((cap, slot, width), BF)] * 3
        + [VM((rows, hidden), BF)] * 2
        + [VM((cap, slot, width), BF)] * 2
        + [VM((2,) + cube, BF), VM((8, cap, 128), F32)]
        + [VM((hidden, width), F32), VM((width, hidden), F32)]
        + [
            pltpu.SemaphoreType.DMA((38,)),
            pltpu.SemaphoreType.DMA((38,)),
            pltpu.SemaphoreType.DMA((9,)),
        ],
        compiler_params=pltpu.CompilerParams(
            collective_id=1, has_side_effects=True, vmem_limit_bytes=63 * 2**20
        ),
        cost_estimate=pl.CostEstimate(
            flops=12 * 8 * rows * width * hidden, bytes_accessed=40 * 2**20, transcendentals=0
        ),
    )(tab, gates, m, cot, near, far, core, win, wback)


def line_peer(offset, depth):
    return lax.rem(lax.axis_index("dp") + offset, depth)


def along(src, dst, sends, recvs, index, offset, depth):
    return pltpu.make_async_remote_copy(
        src_ref=src,
        dst_ref=dst,
        send_sem=sends.at[index],
        recv_sem=recvs.at[index],
        device_id=(line_peer(offset, depth), lax.axis_index("expert")),
        device_id_type=MESH_ID,
    )


class Reduction:
    def __init__(self, depth, value, wide, core_r, plane_r, line_s, line_r, final, sems, base):
        self.depth, self.value, self.wide, self.final = depth, value, wide, final
        self.core_r, self.plane_r, self.line_s, self.line_r = core_r, plane_r, line_s, line_r
        sends, recvs = sems
        me = lax.axis_index("expert")
        z = lax.axis_index("dp")
        core = me % 2
        self.half = value.shape[0] // 2
        self.quarter = self.half // 4
        self.share = self.quarter // depth
        self.mine = core * self.half
        self.other = (1 - core) * self.half
        self.block = self.mine + (me // 2) * self.quarter
        self.own = self.block + z * self.share
        self.to_core = remote(wide, core_r, sends, recvs, base, CORE)
        self.to_plane = []
        self.from_plane = []
        for place, relation in enumerate((2, 4, 6)):
            rows = pl.ds((plane_peer(relation) // 2) * self.quarter, self.quarter)
            self.to_plane.append(
                remote(wide.at[rows], plane_r.at[place], sends, recvs, base + 1 + place, relation)
            )
        self.to_line = []
        for offset in range(1, depth):
            rows = pl.ds(line_peer(offset, depth) * self.share, self.share)
            self.to_line.append(
                along(
                    line_s.at[rows], line_r.at[offset - 1], sends, recvs, base + 3 + offset,
                    offset, depth,
                )
            )
        after = base + 3 + depth
        rows = final.at[pl.ds(self.own, self.share)]
        self.back_line = [
            along(rows, rows, sends, recvs, after + offset - 1, offset, depth)
            for offset in range(1, depth)
        ]
        after = after + depth - 1
        rows = final.at[pl.ds(self.block, self.quarter)]
        self.back_plane = [
            remote(rows, rows, sends, recvs, after + place, relation)
            for place, relation in enumerate((2, 4, 6))
        ]
        rows = final.at[pl.ds(self.mine, self.half)]
        self.back_core = remote(rows, rows, sends, recvs, after + 3, CORE)

    @staticmethod
    def semaphores(depth):
        return 2 * depth + 6

    def send_core(self):
        self.wide[...] = self.value[pl.ds(self.other, self.half), :].astype(BF)
        self.to_core.start()

    def send_plane(self):
        self.to_core.wait()
        rows = pl.ds(self.mine, self.half)
        total = self.value[rows, :] + self.core_r[...].astype(F32)
        self.value[rows, :] = total
        self.wide[...] = total.astype(BF)
        for copy in self.to_plane:
            copy.start()

    def send_line(self):
        for copy in self.to_plane:
            copy.wait()
        rows = pl.ds(self.block, self.quarter)
        total = self.value[rows, :]
        for place in range(3):
            total = total + self.plane_r[place].astype(F32)
        self.value[rows, :] = total
        self.line_s[...] = total.astype(BF)
        for copy in self.to_line:
            copy.start()

    def send_back_line(self):
        for copy in self.to_line:
            copy.wait()
        rows = pl.ds(self.own, self.share)
        total = self.value[rows, :]
        for offset in range(1, self.depth):
            total = total + self.line_r[offset - 1].astype(F32)
        self.final[rows, :] = total.astype(BF)
        for copy in self.back_line:
            copy.start()

    def send_back_plane(self):
        for copy in self.back_line:
            copy.wait()
        for copy in self.back_plane:
            copy.start()

    def send_back_core(self):
        for copy in self.back_plane:
            copy.wait()
        self.back_core.start()

    def finish(self):
        self.back_core.wait()


def backward_kernel(
    heads, depth, len_ref, x_ref, cot_ref, dm_ref, h_ref, act, q, k, v, ctx, p_ref,
    wq, wk, wv, wo, g1, g2, attn_sum, plan, tasks, lengths, dots, py, gin, gback,
    ig_o, out_o, fin_o, fin_0, fin_1, gin_o, gback_o, small_o, *scratch
):
    sents, slot, width = x_ref.shape
    total_rows = sents * slot
    head = width // heads
    group = max(1, min(heads, 256 // head))
    span = group * head
    scale = head ** -0.5
    count = 4 if sents % 4 == 0 else 1
    rows_per = count * slot
    z = lax.axis_index("dp")
    parts = {0: scratch[0], 2: scratch[1], 4: scratch[2], 6: scratch[3]}
    cores = dict(zip((0, 2, 4, 6), scratch[4:8]))
    sides = scratch[8:14]
    dh_s, da_s, dctx_s, dq_s, dk_s, dv_s = scratch[14:20]
    red = scratch[20:38]
    line_in, line_back, extra_in, extra_back = scratch[38:42]
    small, small_core, small_plane, small_line = scratch[42:46]
    gin_s, gback_s = scratch[46:48]
    sends, recvs, local = scratch[48:]
    sems = (sends, recvs)
    grad_loads = [
        pltpu.make_async_copy(gin, gin_s, local.at[4]),
        pltpu.make_async_copy(gback, gback_s, local.at[5]),
    ]
    for load in grad_loads:
        load.start()

    loads = {
        r: pltpu.make_async_copy(py.at[r], parts[r], local.at[r // 2]) for r in (0, 2, 4, 6)
    }
    for r in (6, 2, 4, 0):
        loads[r].start()
    barrier = pltpu.get_barrier_semaphore()
    for relation in range(1, 8):
        pl.semaphore_signal(
            barrier, inc=1, device_id=(z, plane_peer(relation)), device_id_type=MESH_ID
        )
    for offset in range(1, depth):
        pl.semaphore_signal(
            barrier,
            inc=1,
            device_id=(line_peer(offset, depth), lax.axis_index("expert")),
            device_id_type=MESH_ID,
        )
    pl.semaphore_wait(barrier, 6 + depth)

    all_parts = dict(parts)
    for r in (1, 3, 5, 7):
        all_parts[r] = py.at[r]
    back = return_copies(all_parts, cores, sides, sends, recvs, 0)
    for r in (7, 3, 5, 1):
        back[r // 2].start()

    base = 10
    in_rows = gin.shape[0] // depth
    back_rows = gback.shape[0] // depth

    def line_piece(s, array, right, last):
        offset = 1 if right else depth - 1
        index = base + (0 if right else 2 * depth) + 2 * s + array
        share, source = ((in_rows, gin_s), (back_rows, gback_s))[array]
        into = (line_in, line_back)[array].at[s]
        if last and not right:
            into = (extra_in, extra_back)[array]
        here = source.at[pl.ds(s * share, share)]
        return along(here, into, sends, recvs, index, offset, depth)

    def add_piece(s, array):
        share, source = ((in_rows, gin_s), (back_rows, gback_s))[array]
        other = (line_in, line_back)[array]
        here = pl.ds(s * share, share)
        source[here, :] = (source[here, :].astype(F32) + other[s].astype(F32)).astype(BF)

    def pieces(right):
        order = range(depth - 1, 0, -1) if right else range(depth - 1)
        return [(s, array) for s in order for array in (0, 1)]

    def start_piece(s, array, right):
        if right:
            line_piece(s, array, True, False).start()
            return
        near = z == s + 1

        @pl.when(near)
        def _():
            line_piece(s, array, False, True).start()

        @pl.when(jnp.logical_not(near))
        def _():
            line_piece(s, array, False, False).start()

    def line_service(t, ahead=1):
        for right in (True, False):
            every = pieces(right)
            edge = 0 if right else depth - 1
            opening = range(0, 1 + ahead) if t == 0 else range(t + ahead, t + ahead + 1)

            @pl.when(z == edge)
            def _():
                for number in opening:
                    if number < len(every):
                        start_piece(*every[number], right)

            for number, (s, array) in enumerate(every):
                hops = t - number
                away = s if right else depth - 1 - s
                if 0 < hops < away:

                    @pl.when(z == (hops if right else depth - 1 - hops))
                    def _():
                        line_piece(s, array, right, False).wait_recv()
                        add_piece(s, array)
                        start_piece(s, array, right)

    def line_end():
        for s in range(depth):

            @pl.when(z == s)
            def _():
                here = pl.ds(s * in_rows, in_rows)
                there = pl.ds(s * back_rows, back_rows)
                gin_o[...] = gin_s[here, :].astype(F32)
                gback_o[...] = gback_s[there, :].astype(F32)
                if s > 0:
                    for array in (0, 1):
                        line_piece(s, array, True, True).wait_recv()
                    gin_o[...] += line_in[s].astype(F32)
                    gback_o[...] += line_back[s].astype(F32)
                if s < depth - 1:
                    for array in (0, 1):
                        line_piece(s, array, False, True).wait_recv()
                    gin_o[...] += extra_in[...].astype(F32)
                    gback_o[...] += extra_back[...].astype(F32)

        for s in range(depth):
            for array in (0, 1):

                @pl.when(z < s)
                def _():
                    line_piece(s, array, True, False).wait_send()

                @pl.when(z > s)
                def _():
                    line_piece(s, array, False, False).wait_send()

    for load in grad_loads:
        load.wait()
    line_service(0)

    base_red = base + 4 * depth
    per = Reduction.semaphores(depth)
    reds = []
    for place, final in enumerate((fin_o, fin_0, fin_1)):
        value, wide, core_r, plane_r, line_s, line_r = red[6 * place : 6 * place + 6]
        reds.append(
            Reduction(
                depth, value, wide, core_r, plane_r, line_s, line_r, final, sems,
                base_red + place * per,
            )
        )
    red_o, red_0, red_1 = reds

    small[...] = jnp.zeros_like(small)
    small[4:5] = attn_sum[...]
    small[7:8, 0:sents] = lengths[...].astype(F32)
    experts = plan.shape[0] // 3
    chunk_place = lax.broadcasted_iota(jnp.int32, (slot, width), 0)

    def masked(ref, c):
        return jnp.concatenate(
            [
                jnp.where(
                    chunk_place < len_ref[c * count + s], ref[c * count + s].astype(F32), 0.0
                )
                for s in range(count)
            ],
            axis=0,
        )

    def flat(ref, c):
        block = ref[pl.ds(c * count, count)]
        return block.astype(F32).reshape(rows_per, width)

    def first(c, carry):
        rows = pl.ds(pl.multiple_of(c * rows_per, rows_per), rows_per)
        normed2, inverse2 = normalize(h_ref[rows, :])
        dm = flat(dm_ref, c)
        dhidden = masked(cot_ref, c) + layer_norm_pull(dm, normed2, inverse2, g2[...])
        small[2:3] += row_sum(dm * normed2, width)
        small[3:4] += row_sum(dm, width)
        dh_s[rows, :] = dhidden
        dattn = dhidden.astype(BF)
        da_s[rows, :] = dattn
        dctx_s[rows, :] = mm(dattn, wo[...], 1, 1).astype(BF)
        return carry

    lax.fori_loop(0, sents // count, first, 0)
    hit = plan[0:experts] > 0.5
    place = plan[experts : 2 * experts]
    gate = plan[2 * experts : 3 * experts]
    taken = jnp.zeros(gate.shape, F32)
    for j in range(dots.shape[1]):
        taken = taken + jnp.where(place == float(j), dots[:, j, 0:sents], 0.0)
    inner = jnp.sum(gate * taken, axis=0, keepdims=True)
    dlogit = jnp.where(hit, gate * (taken - inner), 0.0)
    hot = lax.broadcasted_iota(jnp.int32, (slot, sents), 0) == tasks[...]
    small[8 : 8 + experts, 0:slot] = lax.dot_general(
        dlogit, hot.astype(F32), (((1,), (1,)), ((), ())), precision=lax.Precision.HIGHEST,
        preferred_element_type=F32,
    )
    red_o.value[...] = mm(ctx[...], da_s[...], 0, 0)
    red_o.send_core()
    mask = block_diagonal(group, slot, head)

    def pull(part, into):
        cols = slice(part * span, (part + 1) * span)

        def one(c, carry):
            for s in range(count):
                at = c * count + s
                rows = pl.ds(pl.multiple_of(at * slot, slot), slot)
                dq_s[rows, cols], dk_s[rows, cols], dv_s[rows, cols] = attention_pull(
                    dctx_s[rows, cols], q[rows, cols], k[rows, cols], v[rows, cols],
                    p_ref[at, part], mask, slot, group, scale,
                )
            return carry

        lax.fori_loop(0, sents // count, one, 0)
        into.value[0:width, :] = mm(act[...], dq_s[:, cols], 0, 0)
        into.value[width : 2 * width, :] = mm(act[...], dk_s[:, cols], 0, 0)
        into.value[2 * width : 3 * width, :] = mm(act[...], dv_s[:, cols], 0, 0)
        into.send_core()

    def returned(r, starts):
        loads[r].wait()
        back[r // 2].wait_recv()
        add_into(parts[r], 0, cores[r], sents)
        for index in starts:
            back[index].start()

    pull(0, red_0)
    red_o.send_plane()
    line_service(1)
    returned(6, (5, 7))
    pull(1, red_1)
    red_0.send_plane()
    red_o.send_line()
    line_service(2)
    returned(2, ())
    returned(4, ())
    returned(0, ())

    def last(c, carry):
        rows = pl.ds(pl.multiple_of(c * rows_per, rows_per), rows_per)
        dact = (
            mm(dq_s[rows, :], wq[...], 1, 1)
            + mm(dk_s[rows, :], wk[...], 1, 1)
            + mm(dv_s[rows, :], wv[...], 1, 1)
        )
        normed1, inverse1 = normalize(flat(x_ref, c))
        small[0:1] += row_sum(dact * normed1, width)
        small[1:2] += row_sum(dact, width)
        dx = dh_s[rows, :] + layer_norm_pull(dact, normed1, inverse1, g1[...])
        ig_o[pl.ds(c * count, count)] = dx.astype(BF).reshape(count, slot, width)
        return carry

    lax.fori_loop(0, sents // count, last, 0)
    red_1.send_plane()
    back[4].start()
    back[6].start()
    red_o.send_back_line()
    red_0.send_line()
    line_service(3)
    red_o.send_back_plane()
    red_0.send_back_line()
    red_1.send_line()
    half = sents // 2
    back[5].wait_recv()
    add_into(parts[4], 0, sides[1], half)
    back[7].wait_recv()
    add_into(parts[2], half, sides[3], half)
    line_service(4)
    red_o.send_back_core()
    red_0.send_back_plane()
    red_1.send_back_line()
    back[8].start()
    back[9].start()
    red_1.send_back_plane()
    red_0.send_back_core()
    back[4].wait_recv()
    add_into(parts[0], 0, sides[0], half)
    back[6].wait_recv()
    add_into(parts[0], half, sides[2], half)
    line_service(5)
    red_1.send_back_core()
    back[8].wait_recv()
    back[9].wait_recv()

    def outcome(low, side):
        def one(i, carry):
            at = low + i
            valid = chunk_place < len_ref[at]
            moe = jnp.where(valid, parts[0][at].astype(F32) + side[i].astype(F32), 0.0)
            rows = pl.ds(pl.multiple_of(at * slot, slot), slot)
            total = jnp.where(valid, h_ref[rows, :], 0.0) + moe
            out_o[at] = total.astype(BF)
            small[5:6] += row_sum(total * total, width)
            small[6:7] += row_sum(moe * moe, width)
            return carry

        lax.fori_loop(0, half, one, 0)

    outcome(0, sides[4])
    outcome(half, sides[5])

    base_small = base_red + 3 * per
    me = lax.axis_index("expert")
    to_core = remote(small, small_core, sends, recvs, base_small, CORE)
    to_core.start()
    to_core.wait()
    spot = me // 2
    small_plane[spot] = small[...] + small_core[...]
    to_plane = [
        remote(
            small_plane.at[spot], small_plane.at[spot], sends, recvs, base_small + 1 + place,
            relation,
        )
        for place, relation in enumerate((2, 4, 6))
    ]
    for copy in to_plane:
        copy.start()
    for copy in to_plane:
        copy.wait()
    total = small_plane[0]
    for place in range(1, 4):
        total = total + small_plane[place]
    small_line[z] = total
    to_line = [
        along(
            small_line.at[z], small_line.at[z], sends, recvs, base_small + 3 + offset, offset,
            depth,
        )
        for offset in range(1, depth)
    ]
    for copy in to_line:
        copy.start()
    for copy in to_line:
        copy.wait()
    total = small_line[0]
    for place in range(1, depth):
        total = total + small_line[place]
    small_o[...] = total
    for one in reds:
        one.finish()
    line_end()
    for copy in back:
        copy.wait_send()


def backward_exchange(
    depth, lengths, tokens, cot, dm, hidden, act, q, k, v, ctx, prob, wq, wk, wv, wo, g1, g2,
    attn_sum, plan, tasks, dots, py, gin, gback, heads,
):
    sents, slot, width = tokens.shape
    total = sents * slot
    small = jax.ShapeDtypeStruct((16, width), F32)
    vm = pl.BlockSpec(memory_space=VM)
    shape = jax.ShapeDtypeStruct
    cube = (sents, slot, width)
    head = width // heads
    span = max(1, min(heads, 256 // head)) * head
    pieces = [(width, width), (3 * width, span), (3 * width, width - span)]
    red = []
    for rows, cols in pieces:
        red += [
            VM((rows, cols), F32),
            VM((rows // 2, cols), BF),
            VM((rows // 2, cols), BF),
            VM((3, rows // 8, cols), BF),
            VM((rows // 8, cols), BF),
            VM((depth - 1, rows // 8 // depth, cols), BF),
        ]
    in_share = (gin.shape[0] // depth, gin.shape[1])
    back_share = (gback.shape[0] // depth, gback.shape[1])
    semaphores = 10 + 4 * depth + 3 * Reduction.semaphores(depth) + 4 + depth
    return pl.pallas_call(
        functools.partial(backward_kernel, heads, depth),
        in_specs=[pl.BlockSpec(memory_space=pltpu.SMEM)]
        + [vm] * 21
        + [pl.BlockSpec(memory_space=pl.ANY), pl.BlockSpec(memory_space=pl.ANY)]
        + [pl.BlockSpec(memory_space=pl.ANY)],
        out_specs=[vm] * 8,
        out_shape=[shape(cube, BF), shape(cube, BF)]
        + [shape(piece, BF) for piece in pieces]
        + [shape(in_share, F32), shape(back_share, F32), shape(small.shape, F32)],
        scratch_shapes=[VM(cube, BF)] * 8
        + [VM((sents // 2, slot, width), BF)] * 6
        + [VM((total, width), F32)]
        + [VM((total, width), BF)] * 5
        + red
        + [VM((depth,) + in_share, BF), VM((depth,) + back_share, BF)]
        + [VM(in_share, BF), VM(back_share, BF)]
        + [VM(small.shape, F32)] * 2
        + [VM((4,) + small.shape, F32), VM((depth,) + small.shape, F32)]
        + [VM(gin.shape, BF), VM(gback.shape, BF)]
        + [
            pltpu.SemaphoreType.DMA((semaphores,)),
            pltpu.SemaphoreType.DMA((semaphores,)),
            pltpu.SemaphoreType.DMA((6,)),
        ],
        compiler_params=pltpu.CompilerParams(
            collective_id=2, has_side_effects=True, vmem_limit_bytes=63 * 2**20
        ),
        cost_estimate=pl.CostEstimate(
            flops=16 * total * width * width, bytes_accessed=40 * 2**20, transcendentals=0
        ),
    )(
        lengths, tokens, cot, dm, hidden, act, q, k, v, ctx, prob, wq, wk, wv, wo,
        g1[None], g2[None], attn_sum, plan, tasks[None], lengths[None], dots, py, gin, gback,
    )


def local(
    tokens,
    lengths,
    tasks,
    routes,
    gate_table,
    ln1_gain,
    ln1_bias,
    ln2_gain,
    ln2_bias,
    w_query,
    w_key,
    w_value,
    w_out,
    w_in,
    w_back,
    cotangent,
):
    sents, slot, width = tokens.shape
    heads = HEADS
    head = width // heads
    experts = gate_table.shape[1]
    ntasks = routes.shape[0]
    capacity = max(1, 4 * sents // experts)
    scale = 1.0 / jnp.sqrt(jnp.float32(head))
    task_hot = (tasks[:, None] == jnp.arange(ntasks)[None, :]).astype(jnp.int32)
    chosen = jnp.sum(task_hot[:, :, None] * routes[None, :, :], axis=1)
    flat = chosen.reshape(-1)
    order = jnp.arange(2 * sents)
    earlier = (flat[:, None] == flat[None, :]) & (order[None, :] < order[:, None])
    rank = jnp.sum(earlier.astype(jnp.int32), axis=1)
    slot_id = flat * capacity + rank
    placed = rank < capacity
    dispatch = (
        (jnp.arange(experts * capacity)[:, None] == slot_id[None, :]) & placed[None, :]
    ).astype(jnp.bfloat16)
    collect = dispatch.T
    expert_hot = (chosen[:, :, None] == jnp.arange(experts)[None, None, :]).astype(jnp.float32)
    valid = (jnp.arange(slot)[None, :] < lengths[:, None]).astype(jnp.float32)
    keymask = valid[:, None, None, :] > 0.5
    mask3 = valid[:, :, None]
    xfull = tokens.astype(jnp.float32)
    normed1, inverse1 = normalize(xfull)
    act = (normed1 * ln1_gain + ln1_bias).astype(jnp.bfloat16).reshape(-1, width)
    query = project(act, w_query).astype(jnp.bfloat16).reshape(sents, slot, heads, head)
    keyed = project(act, w_key).astype(jnp.bfloat16).reshape(sents, slot, heads, head)
    valued = project(act, w_value).astype(jnp.bfloat16).reshape(sents, slot, heads, head)

    def scores_of(qpart, kpart):
        raw = (
            jnp.einsum("sqhd,skhd->shqk", qpart, kpart, preferred_element_type=jnp.float32) * scale
        )
        return jnp.where(keymask, raw, -1000000000.0)

    scores = scores_of(query, keyed)
    peak = jnp.max(scores, axis=-1, keepdims=True)
    logsum = peak + jnp.log(jnp.sum(jnp.exp(scores - peak), axis=-1, keepdims=True))
    prob_low = jnp.exp(scores - logsum).astype(jnp.bfloat16)
    context = jnp.einsum("shqk,skhd->sqhd", prob_low, valued, preferred_element_type=jnp.float32)
    context = context.astype(jnp.bfloat16).reshape(-1, width)
    attention_block = project(context, w_out).reshape(sents, slot, width)
    hidden_res = xfull + attention_block
    normed2, inverse2 = normalize(hidden_res)
    mixed = (normed2 * ln2_gain + ln2_bias).astype(jnp.bfloat16)
    table_rows = jnp.dot(task_hot.astype(jnp.float32), gate_table, precision=lax.Precision.HIGHEST)
    picked = jnp.sum(expert_hot * table_rows[:, None, :], axis=-1)
    gate_values = jax.nn.softmax(picked, axis=-1)
    grad_total = cotangent.astype(jnp.float32) * mask3
    copies = jnp.broadcast_to(mixed[:, None], (sents, 2, slot, width)).reshape(
        2 * sents, slot * width
    )
    outgoing = (
        project(dispatch, copies).astype(jnp.bfloat16).reshape(experts, capacity, slot, width)
    )
    dycopy = (
        (gate_values[:, :, None, None] * grad_total[:, None])
        .astype(jnp.bfloat16)
        .reshape(2 * sents, slot * width)
    )
    grad_out = (
        project(dispatch, dycopy).astype(jnp.bfloat16).reshape(experts, capacity, slot, width)
    )
    incoming = lax.all_to_all(outgoing, "expert", split_axis=0, concat_axis=0, tiled=True).reshape(
        -1, width
    )
    pre_act, active, produced = expert_forward(incoming, w_in[0], w_back[0])
    returned = lax.all_to_all(
        produced.reshape(experts, capacity, slot, width),
        "expert",
        split_axis=0,
        concat_axis=0,
        tiled=True,
    )
    grad_in = lax.all_to_all(grad_out, "expert", split_axis=0, concat_axis=0, tiled=True).reshape(
        -1, width
    )
    in_local, back_local, dincoming = expert_backward(
        incoming, pre_act, active, grad_in, w_in[0], w_back[0]
    )
    grad_back = lax.all_to_all(
        dincoming.reshape(experts, capacity, slot, width),
        "expert",
        split_axis=0,
        concat_axis=0,
        tiled=True,
    )
    ycopy = project(collect, returned.reshape(experts * capacity, slot * width)).reshape(
        sents, 2, slot, width
    )
    expert_mixture = jnp.sum(gate_values[:, :, None, None] * ycopy, axis=1)
    total = mask3 * (hidden_res + expert_mixture)
    output = total.astype(jnp.bfloat16)
    stats_local = jnp.stack(
        [
            jnp.sum(total * total),
            jnp.sum(mask3 * attention_block * attention_block),
            jnp.sum(mask3 * expert_mixture * expert_mixture),
            jnp.sum(valid),
        ]
    )
    stat_totals = lax.psum(stats_local, ("dp", "expert"))
    gate_dot = jnp.sum(ycopy * grad_total[:, None], axis=(2, 3))
    dpicked = gate_values * (gate_dot - jnp.sum(gate_values * gate_dot, axis=-1, keepdims=True))
    dlogits = jnp.sum(expert_hot * dpicked[:, :, None], axis=1)
    table_grad = jnp.dot(task_hot.T.astype(jnp.float32), dlogits, precision=lax.Precision.HIGHEST)
    dmixed = project(collect, grad_back.reshape(experts * capacity, slot * width)).reshape(
        sents, 2, slot, width
    )
    dmixed = jnp.sum(dmixed, axis=1)
    dres2, gain2_grad, bias2_grad = norm_backward(dmixed, normed2, inverse2, ln2_gain)
    dhidden = grad_total + dres2
    dattn = dhidden.astype(jnp.bfloat16).reshape(-1, width)
    wout_grad = project(context.T, dattn)
    dcontext = project(dattn, w_out.T).astype(jnp.bfloat16).reshape(sents, slot, heads, head)
    again = jnp.exp(scores_of(query, keyed) - logsum)
    dprob = jnp.einsum("sqhd,skhd->shqk", dcontext, valued, preferred_element_type=jnp.float32)
    dscores = (again * (dprob - jnp.sum(dprob * again, axis=-1, keepdims=True))).astype(
        jnp.bfloat16
    )
    dquery = (
        jnp.einsum("shqk,skhd->sqhd", dscores, keyed, preferred_element_type=jnp.float32) * scale
    )
    dkeyed = (
        jnp.einsum("shqk,sqhd->skhd", dscores, query, preferred_element_type=jnp.float32) * scale
    )
    dvalued = jnp.einsum("shqk,sqhd->skhd", prob_low, dcontext, preferred_element_type=jnp.float32)
    dquery = dquery.astype(jnp.bfloat16).reshape(-1, width)
    dkeyed = dkeyed.astype(jnp.bfloat16).reshape(-1, width)
    dvalued = dvalued.astype(jnp.bfloat16).reshape(-1, width)
    wq_grad = project(act.T, dquery)
    wk_grad = project(act.T, dkeyed)
    wv_grad = project(act.T, dvalued)
    dact = project(dquery, w_query.T) + project(dkeyed, w_key.T) + project(dvalued, w_value.T)
    dres1, gain1_grad, bias1_grad = norm_backward(
        dact.reshape(sents, slot, width), normed1, inverse1, ln1_gain
    )
    input_grad = (dhidden + dres1).astype(jnp.bfloat16)
    members = (
        wq_grad,
        wk_grad,
        wv_grad,
        wout_grad,
        gain1_grad,
        bias1_grad,
        gain2_grad,
        bias2_grad,
        table_grad,
    )
    members = members + ()
    summed = lax.psum(members, ("dp", "expert"))
    rms = jnp.sqrt(stat_totals[0:3] / (stat_totals[3] * width))
    in_share, back_share = (
        lax.psum_scatter(
            in_local.astype(jnp.bfloat16), "dp", scatter_dimension=0, tiled=True
        ).astype(jnp.float32),
        lax.psum_scatter(
            back_local.astype(jnp.bfloat16), "dp", scatter_dimension=0, tiled=True
        ).astype(jnp.float32),
    )
    return (
        output,
        input_grad,
        summed[8],
        summed[4],
        summed[5],
        summed[6],
        summed[7],
        summed[0],
        summed[1],
        summed[2],
        summed[3],
        in_share[None],
        back_share[None],
        rms,
    )


def local_plane(
    depth,
    tokens,
    lengths,
    tasks,
    routes,
    gate_table,
    ln1_gain,
    ln1_bias,
    ln2_gain,
    ln2_bias,
    w_query,
    w_key,
    w_value,
    w_out,
    w_in,
    w_back,
    cotangent,
):
    experts = gate_table.shape[1]
    sents, slot, width = tokens.shape
    heads = HEADS
    capacity = max(1, 4 * sents // experts)
    (
        act, query, keyed, valued, context, prob, hidden, mixed, attn_sum, plan, places,
        gate_slots, near, far, core,
    ) = attention_forward(
        tokens, lengths, w_query, w_key, w_value, w_out, ln1_gain, ln1_bias, ln2_gain, ln2_bias,
        tasks, routes, gate_table, cotangent, heads, capacity,
    )
    dmixed, parts_back, in_local, back_local, slot_dots = expert_exchange(
        places, gate_slots, mixed, cotangent, near, far, core, w_in[0], w_back[0], capacity
    )
    input_grad, output, sum_o, sum_0, sum_1, in_share, back_share, small = backward_exchange(
        depth, lengths, tokens, cotangent, dmixed, hidden, act, query, keyed, valued, context,
        prob, w_query, w_key, w_value, w_out, ln1_gain, ln2_gain,
        attn_sum, plan, tasks, slot_dots, parts_back, in_local, back_local, heads,
    )
    sides = jnp.concatenate([sum_0, sum_1], axis=1).astype(jnp.float32)
    wide = lambda place: sides[place * width : (place + 1) * width]
    sums = jnp.sum(small[4:8], axis=1)
    rms = jnp.sqrt(jnp.stack([sums[1], sums[0], sums[2]]) / (sums[3] * width))
    return (
        output,
        input_grad,
        small[8 : 8 + experts, : gate_table.shape[0]].T,
        small[0],
        small[1],
        small[2],
        small[3],
        wide(0),
        wide(1),
        wide(2),
        sum_o.astype(jnp.float32),
        in_share[None],
        back_share[None],
        rms,
    )


def solution(mesh):
    in_specs = (
        P(("dp", "expert"), None, None),
        P(("dp", "expert")),
        P(("dp", "expert")),
        P(),
        P(),
        P(),
        P(),
        P(),
        P(),
        P(),
        P(),
        P(),
        P(),
        P("expert", None, None),
        P("expert", None, None),
        P(("dp", "expert"), None, None),
    )
    out_specs = (
        P(("dp", "expert"), None, None),
        P(("dp", "expert"), None, None),
        P(),
        P(),
        P(),
        P(),
        P(),
        P(),
        P(),
        P(),
        P(),
        P("expert", "dp", None),
        P("expert", "dp", None),
        P(),
    )
    plane = dict(mesh.shape)["expert"]
    depth = dict(mesh.shape)["dp"]
    body = functools.partial(local_plane, depth) if plane == 2 * 2 * 2 else local
    return jax.shard_map(body, mesh=mesh, in_specs=in_specs, out_specs=out_specs, check_vma=False)
```

```python
import functools

import jax
import jax.numpy as jnp
from jax import lax
from jax.experimental import pallas as pl
from jax.experimental.pallas import tpu as pltpu
from jax.sharding import PartitionSpec as P

HEADS = 8


def normalize(value):
    centered = value - jnp.mean(value, axis=-1, keepdims=True)
    variance = jnp.mean(centered * centered, axis=-1, keepdims=True)
    inverse = lax.rsqrt(variance + 1e-05)
    return (centered * inverse, inverse)


def norm_backward(grad, normed, inverse, gain):
    scaled = grad * gain
    inner = scaled - jnp.mean(scaled, axis=-1, keepdims=True)
    inner = inner - normed * jnp.mean(scaled * normed, axis=-1, keepdims=True)
    return (inverse * inner, jnp.sum(grad * normed, axis=(0, 1)), jnp.sum(grad, axis=(0, 1)))


def project(left, right):
    return jnp.dot(left, right, preferred_element_type=jnp.float32)


def expert_forward(incoming, first, second):
    pre_act = project(incoming, first)
    active = jax.nn.gelu(pre_act).astype(jnp.bfloat16)
    produced = project(active, second).astype(jnp.bfloat16)
    return (pre_act, active, produced)


def expert_backward(incoming, pre_act, active, grad_in, first, second):
    dactive = project(grad_in, second.T)
    back_local = project(active.T, grad_in)
    gelu_pull = jax.vjp(jax.nn.gelu, pre_act)[1]
    dpre = gelu_pull(dactive)[0].astype(jnp.bfloat16)
    in_local = project(incoming.T, dpre)
    dincoming = project(dpre, first.T).astype(jnp.bfloat16)
    return (in_local, back_local, dincoming)


BF = jnp.bfloat16
F32 = jnp.float32
VM = pltpu.VMEM


def mm(a, b, ca=1, cb=0):
    return lax.dot_general(a, b, (((ca,), (cb,)), ((), ())), preferred_element_type=F32)


def block_diagonal(group, slot, head):
    shape = (group * slot, group * head)
    rows = lax.broadcasted_iota(jnp.int32, shape, 0) // slot
    cols = lax.broadcasted_iota(jnp.int32, shape, 1) // head
    return rows == cols


def spread(part, mask, group):
    return jnp.where(mask, jnp.concatenate([part] * group, axis=0), jnp.zeros((), part.dtype))


def fold(product, mask, slot, group):
    kept = jnp.where(mask, product, 0.0)
    total = kept[0:slot]
    for one in range(1, group):
        total = total + kept[one * slot : (one + 1) * slot]
    return total


def attend(query, keyed, valued, length, mask, slot, group, scale):
    scores = mm(keyed, spread(query, mask, group), 1, 1) * scale
    place = lax.broadcasted_iota(jnp.int32, scores.shape, 0)
    scores = jnp.where(place < length, scores, -1000000000.0)
    raised = jnp.exp(scores - jnp.max(scores, axis=0, keepdims=True))
    prob = raised / jnp.sum(raised, axis=0, keepdims=True)
    context = fold(mm(prob.astype(BF), valued, 0, 0), mask, slot, group)
    return prob, context


def route_tables(cap, tasks, lengths, routes, gate_table):
    sents = tasks.shape[1]
    experts, ntasks = gate_table.shape
    iota = lambda rows, cols, axis: lax.broadcasted_iota(jnp.int32, (rows, cols), axis)
    hot = (iota(ntasks, sents, 0) == tasks).astype(F32)
    exact = functools.partial(
        lax.dot_general,
        dimension_numbers=(((1,), (0,)), ((), ())),
        precision=lax.Precision.HIGHEST,
        preferred_element_type=F32,
    )
    chosen = exact(routes.astype(F32), hot)
    first, second = chosen[0:1], chosen[1:2]
    expert = iota(experts, sents, 0).astype(F32)
    is_first, is_second = expert == first, expert == second
    hit = jnp.logical_or(is_first, is_second)
    before = (iota(sents, sents, 0) < iota(sents, sents, 1)).astype(BF)
    rank = mm(hit.astype(F32).astype(BF), before)
    place = jnp.where(hit, jnp.where(rank < cap, rank, -1.0), -1.0)
    logits = exact(gate_table, hot)
    one = jnp.sum(jnp.where(is_first, logits, 0.0), axis=0, keepdims=True)
    two = jnp.sum(jnp.where(is_second, logits, 0.0), axis=0, keepdims=True)
    peak = jnp.maximum(one, two)
    one, two = jnp.exp(one - peak), jnp.exp(two - peak)
    gate = jnp.where(is_first, one / (one + two), 0.0)
    gate = gate + jnp.where(is_second, two / (one + two), 0.0)
    lane = iota(experts, 128, 1)
    index = iota(experts, sents, 1).astype(F32)
    table = jnp.zeros((experts, 128), F32)
    gates = jnp.zeros((experts, 128), F32)
    for j in range(cap):
        here = place == float(j)
        pick = lambda value: jnp.sum(jnp.where(here, value, 0.0), axis=1, keepdims=True)
        table = jnp.where(lane == j, pick(index), table)
        table = jnp.where(lane == cap + j, pick(lengths.astype(F32)), table)
        gates = jnp.where(lane == j, pick(gate), gates)
    shift = (iota(sents, 128, 1) == iota(sents, 128, 0) + 2 * cap).astype(BF)
    spots = mm((place + 1.0).astype(BF), shift)
    inside = jnp.logical_and(lane >= 2 * cap, lane < 2 * cap + sents)
    table = jnp.where(inside, spots - 1.0, table)
    return table.astype(jnp.int32), gates, hit.astype(F32), place, gate


def attention_forward_kernel(
    heads, cap, len_ref, x_ref, wq, wk, wv, wo, g1, b1, g2, b2, tasks, lengths, routes,
    gate_table, cot_in,
    act_o, q_o, k_o, v_o, ctx_o, p_o, h_o, m_o, st_o, plan_o, tab_o, gates_o, near_o, far_o,
    core_o, cot, tab_s, gates_s, sends, recvs, local,
):
    count, slot, width = x_ref.shape
    head = width // heads
    group = max(1, min(heads, 256 // head))
    span = group * head
    step = pl.program_id(0)
    scale = head ** -0.5
    mask = block_diagonal(group, slot, head)
    experts = gate_table.shape[0]
    me = lax.axis_index("expert")
    half = cot.shape[0] // 2
    copies = [
        remote(cot.at[pl.ds(0, half)], near_o, sends, recvs, 0, NEAR),
        remote(cot.at[pl.ds(half, half)], far_o, sends, recvs, 1, FAR),
        remote(cot, core_o, sends, recvs, 2, CORE),
    ]
    for relation in range(1, 8):
        there = plane_peer(relation)
        copies += [
            remote(tab_s.at[there], tab_o.at[me], sends, recvs, 1 + 2 * relation, relation),
            remote(gates_s.at[there], gates_o.at[me], sends, recvs, 2 + 2 * relation, relation),
        ]
    own = [
        pltpu.make_async_copy(tab_s.at[me], tab_o.at[me], local.at[0]),
        pltpu.make_async_copy(gates_s.at[me], gates_o.at[me], local.at[1]),
    ]

    @pl.when(step == 0)
    def _():
        load = pltpu.make_async_copy(cot_in, cot, local.at[2])
        load.start()
        plane_barrier()
        load.wait()
        for copy in copies[0:3]:
            copy.start()
        table, gates, hit, place, gate = route_tables(
            cap, tasks[...], lengths[...], routes[...], gate_table[...]
        )
        for e in range(experts):
            tab_s[e] = jnp.broadcast_to(table[e : e + 1], (8, 128))
            gates_s[e] = jnp.broadcast_to(gates[e : e + 1], (8, 128))
        for copy in copies[3:]:
            copy.start()
        for copy in own:
            copy.start()
        plan_o[0:experts] = hit
        plan_o[experts : 2 * experts] = place
        plan_o[2 * experts : 3 * experts] = gate
        st_o[...] = jnp.zeros_like(st_o)

    x = x_ref[...].astype(F32).reshape(count * slot, width)
    normed, _ = normalize(x)
    act = (normed * g1[...] + b1[...]).astype(BF)
    act_o[...] = act
    q_o[...] = mm(act, wq[...]).astype(BF)
    k_o[...] = mm(act, wk[...]).astype(BF)
    v_o[...] = mm(act, wv[...]).astype(BF)
    for s in range(count):
        length = len_ref[step * count + s]
        rows = slice(s * slot, (s + 1) * slot)
        for part in range(heads // group):
            cols = slice(part * span, (part + 1) * span)
            prob, context = attend(
                q_o[rows, cols], k_o[rows, cols], v_o[rows, cols], length, mask, slot, group, scale
            )
            p_o[s, part] = prob
            ctx_o[rows, cols] = context.astype(BF)
    attn = mm(ctx_o[...], wo[...])
    hidden = x + attn
    h_o[...] = hidden
    normed2, _ = normalize(hidden)
    m_o[...] = (normed2 * g2[...] + b2[...]).astype(BF).reshape(count, slot, width)
    place = lax.broadcasted_iota(jnp.int32, (slot, width), 0)
    total = jnp.zeros((1, width), F32)
    for s in range(count):
        length = len_ref[step * count + s]
        part = attn[s * slot : (s + 1) * slot]
        total = total + jnp.sum(jnp.where(place < length, part * part, 0.0), axis=0, keepdims=True)
    st_o[...] += total

    @pl.when(step == pl.num_programs(0) - 1)
    def _():
        for copy in copies + own:
            copy.wait()


def attention_forward(
    tokens, lengths, wq, wk, wv, wo, g1, b1, g2, b2, tasks, routes, gate_table, cot, heads, cap
):
    sents, slot, width = tokens.shape
    experts = gate_table.shape[0]
    count = 4 if sents % 4 == 0 else 1
    rows = count * slot
    head = width // heads
    group = max(1, min(heads, 256 // head))
    whole = lambda *shape: pl.BlockSpec(shape, lambda i: (0,) * len(shape))
    flat = pl.BlockSpec((rows, width), lambda i: (i, 0))
    cube = pl.BlockSpec((count, slot, width), lambda i: (i, 0, 0))
    probs = pl.BlockSpec((count, heads // group, slot, group * slot), lambda i: (i, 0, 0, 0))
    anywhere = pl.BlockSpec(memory_space=pl.ANY)
    shape = jax.ShapeDtypeStruct
    total = sents * slot
    half = (sents // 2, slot, width)
    return pl.pallas_call(
        functools.partial(attention_forward_kernel, heads, cap),
        grid=(sents // count,),
        in_specs=[pl.BlockSpec(memory_space=pltpu.SMEM), cube]
        + [whole(width, width)] * 4
        + [whole(1, width)] * 4
        + [whole(1, sents)] * 2
        + [whole(*routes.shape), whole(*gate_table.shape), anywhere],
        out_specs=[flat] * 5
        + [probs, flat, cube, whole(1, width), whole(3 * experts, sents)]
        + [anywhere] * 5,
        out_shape=[shape((total, width), BF)] * 5
        + [
            shape((sents, heads // group, slot, group * slot), F32),
            shape((total, width), F32),
            shape((sents, slot, width), BF),
            shape((1, width), F32),
            shape((3 * experts, sents), F32),
            shape((experts, 8, 128), jnp.int32),
            shape((experts, 8, 128), F32),
            shape(half, BF),
            shape(half, BF),
            shape(tokens.shape, BF),
        ],
        scratch_shapes=[
            VM(cot.shape, BF),
            VM((experts, 8, 128), jnp.int32),
            VM((experts, 8, 128), F32),
            pltpu.SemaphoreType.DMA((17,)),
            pltpu.SemaphoreType.DMA((17,)),
            pltpu.SemaphoreType.DMA((3,)),
        ],
        compiler_params=pltpu.CompilerParams(
            dimension_semantics=("arbitrary",), vmem_limit_bytes=56 * 2**20,
            collective_id=0, has_side_effects=True,
        ),
        cost_estimate=pl.CostEstimate(
            flops=8 * total * width * width + 4 * total * slot * width,
            bytes_accessed=16 * total * width,
            transcendentals=total * slot * heads,
        ),
    )(
        lengths, tokens, wq, wk, wv, wo, g1[None], b1[None], g2[None], b2[None],
        tasks[None], lengths[None], routes, gate_table, cot,
    )


def row_sum(value, width):
    return jnp.sum(value, axis=0, keepdims=True)


def layer_norm_pull(grad, normed, inverse, gain):
    scaled = grad * gain
    inner = scaled - jnp.mean(scaled, axis=-1, keepdims=True)
    inner = inner - normed * jnp.mean(scaled * normed, axis=-1, keepdims=True)
    return inverse * inner


def attention_pull(dcontext, query, keyed, valued, prob, mask, slot, group, scale):
    low = prob.astype(BF)
    dspread = spread(dcontext, mask, group)
    dprob = mm(valued, dspread, 1, 1)
    inner = jnp.sum(dprob * prob, axis=0, keepdims=True)
    dscores = (prob * (dprob - inner)).astype(BF)
    dquery = fold(mm(dscores, keyed, 0, 0), mask, slot, group) * scale
    dkeyed = mm(dscores, spread(query, mask, group)) * scale
    dvalued = mm(low, dspread)
    return dquery.astype(BF), dkeyed.astype(BF), dvalued.astype(BF)


MESH_ID = pl.DeviceIdType.MESH
CORE, NEAR, FAR = 1, 2, 4


def plane_peer(relation):
    me = lax.axis_index("expert")
    bits = []
    for bit in (CORE, NEAR, FAR):
        value = (me // bit) % 2
        bits.append((1 - value if relation & bit else value) * bit)
    return bits[0] + bits[1] + bits[2]


def remote(src, dst, sends, recvs, index, relation):
    return pltpu.make_async_remote_copy(
        src_ref=src,
        dst_ref=dst,
        send_sem=sends.at[index],
        recv_sem=recvs.at[index],
        device_id=(lax.axis_index("dp"), plane_peer(relation)),
        device_id_type=MESH_ID,
    )


def line_peer(offset, depth):
    return lax.rem(lax.axis_index("dp") + offset, depth)


def along(src, dst, sends, recvs, index, offset, depth):
    return pltpu.make_async_remote_copy(
        src_ref=src,
        dst_ref=dst,
        send_sem=sends.at[index],
        recv_sem=recvs.at[index],
        device_id=(line_peer(offset, depth), lax.axis_index("expert")),
        device_id_type=MESH_ID,
    )


def plane_barrier(depth=1):
    barrier = pltpu.get_barrier_semaphore()
    targets = [(lax.axis_index("dp"), plane_peer(relation)) for relation in range(1, 8)]
    for offset in range(1, depth):
        targets.append((line_peer(offset, depth), lax.axis_index("expert")))
    for target in targets:
        pl.semaphore_signal(barrier, inc=1, device_id=target, device_id_type=MESH_ID)
    pl.semaphore_wait(barrier, len(targets))


def gather_copies(own, held, sends, recvs, base):
    half = own.shape[0] // 2
    low, high = pl.ds(0, half), pl.ds(half, half)
    plan = [
        (own.at[low], held[2].at[low], NEAR),
        (own.at[high], held[4].at[high], FAR),
        (own, held[1], CORE),
        (own.at[high], held[2].at[high], NEAR),
        (own.at[low], held[4].at[low], FAR),
        (held[2].at[low], held[6].at[low], FAR),
        (held[4].at[high], held[6].at[high], NEAR),
        (held[2], held[3], CORE),
        (held[4], held[5], CORE),
        (held[6], held[7], CORE),
    ]
    return [
        remote(src, dst, sends, recvs, base + place, relation)
        for place, (src, dst, relation) in enumerate(plan)
    ]


def return_copies(parts, cores, sides, sends, recvs, base):
    half = parts[0].shape[0] // 2
    low, high = pl.ds(0, half), pl.ds(half, half)
    plan = [
        (parts[1], cores[0], CORE),
        (parts[3], cores[2], CORE),
        (parts[5], cores[4], CORE),
        (parts[7], cores[6], CORE),
        (parts[2].at[low], sides[0], NEAR),
        (parts[6].at[low], sides[1], NEAR),
        (parts[4].at[high], sides[2], FAR),
        (parts[6].at[high], sides[3], FAR),
        (parts[4].at[low], sides[4], FAR),
        (parts[2].at[high], sides[5], NEAR),
    ]
    return [
        remote(src, dst, sends, recvs, base + place, relation)
        for place, (src, dst, relation) in enumerate(plan)
    ]


def add_into(target, start, other, count):
    def one(i, carry):
        total = target[start + i].astype(F32) + other[i].astype(F32)
        target[start + i] = total.astype(BF)
        return carry

    lax.fori_loop(0, count, one, 0)


def return_finish(parts, sides, back):
    half = parts[0].shape[0] // 2
    back[4].wait_recv()
    add_into(parts[0], 0, sides[0], half)
    back[5].wait_recv()
    add_into(parts[4], 0, sides[1], half)
    back[8].start()
    back[6].wait_recv()
    add_into(parts[0], half, sides[2], half)
    back[7].wait_recv()
    add_into(parts[2], half, sides[3], half)
    back[9].start()
    back[8].wait_recv()
    add_into(parts[0], 0, sides[4], half)
    back[9].wait_recv()
    add_into(parts[0], half, sides[5], half)
    for copy in back:
        copy.wait_send()


GELU_A = 0.7978845608028654
GELU_B = 0.044715


def expert_kernel(
    cap, depth, tab, gates, m_in, cot_in, near_in, far_in, core_in, win_in, wback_in,
    dm_o, py_o, cy_o, gin_o, gback_o, dg_o, *scratch
):
    sents, slot, width = m_in.shape
    hidden = win_in.shape[1]
    half = sents // 2
    held_m = dict(zip(range(8), scratch[0:8]))
    held_c = dict(zip(range(8), scratch[8:16]))
    parts = dict(zip(range(8), scratch[16:24]))
    cores = dict(zip((0, 2, 4, 6), scratch[24:28]))
    sides = scratch[28:34]
    win, wback = scratch[34:36]
    xs, gs, dys, zs, dus, ys, dms, stage, dg_s, accb, acci = scratch[36:47]
    line_in, line_back, sends, recvs, local = scratch[47:]
    me = lax.axis_index("expert")
    tile = min(1024, hidden)
    low, high = pl.ds(0, half), pl.ds(half, half)
    loads = [
        pltpu.make_async_copy(src, dst, local.at[2 + place])
        for place, (src, dst) in enumerate(
            [
                (m_in, held_m[0]),
                (cot_in, held_c[0]),
                (win_in, win),
                (wback_in, wback),
                (core_in, held_c[1]),
                (near_in, held_c[2].at[low]),
                (far_in, held_c[4].at[high]),
            ]
        )
    ]
    for load in loads:
        load.start()

    z = lax.axis_index("dp")
    plane_barrier(depth)
    to_m = gather_copies(held_m[0], held_m, sends, recvs, 0)
    to_c = gather_copies(held_c[0], held_c, sends, recvs, 10)
    back = return_copies(parts, cores, sides, sends, recvs, 20)
    gates_back = {
        r: remote(dg_s.at[r], dg_o.at[me], sends, recvs, 30 + r, r) for r in range(1, 8)
    }
    outputs_back = {
        r: remote(stage.at[1], cy_o.at[r // 2], sends, recvs, 38 + r // 2, CORE)
        for r in (1, 3, 5, 7)
    }

    def line_first(right, array):
        offset = 1 if right else depth - 1
        s = depth - 1 if right else 0
        source, into = ((win, line_in), (wback, line_back))[array]
        share = source.shape[0] // depth
        here = pl.ds(s * share, share)
        index = 42 + 2 * int(right) + array
        return here, along(
            source.at[here], into.at[int(right)], sends, recvs, index, offset, depth
        )

    for load in loads[0:2]:
        load.wait()
    for place in (0, 1, 2, 3, 4):
        to_m[place].start()
    for place in (3, 4):
        to_c[place].start()
    accb[...] = jnp.zeros_like(accb)
    acci[...] = jnp.zeros_like(acci)
    place = lax.broadcasted_iota(jnp.int32, (slot, width), 0)
    for load in loads[2:4]:
        load.wait()

    def arrive(*indices):
        for index in indices:
            to_m[index].wait_recv()
            if index > 2:
                to_c[index].wait_recv()

    def forward(*indices):
        for index in indices:
            to_m[index].start()
            to_c[index].start()

    def before(r):
        if r == 1:
            arrive(2)
            loads[4].wait()
        if r == 2:
            loads[5].wait()
            loads[6].wait()
            arrive(0, 1)
            forward(5, 6)
            arrive(3)
            forward(7)
            arrive(4)
            forward(8)
        if r == 3:
            arrive(7)
        if r == 5:
            arrive(8)
        if r == 6:
            arrive(5, 6)
            forward(9)
        if r == 7:
            arrive(9)
        source = plane_peer(r)

        def fetch(j, carry):
            index = tab[source, 0, j]
            length = tab[source, 0, cap + j]
            gate = gates[source, 0, j]
            xs[j] = held_m[r][index]
            gt = jnp.where(place < length, held_c[r][index].astype(F32), 0.0)
            gs[j] = gt.astype(BF)
            dys[j] = (gt * gate).astype(BF)
            return carry

        lax.fori_loop(0, cap, fetch, 0, unroll=2)

    def after(r):
        source = plane_peer(r)
        if r >= 2 and r % 2 == 0:
            pltpu.make_async_copy(stage.at[0], py_o.at[r // 2 - 1], local.at[0]).wait()
        if r >= 2 and r % 2 == 1:
            outputs_back[r - 2].wait_send()

        def give(i, carry):
            index = tab[source, 0, 2 * cap + i]
            there = jnp.maximum(index, 0)
            gate = gates[source, 0, there]
            hit = (index >= 0).astype(F32)
            parts[r][i] = (dms[there].astype(F32) * hit).astype(BF)
            stage[r % 2, i] = (ys[there].astype(F32) * (hit * gate)).astype(BF)
            return carry

        lax.fori_loop(0, sents, give, 0, unroll=2)
        if r % 2 == 0:
            pltpu.make_async_copy(stage.at[0], py_o.at[r // 2], local.at[0]).start()
        else:
            outputs_back[r].start()

        def dots(j, carry):
            product = ys[j].astype(F32) * gs[j].astype(F32)
            total = jnp.sum(jnp.sum(product, axis=0, keepdims=True), axis=1, keepdims=True)
            if r == 0:
                dg_o[me, pl.ds(j, 1)] = jnp.broadcast_to(total, (1, 128))
            else:
                dg_s[r, pl.ds(j, 1)] = jnp.broadcast_to(total, (1, 128))
            return carry

        lax.fori_loop(0, cap, dots, 0, unroll=4)
        if r > 0:
            gates_back[r].start()
        if r % 2 == 1:
            back[r // 2].start()
        if r == 4:
            back[1].wait_recv()
            add_into(parts[2], 0, cores[2], sents)
            back[4].start()
        if r == 6:
            back[2].wait_recv()
            add_into(parts[4], 0, cores[4], sents)
            back[6].start()
        if r == 7:
            back[3].wait_recv()
            add_into(parts[6], 0, cores[6], sents)
            back[5].start()
            back[7].start()
            back[0].wait_recv()
            add_into(parts[0], 0, cores[0], sents)

    def chunk(t, carry):
        for r in range(8):
            pl.when(t == r)(functools.partial(before, r))
        x = xs[...].reshape(cap * slot, width)
        dy = dys[...].reshape(cap * slot, width)

        def inner(f, carry):
            cols = pl.ds(pl.multiple_of(f * tile, tile), tile)
            u = mm(x, win[:, cols])
            square = u * u
            th = jnp.tanh(u * (GELU_A + GELU_A * GELU_B * square))
            cdf = 0.5 + 0.5 * th
            slope = cdf + (0.5 * u) * (1.0 - th * th) * (GELU_A + 3 * GELU_A * GELU_B * square)
            z = (u * cdf).astype(BF)
            zs[:, cols] = z
            dz = mm(dy, wback[cols, :], 1, 1)
            du = (dz * slope).astype(BF)
            dus[:, cols] = du
            accb[cols, :] += mm(z, dy, 0, 0)
            acci[:, cols] += mm(x, du, 0, 0)
            return carry

        lax.fori_loop(0, hidden // tile, inner, 0)
        ys[...] = mm(zs[...], wback[...]).astype(BF).reshape(cap, slot, width)
        dms[...] = mm(dus[...], win[...], 1, 1).astype(BF).reshape(cap, slot, width)
        for r in range(8):
            pl.when(t == r)(functools.partial(after, r))
        return carry

    lax.fori_loop(0, 8, chunk, 0)
    win[...] = acci[...].astype(BF)
    wback[...] = accb[...].astype(BF)
    for right in (True, False):

        @pl.when(z == (0 if right else depth - 1))
        def _():
            for array in (0, 1):
                line_first(right, array)[1].start()

    return_finish(parts, sides, back)
    kept = pltpu.make_async_copy(parts[0], dm_o, local.at[2])
    kept.start()
    for right in (True, False):

        @pl.when(z == (1 if right else depth - 2))
        def _():
            for array in (0, 1):
                here, copy = line_first(right, array)
                copy.wait_recv()
                source, into = ((win, line_in), (wback, line_back))[array]
                total = source[here, :].astype(F32) + into[int(right)].astype(F32)
                source[here, :] = total.astype(BF)

    stores = [
        pltpu.make_async_copy(win, gin_o, local.at[4]),
        pltpu.make_async_copy(wback, gback_o, local.at[5]),
    ]
    for store in stores:
        store.start()
    for store in stores:
        store.wait()
    kept.wait()
    for right in (True, False):

        @pl.when(z == (0 if right else depth - 1))
        def _():
            for array in (0, 1):
                line_first(right, array)[1].wait_send()

    for r in (1, 3, 5, 7):
        outputs_back[r].wait_recv()
    outputs_back[7].wait_send()
    pltpu.make_async_copy(stage.at[0], py_o.at[3], local.at[0]).wait()
    for r in range(1, 8):
        gates_back[r].wait()
    for index in range(10):
        to_m[index].wait_send()
        if index > 2:
            to_c[index].wait_send()


def expert_exchange(tab, gates, m, cot, near, far, core, win, wback, cap, depth):
    sents, slot, width = m.shape
    hidden = win.shape[1]
    vm = pl.BlockSpec(memory_space=VM)
    sm = pl.BlockSpec(memory_space=pltpu.SMEM)
    anywhere = pl.BlockSpec(memory_space=pl.ANY)
    shape = jax.ShapeDtypeStruct
    cube = (sents, slot, width)
    rows = cap * slot
    return pl.pallas_call(
        functools.partial(expert_kernel, cap, depth),
        in_specs=[sm, sm] + [anywhere] * 7,
        out_specs=[anywhere] * 5 + [vm],
        out_shape=[
            shape(cube, BF),
            shape((4,) + cube, BF),
            shape((4,) + cube, BF),
            shape((width, hidden), BF),
            shape((hidden, width), BF),
            shape((8, cap, 128), F32),
        ],
        scratch_shapes=[VM(cube, BF)] * (16 + 8 + 4)
        + [VM((sents // 2, slot, width), BF)] * 6
        + [VM((width, hidden), BF), VM((hidden, width), BF)]
        + [VM((cap, slot, width), BF)] * 3
        + [VM((rows, hidden), BF)] * 2
        + [VM((cap, slot, width), BF)] * 2
        + [VM((2,) + cube, BF), VM((8, cap, 128), F32)]
        + [VM((hidden, width), F32), VM((width, hidden), F32)]
        + [VM((2, width // depth, hidden), BF), VM((2, hidden // depth, width), BF)]
        + [
            pltpu.SemaphoreType.DMA((46,)),
            pltpu.SemaphoreType.DMA((46,)),
            pltpu.SemaphoreType.DMA((9,)),
        ],
        compiler_params=pltpu.CompilerParams(
            collective_id=1, has_side_effects=True, vmem_limit_bytes=63 * 2**20
        ),
        cost_estimate=pl.CostEstimate(
            flops=12 * 8 * rows * width * hidden, bytes_accessed=40 * 2**20, transcendentals=0
        ),
    )(tab, gates, m, cot, near, far, core, win, wback)


class Reduction:
    def __init__(self, depth, value, wide, core_r, plane_r, line_s, line_r, final, sems, base):
        self.depth, self.value, self.wide, self.final = depth, value, wide, final
        self.core_r, self.plane_r, self.line_s, self.line_r = core_r, plane_r, line_s, line_r
        sends, recvs = sems
        me = lax.axis_index("expert")
        z = lax.axis_index("dp")
        core = me % 2
        self.half = value.shape[0] // 2
        self.quarter = self.half // 4
        self.share = self.quarter // depth
        self.mine = core * self.half
        self.other = (1 - core) * self.half
        self.block = self.mine + (me // 2) * self.quarter
        self.own = self.block + z * self.share
        self.to_core = remote(wide, core_r, sends, recvs, base, CORE)
        self.to_plane = []
        self.from_plane = []
        for place, relation in enumerate((2, 4, 6)):
            rows = pl.ds((plane_peer(relation) // 2) * self.quarter, self.quarter)
            self.to_plane.append(
                remote(wide.at[rows], plane_r.at[place], sends, recvs, base + 1 + place, relation)
            )
        self.to_line = []
        for offset in range(1, depth):
            rows = pl.ds(line_peer(offset, depth) * self.share, self.share)
            self.to_line.append(
                along(
                    line_s.at[rows], line_r.at[offset - 1], sends, recvs, base + 3 + offset,
                    offset, depth,
                )
            )
        after = base + 3 + depth
        rows = final.at[pl.ds(self.own, self.share)]
        self.back_line = [
            along(rows, rows, sends, recvs, after + offset - 1, offset, depth)
            for offset in range(1, depth)
        ]
        after = after + depth - 1
        rows = final.at[pl.ds(self.block, self.quarter)]
        self.back_plane = [
            remote(rows, rows, sends, recvs, after + place, relation)
            for place, relation in enumerate((2, 4, 6))
        ]
        rows = final.at[pl.ds(self.mine, self.half)]
        self.back_core = remote(rows, rows, sends, recvs, after + 3, CORE)

    @staticmethod
    def semaphores(depth):
        return 2 * depth + 6

    def send_core(self):
        self.wide[...] = self.value[pl.ds(self.other, self.half), :].astype(BF)
        self.to_core.start()

    def send_plane(self):
        self.to_core.wait()
        rows = pl.ds(self.mine, self.half)
        total = self.value[rows, :] + self.core_r[...].astype(F32)
        self.value[rows, :] = total
        self.wide[...] = total.astype(BF)
        for copy in self.to_plane:
            copy.start()

    def send_line(self):
        for copy in self.to_plane:
            copy.wait()
        rows = pl.ds(self.block, self.quarter)
        total = self.value[rows, :]
        for place in range(3):
            total = total + self.plane_r[place].astype(F32)
        self.value[rows, :] = total
        self.line_s[...] = total.astype(BF)
        for copy in self.to_line:
            copy.start()

    def send_back_line(self):
        for copy in self.to_line:
            copy.wait()
        rows = pl.ds(self.own, self.share)
        total = self.value[rows, :]
        for offset in range(1, self.depth):
            total = total + self.line_r[offset - 1].astype(F32)
        self.final[rows, :] = total.astype(BF)
        for copy in self.back_line:
            copy.start()

    def send_back_plane(self):
        for copy in self.back_line:
            copy.wait()
        for copy in self.back_plane:
            copy.start()

    def send_back_core(self):
        for copy in self.back_plane:
            copy.wait()
        self.back_core.start()

    def finish(self):
        self.back_core.wait()


class SmallSum:
    @staticmethod
    def semaphores(depth):
        return 4 + depth

    def __init__(self, depth, value, core_r, plane, line, sems, base):
        sends, recvs = sems
        self.value, self.core_r, self.plane, self.line = value, core_r, plane, line
        self.spot = lax.axis_index("expert") // 2
        self.z = lax.axis_index("dp")
        self.to_core = remote(value, core_r, sends, recvs, base, CORE)
        spot = plane.at[self.spot]
        self.to_plane = [
            remote(spot, spot, sends, recvs, base + 1 + place, relation)
            for place, relation in enumerate((2, 4, 6))
        ]
        spot = line.at[self.z]
        self.to_line = [
            along(spot, spot, sends, recvs, base + 3 + offset, offset, depth)
            for offset in range(1, depth)
        ]

    def send_core(self):
        self.to_core.start()

    def send_plane(self):
        self.to_core.wait()
        self.plane[self.spot] = self.value[...] + self.core_r[...]
        for copy in self.to_plane:
            copy.start()

    def send_line(self):
        for copy in self.to_plane:
            copy.wait()
        total = self.plane[0]
        for place in range(1, 4):
            total = total + self.plane[place]
        self.line[self.z] = total
        for copy in self.to_line:
            copy.start()

    def finish(self, out):
        for copy in self.to_line:
            copy.wait()
        total = self.line[0]
        for place in range(1, self.line.shape[0]):
            total = total + self.line[place]
        out[...] = total


def backward_kernel(
    heads, depth, len_ref, g1, g2, attn_sum, plan, tasks, lengths, dots,
    x_in, cot_in, dm_in, h_in, act_in, q_in, k_in, v_in, ctx_in, p_in,
    wq_in, wk_in, wv_in, wo_in, py, cy, gin, gback,
    ig_o, out_o, gq_o, gk_o, gv_o, go_o, gin_o, gback_o, small_o, *scratch
):
    inputs = (
        x_in, cot_in, dm_in, h_in, act_in, q_in, k_in, v_in, ctx_in, p_in,
        wq_in, wk_in, wv_in, wo_in, gin, gback,
    )
    held = scratch[0:16]
    (
        x_ref, cot_ref, dm_ref, h_ref, act, q, k, v, ctx, p_ref, wq, wk, wv, wo, gin_s, gback_s,
    ) = held
    parts = dict(zip((0, 2, 4, 6), scratch[16:20]))
    cores = dict(zip((0, 2, 4, 6), scratch[20:24]))
    sides = scratch[24:30]
    dh_s, da_s, dctx_s, dq_s, dk_s, dv_s = scratch[30:36]
    red = scratch[36:57]
    line_in, line_back, extra_in, extra_back = scratch[57:61]
    small, small_core, small_plane, small_line = scratch[61:65]
    sends, recvs, local = scratch[65:]
    sems = (sends, recvs)
    sents, slot, width = x_ref.shape
    head = width // heads
    group = max(1, min(heads, 256 // head))
    span = group * head
    scale = head ** -0.5
    count = 4 if sents % 4 == 0 else 1
    rows_per = count * slot
    half = sents // 2
    z = lax.axis_index("dp")

    loads = {
        id(ref): pltpu.make_async_copy(source, ref, local.at[place])
        for place, (source, ref) in enumerate(zip(inputs, held))
    }
    for place, r in enumerate((0, 2, 4, 6)):
        loads[id(parts[r])] = pltpu.make_async_copy(
            py.at[r // 2], parts[r], local.at[16 + place]
        )
        loads[id(cores[r])] = pltpu.make_async_copy(
            cy.at[r // 2], cores[r], local.at[20 + place]
        )

    def begin(*refs):
        for ref in refs:
            loads[id(ref)].start()

    def ready(*refs):
        for ref in refs:
            loads[id(ref)].wait()

    begin(gin_s, gback_s, h_ref, dm_ref, cot_ref, wo, parts[6], cores[6], ctx)
    begin(parts[2], cores[2], parts[4], cores[4], q, k, v, p_ref, act, parts[0], cores[0])
    begin(wq, wk, wv, x_ref)
    plane_barrier(depth)

    all_parts = {r: parts[r - r % 2] for r in range(8)}
    back = return_copies(all_parts, cores, sides, sends, recvs, 0)

    base = 10
    in_rows = gin_s.shape[0] // depth
    back_rows = gback_s.shape[0] // depth

    def line_piece(s, array, right, last):
        offset = 1 if right else depth - 1
        index = base + (0 if right else 2 * depth) + 2 * s + array
        share, source = ((in_rows, gin_s), (back_rows, gback_s))[array]
        into = (line_in, line_back)[array].at[s]
        if last and not right:
            into = (extra_in, extra_back)[array]
        here = source.at[pl.ds(s * share, share)]
        return along(here, into, sends, recvs, index, offset, depth)

    def add_piece(s, array):
        share, source = ((in_rows, gin_s), (back_rows, gback_s))[array]
        other = (line_in, line_back)[array]
        here = pl.ds(s * share, share)
        source[here, :] = (source[here, :].astype(F32) + other[s].astype(F32)).astype(BF)

    def pieces(right):
        order = range(depth - 1, 0, -1) if right else range(depth - 1)
        return [(s, array) for s in order for array in (0, 1)]

    def start_piece(s, array, right):
        if right:
            line_piece(s, array, True, False).start()
            return
        near = z == s + 1

        @pl.when(near)
        def _():
            line_piece(s, array, False, True).start()

        @pl.when(jnp.logical_not(near))
        def _():
            line_piece(s, array, False, False).start()

    def line_service(t, ahead=1):
        for right in (True, False):
            every = pieces(right)
            edge = 0 if right else depth - 1
            opening = range(2, 3 + ahead) if t == 0 else range(t + ahead + 2, t + ahead + 3)

            @pl.when(z == edge)
            def _():
                for number in opening:
                    if number < len(every):
                        start_piece(*every[number], right)

            for number, (s, array) in enumerate(every):
                away = s if right else depth - 1 - s
                for hops in range(1, away):
                    given = hops == 1 and number < 2
                    if t != (0 if given else number + hops - 1):
                        continue

                    @pl.when(z == (hops if right else depth - 1 - hops))
                    def _():
                        if not given:
                            line_piece(s, array, right, False).wait_recv()
                            add_piece(s, array)
                        start_piece(s, array, right)

    def line_end():
        for s in range(depth):

            @pl.when(z == s)
            def _():
                here = pl.ds(s * in_rows, in_rows)
                there = pl.ds(s * back_rows, back_rows)
                gin_o[...] = gin_s[here, :].astype(F32)
                gback_o[...] = gback_s[there, :].astype(F32)
                if s > 0:
                    for array in (0, 1):
                        line_piece(s, array, True, True).wait_recv()
                    gin_o[...] += line_in[s].astype(F32)
                    gback_o[...] += line_back[s].astype(F32)
                if s < depth - 1:
                    for array in (0, 1):
                        line_piece(s, array, False, True).wait_recv()
                    gin_o[...] += extra_in[...].astype(F32)
                    gback_o[...] += extra_back[...].astype(F32)

        for s in range(depth):
            for array in (0, 1):
                first_right = 1 if s == depth - 1 else 0
                first_left = depth - 2 if s == 0 else depth - 1

                @pl.when(jnp.logical_and(z < s, z >= first_right))
                def _():
                    line_piece(s, array, True, False).wait_send()

                @pl.when(jnp.logical_and(z > s, z <= first_left))
                def _():
                    line_piece(s, array, False, False).wait_send()

    base_red = base + 4 * depth
    per = Reduction.semaphores(depth)
    red_o, red_0, red_1 = [
        Reduction(depth, *red[7 * place : 7 * place + 7], sems, base_red + place * per)
        for place in range(3)
    ]
    sums = SmallSum(
        depth, small, small_core, small_plane, small_line, sems, base_red + 3 * per
    )

    small[...] = jnp.zeros_like(small)
    small[4:5] = attn_sum[...]
    small[7:8, 0:sents] = lengths[...].astype(F32)
    experts = plan.shape[0] // 3
    chunk_place = lax.broadcasted_iota(jnp.int32, (slot, width), 0)

    def masked(ref, c):
        return jnp.concatenate(
            [
                jnp.where(
                    chunk_place < len_ref[c * count + s], ref[c * count + s].astype(F32), 0.0
                )
                for s in range(count)
            ],
            axis=0,
        )

    def flat(ref, c):
        block = ref[pl.ds(c * count, count)]
        return block.astype(F32).reshape(rows_per, width)

    def first(c, carry):
        rows = pl.ds(pl.multiple_of(c * rows_per, rows_per), rows_per)
        normed2, inverse2 = normalize(h_ref[rows, :])
        dm = flat(dm_ref, c)
        dhidden = masked(cot_ref, c) + layer_norm_pull(dm, normed2, inverse2, g2[...])
        small[2:3] += row_sum(dm * normed2, width)
        small[3:4] += row_sum(dm, width)
        dh_s[rows, :] = dhidden
        dattn = dhidden.astype(BF)
        da_s[rows, :] = dattn
        dctx_s[rows, :] = mm(dattn, wo[...], 1, 1).astype(BF)
        return carry

    mask = block_diagonal(group, slot, head)

    def pull(part, into):
        cols = slice(part * span, (part + 1) * span)

        def one(c, carry):
            for s in range(count):
                at = c * count + s
                rows = pl.ds(pl.multiple_of(at * slot, slot), slot)
                dq_s[rows, cols], dk_s[rows, cols], dv_s[rows, cols] = attention_pull(
                    dctx_s[rows, cols], q[rows, cols], k[rows, cols], v[rows, cols],
                    p_ref[at, part], mask, slot, group, scale,
                )
            return carry

        lax.fori_loop(0, sents // count, one, 0)
        into.value[0:width, :] = mm(act[...], dq_s[:, cols], 0, 0)
        into.value[width : 2 * width, :] = mm(act[...], dk_s[:, cols], 0, 0)
        into.value[2 * width : 3 * width, :] = mm(act[...], dv_s[:, cols], 0, 0)
        into.send_core()

    def returned(r):
        ready(parts[r], cores[r])
        add_into(parts[r], 0, cores[r], sents)

    def last(c, carry):
        rows = pl.ds(pl.multiple_of(c * rows_per, rows_per), rows_per)
        dact = (
            mm(dq_s[rows, :], wq[...], 1, 1)
            + mm(dk_s[rows, :], wk[...], 1, 1)
            + mm(dv_s[rows, :], wv[...], 1, 1)
        )
        normed1, inverse1 = normalize(flat(x_ref, c))
        small[0:1] += row_sum(dact * normed1, width)
        small[1:2] += row_sum(dact, width)
        dx = dh_s[rows, :] + layer_norm_pull(dact, normed1, inverse1, g1[...])
        ig_o[pl.ds(c * count, count)] = dx.astype(BF).reshape(count, slot, width)
        return carry

    def outcome(low, side):
        def one(i, carry):
            at = low + i
            valid = chunk_place < len_ref[at]
            moe = jnp.where(valid, parts[0][at].astype(F32) + side[i].astype(F32), 0.0)
            rows = pl.ds(pl.multiple_of(at * slot, slot), slot)
            total = jnp.where(valid, h_ref[rows, :], 0.0) + moe
            out_o[at] = total.astype(BF)
            small[5:6] += row_sum(total * total, width)
            small[6:7] += row_sum(moe * moe, width)
            return carry

        lax.fori_loop(0, half, one, 0)

    def gate_gradient():
        hit = plan[0:experts] > 0.5
        place = plan[experts : 2 * experts]
        gate = plan[2 * experts : 3 * experts]
        taken = jnp.zeros(gate.shape, F32)
        for j in range(dots.shape[1]):
            taken = taken + jnp.where(place == float(j), dots[:, j, 0:sents], 0.0)
        inner = jnp.sum(gate * taken, axis=0, keepdims=True)
        dlogit = jnp.where(hit, gate * (taken - inner), 0.0)
        hot = lax.broadcasted_iota(jnp.int32, (slot, sents), 0) == tasks[...]
        small[8 : 8 + experts, 0:slot] = lax.dot_general(
            dlogit, hot.astype(F32), (((1,), (1,)), ((), ())),
            precision=lax.Precision.HIGHEST, preferred_element_type=F32,
        )

    ready(gin_s, gback_s)
    line_service(0)
    returned(6)
    back[5].start()
    back[7].start()
    ready(h_ref, dm_ref, cot_ref, wo)
    lax.fori_loop(0, sents // count, first, 0)
    ready(ctx)
    red_o.value[...] = mm(ctx[...], da_s[...], 0, 0)
    red_o.send_core()
    returned(2)
    returned(4)
    ready(q, k, v, p_ref, act)
    pull(0, red_0)
    red_o.send_plane()
    back[4].start()
    back[6].start()
    line_service(1)
    back[5].wait_recv()
    add_into(parts[4], 0, sides[1], half)
    back[7].wait_recv()
    add_into(parts[2], half, sides[3], half)
    pull(1, red_1)
    red_0.send_plane()
    back[8].start()
    back[9].start()
    red_o.send_line()
    line_service(2)
    ready(wq, wk, wv, x_ref)
    lax.fori_loop(0, sents // count, last, 0)
    red_1.send_plane()
    red_o.send_back_line()
    gate_gradient()
    returned(0)
    red_0.send_line()
    line_service(3)
    back[4].wait_recv()
    add_into(parts[0], 0, sides[0], half)
    back[6].wait_recv()
    add_into(parts[0], half, sides[2], half)
    red_o.send_back_plane()
    red_0.send_back_line()
    red_1.send_line()
    back[8].wait_recv()
    outcome(0, sides[4])
    back[9].wait_recv()
    outcome(half, sides[5])
    sums.send_core()
    red_o.send_back_core()
    red_0.send_back_plane()
    red_1.send_back_line()
    sums.send_plane()
    red_1.send_back_plane()
    red_0.send_back_core()
    sums.send_line()
    red_1.send_back_core()
    red_o.finish()
    go_o[...] = red_o.final[...]
    red_0.finish()

    def share(red, low):
        for place, ref in enumerate((gq_o, gk_o, gv_o)):
            ref[:, low : low + red.final.shape[1]] = red.final[
                place * width : (place + 1) * width, :
            ]

    share(red_0, 0)
    sums.finish(small_o)
    red_1.finish()
    share(red_1, span)
    line_end()
    for copy in back[4:]:
        copy.wait_send()


def backward_exchange(
    depth, lengths, tokens, cot, dm, hidden, act, q, k, v, ctx, prob, wq, wk, wv, wo, g1, g2,
    attn_sum, plan, tasks, dots, py, cy, gin, gback, heads,
):
    sents, slot, width = tokens.shape
    total = sents * slot
    small = jax.ShapeDtypeStruct((16, width), F32)
    vm = pl.BlockSpec(memory_space=VM)
    anywhere = pl.BlockSpec(memory_space=pl.ANY)
    shape = jax.ShapeDtypeStruct
    cube = (sents, slot, width)
    head = width // heads
    span = max(1, min(heads, 256 // head)) * head
    pieces = [(width, width), (3 * width, span), (3 * width, width - span)]
    red = []
    for rows, cols in pieces:
        red += [
            VM((rows, cols), F32),
            VM((rows // 2, cols), BF),
            VM((rows // 2, cols), BF),
            VM((3, rows // 8, cols), BF),
            VM((rows // 8, cols), BF),
            VM((depth - 1, rows // 8 // depth, cols), BF),
            VM((rows, cols), BF),
        ]
    in_share = (gin.shape[0] // depth, gin.shape[1])
    back_share = (gback.shape[0] // depth, gback.shape[1])
    semaphores = 10 + 4 * depth + 3 * Reduction.semaphores(depth) + SmallSum.semaphores(depth)
    large = (
        tokens, cot, dm, hidden, act, q, k, v, ctx, prob, wq, wk, wv, wo, py, cy, gin, gback,
    )
    return pl.pallas_call(
        functools.partial(backward_kernel, heads, depth),
        in_specs=[pl.BlockSpec(memory_space=pltpu.SMEM)] + [vm] * 7 + [anywhere] * len(large),
        out_specs=[vm] * 9,
        out_shape=[shape(cube, BF), shape(cube, BF)]
        + [shape((width, width), BF)] * 4
        + [shape(in_share, F32), shape(back_share, F32), shape(small.shape, F32)],
        scratch_shapes=[VM(ref.shape, ref.dtype) for ref in large[:14] + large[16:]]
        + [VM(cube, BF)] * 8
        + [VM((sents // 2, slot, width), BF)] * 6
        + [VM((total, width), F32)]
        + [VM((total, width), BF)] * 5
        + red
        + [VM((depth,) + in_share, BF), VM((depth,) + back_share, BF)]
        + [VM(in_share, BF), VM(back_share, BF)]
        + [VM(small.shape, F32)] * 2
        + [VM((4,) + small.shape, F32), VM((depth,) + small.shape, F32)]
        + [
            pltpu.SemaphoreType.DMA((semaphores,)),
            pltpu.SemaphoreType.DMA((semaphores,)),
            pltpu.SemaphoreType.DMA((24,)),
        ],
        compiler_params=pltpu.CompilerParams(
            collective_id=2, has_side_effects=True, vmem_limit_bytes=63 * 2**20
        ),
        cost_estimate=pl.CostEstimate(
            flops=16 * total * width * width, bytes_accessed=40 * 2**20, transcendentals=0
        ),
    )(
        lengths, g1[None], g2[None], attn_sum, plan, tasks[None], lengths[None], dots, *large
    )


def outputs_kernel(
    out_in, ig_in, gin_in, gback_in, q_in, k_in, v_in, o_in, small,
    out_o, ig_o, gin_o, gback_o, q_o, k_o, v_o, o_o, l1g, l1b, l2g, l2b, table_o, rms_o,
    low, wide, cubes, share_in, share_back, sems,
):
    fetches = [
        pltpu.make_async_copy(src, low.at[place], sems.at[place])
        for place, src in enumerate((q_in, k_in, v_in, o_in))
    ]
    stores = [
        pltpu.make_async_copy(wide.at[place], dst, sems.at[4 + place])
        for place, dst in enumerate((q_o, k_o, v_o, o_o))
    ]
    moves = [
        (pltpu.make_async_copy(src, held, sems.at[8 + place]),
         pltpu.make_async_copy(held, dst, sems.at[12 + place]))
        for place, (src, held, dst) in enumerate(
            [
                (out_in, cubes.at[0], out_o),
                (ig_in, cubes.at[1], ig_o),
                (gin_in, share_in, gin_o),
                (gback_in, share_back, gback_o),
            ]
        )
    ]
    for fetch in fetches:
        fetch.start()
    for enter, _ in moves:
        enter.start()
    width = small.shape[1]
    for row, ref in enumerate((l1g, l1b, l2g, l2b)):
        ref[...] = small[row : row + 1]
    table_o[...] = small[8 : 8 + table_o.shape[0], 0 : table_o.shape[1]]
    sums = jnp.sum(small[4:8], axis=1, keepdims=True)
    ratio = jnp.sqrt(sums / (sums[3:4] * width))
    lane = lax.broadcasted_iota(jnp.int32, (1, 3), 1)
    pair = jnp.where(lane == 1, ratio[0:1], ratio[2:3])
    rms_o[...] = jnp.where(lane == 0, ratio[1:2], pair)
    for place in range(4):
        fetches[place].wait()
        wide[place] = low[place].astype(F32)
        stores[place].start()
    for enter, leave in moves:
        enter.wait()
        leave.start()
    for store in stores:
        store.wait()
    for _, leave in moves:
        leave.wait()


def place_outputs(out, ig, gin, gback, q, k, v, o, small, experts, ntasks):
    width = small.shape[1]
    vm = pl.BlockSpec(memory_space=VM)
    anywhere = pl.BlockSpec(memory_space=pl.ANY)
    shape = jax.ShapeDtypeStruct
    return pl.pallas_call(
        outputs_kernel,
        in_specs=[anywhere] * 8 + [vm],
        out_specs=[anywhere] * 8 + [vm] * 6,
        out_shape=[shape(a.shape, a.dtype) for a in (out, ig, gin, gback)]
        + [shape(q.shape, F32)] * 4
        + [shape((1, width), F32)] * 4
        + [shape((experts, ntasks), F32), shape((1, 3), F32)],
        scratch_shapes=[
            VM((4,) + q.shape, BF),
            VM((4,) + q.shape, F32),
            VM((2,) + out.shape, BF),
            VM(gin.shape, F32),
            VM(gback.shape, F32),
            pltpu.SemaphoreType.DMA((16,)),
        ],
        compiler_params=pltpu.CompilerParams(vmem_limit_bytes=60 * 2**20),
    )(out, ig, gin, gback, q, k, v, o, small)


def local(
    tokens,
    lengths,
    tasks,
    routes,
    gate_table,
    ln1_gain,
    ln1_bias,
    ln2_gain,
    ln2_bias,
    w_query,
    w_key,
    w_value,
    w_out,
    w_in,
    w_back,
    cotangent,
):
    sents, slot, width = tokens.shape
    heads = HEADS
    head = width // heads
    experts = gate_table.shape[1]
    ntasks = routes.shape[0]
    capacity = max(1, 4 * sents // experts)
    scale = 1.0 / jnp.sqrt(jnp.float32(head))
    task_hot = (tasks[:, None] == jnp.arange(ntasks)[None, :]).astype(jnp.int32)
    chosen = jnp.sum(task_hot[:, :, None] * routes[None, :, :], axis=1)
    flat = chosen.reshape(-1)
    order = jnp.arange(2 * sents)
    earlier = (flat[:, None] == flat[None, :]) & (order[None, :] < order[:, None])
    rank = jnp.sum(earlier.astype(jnp.int32), axis=1)
    slot_id = flat * capacity + rank
    placed = rank < capacity
    dispatch = (
        (jnp.arange(experts * capacity)[:, None] == slot_id[None, :]) & placed[None, :]
    ).astype(jnp.bfloat16)
    collect = dispatch.T
    expert_hot = (chosen[:, :, None] == jnp.arange(experts)[None, None, :]).astype(jnp.float32)
    valid = (jnp.arange(slot)[None, :] < lengths[:, None]).astype(jnp.float32)
    keymask = valid[:, None, None, :] > 0.5
    mask3 = valid[:, :, None]
    xfull = tokens.astype(jnp.float32)
    normed1, inverse1 = normalize(xfull)
    act = (normed1 * ln1_gain + ln1_bias).astype(jnp.bfloat16).reshape(-1, width)
    query = project(act, w_query).astype(jnp.bfloat16).reshape(sents, slot, heads, head)
    keyed = project(act, w_key).astype(jnp.bfloat16).reshape(sents, slot, heads, head)
    valued = project(act, w_value).astype(jnp.bfloat16).reshape(sents, slot, heads, head)

    def scores_of(qpart, kpart):
        raw = (
            jnp.einsum("sqhd,skhd->shqk", qpart, kpart, preferred_element_type=jnp.float32) * scale
        )
        return jnp.where(keymask, raw, -1000000000.0)

    scores = scores_of(query, keyed)
    peak = jnp.max(scores, axis=-1, keepdims=True)
    logsum = peak + jnp.log(jnp.sum(jnp.exp(scores - peak), axis=-1, keepdims=True))
    prob_low = jnp.exp(scores - logsum).astype(jnp.bfloat16)
    context = jnp.einsum("shqk,skhd->sqhd", prob_low, valued, preferred_element_type=jnp.float32)
    context = context.astype(jnp.bfloat16).reshape(-1, width)
    attention_block = project(context, w_out).reshape(sents, slot, width)
    hidden_res = xfull + attention_block
    normed2, inverse2 = normalize(hidden_res)
    mixed = (normed2 * ln2_gain + ln2_bias).astype(jnp.bfloat16)
    table_rows = jnp.dot(task_hot.astype(jnp.float32), gate_table, precision=lax.Precision.HIGHEST)
    picked = jnp.sum(expert_hot * table_rows[:, None, :], axis=-1)
    gate_values = jax.nn.softmax(picked, axis=-1)
    grad_total = cotangent.astype(jnp.float32) * mask3
    copies = jnp.broadcast_to(mixed[:, None], (sents, 2, slot, width)).reshape(
        2 * sents, slot * width
    )
    outgoing = (
        project(dispatch, copies).astype(jnp.bfloat16).reshape(experts, capacity, slot, width)
    )
    dycopy = (
        (gate_values[:, :, None, None] * grad_total[:, None])
        .astype(jnp.bfloat16)
        .reshape(2 * sents, slot * width)
    )
    grad_out = (
        project(dispatch, dycopy).astype(jnp.bfloat16).reshape(experts, capacity, slot, width)
    )
    incoming = lax.all_to_all(outgoing, "expert", split_axis=0, concat_axis=0, tiled=True).reshape(
        -1, width
    )
    pre_act, active, produced = expert_forward(incoming, w_in[0], w_back[0])
    returned = lax.all_to_all(
        produced.reshape(experts, capacity, slot, width),
        "expert",
        split_axis=0,
        concat_axis=0,
        tiled=True,
    )
    grad_in = lax.all_to_all(grad_out, "expert", split_axis=0, concat_axis=0, tiled=True).reshape(
        -1, width
    )
    in_local, back_local, dincoming = expert_backward(
        incoming, pre_act, active, grad_in, w_in[0], w_back[0]
    )
    grad_back = lax.all_to_all(
        dincoming.reshape(experts, capacity, slot, width),
        "expert",
        split_axis=0,
        concat_axis=0,
        tiled=True,
    )
    ycopy = project(collect, returned.reshape(experts * capacity, slot * width)).reshape(
        sents, 2, slot, width
    )
    expert_mixture = jnp.sum(gate_values[:, :, None, None] * ycopy, axis=1)
    total = mask3 * (hidden_res + expert_mixture)
    output = total.astype(jnp.bfloat16)
    stats_local = jnp.stack(
        [
            jnp.sum(total * total),
            jnp.sum(mask3 * attention_block * attention_block),
            jnp.sum(mask3 * expert_mixture * expert_mixture),
            jnp.sum(valid),
        ]
    )
    stat_totals = lax.psum(stats_local, ("dp", "expert"))
    gate_dot = jnp.sum(ycopy * grad_total[:, None], axis=(2, 3))
    dpicked = gate_values * (gate_dot - jnp.sum(gate_values * gate_dot, axis=-1, keepdims=True))
    dlogits = jnp.sum(expert_hot * dpicked[:, :, None], axis=1)
    table_grad = jnp.dot(task_hot.T.astype(jnp.float32), dlogits, precision=lax.Precision.HIGHEST)
    dmixed = project(collect, grad_back.reshape(experts * capacity, slot * width)).reshape(
        sents, 2, slot, width
    )
    dmixed = jnp.sum(dmixed, axis=1)
    dres2, gain2_grad, bias2_grad = norm_backward(dmixed, normed2, inverse2, ln2_gain)
    dhidden = grad_total + dres2
    dattn = dhidden.astype(jnp.bfloat16).reshape(-1, width)
    wout_grad = project(context.T, dattn)
    dcontext = project(dattn, w_out.T).astype(jnp.bfloat16).reshape(sents, slot, heads, head)
    again = jnp.exp(scores_of(query, keyed) - logsum)
    dprob = jnp.einsum("sqhd,skhd->shqk", dcontext, valued, preferred_element_type=jnp.float32)
    dscores = (again * (dprob - jnp.sum(dprob * again, axis=-1, keepdims=True))).astype(
        jnp.bfloat16
    )
    dquery = (
        jnp.einsum("shqk,skhd->sqhd", dscores, keyed, preferred_element_type=jnp.float32) * scale
    )
    dkeyed = (
        jnp.einsum("shqk,sqhd->skhd", dscores, query, preferred_element_type=jnp.float32) * scale
    )
    dvalued = jnp.einsum("shqk,sqhd->skhd", prob_low, dcontext, preferred_element_type=jnp.float32)
    dquery = dquery.astype(jnp.bfloat16).reshape(-1, width)
    dkeyed = dkeyed.astype(jnp.bfloat16).reshape(-1, width)
    dvalued = dvalued.astype(jnp.bfloat16).reshape(-1, width)
    wq_grad = project(act.T, dquery)
    wk_grad = project(act.T, dkeyed)
    wv_grad = project(act.T, dvalued)
    dact = project(dquery, w_query.T) + project(dkeyed, w_key.T) + project(dvalued, w_value.T)
    dres1, gain1_grad, bias1_grad = norm_backward(
        dact.reshape(sents, slot, width), normed1, inverse1, ln1_gain
    )
    input_grad = (dhidden + dres1).astype(jnp.bfloat16)
    members = (
        wq_grad,
        wk_grad,
        wv_grad,
        wout_grad,
        gain1_grad,
        bias1_grad,
        gain2_grad,
        bias2_grad,
        table_grad,
    )
    members = members + ()
    summed = lax.psum(members, ("dp", "expert"))
    rms = jnp.sqrt(stat_totals[0:3] / (stat_totals[3] * width))
    in_share, back_share = (
        lax.psum_scatter(
            in_local.astype(jnp.bfloat16), "dp", scatter_dimension=0, tiled=True
        ).astype(jnp.float32),
        lax.psum_scatter(
            back_local.astype(jnp.bfloat16), "dp", scatter_dimension=0, tiled=True
        ).astype(jnp.float32),
    )
    return (
        output,
        input_grad,
        summed[8],
        summed[4],
        summed[5],
        summed[6],
        summed[7],
        summed[0],
        summed[1],
        summed[2],
        summed[3],
        in_share[None],
        back_share[None],
        rms,
    )


def local_plane(
    depth,
    tokens,
    lengths,
    tasks,
    routes,
    gate_table,
    ln1_gain,
    ln1_bias,
    ln2_gain,
    ln2_bias,
    w_query,
    w_key,
    w_value,
    w_out,
    w_in,
    w_back,
    cotangent,
):
    experts = gate_table.shape[1]
    sents, slot, width = tokens.shape
    heads = HEADS
    capacity = max(1, 4 * sents // experts)
    (
        act, query, keyed, valued, context, prob, hidden, mixed, attn_sum, plan, places,
        gate_slots, near, far, core,
    ) = attention_forward(
        tokens, lengths, w_query, w_key, w_value, w_out, ln1_gain, ln1_bias, ln2_gain, ln2_bias,
        tasks, routes.T, gate_table.T, cotangent, heads, capacity,
    )
    dmixed, parts_back, cores_back, in_local, back_local, slot_dots = expert_exchange(
        places, gate_slots, mixed, cotangent, near, far, core, w_in[0], w_back[0], capacity, depth
    )
    input_grad, output, sum_q, sum_k, sum_v, sum_o, in_share, back_share, small = (
        backward_exchange(
            depth, lengths, tokens, cotangent, dmixed, hidden, act, query, keyed, valued,
            context, prob, w_query, w_key, w_value, w_out, ln1_gain, ln2_gain, attn_sum, plan,
            tasks, slot_dots, parts_back, cores_back, in_local, back_local, heads,
        )
    )
    (
        output, input_grad, in_share, back_share, grad_q, grad_k, grad_v, grad_o,
        gain1, bias1, gain2, bias2, table_grad, rms,
    ) = place_outputs(
        output, input_grad, in_share, back_share, sum_q, sum_k, sum_v, sum_o, small,
        experts, gate_table.shape[0],
    )
    return (
        output,
        input_grad,
        table_grad.T,
        gain1.reshape(-1),
        bias1.reshape(-1),
        gain2.reshape(-1),
        bias2.reshape(-1),
        grad_q,
        grad_k,
        grad_v,
        grad_o,
        in_share[None],
        back_share[None],
        rms.reshape(-1),
    )


def solution(mesh):
    in_specs = (
        P(("dp", "expert"), None, None),
        P(("dp", "expert")),
        P(("dp", "expert")),
        P(),
        P(),
        P(),
        P(),
        P(),
        P(),
        P(),
        P(),
        P(),
        P(),
        P("expert", None, None),
        P("expert", None, None),
        P(("dp", "expert"), None, None),
    )
    out_specs = (
        P(("dp", "expert"), None, None),
        P(("dp", "expert"), None, None),
        P(),
        P(),
        P(),
        P(),
        P(),
        P(),
        P(),
        P(),
        P(),
        P("expert", "dp", None),
        P("expert", "dp", None),
        P(),
    )
    plane = dict(mesh.shape)["expert"]
    depth = dict(mesh.shape)["dp"]
    cube = plane == 2 * 2 * 2 and depth > 2
    body = functools.partial(local_plane, depth) if cube else local
    return jax.shard_map(body, mesh=mesh, in_specs=in_specs, out_specs=out_specs, check_vma=False)
```

```python
import functools

import jax
import jax.numpy as jnp
from jax import lax
from jax.experimental import pallas as pl
from jax.experimental.pallas import tpu as pltpu
from jax.sharding import PartitionSpec as P

HEADS = 8


def normalize(value):
    centered = value - jnp.mean(value, axis=-1, keepdims=True)
    variance = jnp.mean(centered * centered, axis=-1, keepdims=True)
    inverse = lax.rsqrt(variance + 1e-05)
    return (centered * inverse, inverse)


def norm_backward(grad, normed, inverse, gain):
    scaled = grad * gain
    inner = scaled - jnp.mean(scaled, axis=-1, keepdims=True)
    inner = inner - normed * jnp.mean(scaled * normed, axis=-1, keepdims=True)
    return (inverse * inner, jnp.sum(grad * normed, axis=(0, 1)), jnp.sum(grad, axis=(0, 1)))


def project(left, right):
    return jnp.dot(left, right, preferred_element_type=jnp.float32)


def expert_forward(incoming, first, second):
    pre_act = project(incoming, first)
    active = jax.nn.gelu(pre_act).astype(jnp.bfloat16)
    produced = project(active, second).astype(jnp.bfloat16)
    return (pre_act, active, produced)


def expert_backward(incoming, pre_act, active, grad_in, first, second):
    dactive = project(grad_in, second.T)
    back_local = project(active.T, grad_in)
    gelu_pull = jax.vjp(jax.nn.gelu, pre_act)[1]
    dpre = gelu_pull(dactive)[0].astype(jnp.bfloat16)
    in_local = project(incoming.T, dpre)
    dincoming = project(dpre, first.T).astype(jnp.bfloat16)
    return (in_local, back_local, dincoming)


BF = jnp.bfloat16
F32 = jnp.float32
VM = pltpu.VMEM


def mm(a, b, ca=1, cb=0):
    return lax.dot_general(a, b, (((ca,), (cb,)), ((), ())), preferred_element_type=F32)


def block_diagonal(group, slot, head):
    shape = (group * slot, group * head)
    rows = lax.broadcasted_iota(jnp.int32, shape, 0) // slot
    cols = lax.broadcasted_iota(jnp.int32, shape, 1) // head
    return rows == cols


def spread(part, mask, group):
    return jnp.where(mask, jnp.concatenate([part] * group, axis=0), jnp.zeros((), part.dtype))


def fold(product, mask, slot, group):
    kept = jnp.where(mask, product, 0.0)
    total = kept[0:slot]
    for one in range(1, group):
        total = total + kept[one * slot : (one + 1) * slot]
    return total


def attend(query, keyed, valued, length, mask, slot, group, scale):
    scores = mm(keyed, spread(query, mask, group), 1, 1) * scale
    place = lax.broadcasted_iota(jnp.int32, scores.shape, 0)
    scores = jnp.where(place < length, scores, -1000000000.0)
    raised = jnp.exp(scores - jnp.max(scores, axis=0, keepdims=True))
    prob = raised / jnp.sum(raised, axis=0, keepdims=True)
    context = fold(mm(prob.astype(BF), valued, 0, 0), mask, slot, group)
    return prob, context


def route_tables(cap, tasks, lengths, routes, gate_table):
    sents = tasks.shape[1]
    experts, ntasks = gate_table.shape
    iota = lambda rows, cols, axis: lax.broadcasted_iota(jnp.int32, (rows, cols), axis)
    hot = (iota(ntasks, sents, 0) == tasks).astype(F32)
    exact = functools.partial(
        lax.dot_general,
        dimension_numbers=(((1,), (0,)), ((), ())),
        precision=lax.Precision.HIGHEST,
        preferred_element_type=F32,
    )
    chosen = exact(routes.astype(F32), hot)
    first, second = chosen[0:1], chosen[1:2]
    expert = iota(experts, sents, 0).astype(F32)
    is_first, is_second = expert == first, expert == second
    hit = jnp.logical_or(is_first, is_second)
    before = (iota(sents, sents, 0) < iota(sents, sents, 1)).astype(BF)
    rank = mm(hit.astype(F32).astype(BF), before)
    place = jnp.where(hit, jnp.where(rank < cap, rank, -1.0), -1.0)
    logits = exact(gate_table, hot)
    one = jnp.sum(jnp.where(is_first, logits, 0.0), axis=0, keepdims=True)
    two = jnp.sum(jnp.where(is_second, logits, 0.0), axis=0, keepdims=True)
    peak = jnp.maximum(one, two)
    one, two = jnp.exp(one - peak), jnp.exp(two - peak)
    gate = jnp.where(is_first, one / (one + two), 0.0)
    gate = gate + jnp.where(is_second, two / (one + two), 0.0)
    lane = iota(experts, 128, 1)
    index = iota(experts, sents, 1).astype(F32)
    table = jnp.zeros((experts, 128), F32)
    gates = jnp.zeros((experts, 128), F32)
    for j in range(cap):
        here = place == float(j)
        pick = lambda value: jnp.sum(jnp.where(here, value, 0.0), axis=1, keepdims=True)
        table = jnp.where(lane == j, pick(index), table)
        table = jnp.where(lane == cap + j, pick(lengths.astype(F32)), table)
        gates = jnp.where(lane == j, pick(gate), gates)
    shift = (iota(sents, 128, 1) == iota(sents, 128, 0) + 2 * cap).astype(BF)
    spots = mm((place + 1.0).astype(BF), shift)
    inside = jnp.logical_and(lane >= 2 * cap, lane < 2 * cap + sents)
    table = jnp.where(inside, spots - 1.0, table)
    return table.astype(jnp.int32), gates, hit.astype(F32), place, gate


def attention_forward_kernel(
    heads, cap, len_ref, x_ref, wq, wk, wv, wo, g1, b1, g2, b2, tasks, lengths, routes,
    gate_table, cot_in,
    act_o, q_o, k_o, v_o, ctx_o, p_o, h_o, m_o, st_o, plan_o, tab_o, gates_o, near_o, far_o,
    core_o, cot, tab_s, gates_s, sends, recvs, local,
):
    count, slot, width = x_ref.shape
    head = width // heads
    group = max(1, min(heads, 256 // head))
    span = group * head
    step = pl.program_id(0)
    scale = head ** -0.5
    mask = block_diagonal(group, slot, head)
    experts = gate_table.shape[0]
    me = lax.axis_index("expert")
    half = cot.shape[0] // 2
    copies = [
        remote(cot.at[pl.ds(0, half)], near_o, sends, recvs, 0, NEAR),
        remote(cot.at[pl.ds(half, half)], far_o, sends, recvs, 1, FAR),
        remote(cot, core_o, sends, recvs, 2, CORE),
    ]
    for relation in range(1, 8):
        there = plane_peer(relation)
        copies += [
            remote(tab_s.at[there], tab_o.at[me], sends, recvs, 1 + 2 * relation, relation),
            remote(gates_s.at[there], gates_o.at[me], sends, recvs, 2 + 2 * relation, relation),
        ]
    own = [
        pltpu.make_async_copy(tab_s.at[me], tab_o.at[me], local.at[0]),
        pltpu.make_async_copy(gates_s.at[me], gates_o.at[me], local.at[1]),
    ]

    @pl.when(step == 0)
    def _():
        load = pltpu.make_async_copy(cot_in, cot, local.at[2])
        load.start()
        plane_barrier()
        load.wait()
        for copy in copies[0:3]:
            copy.start()
        table, gates, hit, place, gate = route_tables(
            cap, tasks[...], lengths[...], routes[...], gate_table[...]
        )
        for e in range(experts):
            tab_s[e] = jnp.broadcast_to(table[e : e + 1], (8, 128))
            gates_s[e] = jnp.broadcast_to(gates[e : e + 1], (8, 128))
        for copy in copies[3:]:
            copy.start()
        for copy in own:
            copy.start()
        plan_o[0:experts] = hit
        plan_o[experts : 2 * experts] = place
        plan_o[2 * experts : 3 * experts] = gate
        st_o[...] = jnp.zeros_like(st_o)

    x = x_ref[...].astype(F32).reshape(count * slot, width)
    normed, _ = normalize(x)
    act = (normed * g1[...] + b1[...]).astype(BF)
    act_o[...] = act
    q_o[...] = mm(act, wq[...]).astype(BF)
    k_o[...] = mm(act, wk[...]).astype(BF)
    v_o[...] = mm(act, wv[...]).astype(BF)
    for s in range(count):
        length = len_ref[step * count + s]
        rows = slice(s * slot, (s + 1) * slot)
        for part in range(heads // group):
            cols = slice(part * span, (part + 1) * span)
            prob, context = attend(
                q_o[rows, cols], k_o[rows, cols], v_o[rows, cols], length, mask, slot, group, scale
            )
            p_o[s, part] = prob
            ctx_o[rows, cols] = context.astype(BF)
    attn = mm(ctx_o[...], wo[...])
    hidden = x + attn
    h_o[...] = hidden
    normed2, _ = normalize(hidden)
    m_o[...] = (normed2 * g2[...] + b2[...]).astype(BF).reshape(count, slot, width)
    place = lax.broadcasted_iota(jnp.int32, (slot, width), 0)
    total = jnp.zeros((1, width), F32)
    for s in range(count):
        length = len_ref[step * count + s]
        part = attn[s * slot : (s + 1) * slot]
        total = total + jnp.sum(jnp.where(place < length, part * part, 0.0), axis=0, keepdims=True)
    st_o[...] += total

    @pl.when(step == pl.num_programs(0) - 1)
    def _():
        for copy in copies + own:
            copy.wait()


def attention_forward(
    tokens, lengths, wq, wk, wv, wo, g1, b1, g2, b2, tasks, routes, gate_table, cot, heads, cap
):
    sents, slot, width = tokens.shape
    experts = gate_table.shape[0]
    count = 4 if sents % 4 == 0 else 1
    rows = count * slot
    head = width // heads
    group = max(1, min(heads, 256 // head))
    whole = lambda *shape: pl.BlockSpec(shape, lambda i: (0,) * len(shape))
    flat = pl.BlockSpec((rows, width), lambda i: (i, 0))
    cube = pl.BlockSpec((count, slot, width), lambda i: (i, 0, 0))
    probs = pl.BlockSpec((count, heads // group, slot, group * slot), lambda i: (i, 0, 0, 0))
    anywhere = pl.BlockSpec(memory_space=pl.ANY)
    shape = jax.ShapeDtypeStruct
    total = sents * slot
    half = (sents // 2, slot, width)
    return pl.pallas_call(
        functools.partial(attention_forward_kernel, heads, cap),
        grid=(sents // count,),
        in_specs=[pl.BlockSpec(memory_space=pltpu.SMEM), cube]
        + [whole(width, width)] * 4
        + [whole(1, width)] * 4
        + [whole(1, sents)] * 2
        + [whole(*routes.shape), whole(*gate_table.shape), anywhere],
        out_specs=[flat] * 5
        + [probs, flat, cube, whole(1, width), whole(3 * experts, sents)]
        + [anywhere] * 5,
        out_shape=[shape((total, width), BF)] * 5
        + [
            shape((sents, heads // group, slot, group * slot), F32),
            shape((total, width), F32),
            shape((sents, slot, width), BF),
            shape((1, width), F32),
            shape((3 * experts, sents), F32),
            shape((experts, 8, 128), jnp.int32),
            shape((experts, 8, 128), F32),
            shape(half, BF),
            shape(half, BF),
            shape(tokens.shape, BF),
        ],
        scratch_shapes=[
            VM(cot.shape, BF),
            VM((experts, 8, 128), jnp.int32),
            VM((experts, 8, 128), F32),
            pltpu.SemaphoreType.DMA((17,)),
            pltpu.SemaphoreType.DMA((17,)),
            pltpu.SemaphoreType.DMA((3,)),
        ],
        compiler_params=pltpu.CompilerParams(
            dimension_semantics=("arbitrary",), vmem_limit_bytes=56 * 2**20,
            collective_id=0, has_side_effects=True,
        ),
        cost_estimate=pl.CostEstimate(
            flops=8 * total * width * width + 4 * total * slot * width,
            bytes_accessed=16 * total * width,
            transcendentals=total * slot * heads,
        ),
    )(
        lengths, tokens, wq, wk, wv, wo, g1[None], b1[None], g2[None], b2[None],
        tasks[None], lengths[None], routes, gate_table, cot,
    )


def row_sum(value, width):
    return jnp.sum(value, axis=0, keepdims=True)


def layer_norm_pull(grad, normed, inverse, gain):
    scaled = grad * gain
    inner = scaled - jnp.mean(scaled, axis=-1, keepdims=True)
    inner = inner - normed * jnp.mean(scaled * normed, axis=-1, keepdims=True)
    return inverse * inner


def attention_pull(dcontext, query, keyed, valued, prob, mask, slot, group, scale):
    low = prob.astype(BF)
    dspread = spread(dcontext, mask, group)
    dprob = mm(valued, dspread, 1, 1)
    inner = jnp.sum(dprob * prob, axis=0, keepdims=True)
    dscores = (prob * (dprob - inner)).astype(BF)
    dquery = fold(mm(dscores, keyed, 0, 0), mask, slot, group) * scale
    dkeyed = mm(dscores, spread(query, mask, group)) * scale
    dvalued = mm(low, dspread)
    return dquery.astype(BF), dkeyed.astype(BF), dvalued.astype(BF)


MESH_ID = pl.DeviceIdType.MESH
CORE, NEAR, FAR = 1, 2, 4


def plane_peer(relation):
    me = lax.axis_index("expert")
    bits = []
    for bit in (CORE, NEAR, FAR):
        value = (me // bit) % 2
        bits.append((1 - value if relation & bit else value) * bit)
    return bits[0] + bits[1] + bits[2]


def remote(src, dst, sends, recvs, index, relation):
    return pltpu.make_async_remote_copy(
        src_ref=src,
        dst_ref=dst,
        send_sem=sends.at[index],
        recv_sem=recvs.at[index],
        device_id=(lax.axis_index("dp"), plane_peer(relation)),
        device_id_type=MESH_ID,
    )


def line_peer(offset, depth):
    return lax.rem(lax.axis_index("dp") + offset, depth)


def along(src, dst, sends, recvs, index, offset, depth):
    return pltpu.make_async_remote_copy(
        src_ref=src,
        dst_ref=dst,
        send_sem=sends.at[index],
        recv_sem=recvs.at[index],
        device_id=(line_peer(offset, depth), lax.axis_index("expert")),
        device_id_type=MESH_ID,
    )


def plane_barrier(depth=1):
    barrier = pltpu.get_barrier_semaphore()
    targets = [(lax.axis_index("dp"), plane_peer(relation)) for relation in range(1, 8)]
    for offset in range(1, depth):
        targets.append((line_peer(offset, depth), lax.axis_index("expert")))
    for target in targets:
        pl.semaphore_signal(barrier, inc=1, device_id=target, device_id_type=MESH_ID)
    pl.semaphore_wait(barrier, len(targets))


def gather_copies(own, held, sends, recvs, base):
    half = own.shape[0] // 2
    low, high = pl.ds(0, half), pl.ds(half, half)
    plan = [
        (own.at[low], held[2].at[low], NEAR),
        (own.at[high], held[4].at[high], FAR),
        (own, held[1], CORE),
        (own.at[high], held[2].at[high], NEAR),
        (own.at[low], held[4].at[low], FAR),
        (held[2].at[low], held[6].at[low], FAR),
        (held[4].at[high], held[6].at[high], NEAR),
        (held[2], held[3], CORE),
        (held[4], held[5], CORE),
        (held[6], held[7], CORE),
    ]
    return [
        remote(src, dst, sends, recvs, base + place, relation)
        for place, (src, dst, relation) in enumerate(plan)
    ]


def return_copies(parts, cores, sides, sends, recvs, base):
    half = parts[0].shape[0] // 2
    low, high = pl.ds(0, half), pl.ds(half, half)
    plan = [
        (parts[1], cores[0], CORE),
        (parts[3], cores[2], CORE),
        (parts[5], cores[4], CORE),
        (parts[7], cores[6], CORE),
        (parts[2].at[low], sides[0], NEAR),
        (parts[6].at[low], sides[1], NEAR),
        (parts[4].at[high], sides[2], FAR),
        (parts[6].at[high], sides[3], FAR),
        (parts[4].at[low], sides[4], FAR),
        (parts[2].at[high], sides[5], NEAR),
    ]
    return [
        remote(src, dst, sends, recvs, base + place, relation)
        for place, (src, dst, relation) in enumerate(plan)
    ]


def add_into(target, start, other, count):
    def one(i, carry):
        target[start + i] = target[start + i] + other[i]
        return carry

    lax.fori_loop(0, count, one, 0, unroll=8)


def return_finish(parts, sides, back):
    half = parts[0].shape[0] // 2
    back[4].wait_recv()
    add_into(parts[0], 0, sides[0], half)
    back[5].wait_recv()
    add_into(parts[4], 0, sides[1], half)
    back[8].start()
    back[6].wait_recv()
    add_into(parts[0], half, sides[2], half)
    back[7].wait_recv()
    add_into(parts[2], half, sides[3], half)
    back[9].start()
    back[8].wait_recv()
    add_into(parts[0], 0, sides[4], half)
    back[9].wait_recv()
    add_into(parts[0], half, sides[5], half)
    for copy in back:
        copy.wait_send()


GELU_A = 0.7978845608028654
GELU_B = 0.044715


def expert_steps():
    waves = (((0, 1), (0,)), ((2, 3, 4, 5), (2,)), ((6, 7), ()))
    steps = []
    for taken, closed in waves:
        steps += [("F", r) for r in taken] + [("B", r) for r in taken]
        steps += [("U", r) for r in closed] + [("V", r) for r in closed]
    return steps


def expert_kernel(
    cap, depth, tab, gates, m_in, cot_in, near_in, far_in, core_in, win_in, wback_in,
    dm_o, py_o, cy_o, gin_o, gback_o, dg_o, *scratch
):
    sents, slot, width = m_in.shape
    hidden = win_in.shape[1]
    half = sents // 2
    held_m = dict(zip(range(8), scratch[0:8]))
    held_c = dict(zip(range(8), scratch[8:16]))
    sides = scratch[16:22]
    win, wback = scratch[22:24]
    first_part, xs, dys, zs, dus, ys, dms, stage, dg_s, accb, acci = scratch[24:35]
    line_in, line_back, sends, recvs, local, free = scratch[35:]
    parts = {
        0: first_part, 1: held_c[1], 2: held_m[0], 3: held_c[3],
        4: held_c[0], 5: held_c[5], 6: held_c[6], 7: held_c[7],
    }
    cores = {0: held_m[1], 2: held_m[3], 4: held_m[5], 6: held_m[7]}
    sets = {r: r - 2 if r in (4, 5) else r % 2 for r in range(8)}
    me = lax.axis_index("expert")
    z = lax.axis_index("dp")
    tile = min(512, hidden)
    rows = cap * slot
    low, high = pl.ds(0, half), pl.ds(half, half)
    loads = [
        pltpu.make_async_copy(src, dst, local.at[2 + place])
        for place, (src, dst) in enumerate(
            [
                (m_in, held_m[0]),
                (cot_in, held_c[0]),
                (win_in, win),
                (wback_in, wback),
                (core_in, held_c[1]),
                (near_in, held_c[2].at[low]),
                (far_in, held_c[4].at[high]),
            ]
        )
    ]
    for load in loads:
        load.start()
    plane_barrier(depth)
    to_m = gather_copies(held_m[0], held_m, sends, recvs, 0)
    to_c = gather_copies(held_c[0], held_c, sends, recvs, 10)
    back = return_copies(parts, cores, sides, sends, recvs, 20)
    gates_back = {
        r: remote(dg_s.at[r], dg_o.at[me], sends, recvs, 30 + r, r) for r in range(1, 8)
    }
    outputs_back = {
        r: remote(stage, cy_o.at[r // 2], sends, recvs, 38 + r // 2, CORE) for r in (1, 3, 5, 7)
    }
    outputs_here = {
        r: pltpu.make_async_copy(stage, py_o.at[r // 2], local.at[0]) for r in (0, 2, 4, 6)
    }

    def line_first(right, array):
        offset = 1 if right else depth - 1
        s = depth - 1 if right else 0
        source, into = ((win, line_in), (wback, line_back))[array]
        share = source.shape[0] // depth
        here = pl.ds(s * share, share)
        index = 42 + 2 * int(right) + array
        return here, along(source.at[here], into, sends, recvs, index, offset, depth)

    def line_open(array):
        for right in (True, False):

            @pl.when(z == (0 if right else depth - 1))
            def _():
                line_first(right, array)[1].start()

    for load in loads[0:2]:
        load.wait()
    for index in (0, 1, 2, 3, 4):
        to_m[index].start()
    for index in (3, 4):
        to_c[index].start()
    accb[...] = jnp.zeros_like(accb)
    acci[...] = jnp.zeros_like(acci)
    place = lax.broadcasted_iota(jnp.int32, (slot, width), 0)
    for load in loads[2:4]:
        load.wait()

    def before_forward(r):
        if r == 1:
            to_m[2].wait_recv()
        if r == 2:
            to_m[0].wait_recv()
            to_m[5].start()
            to_m[1].wait_recv()
            to_m[6].start()
            for load in loads[5:7]:
                load.wait()
            to_c[5].start()
            to_c[6].start()
            to_m[3].wait_recv()
            to_m[7].start()
            to_m[4].wait_recv()
            to_m[8].start()
        if r == 3:
            to_m[7].wait_recv()
        if r == 5:
            to_m[8].wait_recv()
        if r == 6:
            to_m[5].wait_recv()
            to_m[6].wait_recv()
            to_m[9].start()
        if r == 7:
            to_m[9].wait_recv()
        source = plane_peer(r)

        def fetch(j, carry):
            xs[sets[r], j] = held_m[r][tab[source, 0, j]]
            return carry

        lax.fori_loop(0, cap, fetch, 0, unroll=True)
        if r % 2 == 1:
            pl.semaphore_signal(
                free.at[r // 2], inc=1, device_id=(z, plane_peer(CORE)), device_id_type=MESH_ID
            )

    def after_forward(r):
        source = plane_peer(r)
        if r > 0 and r % 2 == 1:
            outputs_here[r - 1].wait()
        if r > 0 and r % 2 == 0:
            outputs_back[r - 1].wait_send()

        def give(i, carry):
            index = tab[source, 0, 2 * cap + i]
            there = jnp.maximum(index, 0)
            gate = jnp.where(index >= 0, gates[source, 0, there], 0.0)
            stage[i] = (ys[sets[r], there].astype(F32) * gate).astype(BF)
            return carry

        lax.fori_loop(0, sents, give, 0, unroll=8)
        if r % 2 == 0:
            outputs_here[r].start()
        else:
            outputs_back[r].start()

    def before_backward(r):
        if r == 1:
            loads[4].wait()
        if r == 2:
            to_c[3].wait_recv()
            to_c[7].start()
            to_c[4].wait_recv()
            to_c[8].start()
        if r == 3:
            to_c[7].wait_recv()
        if r == 5:
            to_c[8].wait_recv()
        if r == 6:
            to_c[5].wait_recv()
            to_c[6].wait_recv()
            to_c[9].start()
        if r == 7:
            to_c[9].wait_recv()
        source = plane_peer(r)

        def fetch(j, carry):
            index = tab[source, 0, j]
            length = tab[source, 0, cap + j]
            gate = gates[source, 0, j]
            gt = jnp.where(place < length, held_c[r][index].astype(F32), 0.0)
            dys[sets[r], j] = (gt * gate).astype(BF)
            product = ys[sets[r], j].astype(F32) * gt
            total = jnp.sum(jnp.sum(product, axis=0, keepdims=True), axis=1, keepdims=True)
            if r == 0:
                dg_o[me, pl.ds(j, 1)] = jnp.broadcast_to(total, (1, 128))
            else:
                dg_s[r, pl.ds(j, 1)] = jnp.broadcast_to(total, (1, 128))
            return carry

        lax.fori_loop(0, cap, fetch, 0, unroll=True)
        if r > 0:
            gates_back[r].start()

    def after_backward(r):
        source = plane_peer(r)
        if r == 2:
            for copy in to_m[0:5]:
                copy.wait_send()
        if r == 4:
            for copy in to_c[3:5]:
                copy.wait_send()
        if r == 6:
            to_c[9].wait_send()

        def give(i, carry):
            index = tab[source, 0, 2 * cap + i]
            kept = dms[jnp.maximum(index, 0)]
            parts[r][i] = jnp.where(index >= 0, kept, jnp.zeros_like(kept))
            return carry

        lax.fori_loop(0, sents, give, 0, unroll=8)
        if r % 2 == 1:
            pl.semaphore_wait(free.at[r // 2], 1)
            back[r // 2].start()
        if r == 4:
            join(2)
            back[4].start()

    def join(r):
        back[r // 2].wait_recv()
        add_into(parts[r], 0, cores[r], sents)

    def after_back_grad(r):
        if r == 2:
            join(4)
            back[6].start()

    def after_in_grad(r):
        if r == 2:
            join(0)

    tiles = [slice(f * tile, (f + 1) * tile) for f in range(hidden // tile)]

    def forward(spot):
        x = xs[spot].reshape(rows, width)
        here = pl.ds(pl.multiple_of(spot * rows, rows), rows)
        for cols in tiles:
            u = mm(x, win[:, cols])
            square = u * u
            th = jnp.tanh(u * (GELU_A + GELU_A * GELU_B * square))
            cdf = 0.5 + 0.5 * th
            slope = cdf + (0.5 * u) * (1.0 - th * th) * (GELU_A + 3 * GELU_A * GELU_B * square)
            zs[here, cols] = (u * cdf).astype(BF)
            dus[here, cols] = slope.astype(BF)
        ys[spot] = mm(zs[here, :], wback[...]).astype(BF).reshape(cap, slot, width)

    def backward(spot):
        dy = dys[spot].reshape(rows, width)
        here = pl.ds(pl.multiple_of(spot * rows, rows), rows)
        for cols in tiles:
            dz = mm(dy, wback[cols, :], 1, 1)
            dus[here, cols] = (dz * dus[here, cols].astype(F32)).astype(BF)
        dms[...] = mm(dus[here, :], win[...], 1, 1).astype(BF).reshape(cap, slot, width)

    def back_grad(count):
        dy = dys[0:count].reshape(count * rows, width)
        for cols in tiles:
            yield cols, mm(zs[0 : count * rows, cols], dy, 0, 0)

    def in_grad(count):
        x = xs[0:count].reshape(count * rows, width)
        for cols in tiles:
            yield cols, mm(x, dus[0 : count * rows, cols], 0, 0)

    def back_pair(spot):
        for cols, total in back_grad(2):
            accb[cols, :] += total

    def in_pair(spot):
        for cols, total in in_grad(2):
            acci[:, cols] += total

    steps = expert_steps()
    actions = {
        "F": (before_forward, forward, after_forward),
        "B": (before_backward, backward, after_backward),
        "U": (None, back_pair, after_back_grad),
        "V": (None, in_pair, after_in_grad),
    }

    def spot_of(t, kind):
        spot = jnp.int32(0)
        for number, (other, r) in enumerate(steps):
            if other == kind and sets[r]:
                spot = spot + jnp.where(t == number, sets[r], 0)
        return spot

    def step(t, carry):
        for kind, (pre, work, post) in actions.items():
            mine = [number for number, (other, _) in enumerate(steps) if other == kind]
            spans = [n for n in mine if n - 1 not in mine]
            ends = [n for n in mine if n + 1 not in mine]
            inside = functools.reduce(
                jnp.logical_or,
                [jnp.logical_and(t >= a, t <= b) for a, b in zip(spans, ends)],
            )

            @pl.when(inside)
            def _():
                if pre is not None:
                    for number in mine:
                        pl.when(t == number)(functools.partial(pre, steps[number][1]))
                work(spot_of(t, kind))
                for number in mine:
                    pl.when(t == number)(functools.partial(post, steps[number][1]))

        return carry

    lax.fori_loop(0, len(steps), step, 0)
    for cols, total in back_grad(4):
        wback[cols, :] = (accb[cols, :] + total).astype(BF)
        if cols.start == 0:
            join(6)
            back[5].start()
            back[7].start()
    line_open(1)
    for cols, total in in_grad(4):
        win[:, cols] = (acci[:, cols] + total).astype(BF)
    line_open(0)
    return_finish(parts, sides, back)
    kept = pltpu.make_async_copy(parts[0], dm_o, local.at[2])
    kept.start()
    for right in (True, False):

        @pl.when(z == (1 if right else depth - 2))
        def _():
            for array in (1, 0):
                here, copy = line_first(right, array)
                copy.wait_recv()
                source, into = ((win, line_in), (wback, line_back))[array]
                total = source[here, :].astype(F32) + into[...].astype(F32)
                source[here, :] = total.astype(BF)

    stores = [
        pltpu.make_async_copy(win, gin_o, local.at[4]),
        pltpu.make_async_copy(wback, gback_o, local.at[5]),
    ]
    for store in stores:
        store.start()
    for store in stores:
        store.wait()
    kept.wait()
    for right in (True, False):

        @pl.when(z == (0 if right else depth - 1))
        def _():
            for array in (0, 1):
                line_first(right, array)[1].wait_send()

    for r in (1, 3, 5, 7):
        outputs_back[r].wait_recv()
    outputs_back[7].wait_send()
    for r in range(1, 8):
        gates_back[r].wait()
    for index in range(5, 10):
        to_m[index].wait_send()
    for index in range(5, 9):
        to_c[index].wait_send()


def expert_exchange(tab, gates, m, cot, near, far, core, win, wback, cap, depth):
    sents, slot, width = m.shape
    hidden = win.shape[1]
    vm = pl.BlockSpec(memory_space=VM)
    sm = pl.BlockSpec(memory_space=pltpu.SMEM)
    anywhere = pl.BlockSpec(memory_space=pl.ANY)
    shape = jax.ShapeDtypeStruct
    cube = (sents, slot, width)
    taken = (cap, slot, width)
    rows = cap * slot
    return pl.pallas_call(
        functools.partial(expert_kernel, cap, depth),
        in_specs=[sm, sm] + [anywhere] * 7,
        out_specs=[anywhere] * 5 + [vm],
        out_shape=[
            shape(cube, BF),
            shape((4,) + cube, BF),
            shape((4,) + cube, BF),
            shape((width, hidden), BF),
            shape((hidden, width), BF),
            shape((8, cap, 128), F32),
        ],
        scratch_shapes=[VM(cube, BF)] * 16
        + [VM((sents // 2, slot, width), BF)] * 6
        + [VM((width, hidden), BF), VM((hidden, width), BF)]
        + [VM(cube, BF)]
        + [VM((4,) + taken, BF)] * 2
        + [VM((4 * rows, hidden), BF)] * 2
        + [VM((4,) + taken, BF), VM(taken, BF), VM(cube, BF)]
        + [VM((8, cap, 128), F32)]
        + [VM((hidden, width), F32), VM((width, hidden), F32)]
        + [VM((width // depth, hidden), BF), VM((hidden // depth, width), BF)]
        + [
            pltpu.SemaphoreType.DMA((46,)),
            pltpu.SemaphoreType.DMA((46,)),
            pltpu.SemaphoreType.DMA((9,)),
            pltpu.SemaphoreType.REGULAR((4,)),
        ],
        compiler_params=pltpu.CompilerParams(
            collective_id=1, has_side_effects=True, vmem_limit_bytes=63 * 2**20
        ),
        cost_estimate=pl.CostEstimate(
            flops=12 * 8 * rows * width * hidden, bytes_accessed=40 * 2**20, transcendentals=0
        ),
    )(tab, gates, m, cot, near, far, core, win, wback)


class Reduction:
    def __init__(self, depth, value, wide, core_r, plane_r, line_s, line_r, final, sems, base):
        self.depth, self.value, self.wide, self.final = depth, value, wide, final
        self.core_r, self.plane_r, self.line_s, self.line_r = core_r, plane_r, line_s, line_r
        sends, recvs = sems
        me = lax.axis_index("expert")
        z = lax.axis_index("dp")
        core = me % 2
        self.half = value.shape[0] // 2
        self.quarter = self.half // 4
        self.share = self.quarter // depth
        self.mine = core * self.half
        self.other = (1 - core) * self.half
        self.block = self.mine + (me // 2) * self.quarter
        self.own = self.block + z * self.share
        self.to_core = remote(wide, core_r, sends, recvs, base, CORE)
        self.to_plane = []
        self.from_plane = []
        for place, relation in enumerate((2, 4, 6)):
            rows = pl.ds((plane_peer(relation) // 2) * self.quarter, self.quarter)
            self.to_plane.append(
                remote(wide.at[rows], plane_r.at[place], sends, recvs, base + 1 + place, relation)
            )
        self.to_line = []
        for offset in range(1, depth):
            rows = pl.ds(line_peer(offset, depth) * self.share, self.share)
            self.to_line.append(
                along(
                    line_s.at[rows], line_r.at[offset - 1], sends, recvs, base + 3 + offset,
                    offset, depth,
                )
            )
        after = base + 3 + depth
        rows = final.at[pl.ds(self.own, self.share)]
        self.back_line = [
            along(rows, rows, sends, recvs, after + offset - 1, offset, depth)
            for offset in range(1, depth)
        ]
        after = after + depth - 1
        rows = final.at[pl.ds(self.block, self.quarter)]
        self.back_plane = [
            remote(rows, rows, sends, recvs, after + place, relation)
            for place, relation in enumerate((2, 4, 6))
        ]
        rows = final.at[pl.ds(self.mine, self.half)]
        self.back_core = remote(rows, rows, sends, recvs, after + 3, CORE)

    @staticmethod
    def semaphores(depth):
        return 2 * depth + 6

    def send_core(self):
        self.wide[...] = self.value[pl.ds(self.other, self.half), :].astype(BF)
        self.to_core.start()

    def send_plane(self):
        self.to_core.wait()
        rows = pl.ds(self.mine, self.half)
        total = self.value[rows, :] + self.core_r[...].astype(F32)
        self.value[rows, :] = total
        self.wide[...] = total.astype(BF)
        for copy in self.to_plane:
            copy.start()

    def send_line(self):
        for copy in self.to_plane:
            copy.wait()
        rows = pl.ds(self.block, self.quarter)
        total = self.value[rows, :]
        for place in range(3):
            total = total + self.plane_r[place].astype(F32)
        self.value[rows, :] = total
        self.line_s[...] = total.astype(BF)
        for copy in self.to_line:
            copy.start()

    def send_back_line(self):
        for copy in self.to_line:
            copy.wait()
        rows = pl.ds(self.own, self.share)
        total = self.value[rows, :]
        for offset in range(1, self.depth):
            total = total + self.line_r[offset - 1].astype(F32)
        self.final[rows, :] = total.astype(BF)
        for copy in self.back_line:
            copy.start()

    def send_back_plane(self):
        for copy in self.back_line:
            copy.wait()
        for copy in self.back_plane:
            copy.start()

    def send_back_core(self):
        for copy in self.back_plane:
            copy.wait()
        self.back_core.start()

    def finish(self):
        self.back_core.wait()


class SmallSum:
    @staticmethod
    def semaphores(depth):
        return 4 + depth

    def __init__(self, depth, value, core_r, plane, line, sems, base):
        sends, recvs = sems
        self.value, self.core_r, self.plane, self.line = value, core_r, plane, line
        self.spot = lax.axis_index("expert") // 2
        self.z = lax.axis_index("dp")
        self.to_core = remote(value, core_r, sends, recvs, base, CORE)
        spot = plane.at[self.spot]
        self.to_plane = [
            remote(spot, spot, sends, recvs, base + 1 + place, relation)
            for place, relation in enumerate((2, 4, 6))
        ]
        spot = line.at[self.z]
        self.to_line = [
            along(spot, spot, sends, recvs, base + 3 + offset, offset, depth)
            for offset in range(1, depth)
        ]

    def send_core(self):
        self.to_core.start()

    def send_plane(self):
        self.to_core.wait()
        self.plane[self.spot] = self.value[...] + self.core_r[...]
        for copy in self.to_plane:
            copy.start()

    def send_line(self):
        for copy in self.to_plane:
            copy.wait()
        total = self.plane[0]
        for place in range(1, 4):
            total = total + self.plane[place]
        self.line[self.z] = total
        for copy in self.to_line:
            copy.start()

    def finish(self, out):
        for copy in self.to_line:
            copy.wait()
        total = self.line[0]
        for place in range(1, self.line.shape[0]):
            total = total + self.line[place]
        out[...] = total


def backward_kernel(
    heads, depth, len_ref, g1, g2, attn_sum, plan, tasks, lengths, dots,
    x_in, cot_in, dm_in, h_in, act_in, q_in, k_in, v_in, ctx_in, p_in,
    wq_in, wk_in, wv_in, wo_in, py, cy, gin, gback,
    ig_o, out_o, gq_o, gk_o, gv_o, go_o, gin_o, gback_o, small_o, *scratch
):
    inputs = (
        x_in, cot_in, dm_in, h_in, act_in, q_in, k_in, v_in, ctx_in, p_in,
        wq_in, wk_in, wv_in, wo_in, gin, gback,
    )
    held = scratch[0:16]
    (
        x_ref, cot_ref, dm_ref, h_ref, act, q, k, v, ctx, p_ref, wq, wk, wv, wo, gin_s, gback_s,
    ) = held
    parts = dict(zip((0, 2, 4, 6), scratch[16:20]))
    cores = dict(zip((0, 2, 4, 6), scratch[20:24]))
    sides = scratch[24:30]
    dh_s, da_s, dctx_s, dq_s, dk_s, dv_s = scratch[30:36]
    red = scratch[36:57]
    line_in, line_back, extra_in, extra_back = scratch[57:61]
    small, small_core, small_plane, small_line = scratch[61:65]
    sends, recvs, local = scratch[65:]
    sems = (sends, recvs)
    sents, slot, width = x_ref.shape
    head = width // heads
    group = max(1, min(heads, 256 // head))
    span = group * head
    scale = head ** -0.5
    count = 4 if sents % 4 == 0 else 1
    rows_per = count * slot
    half = sents // 2
    z = lax.axis_index("dp")

    loads = {
        id(ref): pltpu.make_async_copy(source, ref, local.at[place])
        for place, (source, ref) in enumerate(zip(inputs, held))
    }
    for place, r in enumerate((0, 2, 4, 6)):
        loads[id(parts[r])] = pltpu.make_async_copy(
            py.at[r // 2], parts[r], local.at[16 + place]
        )
        loads[id(cores[r])] = pltpu.make_async_copy(
            cy.at[r // 2], cores[r], local.at[20 + place]
        )

    def begin(*refs):
        for ref in refs:
            loads[id(ref)].start()

    def ready(*refs):
        for ref in refs:
            loads[id(ref)].wait()

    begin(gin_s, gback_s, h_ref, dm_ref, cot_ref, wo, parts[6], cores[6], ctx)
    begin(parts[2], cores[2], parts[4], cores[4], q, k, v, p_ref, act, parts[0], cores[0])
    begin(wq, wk, wv, x_ref)
    plane_barrier(depth)

    all_parts = {r: parts[r - r % 2] for r in range(8)}
    back = return_copies(all_parts, cores, sides, sends, recvs, 0)

    base = 10
    in_rows = gin_s.shape[0] // depth
    back_rows = gback_s.shape[0] // depth

    def line_piece(s, array, right, last):
        offset = 1 if right else depth - 1
        index = base + (0 if right else 2 * depth) + 2 * s + array
        share, source = ((in_rows, gin_s), (back_rows, gback_s))[array]
        into = (line_in, line_back)[array].at[s]
        if last and not right:
            into = (extra_in, extra_back)[array]
        here = source.at[pl.ds(s * share, share)]
        return along(here, into, sends, recvs, index, offset, depth)

    def add_piece(s, array):
        share, source = ((in_rows, gin_s), (back_rows, gback_s))[array]
        other = (line_in, line_back)[array]
        here = pl.ds(s * share, share)
        source[here, :] = (source[here, :].astype(F32) + other[s].astype(F32)).astype(BF)

    def pieces(right):
        order = range(depth - 1, 0, -1) if right else range(depth - 1)
        return [(s, array) for s in order for array in (0, 1)]

    def start_piece(s, array, right):
        if right:
            line_piece(s, array, True, False).start()
            return
        near = z == s + 1

        @pl.when(near)
        def _():
            line_piece(s, array, False, True).start()

        @pl.when(jnp.logical_not(near))
        def _():
            line_piece(s, array, False, False).start()

    def line_service(t, ahead=0):
        for right in (True, False):
            every = pieces(right)
            edge = 0 if right else depth - 1
            opening = range(2, 3 + ahead) if t == 0 else range(t + ahead + 2, t + ahead + 3)

            @pl.when(z == edge)
            def _():
                for number in opening:
                    if number < len(every):
                        start_piece(*every[number], right)

            for number, (s, array) in enumerate(every):
                away = s if right else depth - 1 - s
                for hops in range(1, away):
                    given = hops == 1 and number < 2
                    if t != (0 if given else number + hops - 1):
                        continue

                    @pl.when(z == (hops if right else depth - 1 - hops))
                    def _():
                        if not given:
                            line_piece(s, array, right, False).wait_recv()
                            add_piece(s, array)
                        start_piece(s, array, right)

    def line_end():
        for s in range(depth):

            @pl.when(z == s)
            def _():
                here = pl.ds(s * in_rows, in_rows)
                there = pl.ds(s * back_rows, back_rows)
                gin_o[...] = gin_s[here, :].astype(F32)
                gback_o[...] = gback_s[there, :].astype(F32)
                if s > 0:
                    for array in (0, 1):
                        line_piece(s, array, True, True).wait_recv()
                    gin_o[...] += line_in[s].astype(F32)
                    gback_o[...] += line_back[s].astype(F32)
                if s < depth - 1:
                    for array in (0, 1):
                        line_piece(s, array, False, True).wait_recv()
                    gin_o[...] += extra_in[...].astype(F32)
                    gback_o[...] += extra_back[...].astype(F32)

        for s in range(depth):
            for array in (0, 1):
                first_right = 1 if s == depth - 1 else 0
                first_left = depth - 2 if s == 0 else depth - 1

                @pl.when(jnp.logical_and(z < s, z >= first_right))
                def _():
                    line_piece(s, array, True, False).wait_send()

                @pl.when(jnp.logical_and(z > s, z <= first_left))
                def _():
                    line_piece(s, array, False, False).wait_send()

    base_red = base + 4 * depth
    per = Reduction.semaphores(depth)
    red_o, red_0, red_1 = [
        Reduction(depth, *red[7 * place : 7 * place + 7], sems, base_red + place * per)
        for place in range(3)
    ]
    sums = SmallSum(
        depth, small, small_core, small_plane, small_line, sems, base_red + 3 * per
    )

    small[...] = jnp.zeros_like(small)
    small[4:5] = attn_sum[...]
    small[7:8, 0:sents] = lengths[...].astype(F32)
    experts = plan.shape[0] // 3
    chunk_place = lax.broadcasted_iota(jnp.int32, (slot, width), 0)

    def masked(ref, c):
        return jnp.concatenate(
            [
                jnp.where(
                    chunk_place < len_ref[c * count + s], ref[c * count + s].astype(F32), 0.0
                )
                for s in range(count)
            ],
            axis=0,
        )

    def flat(ref, c):
        block = ref[pl.ds(c * count, count)]
        return block.astype(F32).reshape(rows_per, width)

    def first(c, carry):
        rows = pl.ds(pl.multiple_of(c * rows_per, rows_per), rows_per)
        normed2, inverse2 = normalize(h_ref[rows, :])
        dm = flat(dm_ref, c)
        dhidden = masked(cot_ref, c) + layer_norm_pull(dm, normed2, inverse2, g2[...])
        small[2:3] += row_sum(dm * normed2, width)
        small[3:4] += row_sum(dm, width)
        dh_s[rows, :] = dhidden
        dattn = dhidden.astype(BF)
        da_s[rows, :] = dattn
        dctx_s[rows, :] = mm(dattn, wo[...], 1, 1).astype(BF)
        return carry

    mask = block_diagonal(group, slot, head)

    def pull(part, into):
        cols = slice(part * span, (part + 1) * span)

        def one(c, carry):
            for s in range(count):
                at = c * count + s
                rows = pl.ds(pl.multiple_of(at * slot, slot), slot)
                dq_s[rows, cols], dk_s[rows, cols], dv_s[rows, cols] = attention_pull(
                    dctx_s[rows, cols], q[rows, cols], k[rows, cols], v[rows, cols],
                    p_ref[at, part], mask, slot, group, scale,
                )
            return carry

        lax.fori_loop(0, sents // count, one, 0)
        into.value[0:width, :] = mm(act[...], dq_s[:, cols], 0, 0)
        into.value[width : 2 * width, :] = mm(act[...], dk_s[:, cols], 0, 0)
        into.value[2 * width : 3 * width, :] = mm(act[...], dv_s[:, cols], 0, 0)
        into.send_core()

    def returned(r):
        ready(parts[r], cores[r])
        add_into(parts[r], 0, cores[r], sents)

    def last(c, carry):
        rows = pl.ds(pl.multiple_of(c * rows_per, rows_per), rows_per)
        dact = (
            mm(dq_s[rows, :], wq[...], 1, 1)
            + mm(dk_s[rows, :], wk[...], 1, 1)
            + mm(dv_s[rows, :], wv[...], 1, 1)
        )
        normed1, inverse1 = normalize(flat(x_ref, c))
        small[0:1] += row_sum(dact * normed1, width)
        small[1:2] += row_sum(dact, width)
        dx = dh_s[rows, :] + layer_norm_pull(dact, normed1, inverse1, g1[...])
        ig_o[pl.ds(c * count, count)] = dx.astype(BF).reshape(count, slot, width)
        return carry

    def outcome(low, side):
        def one(i, carry):
            at = low + i
            valid = chunk_place < len_ref[at]
            moe = jnp.where(valid, parts[0][at].astype(F32) + side[i].astype(F32), 0.0)
            rows = pl.ds(pl.multiple_of(at * slot, slot), slot)
            total = jnp.where(valid, h_ref[rows, :], 0.0) + moe
            out_o[at] = total.astype(BF)
            small[5:6] += row_sum(total * total, width)
            small[6:7] += row_sum(moe * moe, width)
            return carry

        lax.fori_loop(0, half, one, 0)

    def gate_gradient():
        hit = plan[0:experts] > 0.5
        place = plan[experts : 2 * experts]
        gate = plan[2 * experts : 3 * experts]
        taken = jnp.zeros(gate.shape, F32)
        for j in range(dots.shape[1]):
            taken = taken + jnp.where(place == float(j), dots[:, j, 0:sents], 0.0)
        inner = jnp.sum(gate * taken, axis=0, keepdims=True)
        dlogit = jnp.where(hit, gate * (taken - inner), 0.0)
        hot = lax.broadcasted_iota(jnp.int32, (slot, sents), 0) == tasks[...]
        small[8 : 8 + experts, 0:slot] = lax.dot_general(
            dlogit, hot.astype(F32), (((1,), (1,)), ((), ())),
            precision=lax.Precision.HIGHEST, preferred_element_type=F32,
        )

    ready(gin_s, gback_s)
    line_service(0)
    returned(6)
    back[5].start()
    back[7].start()
    ready(h_ref, dm_ref, cot_ref, wo)
    lax.fori_loop(0, sents // count, first, 0)
    ready(ctx)
    red_o.value[...] = mm(ctx[...], da_s[...], 0, 0)
    red_o.send_core()
    returned(2)
    returned(4)
    ready(q, k, v, p_ref, act)
    pull(0, red_0)
    red_o.send_plane()
    back[4].start()
    back[6].start()
    line_service(1)
    back[5].wait_recv()
    add_into(parts[4], 0, sides[1], half)
    back[7].wait_recv()
    add_into(parts[2], half, sides[3], half)
    pull(1, red_1)
    red_0.send_plane()
    back[8].start()
    back[9].start()
    red_o.send_line()
    line_service(2)
    ready(wq, wk, wv, x_ref)
    lax.fori_loop(0, sents // count, last, 0)
    red_1.send_plane()
    red_o.send_back_line()
    gate_gradient()
    returned(0)
    red_0.send_line()
    line_service(3)
    back[4].wait_recv()
    add_into(parts[0], 0, sides[0], half)
    back[6].wait_recv()
    add_into(parts[0], half, sides[2], half)
    red_o.send_back_plane()
    red_0.send_back_line()
    red_1.send_line()
    back[8].wait_recv()
    outcome(0, sides[4])
    back[9].wait_recv()
    outcome(half, sides[5])
    sums.send_core()
    red_o.send_back_core()
    red_0.send_back_plane()
    red_1.send_back_line()
    sums.send_plane()
    red_1.send_back_plane()
    red_0.send_back_core()
    sums.send_line()
    red_1.send_back_core()
    red_o.finish()
    go_o[...] = red_o.final[...]
    red_0.finish()

    def share(red, low):
        for place, ref in enumerate((gq_o, gk_o, gv_o)):
            ref[:, low : low + red.final.shape[1]] = red.final[
                place * width : (place + 1) * width, :
            ]

    share(red_0, 0)
    sums.finish(small_o)
    red_1.finish()
    share(red_1, span)
    line_end()
    for copy in back[4:]:
        copy.wait_send()


def backward_exchange(
    depth, lengths, tokens, cot, dm, hidden, act, q, k, v, ctx, prob, wq, wk, wv, wo, g1, g2,
    attn_sum, plan, tasks, dots, py, cy, gin, gback, heads,
):
    sents, slot, width = tokens.shape
    total = sents * slot
    small = jax.ShapeDtypeStruct((16, width), F32)
    vm = pl.BlockSpec(memory_space=VM)
    anywhere = pl.BlockSpec(memory_space=pl.ANY)
    shape = jax.ShapeDtypeStruct
    cube = (sents, slot, width)
    head = width // heads
    span = max(1, min(heads, 256 // head)) * head
    pieces = [(width, width), (3 * width, span), (3 * width, width - span)]
    red = []
    for rows, cols in pieces:
        red += [
            VM((rows, cols), F32),
            VM((rows // 2, cols), BF),
            VM((rows // 2, cols), BF),
            VM((3, rows // 8, cols), BF),
            VM((rows // 8, cols), BF),
            VM((depth - 1, rows // 8 // depth, cols), BF),
            VM((rows, cols), BF),
        ]
    in_share = (gin.shape[0] // depth, gin.shape[1])
    back_share = (gback.shape[0] // depth, gback.shape[1])
    semaphores = 10 + 4 * depth + 3 * Reduction.semaphores(depth) + SmallSum.semaphores(depth)
    large = (
        tokens, cot, dm, hidden, act, q, k, v, ctx, prob, wq, wk, wv, wo, py, cy, gin, gback,
    )
    return pl.pallas_call(
        functools.partial(backward_kernel, heads, depth),
        in_specs=[pl.BlockSpec(memory_space=pltpu.SMEM)] + [vm] * 7 + [anywhere] * len(large),
        out_specs=[vm] * 9,
        out_shape=[shape(cube, BF), shape(cube, BF)]
        + [shape((width, width), BF)] * 4
        + [shape(in_share, F32), shape(back_share, F32), shape(small.shape, F32)],
        scratch_shapes=[VM(ref.shape, ref.dtype) for ref in large[:14] + large[16:]]
        + [VM(cube, BF)] * 8
        + [VM((sents // 2, slot, width), BF)] * 6
        + [VM((total, width), F32)]
        + [VM((total, width), BF)] * 5
        + red
        + [VM((depth,) + in_share, BF), VM((depth,) + back_share, BF)]
        + [VM(in_share, BF), VM(back_share, BF)]
        + [VM(small.shape, F32)] * 2
        + [VM((4,) + small.shape, F32), VM((depth,) + small.shape, F32)]
        + [
            pltpu.SemaphoreType.DMA((semaphores,)),
            pltpu.SemaphoreType.DMA((semaphores,)),
            pltpu.SemaphoreType.DMA((24,)),
        ],
        compiler_params=pltpu.CompilerParams(
            collective_id=2, has_side_effects=True, vmem_limit_bytes=63 * 2**20
        ),
        cost_estimate=pl.CostEstimate(
            flops=16 * total * width * width, bytes_accessed=40 * 2**20, transcendentals=0
        ),
    )(
        lengths, g1[None], g2[None], attn_sum, plan, tasks[None], lengths[None], dots, *large
    )


def outputs_kernel(
    out_in, ig_in, gin_in, gback_in, q_in, k_in, v_in, o_in, small,
    out_o, ig_o, gin_o, gback_o, q_o, k_o, v_o, o_o, l1g, l1b, l2g, l2b, table_o, rms_o,
    low, wide, cubes, share_in, share_back, sems,
):
    fetches = [
        pltpu.make_async_copy(src, low.at[place], sems.at[place])
        for place, src in enumerate((q_in, k_in, v_in, o_in))
    ]
    stores = [
        pltpu.make_async_copy(wide.at[place], dst, sems.at[4 + place])
        for place, dst in enumerate((q_o, k_o, v_o, o_o))
    ]
    moves = [
        (pltpu.make_async_copy(src, held, sems.at[8 + place]),
         pltpu.make_async_copy(held, dst, sems.at[12 + place]))
        for place, (src, held, dst) in enumerate(
            [
                (out_in, cubes.at[0], out_o),
                (ig_in, cubes.at[1], ig_o),
                (gin_in, share_in, gin_o),
                (gback_in, share_back, gback_o),
            ]
        )
    ]
    for fetch in fetches:
        fetch.start()
    for enter, _ in moves:
        enter.start()
    width = small.shape[1]
    for row, ref in enumerate((l1g, l1b, l2g, l2b)):
        ref[...] = small[row : row + 1]
    table_o[...] = small[8 : 8 + table_o.shape[0], 0 : table_o.shape[1]]
    sums = jnp.sum(small[4:8], axis=1, keepdims=True)
    ratio = jnp.sqrt(sums / (sums[3:4] * width))
    lane = lax.broadcasted_iota(jnp.int32, (1, 3), 1)
    pair = jnp.where(lane == 1, ratio[0:1], ratio[2:3])
    rms_o[...] = jnp.where(lane == 0, ratio[1:2], pair)
    for place in range(4):
        fetches[place].wait()
        wide[place] = low[place].astype(F32)
        stores[place].start()
    for enter, leave in moves:
        enter.wait()
        leave.start()
    for store in stores:
        store.wait()
    for _, leave in moves:
        leave.wait()


def place_outputs(out, ig, gin, gback, q, k, v, o, small, experts, ntasks):
    width = small.shape[1]
    vm = pl.BlockSpec(memory_space=VM)
    anywhere = pl.BlockSpec(memory_space=pl.ANY)
    shape = jax.ShapeDtypeStruct
    return pl.pallas_call(
        outputs_kernel,
        in_specs=[anywhere] * 8 + [vm],
        out_specs=[anywhere] * 8 + [vm] * 6,
        out_shape=[shape(a.shape, a.dtype) for a in (out, ig, gin, gback)]
        + [shape(q.shape, F32)] * 4
        + [shape((1, width), F32)] * 4
        + [shape((experts, ntasks), F32), shape((1, 3), F32)],
        scratch_shapes=[
            VM((4,) + q.shape, BF),
            VM((4,) + q.shape, F32),
            VM((2,) + out.shape, BF),
            VM(gin.shape, F32),
            VM(gback.shape, F32),
            pltpu.SemaphoreType.DMA((16,)),
        ],
        compiler_params=pltpu.CompilerParams(vmem_limit_bytes=60 * 2**20),
    )(out, ig, gin, gback, q, k, v, o, small)


def local(
    tokens,
    lengths,
    tasks,
    routes,
    gate_table,
    ln1_gain,
    ln1_bias,
    ln2_gain,
    ln2_bias,
    w_query,
    w_key,
    w_value,
    w_out,
    w_in,
    w_back,
    cotangent,
):
    sents, slot, width = tokens.shape
    heads = HEADS
    head = width // heads
    experts = gate_table.shape[1]
    ntasks = routes.shape[0]
    capacity = max(1, 4 * sents // experts)
    scale = 1.0 / jnp.sqrt(jnp.float32(head))
    task_hot = (tasks[:, None] == jnp.arange(ntasks)[None, :]).astype(jnp.int32)
    chosen = jnp.sum(task_hot[:, :, None] * routes[None, :, :], axis=1)
    flat = chosen.reshape(-1)
    order = jnp.arange(2 * sents)
    earlier = (flat[:, None] == flat[None, :]) & (order[None, :] < order[:, None])
    rank = jnp.sum(earlier.astype(jnp.int32), axis=1)
    slot_id = flat * capacity + rank
    placed = rank < capacity
    dispatch = (
        (jnp.arange(experts * capacity)[:, None] == slot_id[None, :]) & placed[None, :]
    ).astype(jnp.bfloat16)
    collect = dispatch.T
    expert_hot = (chosen[:, :, None] == jnp.arange(experts)[None, None, :]).astype(jnp.float32)
    valid = (jnp.arange(slot)[None, :] < lengths[:, None]).astype(jnp.float32)
    keymask = valid[:, None, None, :] > 0.5
    mask3 = valid[:, :, None]
    xfull = tokens.astype(jnp.float32)
    normed1, inverse1 = normalize(xfull)
    act = (normed1 * ln1_gain + ln1_bias).astype(jnp.bfloat16).reshape(-1, width)
    query = project(act, w_query).astype(jnp.bfloat16).reshape(sents, slot, heads, head)
    keyed = project(act, w_key).astype(jnp.bfloat16).reshape(sents, slot, heads, head)
    valued = project(act, w_value).astype(jnp.bfloat16).reshape(sents, slot, heads, head)

    def scores_of(qpart, kpart):
        raw = (
            jnp.einsum("sqhd,skhd->shqk", qpart, kpart, preferred_element_type=jnp.float32) * scale
        )
        return jnp.where(keymask, raw, -1000000000.0)

    scores = scores_of(query, keyed)
    peak = jnp.max(scores, axis=-1, keepdims=True)
    logsum = peak + jnp.log(jnp.sum(jnp.exp(scores - peak), axis=-1, keepdims=True))
    prob_low = jnp.exp(scores - logsum).astype(jnp.bfloat16)
    context = jnp.einsum("shqk,skhd->sqhd", prob_low, valued, preferred_element_type=jnp.float32)
    context = context.astype(jnp.bfloat16).reshape(-1, width)
    attention_block = project(context, w_out).reshape(sents, slot, width)
    hidden_res = xfull + attention_block
    normed2, inverse2 = normalize(hidden_res)
    mixed = (normed2 * ln2_gain + ln2_bias).astype(jnp.bfloat16)
    table_rows = jnp.dot(task_hot.astype(jnp.float32), gate_table, precision=lax.Precision.HIGHEST)
    picked = jnp.sum(expert_hot * table_rows[:, None, :], axis=-1)
    gate_values = jax.nn.softmax(picked, axis=-1)
    grad_total = cotangent.astype(jnp.float32) * mask3
    copies = jnp.broadcast_to(mixed[:, None], (sents, 2, slot, width)).reshape(
        2 * sents, slot * width
    )
    outgoing = (
        project(dispatch, copies).astype(jnp.bfloat16).reshape(experts, capacity, slot, width)
    )
    dycopy = (
        (gate_values[:, :, None, None] * grad_total[:, None])
        .astype(jnp.bfloat16)
        .reshape(2 * sents, slot * width)
    )
    grad_out = (
        project(dispatch, dycopy).astype(jnp.bfloat16).reshape(experts, capacity, slot, width)
    )
    incoming = lax.all_to_all(outgoing, "expert", split_axis=0, concat_axis=0, tiled=True).reshape(
        -1, width
    )
    pre_act, active, produced = expert_forward(incoming, w_in[0], w_back[0])
    returned = lax.all_to_all(
        produced.reshape(experts, capacity, slot, width),
        "expert",
        split_axis=0,
        concat_axis=0,
        tiled=True,
    )
    grad_in = lax.all_to_all(grad_out, "expert", split_axis=0, concat_axis=0, tiled=True).reshape(
        -1, width
    )
    in_local, back_local, dincoming = expert_backward(
        incoming, pre_act, active, grad_in, w_in[0], w_back[0]
    )
    grad_back = lax.all_to_all(
        dincoming.reshape(experts, capacity, slot, width),
        "expert",
        split_axis=0,
        concat_axis=0,
        tiled=True,
    )
    ycopy = project(collect, returned.reshape(experts * capacity, slot * width)).reshape(
        sents, 2, slot, width
    )
    expert_mixture = jnp.sum(gate_values[:, :, None, None] * ycopy, axis=1)
    total = mask3 * (hidden_res + expert_mixture)
    output = total.astype(jnp.bfloat16)
    stats_local = jnp.stack(
        [
            jnp.sum(total * total),
            jnp.sum(mask3 * attention_block * attention_block),
            jnp.sum(mask3 * expert_mixture * expert_mixture),
            jnp.sum(valid),
        ]
    )
    stat_totals = lax.psum(stats_local, ("dp", "expert"))
    gate_dot = jnp.sum(ycopy * grad_total[:, None], axis=(2, 3))
    dpicked = gate_values * (gate_dot - jnp.sum(gate_values * gate_dot, axis=-1, keepdims=True))
    dlogits = jnp.sum(expert_hot * dpicked[:, :, None], axis=1)
    table_grad = jnp.dot(task_hot.T.astype(jnp.float32), dlogits, precision=lax.Precision.HIGHEST)
    dmixed = project(collect, grad_back.reshape(experts * capacity, slot * width)).reshape(
        sents, 2, slot, width
    )
    dmixed = jnp.sum(dmixed, axis=1)
    dres2, gain2_grad, bias2_grad = norm_backward(dmixed, normed2, inverse2, ln2_gain)
    dhidden = grad_total + dres2
    dattn = dhidden.astype(jnp.bfloat16).reshape(-1, width)
    wout_grad = project(context.T, dattn)
    dcontext = project(dattn, w_out.T).astype(jnp.bfloat16).reshape(sents, slot, heads, head)
    again = jnp.exp(scores_of(query, keyed) - logsum)
    dprob = jnp.einsum("sqhd,skhd->shqk", dcontext, valued, preferred_element_type=jnp.float32)
    dscores = (again * (dprob - jnp.sum(dprob * again, axis=-1, keepdims=True))).astype(
        jnp.bfloat16
    )
    dquery = (
        jnp.einsum("shqk,skhd->sqhd", dscores, keyed, preferred_element_type=jnp.float32) * scale
    )
    dkeyed = (
        jnp.einsum("shqk,sqhd->skhd", dscores, query, preferred_element_type=jnp.float32) * scale
    )
    dvalued = jnp.einsum("shqk,sqhd->skhd", prob_low, dcontext, preferred_element_type=jnp.float32)
    dquery = dquery.astype(jnp.bfloat16).reshape(-1, width)
    dkeyed = dkeyed.astype(jnp.bfloat16).reshape(-1, width)
    dvalued = dvalued.astype(jnp.bfloat16).reshape(-1, width)
    wq_grad = project(act.T, dquery)
    wk_grad = project(act.T, dkeyed)
    wv_grad = project(act.T, dvalued)
    dact = project(dquery, w_query.T) + project(dkeyed, w_key.T) + project(dvalued, w_value.T)
    dres1, gain1_grad, bias1_grad = norm_backward(
        dact.reshape(sents, slot, width), normed1, inverse1, ln1_gain
    )
    input_grad = (dhidden + dres1).astype(jnp.bfloat16)
    members = (
        wq_grad,
        wk_grad,
        wv_grad,
        wout_grad,
        gain1_grad,
        bias1_grad,
        gain2_grad,
        bias2_grad,
        table_grad,
    )
    members = members + ()
    summed = lax.psum(members, ("dp", "expert"))
    rms = jnp.sqrt(stat_totals[0:3] / (stat_totals[3] * width))
    in_share, back_share = (
        lax.psum_scatter(
            in_local.astype(jnp.bfloat16), "dp", scatter_dimension=0, tiled=True
        ).astype(jnp.float32),
        lax.psum_scatter(
            back_local.astype(jnp.bfloat16), "dp", scatter_dimension=0, tiled=True
        ).astype(jnp.float32),
    )
    return (
        output,
        input_grad,
        summed[8],
        summed[4],
        summed[5],
        summed[6],
        summed[7],
        summed[0],
        summed[1],
        summed[2],
        summed[3],
        in_share[None],
        back_share[None],
        rms,
    )


def local_plane(
    depth,
    tokens,
    lengths,
    tasks,
    routes,
    gate_table,
    ln1_gain,
    ln1_bias,
    ln2_gain,
    ln2_bias,
    w_query,
    w_key,
    w_value,
    w_out,
    w_in,
    w_back,
    cotangent,
):
    experts = gate_table.shape[1]
    sents, slot, width = tokens.shape
    heads = HEADS
    capacity = max(1, 4 * sents // experts)
    (
        act, query, keyed, valued, context, prob, hidden, mixed, attn_sum, plan, places,
        gate_slots, near, far, core,
    ) = attention_forward(
        tokens, lengths, w_query, w_key, w_value, w_out, ln1_gain, ln1_bias, ln2_gain, ln2_bias,
        tasks, routes.T, gate_table.T, cotangent, heads, capacity,
    )
    dmixed, parts_back, cores_back, in_local, back_local, slot_dots = expert_exchange(
        places, gate_slots, mixed, cotangent, near, far, core, w_in[0], w_back[0], capacity, depth
    )
    input_grad, output, sum_q, sum_k, sum_v, sum_o, in_share, back_share, small = (
        backward_exchange(
            depth, lengths, tokens, cotangent, dmixed, hidden, act, query, keyed, valued,
            context, prob, w_query, w_key, w_value, w_out, ln1_gain, ln2_gain, attn_sum, plan,
            tasks, slot_dots, parts_back, cores_back, in_local, back_local, heads,
        )
    )
    (
        output, input_grad, in_share, back_share, grad_q, grad_k, grad_v, grad_o,
        gain1, bias1, gain2, bias2, table_grad, rms,
    ) = place_outputs(
        output, input_grad, in_share, back_share, sum_q, sum_k, sum_v, sum_o, small,
        experts, gate_table.shape[0],
    )
    return (
        output,
        input_grad,
        table_grad.T,
        gain1.reshape(-1),
        bias1.reshape(-1),
        gain2.reshape(-1),
        bias2.reshape(-1),
        grad_q,
        grad_k,
        grad_v,
        grad_o,
        in_share[None],
        back_share[None],
        rms.reshape(-1),
    )


def solution(mesh):
    in_specs = (
        P(("dp", "expert"), None, None),
        P(("dp", "expert")),
        P(("dp", "expert")),
        P(),
        P(),
        P(),
        P(),
        P(),
        P(),
        P(),
        P(),
        P(),
        P(),
        P("expert", None, None),
        P("expert", None, None),
        P(("dp", "expert"), None, None),
    )
    out_specs = (
        P(("dp", "expert"), None, None),
        P(("dp", "expert"), None, None),
        P(),
        P(),
        P(),
        P(),
        P(),
        P(),
        P(),
        P(),
        P(),
        P("expert", "dp", None),
        P("expert", "dp", None),
        P(),
    )
    plane = dict(mesh.shape)["expert"]
    depth = dict(mesh.shape)["dp"]
    cube = plane == 2 * 2 * 2 and depth > 3
    body = functools.partial(local_plane, depth) if cube else local
    return jax.shard_map(body, mesh=mesh, in_specs=in_specs, out_specs=out_specs, check_vma=False)
```

```python
import functools

import jax
import jax.numpy as jnp
from jax import lax
from jax.experimental import pallas as pl
from jax.experimental.pallas import tpu as pltpu
from jax.sharding import PartitionSpec as P

HEADS = 8


def normalize(value):
    centered = value - jnp.mean(value, axis=-1, keepdims=True)
    variance = jnp.mean(centered * centered, axis=-1, keepdims=True)
    inverse = lax.rsqrt(variance + 1e-05)
    return (centered * inverse, inverse)


def norm_backward(grad, normed, inverse, gain):
    scaled = grad * gain
    inner = scaled - jnp.mean(scaled, axis=-1, keepdims=True)
    inner = inner - normed * jnp.mean(scaled * normed, axis=-1, keepdims=True)
    return (inverse * inner, jnp.sum(grad * normed, axis=(0, 1)), jnp.sum(grad, axis=(0, 1)))


def project(left, right):
    return jnp.dot(left, right, preferred_element_type=jnp.float32)


def expert_forward(incoming, first, second):
    pre_act = project(incoming, first)
    active = jax.nn.gelu(pre_act).astype(jnp.bfloat16)
    produced = project(active, second).astype(jnp.bfloat16)
    return (pre_act, active, produced)


def expert_backward(incoming, pre_act, active, grad_in, first, second):
    dactive = project(grad_in, second.T)
    back_local = project(active.T, grad_in)
    gelu_pull = jax.vjp(jax.nn.gelu, pre_act)[1]
    dpre = gelu_pull(dactive)[0].astype(jnp.bfloat16)
    in_local = project(incoming.T, dpre)
    dincoming = project(dpre, first.T).astype(jnp.bfloat16)
    return (in_local, back_local, dincoming)


BF = jnp.bfloat16
F32 = jnp.float32
VM = pltpu.VMEM


def mm(a, b, ca=1, cb=0):
    return lax.dot_general(a, b, (((ca,), (cb,)), ((), ())), preferred_element_type=F32)


def block_diagonal(group, slot, head):
    shape = (group * slot, group * head)
    rows = lax.broadcasted_iota(jnp.int32, shape, 0) // slot
    cols = lax.broadcasted_iota(jnp.int32, shape, 1) // head
    return rows == cols


def spread(part, mask, group):
    return jnp.where(mask, jnp.concatenate([part] * group, axis=0), jnp.zeros((), part.dtype))


def fold(product, mask, slot, group):
    kept = jnp.where(mask, product, 0.0)
    total = kept[0:slot]
    for one in range(1, group):
        total = total + kept[one * slot : (one + 1) * slot]
    return total


def attend(query, keyed, valued, length, mask, slot, group, scale):
    scores = mm(keyed, spread(query, mask, group), 1, 1) * scale
    place = lax.broadcasted_iota(jnp.int32, scores.shape, 0)
    scores = jnp.where(place < length, scores, -1000000000.0)
    raised = jnp.exp(scores - jnp.max(scores, axis=0, keepdims=True))
    prob = raised / jnp.sum(raised, axis=0, keepdims=True)
    context = fold(mm(prob.astype(BF), valued, 0, 0), mask, slot, group)
    return prob, context


def route_tables(cap, tasks, lengths, routes, gate_table):
    sents = tasks.shape[1]
    experts, ntasks = gate_table.shape
    iota = lambda rows, cols, axis: lax.broadcasted_iota(jnp.int32, (rows, cols), axis)
    hot = (iota(ntasks, sents, 0) == tasks).astype(F32)
    exact = functools.partial(
        lax.dot_general,
        dimension_numbers=(((1,), (0,)), ((), ())),
        precision=lax.Precision.HIGHEST,
        preferred_element_type=F32,
    )
    chosen = exact(routes.astype(F32), hot)
    first, second = chosen[0:1], chosen[1:2]
    expert = iota(experts, sents, 0).astype(F32)
    is_first, is_second = expert == first, expert == second
    hit = jnp.logical_or(is_first, is_second)
    before = (iota(sents, sents, 0) < iota(sents, sents, 1)).astype(BF)
    rank = mm(hit.astype(F32).astype(BF), before)
    place = jnp.where(hit, jnp.where(rank < cap, rank, -1.0), -1.0)
    logits = exact(gate_table, hot)
    one = jnp.sum(jnp.where(is_first, logits, 0.0), axis=0, keepdims=True)
    two = jnp.sum(jnp.where(is_second, logits, 0.0), axis=0, keepdims=True)
    peak = jnp.maximum(one, two)
    one, two = jnp.exp(one - peak), jnp.exp(two - peak)
    gate = jnp.where(is_first, one / (one + two), 0.0)
    gate = gate + jnp.where(is_second, two / (one + two), 0.0)
    lane = iota(experts, 128, 1)
    index = iota(experts, sents, 1).astype(F32)
    table = jnp.zeros((experts, 128), F32)
    gates = jnp.zeros((experts, 128), F32)
    for j in range(cap):
        here = place == float(j)
        pick = lambda value: jnp.sum(jnp.where(here, value, 0.0), axis=1, keepdims=True)
        table = jnp.where(lane == j, pick(index), table)
        table = jnp.where(lane == cap + j, pick(lengths.astype(F32)), table)
        gates = jnp.where(lane == j, pick(gate), gates)
    shift = (iota(sents, 128, 1) == iota(sents, 128, 0) + 2 * cap).astype(BF)
    spots = mm((place + 1.0).astype(BF), shift)
    inside = jnp.logical_and(lane >= 2 * cap, lane < 2 * cap + sents)
    table = jnp.where(inside, spots - 1.0, table)
    return table.astype(jnp.int32), gates, hit.astype(F32), place, gate


def attention_forward_kernel(
    heads, cap, steps, len_ref, x_ref, wq, wk, wv, wo, g1, b1, g2, b2, tasks, lengths, routes,
    gate_table, cot_in,
    act_o, q_o, k_o, v_o, ctx_o, p_o, h_o, m_o, st_o, plan_o, tab_o, gates_o, near_o, far_o,
    core_o, cot, tab_s, gates_s, sends, recvs, local,
):
    count, slot, width = x_ref.shape
    head = width // heads
    group = max(1, min(heads, 256 // head))
    span = group * head
    step = pl.program_id(0)
    scale = head ** -0.5
    mask = block_diagonal(group, slot, head)
    experts = gate_table.shape[0]
    me = lax.axis_index("expert")
    half = cot.shape[0] // 2
    early = near_o.shape[0]
    copies = [
        remote(cot.at[pl.ds(0, early)], near_o, sends, recvs, 0, NEAR),
        remote(cot.at[pl.ds(half, early)], far_o, sends, recvs, 1, FAR),
        remote(cot, core_o, sends, recvs, 2, CORE),
    ]
    for relation in range(1, 8):
        there = plane_peer(relation)
        copies += [
            remote(tab_s.at[there], tab_o.at[me], sends, recvs, 1 + 2 * relation, relation),
            remote(gates_s.at[there], gates_o.at[me], sends, recvs, 2 + 2 * relation, relation),
        ]
    load = pltpu.make_async_copy(cot_in, cot, local.at[2])
    own = [
        pltpu.make_async_copy(tab_s.at[me], tab_o.at[me], local.at[0]),
        pltpu.make_async_copy(gates_s.at[me], gates_o.at[me], local.at[1]),
    ]

    @pl.when(step == 0)
    def _():
        load.start()
        greet()
        table, gates, hit, place, gate = route_tables(
            cap, tasks[...], lengths[...], routes[...], gate_table[...]
        )
        for e in range(experts):
            tab_s[e] = jnp.broadcast_to(table[e : e + 1], (8, 128))
            gates_s[e] = jnp.broadcast_to(gates[e : e + 1], (8, 128))
        plan_o[0:experts] = hit
        plan_o[experts : 2 * experts] = place
        plan_o[2 * experts : 3 * experts] = gate
        st_o[...] = jnp.zeros_like(st_o)

    @pl.when(step == min(1, steps - 1))
    def _():
        await_greetings()
        load.wait()
        for copy in copies + own:
            copy.start()

    x = x_ref[...].astype(F32).reshape(count * slot, width)
    normed, _ = normalize(x)
    act = (normed * g1[...] + b1[...]).astype(BF)
    act_o[...] = act
    q_o[...] = mm(act, wq[...]).astype(BF)
    k_o[...] = mm(act, wk[...]).astype(BF)
    v_o[...] = mm(act, wv[...]).astype(BF)
    for s in range(count):
        length = len_ref[step * count + s]
        rows = slice(s * slot, (s + 1) * slot)
        for part in range(heads // group):
            cols = slice(part * span, (part + 1) * span)
            prob, context = attend(
                q_o[rows, cols], k_o[rows, cols], v_o[rows, cols], length, mask, slot, group, scale
            )
            p_o[s, part] = prob
            ctx_o[rows, cols] = context.astype(BF)
    attn = mm(ctx_o[...], wo[...])
    hidden = x + attn
    h_o[...] = hidden
    normed2, _ = normalize(hidden)
    m_o[...] = (normed2 * g2[...] + b2[...]).astype(BF).reshape(count, slot, width)
    place = lax.broadcasted_iota(jnp.int32, (slot, width), 0)
    total = jnp.zeros((1, width), F32)
    for s in range(count):
        length = len_ref[step * count + s]
        part = attn[s * slot : (s + 1) * slot]
        total = total + jnp.sum(jnp.where(place < length, part * part, 0.0), axis=0, keepdims=True)
    st_o[...] += total

    @pl.when(step == pl.num_programs(0) - 1)
    def _():
        for copy in copies + own:
            copy.wait()


def attention_forward(
    tokens, lengths, wq, wk, wv, wo, g1, b1, g2, b2, tasks, routes, gate_table, cot, heads, cap
):
    sents, slot, width = tokens.shape
    experts = gate_table.shape[0]
    count = 4 if sents % 4 == 0 else 1
    rows = count * slot
    head = width // heads
    group = max(1, min(heads, 256 // head))
    whole = lambda *shape: pl.BlockSpec(shape, lambda i: (0,) * len(shape))
    flat = pl.BlockSpec((rows, width), lambda i: (i, 0))
    cube = pl.BlockSpec((count, slot, width), lambda i: (i, 0, 0))
    probs = pl.BlockSpec((count, heads // group, slot, group * slot), lambda i: (i, 0, 0, 0))
    anywhere = pl.BlockSpec(memory_space=pl.ANY)
    shape = jax.ShapeDtypeStruct
    total = sents * slot
    early = (sents // 4, slot, width)
    return pl.pallas_call(
        functools.partial(attention_forward_kernel, heads, cap, sents // count),
        grid=(sents // count,),
        in_specs=[pl.BlockSpec(memory_space=pltpu.SMEM), cube]
        + [whole(width, width)] * 4
        + [whole(1, width)] * 4
        + [whole(1, sents)] * 2
        + [whole(*routes.shape), whole(*gate_table.shape), anywhere],
        out_specs=[flat] * 5
        + [probs, flat, cube, whole(1, width), whole(3 * experts, sents)]
        + [anywhere] * 5,
        out_shape=[shape((total, width), BF)] * 5
        + [
            shape((sents, heads // group, slot, group * slot), F32),
            shape((total, width), F32),
            shape((sents, slot, width), BF),
            shape((1, width), F32),
            shape((3 * experts, sents), F32),
            shape((experts, 8, 128), jnp.int32),
            shape((experts, 8, 128), F32),
            shape(early, BF),
            shape(early, BF),
            shape(tokens.shape, BF),
        ],
        scratch_shapes=[
            VM(cot.shape, BF),
            VM((experts, 8, 128), jnp.int32),
            VM((experts, 8, 128), F32),
            pltpu.SemaphoreType.DMA((17,)),
            pltpu.SemaphoreType.DMA((17,)),
            pltpu.SemaphoreType.DMA((3,)),
        ],
        compiler_params=pltpu.CompilerParams(
            dimension_semantics=("arbitrary",), vmem_limit_bytes=56 * 2**20,
            collective_id=0, has_side_effects=True,
        ),
        cost_estimate=pl.CostEstimate(
            flops=8 * total * width * width + 4 * total * slot * width,
            bytes_accessed=16 * total * width,
            transcendentals=total * slot * heads,
        ),
    )(
        lengths, tokens, wq, wk, wv, wo, g1[None], b1[None], g2[None], b2[None],
        tasks[None], lengths[None], routes, gate_table, cot,
    )


def row_sum(value, width):
    return jnp.sum(value, axis=0, keepdims=True)


def layer_norm_pull(grad, normed, inverse, gain):
    scaled = grad * gain
    inner = scaled - jnp.mean(scaled, axis=-1, keepdims=True)
    inner = inner - normed * jnp.mean(scaled * normed, axis=-1, keepdims=True)
    return inverse * inner


def attention_pull(dcontext, query, keyed, valued, prob, mask, slot, group, scale):
    low = prob.astype(BF)
    dspread = spread(dcontext, mask, group)
    dprob = mm(valued, dspread, 1, 1)
    inner = jnp.sum(dprob * prob, axis=0, keepdims=True)
    dscores = (prob * (dprob - inner)).astype(BF)
    dquery = fold(mm(dscores, keyed, 0, 0), mask, slot, group) * scale
    dkeyed = mm(dscores, spread(query, mask, group)) * scale
    dvalued = mm(low, dspread)
    return dquery.astype(BF), dkeyed.astype(BF), dvalued.astype(BF)


MESH_ID = pl.DeviceIdType.MESH
CORE, NEAR, FAR = 1, 2, 4


def plane_peer(relation):
    me = lax.axis_index("expert")
    bits = []
    for bit in (CORE, NEAR, FAR):
        value = (me // bit) % 2
        bits.append((1 - value if relation & bit else value) * bit)
    return bits[0] + bits[1] + bits[2]


def remote(src, dst, sends, recvs, index, relation):
    return pltpu.make_async_remote_copy(
        src_ref=src,
        dst_ref=dst,
        send_sem=sends.at[index],
        recv_sem=recvs.at[index],
        device_id=(lax.axis_index("dp"), plane_peer(relation)),
        device_id_type=MESH_ID,
    )


def line_peer(offset, depth):
    return lax.rem(lax.axis_index("dp") + offset, depth)


def along(src, dst, sends, recvs, index, offset, depth):
    return pltpu.make_async_remote_copy(
        src_ref=src,
        dst_ref=dst,
        send_sem=sends.at[index],
        recv_sem=recvs.at[index],
        device_id=(line_peer(offset, depth), lax.axis_index("expert")),
        device_id_type=MESH_ID,
    )


def greet(depth=1):
    barrier = pltpu.get_barrier_semaphore()
    targets = [(lax.axis_index("dp"), plane_peer(relation)) for relation in range(1, 8)]
    for offset in range(1, depth):
        targets.append((line_peer(offset, depth), lax.axis_index("expert")))
    for target in targets:
        pl.semaphore_signal(barrier, inc=1, device_id=target, device_id_type=MESH_ID)


def await_greetings(depth=1):
    pl.semaphore_wait(pltpu.get_barrier_semaphore(), 6 + depth)


def gather_copies(own, held, sends, recvs, base, early=0):
    half = own.shape[0] // 2
    low, high = pl.ds(0, half), pl.ds(half, half)
    near, far = pl.ds(early, half - early), pl.ds(half + early, half - early)
    plan = [
        (own.at[near], held[2].at[near], NEAR),
        (own.at[far], held[4].at[far], FAR),
        (own, held[1], CORE),
        (own.at[high], held[2].at[high], NEAR),
        (own.at[low], held[4].at[low], FAR),
        (held[2].at[low], held[6].at[low], FAR),
        (held[4].at[high], held[6].at[high], NEAR),
        (held[2], held[3], CORE),
        (held[4], held[5], CORE),
        (held[6], held[7], CORE),
    ]
    return [
        remote(src, dst, sends, recvs, base + place, relation)
        for place, (src, dst, relation) in enumerate(plan)
    ]


def return_copies(parts, cores, sides, sends, recvs, base):
    half = parts[0].shape[0] // 2
    low, high = pl.ds(0, half), pl.ds(half, half)
    plan = [
        (parts[1], cores[0], CORE),
        (parts[3], cores[2], CORE),
        (parts[5], cores[4], CORE),
        (parts[7], cores[6], CORE),
        (parts[2].at[low], sides[0], NEAR),
        (parts[6].at[low], sides[1], NEAR),
        (parts[4].at[high], sides[2], FAR),
        (parts[6].at[high], sides[3], FAR),
        (parts[4].at[low], sides[4], FAR),
        (parts[2].at[high], sides[5], NEAR),
    ]
    return [
        remote(src, dst, sends, recvs, base + place, relation)
        for place, (src, dst, relation) in enumerate(plan)
    ]


def add_into(target, start, other, count):
    def one(i, carry):
        target[start + i] = target[start + i] + other[i]
        return carry

    lax.fori_loop(0, count, one, 0, unroll=8)


def return_finish(parts, sides, back):
    half = parts[0].shape[0] // 2
    back[4].wait_recv()
    add_into(parts[0], 0, sides[0], half)
    back[5].wait_recv()
    add_into(parts[4], 0, sides[1], half)
    back[8].start()
    back[6].wait_recv()
    add_into(parts[0], half, sides[2], half)
    back[7].wait_recv()
    add_into(parts[2], half, sides[3], half)
    back[9].start()
    back[8].wait_recv()
    add_into(parts[0], 0, sides[4], half)
    back[9].wait_recv()
    add_into(parts[0], half, sides[5], half)
    for copy in back:
        copy.wait_send()


GELU_A = 0.7978845608028654
GELU_B = 0.044715


def expert_steps():
    waves = (((0, 1), (0,)), ((2, 3, 4, 5), (2,)), ((6, 7), ()))
    steps = []
    for taken, closed in waves:
        steps += [("F", r) for r in taken] + [("B", r) for r in taken]
        steps += [("U", r) for r in closed] + [("V", r) for r in closed]
    return steps


def expert_kernel(
    cap, depth, tab, gates, m_in, cot_in, near_in, far_in, core_in, win_in, wback_in,
    dm_o, py_o, cy_o, gin_o, gback_o, dg_o, *scratch
):
    sents, slot, width = m_in.shape
    hidden = win_in.shape[1]
    half = sents // 2
    held_m = dict(zip(range(8), scratch[0:8]))
    held_c = dict(zip(range(8), scratch[8:16]))
    sides = scratch[16:22]
    win, wback = scratch[22:24]
    first_part, xs, dys, zs, dus, ys, dms, stage, dg_s, accb, acci = scratch[24:35]
    line_in, line_back, sends, recvs, local, free = scratch[35:]
    parts = {
        0: first_part, 1: held_c[1], 2: held_m[0], 3: held_c[3],
        4: held_c[0], 5: held_c[5], 6: held_c[6], 7: held_c[7],
    }
    cores = {0: held_m[1], 2: held_m[3], 4: held_m[5], 6: held_m[7]}
    sets = {r: r - 2 if r in (4, 5) else r % 2 for r in range(8)}
    me = lax.axis_index("expert")
    z = lax.axis_index("dp")
    tile = min(512, hidden)
    rows = cap * slot
    early = near_in.shape[0]
    low, high = pl.ds(0, half), pl.ds(half, half)
    loads = [
        pltpu.make_async_copy(src, dst, local.at[2 + place])
        for place, (src, dst) in enumerate(
            [
                (m_in, held_m[0]),
                (cot_in, held_c[0]),
                (win_in, win),
                (wback_in, wback),
                (core_in, held_c[1]),
                (near_in, held_c[2].at[pl.ds(0, early)]),
                (far_in, held_c[4].at[pl.ds(half, early)]),
            ]
        )
    ]
    for load in loads:
        load.start()
    greet(depth)
    to_m = gather_copies(held_m[0], held_m, sends, recvs, 0)
    to_c = gather_copies(held_c[0], held_c, sends, recvs, 10, early)
    back = return_copies(parts, cores, sides, sends, recvs, 20)
    gates_back = {
        r: remote(dg_s.at[r], dg_o.at[me], sends, recvs, 30 + r, r) for r in range(1, 8)
    }
    outputs_back = {
        r: remote(stage, cy_o.at[r // 2], sends, recvs, 38 + r // 2, CORE) for r in (1, 3, 5, 7)
    }
    outputs_here = {
        r: pltpu.make_async_copy(stage, py_o.at[r // 2], local.at[0]) for r in (0, 2, 4, 6)
    }

    def line_first(right, array):
        offset = 1 if right else depth - 1
        s = depth - 1 if right else 0
        source, into = ((win, line_in), (wback, line_back))[array]
        share = source.shape[0] // depth
        here = pl.ds(s * share, share)
        index = 42 + 2 * int(right) + array
        return here, along(source.at[here], into, sends, recvs, index, offset, depth)

    def line_open(array):
        for right in (True, False):

            @pl.when(z == (0 if right else depth - 1))
            def _():
                line_first(right, array)[1].start()

    accb[...] = jnp.zeros_like(accb)
    acci[...] = jnp.zeros_like(acci)
    for load in loads[0:2]:
        load.wait()
    await_greetings(depth)
    for index in (0, 1, 2, 3, 4):
        to_m[index].start()
    for index in (0, 1, 3, 4):
        to_c[index].start()
    place = lax.broadcasted_iota(jnp.int32, (slot, width), 0)
    for load in loads[2:4]:
        load.wait()

    def before_forward(r):
        if r == 1:
            to_m[2].wait_recv()
        if r == 2:
            to_m[0].wait_recv()
            to_m[5].start()
            to_m[1].wait_recv()
            to_m[6].start()
            to_m[3].wait_recv()
            to_m[7].start()
            to_m[4].wait_recv()
            to_m[8].start()
        if r == 3:
            to_m[7].wait_recv()
        if r == 4:
            for load in loads[5:7]:
                load.wait()
            to_c[0].wait_recv()
            to_c[5].start()
            to_c[1].wait_recv()
            to_c[6].start()
        if r == 5:
            to_m[8].wait_recv()
        if r == 6:
            to_m[5].wait_recv()
            to_m[6].wait_recv()
            to_m[9].start()
        if r == 7:
            to_m[9].wait_recv()
        source = plane_peer(r)

        def fetch(j, carry):
            xs[sets[r], j] = held_m[r][tab[source, 0, j]]
            return carry

        lax.fori_loop(0, cap, fetch, 0, unroll=True)
        if r % 2 == 1:
            pl.semaphore_signal(
                free.at[r // 2], inc=1, device_id=(z, plane_peer(CORE)), device_id_type=MESH_ID
            )

    def after_forward(r):
        source = plane_peer(r)
        if r > 0 and r % 2 == 1:
            outputs_here[r - 1].wait()
        if r > 0 and r % 2 == 0:
            outputs_back[r - 1].wait_send()

        def give(i, carry):
            index = tab[source, 0, 2 * cap + i]
            there = jnp.maximum(index, 0)
            gate = jnp.where(index >= 0, gates[source, 0, there], 0.0)
            stage[i] = (ys[sets[r], there].astype(F32) * gate).astype(BF)
            return carry

        lax.fori_loop(0, sents, give, 0, unroll=8)
        if r % 2 == 0:
            outputs_here[r].start()
        else:
            outputs_back[r].start()

    def before_backward(r):
        if r == 1:
            loads[4].wait()
        if r == 2:
            to_c[3].wait_recv()
            to_c[7].start()
            to_c[4].wait_recv()
            to_c[8].start()
        if r == 3:
            to_c[7].wait_recv()
        if r == 5:
            to_c[8].wait_recv()
        if r == 6:
            to_c[5].wait_recv()
            to_c[6].wait_recv()
            to_c[9].start()
        if r == 7:
            to_c[9].wait_recv()
        source = plane_peer(r)

        def fetch(j, carry):
            index = tab[source, 0, j]
            length = tab[source, 0, cap + j]
            gate = gates[source, 0, j]
            gt = jnp.where(place < length, held_c[r][index].astype(F32), 0.0)
            dys[sets[r], j] = (gt * gate).astype(BF)
            product = ys[sets[r], j].astype(F32) * gt
            total = jnp.sum(jnp.sum(product, axis=0, keepdims=True), axis=1, keepdims=True)
            if r == 0:
                dg_o[me, pl.ds(j, 1)] = jnp.broadcast_to(total, (1, 128))
            else:
                dg_s[r, pl.ds(j, 1)] = jnp.broadcast_to(total, (1, 128))
            return carry

        lax.fori_loop(0, cap, fetch, 0, unroll=True)
        if r > 0:
            gates_back[r].start()

    def after_backward(r):
        source = plane_peer(r)
        if r == 2:
            for copy in to_m[0:5]:
                copy.wait_send()
        if r == 4:
            for copy in to_c[0:2] + to_c[3:5]:
                copy.wait_send()
        if r == 6:
            to_c[9].wait_send()

        def give(i, carry):
            index = tab[source, 0, 2 * cap + i]
            kept = dms[jnp.maximum(index, 0)]
            parts[r][i] = jnp.where(index >= 0, kept, jnp.zeros_like(kept))
            return carry

        lax.fori_loop(0, sents, give, 0, unroll=8)
        if r % 2 == 1:
            pl.semaphore_wait(free.at[r // 2], 1)
            back[r // 2].start()
        if r == 4:
            join(2)
            back[4].start()

    def join(r):
        back[r // 2].wait_recv()
        add_into(parts[r], 0, cores[r], sents)

    def after_back_grad(r):
        if r == 2:
            join(4)
            back[6].start()

    def after_in_grad(r):
        if r == 2:
            join(0)

    tiles = [slice(f * tile, (f + 1) * tile) for f in range(hidden // tile)]

    def forward(spot):
        x = xs[spot].reshape(rows, width)
        here = pl.ds(pl.multiple_of(spot * rows, rows), rows)
        for cols in tiles:
            u = mm(x, win[:, cols])
            square = u * u
            th = jnp.tanh(u * (GELU_A + GELU_A * GELU_B * square))
            cdf = 0.5 + 0.5 * th
            slope = cdf + (0.5 * u) * (1.0 - th * th) * (GELU_A + 3 * GELU_A * GELU_B * square)
            zs[here, cols] = (u * cdf).astype(BF)
            dus[here, cols] = slope.astype(BF)
        ys[spot] = mm(zs[here, :], wback[...]).astype(BF).reshape(cap, slot, width)

    def backward(spot):
        dy = dys[spot].reshape(rows, width)
        here = pl.ds(pl.multiple_of(spot * rows, rows), rows)
        for cols in tiles:
            dz = mm(dy, wback[cols, :], 1, 1)
            dus[here, cols] = (dz * dus[here, cols].astype(F32)).astype(BF)
        dms[...] = mm(dus[here, :], win[...], 1, 1).astype(BF).reshape(cap, slot, width)

    def back_grad(count):
        dy = dys[0:count].reshape(count * rows, width)
        for cols in tiles:
            yield cols, mm(zs[0 : count * rows, cols], dy, 0, 0)

    def in_grad(count):
        x = xs[0:count].reshape(count * rows, width)
        for cols in tiles:
            yield cols, mm(x, dus[0 : count * rows, cols], 0, 0)

    def back_pair(spot):
        for cols, total in back_grad(2):
            accb[cols, :] += total

    def in_pair(spot):
        for cols, total in in_grad(2):
            acci[:, cols] += total

    steps = expert_steps()
    actions = {
        "F": (before_forward, forward, after_forward),
        "B": (before_backward, backward, after_backward),
        "U": (None, back_pair, after_back_grad),
        "V": (None, in_pair, after_in_grad),
    }

    def spot_of(t, kind):
        spot = jnp.int32(0)
        for number, (other, r) in enumerate(steps):
            if other == kind and sets[r]:
                spot = spot + jnp.where(t == number, sets[r], 0)
        return spot

    def step(t, carry):
        for kind, (pre, work, post) in actions.items():
            mine = [number for number, (other, _) in enumerate(steps) if other == kind]
            spans = [n for n in mine if n - 1 not in mine]
            ends = [n for n in mine if n + 1 not in mine]
            inside = functools.reduce(
                jnp.logical_or,
                [jnp.logical_and(t >= a, t <= b) for a, b in zip(spans, ends)],
            )

            @pl.when(inside)
            def _():
                if pre is not None:
                    for number in mine:
                        pl.when(t == number)(functools.partial(pre, steps[number][1]))
                work(spot_of(t, kind))
                for number in mine:
                    pl.when(t == number)(functools.partial(post, steps[number][1]))

        return carry

    lax.fori_loop(0, len(steps), step, 0)
    for cols, total in back_grad(4):
        wback[cols, :] = (accb[cols, :] + total).astype(BF)
        if cols.start == 0:
            join(6)
            back[5].start()
            back[7].start()
    line_open(1)
    for cols, total in in_grad(4):
        win[:, cols] = (acci[:, cols] + total).astype(BF)
    line_open(0)
    return_finish(parts, sides, back)
    kept = pltpu.make_async_copy(parts[0], dm_o, local.at[2])
    kept.start()
    for right in (True, False):

        @pl.when(z == (1 if right else depth - 2))
        def _():
            for array in (1, 0):
                here, copy = line_first(right, array)
                copy.wait_recv()
                source, into = ((win, line_in), (wback, line_back))[array]
                total = source[here, :].astype(F32) + into[...].astype(F32)
                source[here, :] = total.astype(BF)

    stores = [
        pltpu.make_async_copy(win, gin_o, local.at[4]),
        pltpu.make_async_copy(wback, gback_o, local.at[5]),
    ]
    for store in stores:
        store.start()
    for store in stores:
        store.wait()
    kept.wait()
    for right in (True, False):

        @pl.when(z == (0 if right else depth - 1))
        def _():
            for array in (0, 1):
                line_first(right, array)[1].wait_send()

    for r in (1, 3, 5, 7):
        outputs_back[r].wait_recv()
    outputs_back[7].wait_send()
    for r in range(1, 8):
        gates_back[r].wait()
    for index in range(5, 10):
        to_m[index].wait_send()
    for index in range(5, 9):
        to_c[index].wait_send()


def expert_exchange(tab, gates, m, cot, near, far, core, win, wback, cap, depth):
    sents, slot, width = m.shape
    hidden = win.shape[1]
    vm = pl.BlockSpec(memory_space=VM)
    sm = pl.BlockSpec(memory_space=pltpu.SMEM)
    anywhere = pl.BlockSpec(memory_space=pl.ANY)
    shape = jax.ShapeDtypeStruct
    cube = (sents, slot, width)
    taken = (cap, slot, width)
    rows = cap * slot
    return pl.pallas_call(
        functools.partial(expert_kernel, cap, depth),
        in_specs=[sm, sm] + [anywhere] * 7,
        out_specs=[anywhere] * 5 + [vm],
        out_shape=[
            shape(cube, BF),
            shape((4,) + cube, BF),
            shape((4,) + cube, BF),
            shape((width, hidden), BF),
            shape((hidden, width), BF),
            shape((8, cap, 128), F32),
        ],
        scratch_shapes=[VM(cube, BF)] * 16
        + [VM((sents // 2, slot, width), BF)] * 6
        + [VM((width, hidden), BF), VM((hidden, width), BF)]
        + [VM(cube, BF)]
        + [VM((4,) + taken, BF)] * 2
        + [VM((4 * rows, hidden), BF)] * 2
        + [VM((4,) + taken, BF), VM(taken, BF), VM(cube, BF)]
        + [VM((8, cap, 128), F32)]
        + [VM((hidden, width), F32), VM((width, hidden), F32)]
        + [VM((width // depth, hidden), BF), VM((hidden // depth, width), BF)]
        + [
            pltpu.SemaphoreType.DMA((46,)),
            pltpu.SemaphoreType.DMA((46,)),
            pltpu.SemaphoreType.DMA((9,)),
            pltpu.SemaphoreType.REGULAR((4,)),
        ],
        compiler_params=pltpu.CompilerParams(
            collective_id=1, has_side_effects=True, vmem_limit_bytes=63 * 2**20
        ),
        cost_estimate=pl.CostEstimate(
            flops=12 * 8 * rows * width * hidden, bytes_accessed=40 * 2**20, transcendentals=0
        ),
    )(tab, gates, m, cot, near, far, core, win, wback)


class Reduction:
    def __init__(self, depth, value, wide, core_r, plane_r, line_s, line_r, final, sems, base):
        self.depth, self.value, self.wide, self.final = depth, value, wide, final
        self.core_r, self.plane_r, self.line_s, self.line_r = core_r, plane_r, line_s, line_r
        sends, recvs = sems
        me = lax.axis_index("expert")
        z = lax.axis_index("dp")
        core = me % 2
        self.half = value.shape[0] // 2
        self.quarter = self.half // 4
        self.share = self.quarter // depth
        self.mine = core * self.half
        self.other = (1 - core) * self.half
        self.block = self.mine + (me // 2) * self.quarter
        self.own = self.block + z * self.share
        self.to_core = remote(wide, core_r, sends, recvs, base, CORE)
        self.to_plane = []
        self.from_plane = []
        for place, relation in enumerate((2, 4, 6)):
            rows = pl.ds((plane_peer(relation) // 2) * self.quarter, self.quarter)
            self.to_plane.append(
                remote(wide.at[rows], plane_r.at[place], sends, recvs, base + 1 + place, relation)
            )
        self.to_line = []
        for offset in range(1, depth):
            rows = pl.ds(line_peer(offset, depth) * self.share, self.share)
            self.to_line.append(
                along(
                    line_s.at[rows], line_r.at[offset - 1], sends, recvs, base + 3 + offset,
                    offset, depth,
                )
            )
        after = base + 3 + depth
        rows = final.at[pl.ds(self.own, self.share)]
        self.back_line = [
            along(rows, rows, sends, recvs, after + offset - 1, offset, depth)
            for offset in range(1, depth)
        ]
        after = after + depth - 1
        rows = final.at[pl.ds(self.block, self.quarter)]
        self.back_plane = [
            remote(rows, rows, sends, recvs, after + place, relation)
            for place, relation in enumerate((2, 4, 6))
        ]
        rows = final.at[pl.ds(self.mine, self.half)]
        self.back_core = remote(rows, rows, sends, recvs, after + 3, CORE)

    @staticmethod
    def semaphores(depth):
        return 2 * depth + 6

    def send_core(self):
        self.wide[...] = self.value[pl.ds(self.other, self.half), :].astype(BF)
        self.to_core.start()

    def send_plane(self):
        self.to_core.wait()
        rows = pl.ds(self.mine, self.half)
        total = self.value[rows, :] + self.core_r[...].astype(F32)
        self.value[rows, :] = total
        self.wide[...] = total.astype(BF)
        for copy in self.to_plane:
            copy.start()

    def send_line(self):
        for copy in self.to_plane:
            copy.wait()
        rows = pl.ds(self.block, self.quarter)
        total = self.value[rows, :]
        for place in range(3):
            total = total + self.plane_r[place].astype(F32)
        self.value[rows, :] = total
        self.line_s[...] = total.astype(BF)
        for copy in self.to_line:
            copy.start()

    def send_back_line(self):
        for copy in self.to_line:
            copy.wait()
        rows = pl.ds(self.own, self.share)
        total = self.value[rows, :]
        for offset in range(1, self.depth):
            total = total + self.line_r[offset - 1].astype(F32)
        self.final[rows, :] = total.astype(BF)
        for copy in self.back_line:
            copy.start()

    def send_back_plane(self):
        for copy in self.back_line:
            copy.wait()
        for copy in self.back_plane:
            copy.start()

    def send_back_core(self):
        for copy in self.back_plane:
            copy.wait()
        self.back_core.start()

    def finish(self):
        self.back_core.wait()


class SmallSum:
    @staticmethod
    def semaphores(depth):
        return 4 + depth

    def __init__(self, depth, value, core_r, plane, line, sems, base):
        sends, recvs = sems
        self.value, self.core_r, self.plane, self.line = value, core_r, plane, line
        self.spot = lax.axis_index("expert") // 2
        self.z = lax.axis_index("dp")
        self.to_core = remote(value, core_r, sends, recvs, base, CORE)
        spot = plane.at[self.spot]
        self.to_plane = [
            remote(spot, spot, sends, recvs, base + 1 + place, relation)
            for place, relation in enumerate((2, 4, 6))
        ]
        spot = line.at[self.z]
        self.to_line = [
            along(spot, spot, sends, recvs, base + 3 + offset, offset, depth)
            for offset in range(1, depth)
        ]

    def send_core(self):
        self.to_core.start()

    def send_plane(self):
        self.to_core.wait()
        self.plane[self.spot] = self.value[...] + self.core_r[...]
        for copy in self.to_plane:
            copy.start()

    def send_line(self):
        for copy in self.to_plane:
            copy.wait()
        total = self.plane[0]
        for place in range(1, 4):
            total = total + self.plane[place]
        self.line[self.z] = total
        for copy in self.to_line:
            copy.start()

    def finish(self, out):
        for copy in self.to_line:
            copy.wait()
        total = self.line[0]
        for place in range(1, self.line.shape[0]):
            total = total + self.line[place]
        out[...] = total


def backward_kernel(
    heads, depth, len_ref, g1, g2, attn_sum, plan, tasks, lengths, dots,
    x_in, cot_in, dm_in, h_in, act_in, q_in, k_in, v_in, ctx_in, p_in,
    wq_in, wk_in, wv_in, wo_in, py, cy, gin, gback,
    ig_o, out_o, gq_o, gk_o, gv_o, go_o, gin_o, gback_o, small_o, *scratch
):
    inputs = (
        x_in, cot_in, dm_in, h_in, act_in, q_in, k_in, v_in, ctx_in, p_in,
        wq_in, wk_in, wv_in, wo_in, gin, gback,
    )
    held = scratch[0:16]
    (
        x_ref, cot_ref, dm_ref, h_ref, act, q, k, v, ctx, p_ref, wq, wk, wv, wo, gin_s, gback_s,
    ) = held
    parts = dict(zip((0, 2, 4, 6), scratch[16:20]))
    cores = dict(zip((0, 2, 4, 6), scratch[20:24]))
    sides = scratch[24:30]
    dh_s, da_s, dctx_s, dq_s, dk_s, dv_s = scratch[30:36]
    red = scratch[36:57]
    line_in, line_back, extra_in, extra_back = scratch[57:61]
    small, small_core, small_plane, small_line = scratch[61:65]
    sends, recvs, local = scratch[65:]
    sems = (sends, recvs)
    sents, slot, width = x_ref.shape
    head = width // heads
    group = max(1, min(heads, 256 // head))
    span = group * head
    scale = head ** -0.5
    count = 4 if sents % 4 == 0 else 1
    rows_per = count * slot
    half = sents // 2
    z = lax.axis_index("dp")

    loads = {
        id(ref): pltpu.make_async_copy(source, ref, local.at[place])
        for place, (source, ref) in enumerate(zip(inputs, held))
    }
    for place, r in enumerate((0, 2, 4, 6)):
        loads[id(parts[r])] = pltpu.make_async_copy(
            py.at[r // 2], parts[r], local.at[16 + place]
        )
        loads[id(cores[r])] = pltpu.make_async_copy(
            cy.at[r // 2], cores[r], local.at[20 + place]
        )

    def begin(*refs):
        for ref in refs:
            loads[id(ref)].start()

    def ready(*refs):
        for ref in refs:
            loads[id(ref)].wait()

    begin(gin_s, gback_s, h_ref, dm_ref, cot_ref, wo, parts[6], cores[6], ctx)
    begin(parts[2], cores[2], parts[4], cores[4], q, k, v, p_ref, act, parts[0], cores[0])
    begin(wq, wk, wv, x_ref)
    greet(depth)
    await_greetings(depth)

    all_parts = {r: parts[r - r % 2] for r in range(8)}
    back = return_copies(all_parts, cores, sides, sends, recvs, 0)

    base = 10
    in_rows = gin_s.shape[0] // depth
    back_rows = gback_s.shape[0] // depth

    def line_piece(s, array, right, last):
        offset = 1 if right else depth - 1
        index = base + (0 if right else 2 * depth) + 2 * s + array
        share, source = ((in_rows, gin_s), (back_rows, gback_s))[array]
        into = (line_in, line_back)[array].at[s]
        if last and not right:
            into = (extra_in, extra_back)[array]
        here = source.at[pl.ds(s * share, share)]
        return along(here, into, sends, recvs, index, offset, depth)

    def add_piece(s, array):
        share, source = ((in_rows, gin_s), (back_rows, gback_s))[array]
        other = (line_in, line_back)[array]
        here = pl.ds(s * share, share)
        source[here, :] = (source[here, :].astype(F32) + other[s].astype(F32)).astype(BF)

    def pieces(right):
        order = range(depth - 1, 0, -1) if right else range(depth - 1)
        return [(s, array) for s in order for array in (0, 1)]

    def start_piece(s, array, right):
        if right:
            line_piece(s, array, True, False).start()
            return
        near = z == s + 1

        @pl.when(near)
        def _():
            line_piece(s, array, False, True).start()

        @pl.when(jnp.logical_not(near))
        def _():
            line_piece(s, array, False, False).start()

    def line_service(t, ahead=0):
        for right in (True, False):
            every = pieces(right)
            edge = 0 if right else depth - 1
            opening = range(2, 3 + ahead) if t == 0 else range(t + ahead + 2, t + ahead + 3)

            @pl.when(z == edge)
            def _():
                for number in opening:
                    if number < len(every):
                        start_piece(*every[number], right)

            for number, (s, array) in enumerate(every):
                away = s if right else depth - 1 - s
                for hops in range(1, away):
                    given = hops == 1 and number < 2
                    if t != (0 if given else number + hops - 1):
                        continue

                    @pl.when(z == (hops if right else depth - 1 - hops))
                    def _():
                        if not given:
                            line_piece(s, array, right, False).wait_recv()
                            add_piece(s, array)
                        start_piece(s, array, right)

    def line_end():
        for s in range(depth):

            @pl.when(z == s)
            def _():
                here = pl.ds(s * in_rows, in_rows)
                there = pl.ds(s * back_rows, back_rows)
                gin_o[...] = gin_s[here, :].astype(F32)
                gback_o[...] = gback_s[there, :].astype(F32)
                if s > 0:
                    for array in (0, 1):
                        line_piece(s, array, True, True).wait_recv()
                    gin_o[...] += line_in[s].astype(F32)
                    gback_o[...] += line_back[s].astype(F32)
                if s < depth - 1:
                    for array in (0, 1):
                        line_piece(s, array, False, True).wait_recv()
                    gin_o[...] += extra_in[...].astype(F32)
                    gback_o[...] += extra_back[...].astype(F32)

        for s in range(depth):
            for array in (0, 1):
                first_right = 1 if s == depth - 1 else 0
                first_left = depth - 2 if s == 0 else depth - 1

                @pl.when(jnp.logical_and(z < s, z >= first_right))
                def _():
                    line_piece(s, array, True, False).wait_send()

                @pl.when(jnp.logical_and(z > s, z <= first_left))
                def _():
                    line_piece(s, array, False, False).wait_send()

    base_red = base + 4 * depth
    per = Reduction.semaphores(depth)
    red_o, red_0, red_1 = [
        Reduction(depth, *red[7 * place : 7 * place + 7], sems, base_red + place * per)
        for place in range(3)
    ]
    sums = SmallSum(
        depth, small, small_core, small_plane, small_line, sems, base_red + 3 * per
    )

    small[...] = jnp.zeros_like(small)
    small[4:5] = attn_sum[...]
    small[7:8, 0:sents] = lengths[...].astype(F32)
    experts = plan.shape[0] // 3
    chunk_place = lax.broadcasted_iota(jnp.int32, (slot, width), 0)

    def masked(ref, c):
        return jnp.concatenate(
            [
                jnp.where(
                    chunk_place < len_ref[c * count + s], ref[c * count + s].astype(F32), 0.0
                )
                for s in range(count)
            ],
            axis=0,
        )

    def flat(ref, c):
        block = ref[pl.ds(c * count, count)]
        return block.astype(F32).reshape(rows_per, width)

    def first(c, carry):
        rows = pl.ds(pl.multiple_of(c * rows_per, rows_per), rows_per)
        normed2, inverse2 = normalize(h_ref[rows, :])
        dm = flat(dm_ref, c)
        dhidden = masked(cot_ref, c) + layer_norm_pull(dm, normed2, inverse2, g2[...])
        small[2:3] += row_sum(dm * normed2, width)
        small[3:4] += row_sum(dm, width)
        dh_s[rows, :] = dhidden
        dattn = dhidden.astype(BF)
        da_s[rows, :] = dattn
        dctx_s[rows, :] = mm(dattn, wo[...], 1, 1).astype(BF)
        return carry

    mask = block_diagonal(group, slot, head)

    def pull(part, into):
        cols = slice(part * span, (part + 1) * span)

        def one(c, carry):
            for s in range(count):
                at = c * count + s
                rows = pl.ds(pl.multiple_of(at * slot, slot), slot)
                dq_s[rows, cols], dk_s[rows, cols], dv_s[rows, cols] = attention_pull(
                    dctx_s[rows, cols], q[rows, cols], k[rows, cols], v[rows, cols],
                    p_ref[at, part], mask, slot, group, scale,
                )
            return carry

        lax.fori_loop(0, sents // count, one, 0)
        into.value[0:width, :] = mm(act[...], dq_s[:, cols], 0, 0)
        into.value[width : 2 * width, :] = mm(act[...], dk_s[:, cols], 0, 0)
        into.value[2 * width : 3 * width, :] = mm(act[...], dv_s[:, cols], 0, 0)
        into.send_core()

    def returned(r):
        ready(parts[r], cores[r])
        add_into(parts[r], 0, cores[r], sents)

    def last(c, carry):
        rows = pl.ds(pl.multiple_of(c * rows_per, rows_per), rows_per)
        dact = (
            mm(dq_s[rows, :], wq[...], 1, 1)
            + mm(dk_s[rows, :], wk[...], 1, 1)
            + mm(dv_s[rows, :], wv[...], 1, 1)
        )
        normed1, inverse1 = normalize(flat(x_ref, c))
        small[0:1] += row_sum(dact * normed1, width)
        small[1:2] += row_sum(dact, width)
        dx = dh_s[rows, :] + layer_norm_pull(dact, normed1, inverse1, g1[...])
        ig_o[pl.ds(c * count, count)] = dx.astype(BF).reshape(count, slot, width)
        return carry

    def outcome(low, side):
        def one(i, carry):
            at = low + i
            valid = chunk_place < len_ref[at]
            moe = jnp.where(valid, parts[0][at].astype(F32) + side[i].astype(F32), 0.0)
            rows = pl.ds(pl.multiple_of(at * slot, slot), slot)
            total = jnp.where(valid, h_ref[rows, :], 0.0) + moe
            out_o[at] = total.astype(BF)
            small[5:6] += row_sum(total * total, width)
            small[6:7] += row_sum(moe * moe, width)
            return carry

        lax.fori_loop(0, half, one, 0)

    def gate_gradient():
        hit = plan[0:experts] > 0.5
        place = plan[experts : 2 * experts]
        gate = plan[2 * experts : 3 * experts]
        taken = jnp.zeros(gate.shape, F32)
        for j in range(dots.shape[1]):
            taken = taken + jnp.where(place == float(j), dots[:, j, 0:sents], 0.0)
        inner = jnp.sum(gate * taken, axis=0, keepdims=True)
        dlogit = jnp.where(hit, gate * (taken - inner), 0.0)
        hot = lax.broadcasted_iota(jnp.int32, (slot, sents), 0) == tasks[...]
        small[8 : 8 + experts, 0:slot] = lax.dot_general(
            dlogit, hot.astype(F32), (((1,), (1,)), ((), ())),
            precision=lax.Precision.HIGHEST, preferred_element_type=F32,
        )

    ready(gin_s, gback_s)
    line_service(0)
    returned(6)
    back[5].start()
    back[7].start()
    ready(h_ref, dm_ref, cot_ref, wo)
    lax.fori_loop(0, sents // count, first, 0)
    ready(ctx)
    red_o.value[...] = mm(ctx[...], da_s[...], 0, 0)
    red_o.send_core()
    returned(2)
    returned(4)
    ready(q, k, v, p_ref, act)
    pull(0, red_0)
    red_o.send_plane()
    back[4].start()
    back[6].start()
    line_service(1)
    back[5].wait_recv()
    add_into(parts[4], 0, sides[1], half)
    back[7].wait_recv()
    add_into(parts[2], half, sides[3], half)
    pull(1, red_1)
    red_0.send_plane()
    back[8].start()
    back[9].start()
    red_o.send_line()
    line_service(2)
    ready(wq, wk, wv, x_ref)
    lax.fori_loop(0, sents // count, last, 0)
    red_1.send_plane()
    red_o.send_back_line()
    gate_gradient()
    returned(0)
    red_0.send_line()
    line_service(3)
    back[4].wait_recv()
    add_into(parts[0], 0, sides[0], half)
    back[6].wait_recv()
    add_into(parts[0], half, sides[2], half)
    red_o.send_back_plane()
    red_0.send_back_line()
    red_1.send_line()
    back[8].wait_recv()
    outcome(0, sides[4])
    back[9].wait_recv()
    outcome(half, sides[5])
    sums.send_core()
    red_o.send_back_core()
    red_0.send_back_plane()
    red_1.send_back_line()
    sums.send_plane()
    red_1.send_back_plane()
    red_0.send_back_core()
    sums.send_line()
    red_1.send_back_core()
    red_o.finish()
    go_o[...] = red_o.final[...]
    red_0.finish()

    def share(red, low):
        for place, ref in enumerate((gq_o, gk_o, gv_o)):
            ref[:, low : low + red.final.shape[1]] = red.final[
                place * width : (place + 1) * width, :
            ]

    share(red_0, 0)
    sums.finish(small_o)
    red_1.finish()
    share(red_1, span)
    line_end()
    for copy in back[4:]:
        copy.wait_send()


def backward_exchange(
    depth, lengths, tokens, cot, dm, hidden, act, q, k, v, ctx, prob, wq, wk, wv, wo, g1, g2,
    attn_sum, plan, tasks, dots, py, cy, gin, gback, heads,
):
    sents, slot, width = tokens.shape
    total = sents * slot
    small = jax.ShapeDtypeStruct((16, width), F32)
    vm = pl.BlockSpec(memory_space=VM)
    anywhere = pl.BlockSpec(memory_space=pl.ANY)
    shape = jax.ShapeDtypeStruct
    cube = (sents, slot, width)
    head = width // heads
    span = max(1, min(heads, 256 // head)) * head
    pieces = [(width, width), (3 * width, span), (3 * width, width - span)]
    red = []
    for rows, cols in pieces:
        red += [
            VM((rows, cols), F32),
            VM((rows // 2, cols), BF),
            VM((rows // 2, cols), BF),
            VM((3, rows // 8, cols), BF),
            VM((rows // 8, cols), BF),
            VM((depth - 1, rows // 8 // depth, cols), BF),
            VM((rows, cols), BF),
        ]
    in_share = (gin.shape[0] // depth, gin.shape[1])
    back_share = (gback.shape[0] // depth, gback.shape[1])
    semaphores = 10 + 4 * depth + 3 * Reduction.semaphores(depth) + SmallSum.semaphores(depth)
    large = (
        tokens, cot, dm, hidden, act, q, k, v, ctx, prob, wq, wk, wv, wo, py, cy, gin, gback,
    )
    return pl.pallas_call(
        functools.partial(backward_kernel, heads, depth),
        in_specs=[pl.BlockSpec(memory_space=pltpu.SMEM)] + [vm] * 7 + [anywhere] * len(large),
        out_specs=[vm] * 9,
        out_shape=[shape(cube, BF), shape(cube, BF)]
        + [shape((width, width), BF)] * 4
        + [shape(in_share, F32), shape(back_share, F32), shape(small.shape, F32)],
        scratch_shapes=[VM(ref.shape, ref.dtype) for ref in large[:14] + large[16:]]
        + [VM(cube, BF)] * 8
        + [VM((sents // 2, slot, width), BF)] * 6
        + [VM((total, width), F32)]
        + [VM((total, width), BF)] * 5
        + red
        + [VM((depth,) + in_share, BF), VM((depth,) + back_share, BF)]
        + [VM(in_share, BF), VM(back_share, BF)]
        + [VM(small.shape, F32)] * 2
        + [VM((4,) + small.shape, F32), VM((depth,) + small.shape, F32)]
        + [
            pltpu.SemaphoreType.DMA((semaphores,)),
            pltpu.SemaphoreType.DMA((semaphores,)),
            pltpu.SemaphoreType.DMA((24,)),
        ],
        compiler_params=pltpu.CompilerParams(
            collective_id=2, has_side_effects=True, vmem_limit_bytes=63 * 2**20
        ),
        cost_estimate=pl.CostEstimate(
            flops=16 * total * width * width, bytes_accessed=40 * 2**20, transcendentals=0
        ),
    )(
        lengths, g1[None], g2[None], attn_sum, plan, tasks[None], lengths[None], dots, *large
    )


def outputs_kernel(
    out_in, ig_in, gin_in, gback_in, q_in, k_in, v_in, o_in, small,
    out_o, ig_o, gin_o, gback_o, q_o, k_o, v_o, o_o, l1g, l1b, l2g, l2b, table_o, rms_o,
    low, wide, cubes, share_in, share_back, sems,
):
    fetches = [
        pltpu.make_async_copy(src, low.at[place], sems.at[place])
        for place, src in enumerate((q_in, k_in, v_in, o_in))
    ]
    stores = [
        pltpu.make_async_copy(wide.at[place], dst, sems.at[4 + place])
        for place, dst in enumerate((q_o, k_o, v_o, o_o))
    ]
    moves = [
        (pltpu.make_async_copy(src, held, sems.at[8 + place]),
         pltpu.make_async_copy(held, dst, sems.at[12 + place]))
        for place, (src, held, dst) in enumerate(
            [
                (out_in, cubes.at[0], out_o),
                (ig_in, cubes.at[1], ig_o),
                (gin_in, share_in, gin_o),
                (gback_in, share_back, gback_o),
            ]
        )
    ]
    for fetch in fetches:
        fetch.start()
    for enter, _ in moves:
        enter.start()
    width = small.shape[1]
    for row, ref in enumerate((l1g, l1b, l2g, l2b)):
        ref[...] = small[row : row + 1]
    table_o[...] = small[8 : 8 + table_o.shape[0], 0 : table_o.shape[1]]
    sums = jnp.sum(small[4:8], axis=1, keepdims=True)
    ratio = jnp.sqrt(sums / (sums[3:4] * width))
    lane = lax.broadcasted_iota(jnp.int32, (1, 3), 1)
    pair = jnp.where(lane == 1, ratio[0:1], ratio[2:3])
    rms_o[...] = jnp.where(lane == 0, ratio[1:2], pair)
    for place in range(4):
        fetches[place].wait()
        wide[place] = low[place].astype(F32)
        stores[place].start()
    for enter, leave in moves:
        enter.wait()
        leave.start()
    for store in stores:
        store.wait()
    for _, leave in moves:
        leave.wait()


def place_outputs(out, ig, gin, gback, q, k, v, o, small, experts, ntasks):
    width = small.shape[1]
    vm = pl.BlockSpec(memory_space=VM)
    anywhere = pl.BlockSpec(memory_space=pl.ANY)
    shape = jax.ShapeDtypeStruct
    return pl.pallas_call(
        outputs_kernel,
        in_specs=[anywhere] * 8 + [vm],
        out_specs=[anywhere] * 8 + [vm] * 6,
        out_shape=[shape(a.shape, a.dtype) for a in (out, ig, gin, gback)]
        + [shape(q.shape, F32)] * 4
        + [shape((1, width), F32)] * 4
        + [shape((experts, ntasks), F32), shape((1, 3), F32)],
        scratch_shapes=[
            VM((4,) + q.shape, BF),
            VM((4,) + q.shape, F32),
            VM((2,) + out.shape, BF),
            VM(gin.shape, F32),
            VM(gback.shape, F32),
            pltpu.SemaphoreType.DMA((16,)),
        ],
        compiler_params=pltpu.CompilerParams(vmem_limit_bytes=60 * 2**20),
    )(out, ig, gin, gback, q, k, v, o, small)


def local(
    tokens,
    lengths,
    tasks,
    routes,
    gate_table,
    ln1_gain,
    ln1_bias,
    ln2_gain,
    ln2_bias,
    w_query,
    w_key,
    w_value,
    w_out,
    w_in,
    w_back,
    cotangent,
):
    sents, slot, width = tokens.shape
    heads = HEADS
    head = width // heads
    experts = gate_table.shape[1]
    ntasks = routes.shape[0]
    capacity = max(1, 4 * sents // experts)
    scale = 1.0 / jnp.sqrt(jnp.float32(head))
    task_hot = (tasks[:, None] == jnp.arange(ntasks)[None, :]).astype(jnp.int32)
    chosen = jnp.sum(task_hot[:, :, None] * routes[None, :, :], axis=1)
    flat = chosen.reshape(-1)
    order = jnp.arange(2 * sents)
    earlier = (flat[:, None] == flat[None, :]) & (order[None, :] < order[:, None])
    rank = jnp.sum(earlier.astype(jnp.int32), axis=1)
    slot_id = flat * capacity + rank
    placed = rank < capacity
    dispatch = (
        (jnp.arange(experts * capacity)[:, None] == slot_id[None, :]) & placed[None, :]
    ).astype(jnp.bfloat16)
    collect = dispatch.T
    expert_hot = (chosen[:, :, None] == jnp.arange(experts)[None, None, :]).astype(jnp.float32)
    valid = (jnp.arange(slot)[None, :] < lengths[:, None]).astype(jnp.float32)
    keymask = valid[:, None, None, :] > 0.5
    mask3 = valid[:, :, None]
    xfull = tokens.astype(jnp.float32)
    normed1, inverse1 = normalize(xfull)
    act = (normed1 * ln1_gain + ln1_bias).astype(jnp.bfloat16).reshape(-1, width)
    query = project(act, w_query).astype(jnp.bfloat16).reshape(sents, slot, heads, head)
    keyed = project(act, w_key).astype(jnp.bfloat16).reshape(sents, slot, heads, head)
    valued = project(act, w_value).astype(jnp.bfloat16).reshape(sents, slot, heads, head)

    def scores_of(qpart, kpart):
        raw = (
            jnp.einsum("sqhd,skhd->shqk", qpart, kpart, preferred_element_type=jnp.float32) * scale
        )
        return jnp.where(keymask, raw, -1000000000.0)

    scores = scores_of(query, keyed)
    peak = jnp.max(scores, axis=-1, keepdims=True)
    logsum = peak + jnp.log(jnp.sum(jnp.exp(scores - peak), axis=-1, keepdims=True))
    prob_low = jnp.exp(scores - logsum).astype(jnp.bfloat16)
    context = jnp.einsum("shqk,skhd->sqhd", prob_low, valued, preferred_element_type=jnp.float32)
    context = context.astype(jnp.bfloat16).reshape(-1, width)
    attention_block = project(context, w_out).reshape(sents, slot, width)
    hidden_res = xfull + attention_block
    normed2, inverse2 = normalize(hidden_res)
    mixed = (normed2 * ln2_gain + ln2_bias).astype(jnp.bfloat16)
    table_rows = jnp.dot(task_hot.astype(jnp.float32), gate_table, precision=lax.Precision.HIGHEST)
    picked = jnp.sum(expert_hot * table_rows[:, None, :], axis=-1)
    gate_values = jax.nn.softmax(picked, axis=-1)
    grad_total = cotangent.astype(jnp.float32) * mask3
    copies = jnp.broadcast_to(mixed[:, None], (sents, 2, slot, width)).reshape(
        2 * sents, slot * width
    )
    outgoing = (
        project(dispatch, copies).astype(jnp.bfloat16).reshape(experts, capacity, slot, width)
    )
    dycopy = (
        (gate_values[:, :, None, None] * grad_total[:, None])
        .astype(jnp.bfloat16)
        .reshape(2 * sents, slot * width)
    )
    grad_out = (
        project(dispatch, dycopy).astype(jnp.bfloat16).reshape(experts, capacity, slot, width)
    )
    incoming = lax.all_to_all(outgoing, "expert", split_axis=0, concat_axis=0, tiled=True).reshape(
        -1, width
    )
    pre_act, active, produced = expert_forward(incoming, w_in[0], w_back[0])
    returned = lax.all_to_all(
        produced.reshape(experts, capacity, slot, width),
        "expert",
        split_axis=0,
        concat_axis=0,
        tiled=True,
    )
    grad_in = lax.all_to_all(grad_out, "expert", split_axis=0, concat_axis=0, tiled=True).reshape(
        -1, width
    )
    in_local, back_local, dincoming = expert_backward(
        incoming, pre_act, active, grad_in, w_in[0], w_back[0]
    )
    grad_back = lax.all_to_all(
        dincoming.reshape(experts, capacity, slot, width),
        "expert",
        split_axis=0,
        concat_axis=0,
        tiled=True,
    )
    ycopy = project(collect, returned.reshape(experts * capacity, slot * width)).reshape(
        sents, 2, slot, width
    )
    expert_mixture = jnp.sum(gate_values[:, :, None, None] * ycopy, axis=1)
    total = mask3 * (hidden_res + expert_mixture)
    output = total.astype(jnp.bfloat16)
    stats_local = jnp.stack(
        [
            jnp.sum(total * total),
            jnp.sum(mask3 * attention_block * attention_block),
            jnp.sum(mask3 * expert_mixture * expert_mixture),
            jnp.sum(valid),
        ]
    )
    stat_totals = lax.psum(stats_local, ("dp", "expert"))
    gate_dot = jnp.sum(ycopy * grad_total[:, None], axis=(2, 3))
    dpicked = gate_values * (gate_dot - jnp.sum(gate_values * gate_dot, axis=-1, keepdims=True))
    dlogits = jnp.sum(expert_hot * dpicked[:, :, None], axis=1)
    table_grad = jnp.dot(task_hot.T.astype(jnp.float32), dlogits, precision=lax.Precision.HIGHEST)
    dmixed = project(collect, grad_back.reshape(experts * capacity, slot * width)).reshape(
        sents, 2, slot, width
    )
    dmixed = jnp.sum(dmixed, axis=1)
    dres2, gain2_grad, bias2_grad = norm_backward(dmixed, normed2, inverse2, ln2_gain)
    dhidden = grad_total + dres2
    dattn = dhidden.astype(jnp.bfloat16).reshape(-1, width)
    wout_grad = project(context.T, dattn)
    dcontext = project(dattn, w_out.T).astype(jnp.bfloat16).reshape(sents, slot, heads, head)
    again = jnp.exp(scores_of(query, keyed) - logsum)
    dprob = jnp.einsum("sqhd,skhd->shqk", dcontext, valued, preferred_element_type=jnp.float32)
    dscores = (again * (dprob - jnp.sum(dprob * again, axis=-1, keepdims=True))).astype(
        jnp.bfloat16
    )
    dquery = (
        jnp.einsum("shqk,skhd->sqhd", dscores, keyed, preferred_element_type=jnp.float32) * scale
    )
    dkeyed = (
        jnp.einsum("shqk,sqhd->skhd", dscores, query, preferred_element_type=jnp.float32) * scale
    )
    dvalued = jnp.einsum("shqk,sqhd->skhd", prob_low, dcontext, preferred_element_type=jnp.float32)
    dquery = dquery.astype(jnp.bfloat16).reshape(-1, width)
    dkeyed = dkeyed.astype(jnp.bfloat16).reshape(-1, width)
    dvalued = dvalued.astype(jnp.bfloat16).reshape(-1, width)
    wq_grad = project(act.T, dquery)
    wk_grad = project(act.T, dkeyed)
    wv_grad = project(act.T, dvalued)
    dact = project(dquery, w_query.T) + project(dkeyed, w_key.T) + project(dvalued, w_value.T)
    dres1, gain1_grad, bias1_grad = norm_backward(
        dact.reshape(sents, slot, width), normed1, inverse1, ln1_gain
    )
    input_grad = (dhidden + dres1).astype(jnp.bfloat16)
    members = (
        wq_grad,
        wk_grad,
        wv_grad,
        wout_grad,
        gain1_grad,
        bias1_grad,
        gain2_grad,
        bias2_grad,
        table_grad,
    )
    members = members + ()
    summed = lax.psum(members, ("dp", "expert"))
    rms = jnp.sqrt(stat_totals[0:3] / (stat_totals[3] * width))
    in_share, back_share = (
        lax.psum_scatter(
            in_local.astype(jnp.bfloat16), "dp", scatter_dimension=0, tiled=True
        ).astype(jnp.float32),
        lax.psum_scatter(
            back_local.astype(jnp.bfloat16), "dp", scatter_dimension=0, tiled=True
        ).astype(jnp.float32),
    )
    return (
        output,
        input_grad,
        summed[8],
        summed[4],
        summed[5],
        summed[6],
        summed[7],
        summed[0],
        summed[1],
        summed[2],
        summed[3],
        in_share[None],
        back_share[None],
        rms,
    )


def local_plane(
    depth,
    tokens,
    lengths,
    tasks,
    routes,
    gate_table,
    ln1_gain,
    ln1_bias,
    ln2_gain,
    ln2_bias,
    w_query,
    w_key,
    w_value,
    w_out,
    w_in,
    w_back,
    cotangent,
):
    experts = gate_table.shape[1]
    sents, slot, width = tokens.shape
    heads = HEADS
    capacity = max(1, 4 * sents // experts)
    (
        act, query, keyed, valued, context, prob, hidden, mixed, attn_sum, plan, places,
        gate_slots, near, far, core,
    ) = attention_forward(
        tokens, lengths, w_query, w_key, w_value, w_out, ln1_gain, ln1_bias, ln2_gain, ln2_bias,
        tasks, routes.T, gate_table.T, cotangent, heads, capacity,
    )
    dmixed, parts_back, cores_back, in_local, back_local, slot_dots = expert_exchange(
        places, gate_slots, mixed, cotangent, near, far, core, w_in[0], w_back[0], capacity, depth
    )
    input_grad, output, sum_q, sum_k, sum_v, sum_o, in_share, back_share, small = (
        backward_exchange(
            depth, lengths, tokens, cotangent, dmixed, hidden, act, query, keyed, valued,
            context, prob, w_query, w_key, w_value, w_out, ln1_gain, ln2_gain, attn_sum, plan,
            tasks, slot_dots, parts_back, cores_back, in_local, back_local, heads,
        )
    )
    (
        output, input_grad, in_share, back_share, grad_q, grad_k, grad_v, grad_o,
        gain1, bias1, gain2, bias2, table_grad, rms,
    ) = place_outputs(
        output, input_grad, in_share, back_share, sum_q, sum_k, sum_v, sum_o, small,
        experts, gate_table.shape[0],
    )
    return (
        output,
        input_grad,
        table_grad.T,
        gain1.reshape(-1),
        bias1.reshape(-1),
        gain2.reshape(-1),
        bias2.reshape(-1),
        grad_q,
        grad_k,
        grad_v,
        grad_o,
        in_share[None],
        back_share[None],
        rms.reshape(-1),
    )


def solution(mesh):
    in_specs = (
        P(("dp", "expert"), None, None),
        P(("dp", "expert")),
        P(("dp", "expert")),
        P(),
        P(),
        P(),
        P(),
        P(),
        P(),
        P(),
        P(),
        P(),
        P(),
        P("expert", None, None),
        P("expert", None, None),
        P(("dp", "expert"), None, None),
    )
    out_specs = (
        P(("dp", "expert"), None, None),
        P(("dp", "expert"), None, None),
        P(),
        P(),
        P(),
        P(),
        P(),
        P(),
        P(),
        P(),
        P(),
        P("expert", "dp", None),
        P("expert", "dp", None),
        P(),
    )
    plane = dict(mesh.shape)["expert"]
    depth = dict(mesh.shape)["dp"]
    cube = plane == 2 * 2 * 2 and depth > 3
    body = functools.partial(local_plane, depth) if cube else local
    return jax.shard_map(body, mesh=mesh, in_specs=in_specs, out_specs=out_specs, check_vma=False)
```

```python
import functools

import jax
import jax.numpy as jnp
from jax import lax
from jax.experimental import pallas as pl
from jax.experimental.pallas import tpu as pltpu
from jax.sharding import PartitionSpec as P

HEADS = 8


def normalize(value):
    centered = value - jnp.mean(value, axis=-1, keepdims=True)
    variance = jnp.mean(centered * centered, axis=-1, keepdims=True)
    inverse = lax.rsqrt(variance + 1e-05)
    return (centered * inverse, inverse)


def norm_backward(grad, normed, inverse, gain):
    scaled = grad * gain
    inner = scaled - jnp.mean(scaled, axis=-1, keepdims=True)
    inner = inner - normed * jnp.mean(scaled * normed, axis=-1, keepdims=True)
    return (inverse * inner, jnp.sum(grad * normed, axis=(0, 1)), jnp.sum(grad, axis=(0, 1)))


def project(left, right):
    return jnp.dot(left, right, preferred_element_type=jnp.float32)


def expert_forward(incoming, first, second):
    pre_act = project(incoming, first)
    active = jax.nn.gelu(pre_act).astype(jnp.bfloat16)
    produced = project(active, second).astype(jnp.bfloat16)
    return (pre_act, active, produced)


def expert_backward(incoming, pre_act, active, grad_in, first, second):
    dactive = project(grad_in, second.T)
    back_local = project(active.T, grad_in)
    gelu_pull = jax.vjp(jax.nn.gelu, pre_act)[1]
    dpre = gelu_pull(dactive)[0].astype(jnp.bfloat16)
    in_local = project(incoming.T, dpre)
    dincoming = project(dpre, first.T).astype(jnp.bfloat16)
    return (in_local, back_local, dincoming)


BF = jnp.bfloat16
F32 = jnp.float32
VM = pltpu.VMEM


def mm(a, b, ca=1, cb=0):
    return lax.dot_general(a, b, (((ca,), (cb,)), ((), ())), preferred_element_type=F32)


def block_diagonal(group, slot, head):
    shape = (group * slot, group * head)
    rows = lax.broadcasted_iota(jnp.int32, shape, 0) // slot
    cols = lax.broadcasted_iota(jnp.int32, shape, 1) // head
    return rows == cols


def spread(part, mask, group):
    return jnp.where(mask, jnp.concatenate([part] * group, axis=0), jnp.zeros((), part.dtype))


def fold(product, mask, slot, group):
    kept = jnp.where(mask, product, 0.0)
    total = kept[0:slot]
    for one in range(1, group):
        total = total + kept[one * slot : (one + 1) * slot]
    return total


def attend(query, keyed, valued, length, mask, slot, group, scale):
    scores = mm(keyed, spread(query, mask, group), 1, 1) * scale
    place = lax.broadcasted_iota(jnp.int32, scores.shape, 0)
    scores = jnp.where(place < length, scores, -1000000000.0)
    raised = jnp.exp(scores - jnp.max(scores, axis=0, keepdims=True))
    prob = raised / jnp.sum(raised, axis=0, keepdims=True)
    context = fold(mm(prob.astype(BF), valued, 0, 0), mask, slot, group)
    return prob, context


def route_tables(cap, tasks, lengths, routes, gate_table):
    sents = tasks.shape[1]
    experts, ntasks = gate_table.shape
    iota = lambda rows, cols, axis: lax.broadcasted_iota(jnp.int32, (rows, cols), axis)
    hot = (iota(ntasks, sents, 0) == tasks).astype(F32)
    exact = functools.partial(
        lax.dot_general,
        dimension_numbers=(((1,), (0,)), ((), ())),
        precision=lax.Precision.HIGHEST,
        preferred_element_type=F32,
    )
    chosen = exact(routes.astype(F32), hot)
    first, second = chosen[0:1], chosen[1:2]
    expert = iota(experts, sents, 0).astype(F32)
    is_first, is_second = expert == first, expert == second
    hit = jnp.logical_or(is_first, is_second)
    before = (iota(sents, sents, 0) < iota(sents, sents, 1)).astype(BF)
    rank = mm(hit.astype(F32).astype(BF), before)
    place = jnp.where(hit, jnp.where(rank < cap, rank, -1.0), -1.0)
    logits = exact(gate_table, hot)
    one = jnp.sum(jnp.where(is_first, logits, 0.0), axis=0, keepdims=True)
    two = jnp.sum(jnp.where(is_second, logits, 0.0), axis=0, keepdims=True)
    peak = jnp.maximum(one, two)
    one, two = jnp.exp(one - peak), jnp.exp(two - peak)
    gate = jnp.where(is_first, one / (one + two), 0.0)
    gate = gate + jnp.where(is_second, two / (one + two), 0.0)
    lane = iota(experts, 128, 1)
    index = iota(experts, sents, 1).astype(F32)
    table = jnp.zeros((experts, 128), F32)
    gates = jnp.zeros((experts, 128), F32)
    for j in range(cap):
        here = place == float(j)
        pick = lambda value: jnp.sum(jnp.where(here, value, 0.0), axis=1, keepdims=True)
        table = jnp.where(lane == j, pick(index), table)
        table = jnp.where(lane == cap + j, pick(lengths.astype(F32)), table)
        gates = jnp.where(lane == j, pick(gate), gates)
    shift = (iota(sents, 128, 1) == iota(sents, 128, 0) + 2 * cap).astype(BF)
    spots = mm((place + 1.0).astype(BF), shift)
    inside = jnp.logical_and(lane >= 2 * cap, lane < 2 * cap + sents)
    table = jnp.where(inside, spots - 1.0, table)
    return table.astype(jnp.int32), gates, hit.astype(F32), place, gate


def attention_forward_kernel(
    heads, cap, steps, len_ref, x_ref, wq, wk, wv, wo, g1, b1, g2, b2, tasks, lengths, routes,
    gate_table, cot_in,
    act_o, q_o, k_o, v_o, ctx_o, p_o, h_o, m_o, st_o, plan_o, tab_o, gates_o, near_o, far_o,
    core_o, cot, tab_s, gates_s, sends, recvs, local,
):
    count, slot, width = x_ref.shape
    head = width // heads
    group = max(1, min(heads, 256 // head))
    span = group * head
    step = pl.program_id(0)
    scale = head ** -0.5
    mask = block_diagonal(group, slot, head)
    experts = gate_table.shape[0]
    me = lax.axis_index("expert")
    half = cot.shape[0] // 2
    early = near_o.shape[0]
    copies = [
        remote(cot.at[pl.ds(0, early)], near_o, sends, recvs, 0, NEAR),
        remote(cot.at[pl.ds(half, early)], far_o, sends, recvs, 1, FAR),
        remote(cot, core_o, sends, recvs, 2, CORE),
    ]
    for relation in range(1, 8):
        there = plane_peer(relation)
        copies += [
            remote(tab_s.at[there], tab_o.at[me], sends, recvs, 1 + 2 * relation, relation),
            remote(gates_s.at[there], gates_o.at[me], sends, recvs, 2 + 2 * relation, relation),
        ]
    load = pltpu.make_async_copy(cot_in, cot, local.at[2])
    own = [
        pltpu.make_async_copy(tab_s.at[me], tab_o.at[me], local.at[0]),
        pltpu.make_async_copy(gates_s.at[me], gates_o.at[me], local.at[1]),
    ]

    @pl.when(step == 0)
    def _():
        load.start()
        greet()
        table, gates, hit, place, gate = route_tables(
            cap, tasks[...], lengths[...], routes[...], gate_table[...]
        )
        for e in range(experts):
            tab_s[e] = jnp.broadcast_to(table[e : e + 1], (8, 128))
            gates_s[e] = jnp.broadcast_to(gates[e : e + 1], (8, 128))
        plan_o[0:experts] = hit
        plan_o[experts : 2 * experts] = place
        plan_o[2 * experts : 3 * experts] = gate
        st_o[...] = jnp.zeros_like(st_o)

    @pl.when(step == min(1, steps - 1))
    def _():
        await_greetings()
        load.wait()
        for copy in copies + own:
            copy.start()

    x = x_ref[...].astype(F32).reshape(count * slot, width)
    normed, _ = normalize(x)
    act = (normed * g1[...] + b1[...]).astype(BF)
    act_o[...] = act
    q_o[...] = mm(act, wq[...]).astype(BF)
    k_o[...] = mm(act, wk[...]).astype(BF)
    v_o[...] = mm(act, wv[...]).astype(BF)
    for s in range(count):
        length = len_ref[step * count + s]
        rows = slice(s * slot, (s + 1) * slot)
        for part in range(heads // group):
            cols = slice(part * span, (part + 1) * span)
            prob, context = attend(
                q_o[rows, cols], k_o[rows, cols], v_o[rows, cols], length, mask, slot, group, scale
            )
            p_o[s, part] = prob
            ctx_o[rows, cols] = context.astype(BF)
    attn = mm(ctx_o[...], wo[...])
    hidden = x + attn
    h_o[...] = hidden
    normed2, _ = normalize(hidden)
    m_o[...] = (normed2 * g2[...] + b2[...]).astype(BF).reshape(count, slot, width)
    place = lax.broadcasted_iota(jnp.int32, (slot, width), 0)
    total = jnp.zeros((1, width), F32)
    for s in range(count):
        length = len_ref[step * count + s]
        part = attn[s * slot : (s + 1) * slot]
        total = total + jnp.sum(jnp.where(place < length, part * part, 0.0), axis=0, keepdims=True)
    st_o[...] += total

    @pl.when(step == pl.num_programs(0) - 1)
    def _():
        for copy in copies + own:
            copy.wait()


def attention_forward(
    tokens, lengths, wq, wk, wv, wo, g1, b1, g2, b2, tasks, routes, gate_table, cot, heads, cap
):
    sents, slot, width = tokens.shape
    experts = gate_table.shape[0]
    count = 4 if sents % 4 == 0 else 1
    rows = count * slot
    head = width // heads
    group = max(1, min(heads, 256 // head))
    whole = lambda *shape: pl.BlockSpec(shape, lambda i: (0,) * len(shape))
    flat = pl.BlockSpec((rows, width), lambda i: (i, 0))
    cube = pl.BlockSpec((count, slot, width), lambda i: (i, 0, 0))
    probs = pl.BlockSpec((count, heads // group, slot, group * slot), lambda i: (i, 0, 0, 0))
    anywhere = pl.BlockSpec(memory_space=pl.ANY)
    shape = jax.ShapeDtypeStruct
    total = sents * slot
    early = (sents // 4, slot, width)
    return pl.pallas_call(
        functools.partial(attention_forward_kernel, heads, cap, sents // count),
        grid=(sents // count,),
        in_specs=[pl.BlockSpec(memory_space=pltpu.SMEM), cube]
        + [whole(width, width)] * 4
        + [whole(1, width)] * 4
        + [whole(1, sents)] * 2
        + [whole(*routes.shape), whole(*gate_table.shape), anywhere],
        out_specs=[flat] * 5
        + [probs, flat, cube, whole(1, width), whole(3 * experts, sents)]
        + [anywhere] * 5,
        out_shape=[shape((total, width), BF)] * 5
        + [
            shape((sents, heads // group, slot, group * slot), F32),
            shape((total, width), F32),
            shape((sents, slot, width), BF),
            shape((1, width), F32),
            shape((3 * experts, sents), F32),
            shape((experts, 8, 128), jnp.int32),
            shape((experts, 8, 128), F32),
            shape(early, BF),
            shape(early, BF),
            shape(tokens.shape, BF),
        ],
        scratch_shapes=[
            VM(cot.shape, BF),
            VM((experts, 8, 128), jnp.int32),
            VM((experts, 8, 128), F32),
            pltpu.SemaphoreType.DMA((17,)),
            pltpu.SemaphoreType.DMA((17,)),
            pltpu.SemaphoreType.DMA((3,)),
        ],
        compiler_params=pltpu.CompilerParams(
            dimension_semantics=("arbitrary",), vmem_limit_bytes=56 * 2**20,
            collective_id=0, has_side_effects=True,
        ),
        cost_estimate=pl.CostEstimate(
            flops=8 * total * width * width + 4 * total * slot * width,
            bytes_accessed=16 * total * width,
            transcendentals=total * slot * heads,
        ),
    )(
        lengths, tokens, wq, wk, wv, wo, g1[None], b1[None], g2[None], b2[None],
        tasks[None], lengths[None], routes, gate_table, cot,
    )


def row_sum(value, width):
    return jnp.sum(value, axis=0, keepdims=True)


def layer_norm_pull(grad, normed, inverse, gain):
    scaled = grad * gain
    inner = scaled - jnp.mean(scaled, axis=-1, keepdims=True)
    inner = inner - normed * jnp.mean(scaled * normed, axis=-1, keepdims=True)
    return inverse * inner


def attention_pull(dcontext, query, keyed, valued, prob, mask, slot, group, scale):
    low = prob.astype(BF)
    dspread = spread(dcontext, mask, group)
    dprob = mm(valued, dspread, 1, 1)
    inner = jnp.sum(dprob * prob, axis=0, keepdims=True)
    dscores = (prob * (dprob - inner)).astype(BF)
    dquery = fold(mm(dscores, keyed, 0, 0), mask, slot, group) * scale
    dkeyed = mm(dscores, spread(query, mask, group)) * scale
    dvalued = mm(low, dspread)
    return dquery.astype(BF), dkeyed.astype(BF), dvalued.astype(BF)


MESH_ID = pl.DeviceIdType.MESH
CORE, NEAR, FAR = 1, 2, 4


def plane_peer(relation):
    me = lax.axis_index("expert")
    bits = []
    for bit in (CORE, NEAR, FAR):
        value = (me // bit) % 2
        bits.append((1 - value if relation & bit else value) * bit)
    return bits[0] + bits[1] + bits[2]


def remote(src, dst, sends, recvs, index, relation):
    return pltpu.make_async_remote_copy(
        src_ref=src,
        dst_ref=dst,
        send_sem=sends.at[index],
        recv_sem=recvs.at[index],
        device_id=(lax.axis_index("dp"), plane_peer(relation)),
        device_id_type=MESH_ID,
    )


def line_peer(offset, depth):
    return lax.rem(lax.axis_index("dp") + offset, depth)


def along(src, dst, sends, recvs, index, offset, depth):
    return pltpu.make_async_remote_copy(
        src_ref=src,
        dst_ref=dst,
        send_sem=sends.at[index],
        recv_sem=recvs.at[index],
        device_id=(line_peer(offset, depth), lax.axis_index("expert")),
        device_id_type=MESH_ID,
    )


def greet(depth=1):
    barrier = pltpu.get_barrier_semaphore()
    targets = [(lax.axis_index("dp"), plane_peer(relation)) for relation in range(1, 8)]
    for offset in range(1, depth):
        targets.append((line_peer(offset, depth), lax.axis_index("expert")))
    for target in targets:
        pl.semaphore_signal(barrier, inc=1, device_id=target, device_id_type=MESH_ID)


def await_greetings(depth=1):
    pl.semaphore_wait(pltpu.get_barrier_semaphore(), 6 + depth)


def gather_copies(own, held, sends, recvs, base, early=0):
    half = own.shape[0] // 2
    low, high = pl.ds(0, half), pl.ds(half, half)
    near, far = pl.ds(early, half - early), pl.ds(half + early, half - early)
    plan = [
        (own.at[near], held[2].at[near], NEAR),
        (own.at[far], held[4].at[far], FAR),
        (own, held[1], CORE),
        (own.at[high], held[2].at[high], NEAR),
        (own.at[low], held[4].at[low], FAR),
        (held[2].at[low], held[6].at[low], FAR),
        (held[4].at[high], held[6].at[high], NEAR),
        (held[2], held[3], CORE),
        (held[4], held[5], CORE),
        (held[6], held[7], CORE),
    ]
    return [
        remote(src, dst, sends, recvs, base + place, relation)
        for place, (src, dst, relation) in enumerate(plan)
    ]


def return_copies(parts, cores, sides, sends, recvs, base):
    half = parts[0].shape[0] // 2
    low, high = pl.ds(0, half), pl.ds(half, half)
    plan = [
        (parts[1], cores[0], CORE),
        (parts[3], cores[2], CORE),
        (parts[5], cores[4], CORE),
        (parts[7], cores[6], CORE),
        (parts[2].at[low], sides[0], NEAR),
        (parts[6].at[low], sides[1], NEAR),
        (parts[4].at[high], sides[2], FAR),
        (parts[6].at[high], sides[3], FAR),
        (parts[4].at[low], sides[4], FAR),
        (parts[2].at[high], sides[5], NEAR),
    ]
    return [
        remote(src, dst, sends, recvs, base + place, relation)
        for place, (src, dst, relation) in enumerate(plan)
    ]


def add_into(target, start, other, count):
    def one(i, carry):
        target[start + i] = target[start + i] + other[i]
        return carry

    lax.fori_loop(0, count, one, 0, unroll=8)


def return_finish(parts, sides, back):
    half = parts[0].shape[0] // 2
    back[5].wait_recv()
    add_into(parts[4], 0, sides[1], half)
    back[8].start()
    back[7].wait_recv()
    add_into(parts[2], half, sides[3], half)
    back[9].start()
    back[4].wait_recv()
    add_into(parts[0], 0, sides[0], half)
    back[6].wait_recv()
    add_into(parts[0], half, sides[2], half)
    back[8].wait_recv()
    add_into(parts[0], 0, sides[4], half)
    back[9].wait_recv()
    add_into(parts[0], half, sides[5], half)
    for copy in back:
        copy.wait_send()


GELU_A = 0.7978845608028654
GELU_B = 0.044715


def expert_steps():
    waves = (((0, 1), (0,)), ((2, 3, 4, 5), (2,)), ((6, 7), ()))
    steps = []
    for taken, closed in waves:
        steps += [("F", r) for r in taken] + [("B", r) for r in taken]
        steps += [("U", r) for r in closed] + [("V", r) for r in closed]
    return steps


def expert_kernel(
    cap, depth, tab, gates, m_in, cot_in, near_in, far_in, core_in, win_in, wback_in,
    dm_o, py_o, cy_o, gin_o, gback_o, dg_o, *scratch
):
    sents, slot, width = m_in.shape
    hidden = win_in.shape[1]
    half = sents // 2
    held_m = dict(zip(range(8), scratch[0:8]))
    held_c = dict(zip(range(8), scratch[8:16]))
    sides = scratch[16:22]
    win, wback = scratch[22:24]
    first_part, xs, dys, zs, dus, ys, dms, stage, dg_s, accb, acci = scratch[24:35]
    line_in, line_back, sends, recvs, local, free = scratch[35:]
    parts = {
        0: first_part, 1: held_c[1], 2: held_m[0], 3: held_c[3],
        4: held_c[0], 5: held_c[5], 6: held_c[6], 7: held_c[7],
    }
    cores = {0: held_m[1], 2: held_m[3], 4: held_m[5], 6: held_m[7]}
    sets = {r: r - 2 if r in (4, 5) else r % 2 for r in range(8)}
    me = lax.axis_index("expert")
    z = lax.axis_index("dp")
    tile = min(512, hidden)
    rows = cap * slot
    early = near_in.shape[0]
    low, high = pl.ds(0, half), pl.ds(half, half)
    loads = [
        pltpu.make_async_copy(src, dst, local.at[2 + place])
        for place, (src, dst) in enumerate(
            [
                (m_in, held_m[0]),
                (cot_in, held_c[0]),
                (win_in, win),
                (wback_in, wback),
                (core_in, held_c[1]),
                (near_in, held_c[2].at[pl.ds(0, early)]),
                (far_in, held_c[4].at[pl.ds(half, early)]),
            ]
        )
    ]
    for load in loads:
        load.start()
    greet(depth)
    to_m = gather_copies(held_m[0], held_m, sends, recvs, 0)
    to_c = gather_copies(held_c[0], held_c, sends, recvs, 10, early)
    back = return_copies(parts, cores, sides, sends, recvs, 20)
    gates_back = {
        r: remote(dg_s.at[r], dg_o.at[me], sends, recvs, 30 + r, r) for r in range(1, 8)
    }
    outputs_back = {
        r: remote(stage, cy_o.at[r // 2], sends, recvs, 38 + r // 2, CORE) for r in (1, 3, 5, 7)
    }
    outputs_here = {
        r: pltpu.make_async_copy(stage, py_o.at[r // 2], local.at[0]) for r in (0, 2, 4, 6)
    }

    def line_first(right, array):
        offset = 1 if right else depth - 1
        s = depth - 1 if right else 0
        source, into = ((win, line_in), (wback, line_back))[array]
        share = source.shape[0] // depth
        here = pl.ds(s * share, share)
        index = 42 + 2 * int(right) + array
        return here, along(source.at[here], into, sends, recvs, index, offset, depth)

    def line_open(array):
        for right in (True, False):

            @pl.when(z == (0 if right else depth - 1))
            def _():
                line_first(right, array)[1].start()

    accb[...] = jnp.zeros_like(accb)
    acci[...] = jnp.zeros_like(acci)
    for load in loads[0:2]:
        load.wait()
    await_greetings(depth)
    for index in (0, 1, 2, 3, 4):
        to_m[index].start()
    for index in (0, 1, 3, 4):
        to_c[index].start()
    place = lax.broadcasted_iota(jnp.int32, (slot, width), 0)
    for load in loads[2:4]:
        load.wait()

    def before_forward(r):
        if r == 1:
            to_m[2].wait_recv()
        if r == 2:
            to_m[0].wait_recv()
            to_m[5].start()
            to_m[1].wait_recv()
            to_m[6].start()
            to_m[3].wait_recv()
            to_m[7].start()
            to_m[4].wait_recv()
            to_m[8].start()
        if r == 3:
            to_m[7].wait_recv()
        if r == 4:
            for load in loads[5:7]:
                load.wait()
            to_c[0].wait_recv()
            to_c[5].start()
            to_c[1].wait_recv()
            to_c[6].start()
        if r == 5:
            to_m[8].wait_recv()
        if r == 6:
            to_m[5].wait_recv()
            to_m[6].wait_recv()
            to_m[9].start()
        if r == 7:
            to_m[9].wait_recv()
        source = plane_peer(r)

        def fetch(j, carry):
            xs[sets[r], j] = held_m[r][tab[source, 0, j]]
            return carry

        lax.fori_loop(0, cap, fetch, 0, unroll=True)
        if r % 2 == 1:
            pl.semaphore_signal(
                free.at[r // 2], inc=1, device_id=(z, plane_peer(CORE)), device_id_type=MESH_ID
            )

    def after_forward(r):
        source = plane_peer(r)
        if r > 0 and r % 2 == 1:
            outputs_here[r - 1].wait()
        if r > 0 and r % 2 == 0:
            outputs_back[r - 1].wait_send()

        def give(i, carry):
            index = tab[source, 0, 2 * cap + i]
            there = jnp.maximum(index, 0)
            gate = jnp.where(index >= 0, gates[source, 0, there], 0.0)
            stage[i] = (ys[sets[r], there].astype(F32) * gate).astype(BF)
            return carry

        lax.fori_loop(0, sents, give, 0, unroll=8)
        if r % 2 == 0:
            outputs_here[r].start()
        else:
            outputs_back[r].start()

    def before_backward(r):
        if r == 1:
            loads[4].wait()
        if r == 2:
            to_c[3].wait_recv()
            to_c[7].start()
            to_c[4].wait_recv()
            to_c[8].start()
        if r == 3:
            to_c[7].wait_recv()
        if r == 5:
            to_c[8].wait_recv()
        if r == 6:
            to_c[5].wait_recv()
            to_c[6].wait_recv()
            to_c[9].start()
        if r == 7:
            to_c[9].wait_recv()
        source = plane_peer(r)

        def fetch(j, carry):
            index = tab[source, 0, j]
            length = tab[source, 0, cap + j]
            gate = gates[source, 0, j]
            gt = jnp.where(place < length, held_c[r][index].astype(F32), 0.0)
            dys[sets[r], j] = (gt * gate).astype(BF)
            product = ys[sets[r], j].astype(F32) * gt
            total = jnp.sum(jnp.sum(product, axis=0, keepdims=True), axis=1, keepdims=True)
            if r == 0:
                dg_o[me, pl.ds(j, 1)] = jnp.broadcast_to(total, (1, 128))
            else:
                dg_s[r, pl.ds(j, 1)] = jnp.broadcast_to(total, (1, 128))
            return carry

        lax.fori_loop(0, cap, fetch, 0, unroll=True)
        if r > 0:
            gates_back[r].start()

    def after_backward(r):
        source = plane_peer(r)
        if r == 2:
            for copy in to_m[0:5]:
                copy.wait_send()
        if r == 4:
            for copy in to_c[0:2] + to_c[3:5]:
                copy.wait_send()
        if r == 6:
            to_c[9].wait_send()

        def give(i, carry):
            index = tab[source, 0, 2 * cap + i]
            kept = dms[jnp.maximum(index, 0)]
            parts[r][i] = jnp.where(index >= 0, kept, jnp.zeros_like(kept))
            return carry

        lax.fori_loop(0, sents, give, 0, unroll=8)
        if r % 2 == 1:
            pl.semaphore_wait(free.at[r // 2], 1)
            back[r // 2].start()
        if r == 4:
            join(2)
            back[4].start()

    def join(r):
        back[r // 2].wait_recv()
        add_into(parts[r], 0, cores[r], sents)

    def after_back_grad(r):
        if r == 2:
            join(4)
            back[6].start()

    def after_in_grad(r):
        if r == 2:
            join(0)

    tiles = [slice(f * tile, (f + 1) * tile) for f in range(hidden // tile)]

    def forward(spot):
        x = xs[spot].reshape(rows, width)
        here = pl.ds(pl.multiple_of(spot * rows, rows), rows)
        for cols in tiles:
            u = mm(x, win[:, cols])
            square = u * u
            th = jnp.tanh(u * (GELU_A + GELU_A * GELU_B * square))
            cdf = 0.5 + 0.5 * th
            slope = cdf + (0.5 * u) * (1.0 - th * th) * (GELU_A + 3 * GELU_A * GELU_B * square)
            zs[here, cols] = (u * cdf).astype(BF)
            dus[here, cols] = slope.astype(BF)
        ys[spot] = mm(zs[here, :], wback[...]).astype(BF).reshape(cap, slot, width)

    def backward(spot):
        dy = dys[spot].reshape(rows, width)
        here = pl.ds(pl.multiple_of(spot * rows, rows), rows)
        for cols in tiles:
            dz = mm(dy, wback[cols, :], 1, 1)
            dus[here, cols] = (dz * dus[here, cols].astype(F32)).astype(BF)
        dms[...] = mm(dus[here, :], win[...], 1, 1).astype(BF).reshape(cap, slot, width)

    def back_grad(count):
        dy = dys[0:count].reshape(count * rows, width)
        for cols in tiles:
            yield cols, mm(zs[0 : count * rows, cols], dy, 0, 0)

    def in_grad(count):
        x = xs[0:count].reshape(count * rows, width)
        for cols in tiles:
            yield cols, mm(x, dus[0 : count * rows, cols], 0, 0)

    def back_pair(spot):
        for cols, total in back_grad(2):
            accb[cols, :] += total

    def in_pair(spot):
        for cols, total in in_grad(2):
            acci[:, cols] += total

    steps = expert_steps()
    actions = {
        "F": (before_forward, forward, after_forward),
        "B": (before_backward, backward, after_backward),
        "U": (None, back_pair, after_back_grad),
        "V": (None, in_pair, after_in_grad),
    }

    def spot_of(t, kind):
        spot = jnp.int32(0)
        for number, (other, r) in enumerate(steps):
            if other == kind and sets[r]:
                spot = spot + jnp.where(t == number, sets[r], 0)
        return spot

    def step(t, carry):
        for kind, (pre, work, post) in actions.items():
            mine = [number for number, (other, _) in enumerate(steps) if other == kind]
            spans = [n for n in mine if n - 1 not in mine]
            ends = [n for n in mine if n + 1 not in mine]
            inside = functools.reduce(
                jnp.logical_or,
                [jnp.logical_and(t >= a, t <= b) for a, b in zip(spans, ends)],
            )

            @pl.when(inside)
            def _():
                if pre is not None:
                    for number in mine:
                        pl.when(t == number)(functools.partial(pre, steps[number][1]))
                work(spot_of(t, kind))
                for number in mine:
                    pl.when(t == number)(functools.partial(post, steps[number][1]))

        return carry

    lax.fori_loop(0, len(steps), step, 0)
    for cols, total in back_grad(4):
        wback[cols, :] = (accb[cols, :] + total).astype(BF)
        if cols.start == 0:
            join(6)
            back[5].start()
            back[7].start()
    line_open(1)
    for cols, total in in_grad(4):
        win[:, cols] = (acci[:, cols] + total).astype(BF)
    line_open(0)
    stores = [
        pltpu.make_async_copy(win, gin_o, local.at[4]),
        pltpu.make_async_copy(wback, gback_o, local.at[5]),
    ]
    for store in stores:
        store.start()
    return_finish(parts, sides, back)
    kept = pltpu.make_async_copy(parts[0], dm_o, local.at[2])
    kept.start()
    for store in stores:
        store.wait()
    for right in (True, False):

        @pl.when(z == (1 if right else depth - 2))
        def _():
            again = []
            for array in (1, 0):
                here, copy = line_first(right, array)
                copy.wait_recv()
                source, into = ((win, line_in), (wback, line_back))[array]
                total = source[here, :].astype(F32) + into[...].astype(F32)
                source[here, :] = total.astype(BF)
                output = (gin_o, gback_o)[array]
                again.append(
                    pltpu.make_async_copy(source.at[here], output.at[here], local.at[6 + array])
                )
                again[-1].start()
            for store in again:
                store.wait()

    kept.wait()
    for right in (True, False):

        @pl.when(z == (0 if right else depth - 1))
        def _():
            for array in (0, 1):
                line_first(right, array)[1].wait_send()

    for r in (1, 3, 5, 7):
        outputs_back[r].wait_recv()
    outputs_back[7].wait_send()
    for r in range(1, 8):
        gates_back[r].wait()
    for index in range(5, 10):
        to_m[index].wait_send()
    for index in range(5, 9):
        to_c[index].wait_send()


def expert_exchange(tab, gates, m, cot, near, far, core, win, wback, cap, depth):
    sents, slot, width = m.shape
    hidden = win.shape[1]
    vm = pl.BlockSpec(memory_space=VM)
    sm = pl.BlockSpec(memory_space=pltpu.SMEM)
    anywhere = pl.BlockSpec(memory_space=pl.ANY)
    shape = jax.ShapeDtypeStruct
    cube = (sents, slot, width)
    taken = (cap, slot, width)
    rows = cap * slot
    return pl.pallas_call(
        functools.partial(expert_kernel, cap, depth),
        in_specs=[sm, sm] + [anywhere] * 7,
        out_specs=[anywhere] * 5 + [vm],
        out_shape=[
            shape(cube, BF),
            shape((4,) + cube, BF),
            shape((4,) + cube, BF),
            shape((width, hidden), BF),
            shape((hidden, width), BF),
            shape((8, cap, 128), F32),
        ],
        scratch_shapes=[VM(cube, BF)] * 16
        + [VM((sents // 2, slot, width), BF)] * 6
        + [VM((width, hidden), BF), VM((hidden, width), BF)]
        + [VM(cube, BF)]
        + [VM((4,) + taken, BF)] * 2
        + [VM((4 * rows, hidden), BF)] * 2
        + [VM((4,) + taken, BF), VM(taken, BF), VM(cube, BF)]
        + [VM((8, cap, 128), F32)]
        + [VM((hidden, width), F32), VM((width, hidden), F32)]
        + [VM((width // depth, hidden), BF), VM((hidden // depth, width), BF)]
        + [
            pltpu.SemaphoreType.DMA((46,)),
            pltpu.SemaphoreType.DMA((46,)),
            pltpu.SemaphoreType.DMA((9,)),
            pltpu.SemaphoreType.REGULAR((4,)),
        ],
        compiler_params=pltpu.CompilerParams(
            collective_id=1, has_side_effects=True, vmem_limit_bytes=63 * 2**20
        ),
        cost_estimate=pl.CostEstimate(
            flops=12 * 8 * rows * width * hidden, bytes_accessed=40 * 2**20, transcendentals=0
        ),
    )(tab, gates, m, cot, near, far, core, win, wback)


class Reduction:
    def __init__(self, depth, value, wide, core_r, plane_r, line_s, line_r, final, sems, base):
        self.depth, self.value, self.wide, self.final = depth, value, wide, final
        self.core_r, self.plane_r, self.line_s, self.line_r = core_r, plane_r, line_s, line_r
        sends, recvs = sems
        me = lax.axis_index("expert")
        z = lax.axis_index("dp")
        core = me % 2
        self.half = value.shape[0] // 2
        self.quarter = self.half // 4
        self.share = self.quarter // depth
        self.mine = core * self.half
        self.other = (1 - core) * self.half
        self.block = self.mine + (me // 2) * self.quarter
        self.own = self.block + z * self.share
        self.to_core = remote(wide, core_r, sends, recvs, base, CORE)
        self.to_plane = []
        self.from_plane = []
        for place, relation in enumerate((2, 4, 6)):
            rows = pl.ds((plane_peer(relation) // 2) * self.quarter, self.quarter)
            self.to_plane.append(
                remote(wide.at[rows], plane_r.at[place], sends, recvs, base + 1 + place, relation)
            )
        self.to_line = []
        for offset in range(1, depth):
            rows = pl.ds(line_peer(offset, depth) * self.share, self.share)
            self.to_line.append(
                along(
                    line_s.at[rows], line_r.at[offset - 1], sends, recvs, base + 3 + offset,
                    offset, depth,
                )
            )
        after = base + 3 + depth
        rows = final.at[pl.ds(self.own, self.share)]
        self.back_line = [
            along(rows, rows, sends, recvs, after + offset - 1, offset, depth)
            for offset in range(1, depth)
        ]
        after = after + depth - 1
        rows = final.at[pl.ds(self.block, self.quarter)]
        self.back_plane = [
            remote(rows, rows, sends, recvs, after + place, relation)
            for place, relation in enumerate((2, 4, 6))
        ]
        rows = final.at[pl.ds(self.mine, self.half)]
        self.back_core = remote(rows, rows, sends, recvs, after + 3, CORE)

    @staticmethod
    def semaphores(depth):
        return 2 * depth + 6

    def send_core(self):
        self.wide[...] = self.value[pl.ds(self.other, self.half), :].astype(BF)
        self.to_core.start()

    def send_plane(self):
        self.to_core.wait()
        rows = pl.ds(self.mine, self.half)
        total = self.value[rows, :] + self.core_r[...].astype(F32)
        self.value[rows, :] = total
        self.wide[...] = total.astype(BF)
        for copy in self.to_plane:
            copy.start()

    def send_line(self):
        for copy in self.to_plane:
            copy.wait()
        rows = pl.ds(self.block, self.quarter)
        total = self.value[rows, :]
        for place in range(3):
            total = total + self.plane_r[place].astype(F32)
        self.value[rows, :] = total
        self.line_s[...] = total.astype(BF)
        for copy in self.to_line:
            copy.start()

    def send_back_line(self):
        for copy in self.to_line:
            copy.wait()
        rows = pl.ds(self.own, self.share)
        total = self.value[rows, :]
        for offset in range(1, self.depth):
            total = total + self.line_r[offset - 1].astype(F32)
        self.final[rows, :] = total.astype(BF)
        for copy in self.back_line:
            copy.start()

    def send_back_plane(self):
        for copy in self.back_line:
            copy.wait()
        for copy in self.back_plane:
            copy.start()

    def send_back_core(self):
        for copy in self.back_plane:
            copy.wait()
        self.back_core.start()

    def finish(self):
        self.back_core.wait()


class SmallSum:
    @staticmethod
    def semaphores(depth):
        return 4 + depth

    def __init__(self, depth, value, core_r, plane, line, sems, base):
        sends, recvs = sems
        self.value, self.core_r, self.plane, self.line = value, core_r, plane, line
        self.spot = lax.axis_index("expert") // 2
        self.z = lax.axis_index("dp")
        self.to_core = remote(value, core_r, sends, recvs, base, CORE)
        spot = plane.at[self.spot]
        self.to_plane = [
            remote(spot, spot, sends, recvs, base + 1 + place, relation)
            for place, relation in enumerate((2, 4, 6))
        ]
        spot = line.at[self.z]
        self.to_line = [
            along(spot, spot, sends, recvs, base + 3 + offset, offset, depth)
            for offset in range(1, depth)
        ]

    def send_core(self):
        self.to_core.start()

    def send_plane(self):
        self.to_core.wait()
        self.plane[self.spot] = self.value[...] + self.core_r[...]
        for copy in self.to_plane:
            copy.start()

    def send_line(self):
        for copy in self.to_plane:
            copy.wait()
        total = self.plane[0]
        for place in range(1, 4):
            total = total + self.plane[place]
        self.line[self.z] = total
        for copy in self.to_line:
            copy.start()

    def finish(self, out):
        for copy in self.to_line:
            copy.wait()
        total = self.line[0]
        for place in range(1, self.line.shape[0]):
            total = total + self.line[place]
        out[...] = total


def backward_kernel(
    heads, depth, len_ref, g1, g2, attn_sum, plan, tasks, lengths, dots,
    x_in, cot_in, dm_in, h_in, act_in, q_in, k_in, v_in, ctx_in, p_in,
    wq_in, wk_in, wv_in, wo_in, py, cy, gin, gback,
    ig_out, out_out, gq_o, gk_o, gv_o, go_o, gin_o, gback_o, small_o, *scratch
):
    inputs = (
        x_in, cot_in, dm_in, h_in, act_in, q_in, k_in, v_in, ctx_in, p_in,
        wq_in, wk_in, wv_in, wo_in, gin, gback,
    )
    held = scratch[0:16]
    (
        x_ref, cot_ref, dm_ref, h_ref, act, q, k, v, ctx, p_ref, wq, wk, wv, wo, gin_s, gback_s,
    ) = held
    parts = dict(zip((0, 2, 4, 6), scratch[16:20]))
    cores = dict(zip((0, 2, 4, 6), scratch[20:24]))
    sides = scratch[24:30]
    dh_s, da_s, dctx_s, dq_s, dk_s, dv_s = scratch[30:36]
    red = scratch[36:57]
    line_in, line_back, extra_in, extra_back = scratch[57:61]
    small, small_core, small_plane, small_line = scratch[61:65]
    ig_o, out_o, sends, recvs, local = scratch[65:]
    sems = (sends, recvs)
    sents, slot, width = x_ref.shape
    head = width // heads
    group = max(1, min(heads, 256 // head))
    span = group * head
    scale = head ** -0.5
    count = 4 if sents % 4 == 0 else 1
    rows_per = count * slot
    half = sents // 2
    z = lax.axis_index("dp")

    loads = {
        id(ref): pltpu.make_async_copy(source, ref, local.at[place])
        for place, (source, ref) in enumerate(zip(inputs, held))
    }
    for place, r in enumerate((0, 2, 4, 6)):
        loads[id(parts[r])] = pltpu.make_async_copy(
            py.at[r // 2], parts[r], local.at[16 + place]
        )
        loads[id(cores[r])] = pltpu.make_async_copy(
            cy.at[r // 2], cores[r], local.at[20 + place]
        )

    def begin(*refs):
        for ref in refs:
            loads[id(ref)].start()

    def ready(*refs):
        for ref in refs:
            loads[id(ref)].wait()

    begin(gin_s, gback_s, h_ref, dm_ref, cot_ref, wo, parts[6], cores[6], ctx)
    begin(parts[2], cores[2], parts[4], cores[4], q, k, v, p_ref, act, parts[0], cores[0])
    begin(wq, wk, wv, x_ref)
    greet(depth)
    await_greetings(depth)

    all_parts = {r: parts[r - r % 2] for r in range(8)}
    back = return_copies(all_parts, cores, sides, sends, recvs, 0)

    base = 10
    in_rows = gin_s.shape[0] // depth
    back_rows = gback_s.shape[0] // depth

    def line_piece(s, array, right, last):
        offset = 1 if right else depth - 1
        index = base + (0 if right else 2 * depth) + 2 * s + array
        share, source = ((in_rows, gin_s), (back_rows, gback_s))[array]
        into = (line_in, line_back)[array].at[s]
        if last and not right:
            into = (extra_in, extra_back)[array]
        here = source.at[pl.ds(s * share, share)]
        return along(here, into, sends, recvs, index, offset, depth)

    def add_piece(s, array):
        share, source = ((in_rows, gin_s), (back_rows, gback_s))[array]
        other = (line_in, line_back)[array]
        here = pl.ds(s * share, share)
        source[here, :] = (source[here, :].astype(F32) + other[s].astype(F32)).astype(BF)

    def pieces(right):
        order = range(depth - 1, 0, -1) if right else range(depth - 1)
        return [(s, array) for s in order for array in (0, 1)]

    def start_piece(s, array, right):
        if right:
            line_piece(s, array, True, False).start()
            return
        near = z == s + 1

        @pl.when(near)
        def _():
            line_piece(s, array, False, True).start()

        @pl.when(jnp.logical_not(near))
        def _():
            line_piece(s, array, False, False).start()

    def line_service(t, ahead=0):
        for right in (True, False):
            every = pieces(right)
            edge = 0 if right else depth - 1
            opening = range(2, 3 + ahead) if t == 0 else range(t + ahead + 2, t + ahead + 3)

            @pl.when(z == edge)
            def _():
                for number in opening:
                    if number < len(every):
                        start_piece(*every[number], right)

            for number, (s, array) in enumerate(every):
                away = s if right else depth - 1 - s
                for hops in range(1, away):
                    given = hops == 1 and number < 2
                    if t != (0 if given else number + hops - 1):
                        continue

                    @pl.when(z == (hops if right else depth - 1 - hops))
                    def _():
                        if not given:
                            line_piece(s, array, right, False).wait_recv()
                            add_piece(s, array)
                        start_piece(s, array, right)

    def line_end():
        for s in range(depth):

            @pl.when(z == s)
            def _():
                here = pl.ds(s * in_rows, in_rows)
                there = pl.ds(s * back_rows, back_rows)
                gin_o[...] = gin_s[here, :].astype(F32)
                gback_o[...] = gback_s[there, :].astype(F32)
                if s > 0:
                    for array in (0, 1):
                        line_piece(s, array, True, True).wait_recv()
                    gin_o[...] += line_in[s].astype(F32)
                    gback_o[...] += line_back[s].astype(F32)
                if s < depth - 1:
                    for array in (0, 1):
                        line_piece(s, array, False, True).wait_recv()
                    gin_o[...] += extra_in[...].astype(F32)
                    gback_o[...] += extra_back[...].astype(F32)

        for s in range(depth):
            for array in (0, 1):
                first_right = 1 if s == depth - 1 else 0
                first_left = depth - 2 if s == 0 else depth - 1

                @pl.when(jnp.logical_and(z < s, z >= first_right))
                def _():
                    line_piece(s, array, True, False).wait_send()

                @pl.when(jnp.logical_and(z > s, z <= first_left))
                def _():
                    line_piece(s, array, False, False).wait_send()

    base_red = base + 4 * depth
    per = Reduction.semaphores(depth)
    red_o, red_0, red_1 = [
        Reduction(depth, *red[7 * place : 7 * place + 7], sems, base_red + place * per)
        for place in range(3)
    ]
    sums = SmallSum(
        depth, small, small_core, small_plane, small_line, sems, base_red + 3 * per
    )

    small[...] = jnp.zeros_like(small)
    small[4:5] = attn_sum[...]
    small[7:8, 0:sents] = lengths[...].astype(F32)
    experts = plan.shape[0] // 3
    chunk_place = lax.broadcasted_iota(jnp.int32, (slot, width), 0)

    def masked(ref, c):
        return jnp.concatenate(
            [
                jnp.where(
                    chunk_place < len_ref[c * count + s], ref[c * count + s].astype(F32), 0.0
                )
                for s in range(count)
            ],
            axis=0,
        )

    def flat(ref, c):
        block = ref[pl.ds(c * count, count)]
        return block.astype(F32).reshape(rows_per, width)

    def first(c, carry):
        rows = pl.ds(pl.multiple_of(c * rows_per, rows_per), rows_per)
        normed2, inverse2 = normalize(h_ref[rows, :])
        dm = flat(dm_ref, c)
        dhidden = masked(cot_ref, c) + layer_norm_pull(dm, normed2, inverse2, g2[...])
        small[2:3] += row_sum(dm * normed2, width)
        small[3:4] += row_sum(dm, width)
        dh_s[rows, :] = dhidden
        dattn = dhidden.astype(BF)
        da_s[rows, :] = dattn
        dctx_s[rows, :] = mm(dattn, wo[...], 1, 1).astype(BF)
        return carry

    mask = block_diagonal(group, slot, head)

    def pull(part, into):
        cols = slice(part * span, (part + 1) * span)

        def one(c, carry):
            for s in range(count):
                at = c * count + s
                rows = pl.ds(pl.multiple_of(at * slot, slot), slot)
                dq_s[rows, cols], dk_s[rows, cols], dv_s[rows, cols] = attention_pull(
                    dctx_s[rows, cols], q[rows, cols], k[rows, cols], v[rows, cols],
                    p_ref[at, part], mask, slot, group, scale,
                )
            return carry

        lax.fori_loop(0, sents // count, one, 0)
        into.value[0:width, :] = mm(act[...], dq_s[:, cols], 0, 0)
        into.value[width : 2 * width, :] = mm(act[...], dk_s[:, cols], 0, 0)
        into.value[2 * width : 3 * width, :] = mm(act[...], dv_s[:, cols], 0, 0)
        into.send_core()

    def returned(r):
        ready(parts[r], cores[r])
        add_into(parts[r], 0, cores[r], sents)

    def last(c, carry):
        rows = pl.ds(pl.multiple_of(c * rows_per, rows_per), rows_per)
        dact = (
            mm(dq_s[rows, :], wq[...], 1, 1)
            + mm(dk_s[rows, :], wk[...], 1, 1)
            + mm(dv_s[rows, :], wv[...], 1, 1)
        )
        normed1, inverse1 = normalize(flat(x_ref, c))
        small[0:1] += row_sum(dact * normed1, width)
        small[1:2] += row_sum(dact, width)
        dx = dh_s[rows, :] + layer_norm_pull(dact, normed1, inverse1, g1[...])
        ig_o[pl.ds(c * count, count)] = dx.astype(BF).reshape(count, slot, width)
        return carry

    def outcome(low, side):
        def one(i, carry):
            at = low + i
            valid = chunk_place < len_ref[at]
            moe = jnp.where(valid, parts[0][at].astype(F32) + side[i].astype(F32), 0.0)
            rows = pl.ds(pl.multiple_of(at * slot, slot), slot)
            total = jnp.where(valid, h_ref[rows, :], 0.0) + moe
            out_o[at] = total.astype(BF)
            small[5:6] += row_sum(total * total, width)
            small[6:7] += row_sum(moe * moe, width)
            return carry

        lax.fori_loop(0, half, one, 0)

    def gate_gradient():
        hit = plan[0:experts] > 0.5
        place = plan[experts : 2 * experts]
        gate = plan[2 * experts : 3 * experts]
        taken = jnp.zeros(gate.shape, F32)
        for j in range(dots.shape[1]):
            taken = taken + jnp.where(place == float(j), dots[:, j, 0:sents], 0.0)
        inner = jnp.sum(gate * taken, axis=0, keepdims=True)
        dlogit = jnp.where(hit, gate * (taken - inner), 0.0)
        hot = lax.broadcasted_iota(jnp.int32, (slot, sents), 0) == tasks[...]
        small[8 : 8 + experts, 0:slot] = lax.dot_general(
            dlogit, hot.astype(F32), (((1,), (1,)), ((), ())),
            precision=lax.Precision.HIGHEST, preferred_element_type=F32,
        )

    ready(gin_s, gback_s)
    line_service(0)
    returned(6)
    back[5].start()
    back[7].start()
    ready(h_ref, dm_ref, cot_ref, wo)
    lax.fori_loop(0, sents // count, first, 0)
    ready(ctx)
    red_o.value[...] = mm(ctx[...], da_s[...], 0, 0)
    red_o.send_core()
    returned(2)
    returned(4)
    ready(q, k, v, p_ref, act)
    pull(0, red_0)
    red_o.send_plane()
    line_service(1)
    back[5].wait_recv()
    add_into(parts[4], 0, sides[1], half)
    back[8].start()
    back[7].wait_recv()
    add_into(parts[2], half, sides[3], half)
    back[9].start()
    pull(1, red_1)
    red_0.send_plane()
    back[4].start()
    back[6].start()
    red_o.send_line()
    line_service(2)
    ready(wq, wk, wv, x_ref)
    lax.fori_loop(0, sents // count, last, 0)
    leaving = [
        pltpu.make_async_copy(ig_o, ig_out, local.at[24]),
        pltpu.make_async_copy(out_o, out_out, local.at[25]),
    ]
    leaving[0].start()
    red_1.send_plane()
    red_o.send_back_line()
    gate_gradient()
    returned(0)
    red_0.send_line()
    line_service(3)
    back[4].wait_recv()
    add_into(parts[0], 0, sides[0], half)
    back[6].wait_recv()
    add_into(parts[0], half, sides[2], half)
    red_o.send_back_plane()
    red_0.send_back_line()
    red_1.send_line()
    back[8].wait_recv()
    outcome(0, sides[4])
    back[9].wait_recv()
    outcome(half, sides[5])
    leaving[1].start()
    sums.send_core()
    red_o.send_back_core()
    red_0.send_back_plane()
    red_1.send_back_line()
    sums.send_plane()
    red_1.send_back_plane()
    red_0.send_back_core()
    sums.send_line()
    red_1.send_back_core()
    def leave(source, output):
        copy = pltpu.make_async_copy(source, output, local.at[26 + len(leaving)])
        copy.start()
        leaving.append(copy)

    def share(red, low):
        cols = pl.ds(low, red.final.shape[1])
        for place, ref in enumerate((gq_o, gk_o, gv_o)):
            leave(red.final.at[pl.ds(place * width, width)], ref.at[:, cols])

    red_o.finish()
    leave(red_o.final, go_o)
    red_0.finish()
    share(red_0, 0)
    sums.finish(small_o)
    red_1.finish()
    share(red_1, span)
    line_end()
    for copy in leaving:
        copy.wait()
    for copy in back[4:]:
        copy.wait_send()


def backward_exchange(
    depth, lengths, tokens, cot, dm, hidden, act, q, k, v, ctx, prob, wq, wk, wv, wo, g1, g2,
    attn_sum, plan, tasks, dots, py, cy, gin, gback, heads,
):
    sents, slot, width = tokens.shape
    total = sents * slot
    small = jax.ShapeDtypeStruct((16, width), F32)
    vm = pl.BlockSpec(memory_space=VM)
    anywhere = pl.BlockSpec(memory_space=pl.ANY)
    shape = jax.ShapeDtypeStruct
    cube = (sents, slot, width)
    head = width // heads
    span = max(1, min(heads, 256 // head)) * head
    pieces = [(width, width), (3 * width, span), (3 * width, width - span)]
    red = []
    for rows, cols in pieces:
        red += [
            VM((rows, cols), F32),
            VM((rows // 2, cols), BF),
            VM((rows // 2, cols), BF),
            VM((3, rows // 8, cols), BF),
            VM((rows // 8, cols), BF),
            VM((depth - 1, rows // 8 // depth, cols), BF),
            VM((rows, cols), BF),
        ]
    in_share = (gin.shape[0] // depth, gin.shape[1])
    back_share = (gback.shape[0] // depth, gback.shape[1])
    semaphores = 10 + 4 * depth + 3 * Reduction.semaphores(depth) + SmallSum.semaphores(depth)
    large = (
        tokens, cot, dm, hidden, act, q, k, v, ctx, prob, wq, wk, wv, wo, py, cy, gin, gback,
    )
    return pl.pallas_call(
        functools.partial(backward_kernel, heads, depth),
        in_specs=[pl.BlockSpec(memory_space=pltpu.SMEM)] + [vm] * 7 + [anywhere] * len(large),
        out_specs=[anywhere] * 6 + [vm] * 3,
        out_shape=[shape(cube, BF), shape(cube, BF)]
        + [shape((width, width), BF)] * 4
        + [shape(in_share, F32), shape(back_share, F32), shape(small.shape, F32)],
        scratch_shapes=[VM(ref.shape, ref.dtype) for ref in large[:14] + large[16:]]
        + [VM(cube, BF)] * 8
        + [VM((sents // 2, slot, width), BF)] * 6
        + [VM((total, width), F32)]
        + [VM((total, width), BF)] * 5
        + red
        + [VM((depth,) + in_share, BF), VM((depth,) + back_share, BF)]
        + [VM(in_share, BF), VM(back_share, BF)]
        + [VM(small.shape, F32)] * 2
        + [VM((4,) + small.shape, F32), VM((depth,) + small.shape, F32)]
        + [VM(cube, BF)] * 2
        + [
            pltpu.SemaphoreType.DMA((semaphores,)),
            pltpu.SemaphoreType.DMA((semaphores,)),
            pltpu.SemaphoreType.DMA((35,)),
        ],
        compiler_params=pltpu.CompilerParams(
            collective_id=2, has_side_effects=True, vmem_limit_bytes=63 * 2**20
        ),
        cost_estimate=pl.CostEstimate(
            flops=16 * total * width * width, bytes_accessed=40 * 2**20, transcendentals=0
        ),
    )(
        lengths, g1[None], g2[None], attn_sum, plan, tasks[None], lengths[None], dots, *large
    )


def outputs_kernel(
    out_in, ig_in, gin_in, gback_in, q_in, k_in, v_in, o_in, small,
    out_o, ig_o, gin_o, gback_o, q_o, k_o, v_o, o_o, l1g, l1b, l2g, l2b, table_o, rms_o,
    low, wide, cubes, share_in, share_back, sems,
):
    fetches = [
        pltpu.make_async_copy(src, low.at[place], sems.at[place])
        for place, src in enumerate((q_in, k_in, v_in, o_in))
    ]
    stores = [
        pltpu.make_async_copy(wide.at[place], dst, sems.at[4 + place])
        for place, dst in enumerate((q_o, k_o, v_o, o_o))
    ]
    moves = [
        (pltpu.make_async_copy(src, held, sems.at[8 + place]),
         pltpu.make_async_copy(held, dst, sems.at[12 + place]))
        for place, (src, held, dst) in enumerate(
            [
                (out_in, cubes.at[0], out_o),
                (ig_in, cubes.at[1], ig_o),
                (gin_in, share_in, gin_o),
                (gback_in, share_back, gback_o),
            ]
        )
    ]
    for fetch in fetches:
        fetch.start()
    for enter, _ in moves:
        enter.start()
    width = small.shape[1]
    for row, ref in enumerate((l1g, l1b, l2g, l2b)):
        ref[...] = small[row : row + 1]
    table_o[...] = small[8 : 8 + table_o.shape[0], 0 : table_o.shape[1]]
    sums = jnp.sum(small[4:8], axis=1, keepdims=True)
    ratio = jnp.sqrt(sums / (sums[3:4] * width))
    lane = lax.broadcasted_iota(jnp.int32, (1, 3), 1)
    pair = jnp.where(lane == 1, ratio[0:1], ratio[2:3])
    rms_o[...] = jnp.where(lane == 0, ratio[1:2], pair)
    for place in range(4):
        fetches[place].wait()
        wide[place] = low[place].astype(F32)
        stores[place].start()
        enter, leave = moves[place]
        enter.wait()
        leave.start()
    for store in stores:
        store.wait()
    for _, leave in moves:
        leave.wait()


def place_outputs(out, ig, gin, gback, q, k, v, o, small, experts, ntasks):
    width = small.shape[1]
    vm = pl.BlockSpec(memory_space=VM)
    anywhere = pl.BlockSpec(memory_space=pl.ANY)
    shape = jax.ShapeDtypeStruct
    return pl.pallas_call(
        outputs_kernel,
        in_specs=[anywhere] * 8 + [vm],
        out_specs=[anywhere] * 8 + [vm] * 6,
        out_shape=[shape(a.shape, a.dtype) for a in (out, ig, gin, gback)]
        + [shape(q.shape, F32)] * 4
        + [shape((1, width), F32)] * 4
        + [shape((experts, ntasks), F32), shape((1, 3), F32)],
        scratch_shapes=[
            VM((4,) + q.shape, BF),
            VM((4,) + q.shape, F32),
            VM((2,) + out.shape, BF),
            VM(gin.shape, F32),
            VM(gback.shape, F32),
            pltpu.SemaphoreType.DMA((16,)),
        ],
        compiler_params=pltpu.CompilerParams(vmem_limit_bytes=60 * 2**20),
    )(out, ig, gin, gback, q, k, v, o, small)


def local(
    tokens,
    lengths,
    tasks,
    routes,
    gate_table,
    ln1_gain,
    ln1_bias,
    ln2_gain,
    ln2_bias,
    w_query,
    w_key,
    w_value,
    w_out,
    w_in,
    w_back,
    cotangent,
):
    sents, slot, width = tokens.shape
    heads = HEADS
    head = width // heads
    experts = gate_table.shape[1]
    ntasks = routes.shape[0]
    capacity = max(1, 4 * sents // experts)
    scale = 1.0 / jnp.sqrt(jnp.float32(head))
    task_hot = (tasks[:, None] == jnp.arange(ntasks)[None, :]).astype(jnp.int32)
    chosen = jnp.sum(task_hot[:, :, None] * routes[None, :, :], axis=1)
    flat = chosen.reshape(-1)
    order = jnp.arange(2 * sents)
    earlier = (flat[:, None] == flat[None, :]) & (order[None, :] < order[:, None])
    rank = jnp.sum(earlier.astype(jnp.int32), axis=1)
    slot_id = flat * capacity + rank
    placed = rank < capacity
    dispatch = (
        (jnp.arange(experts * capacity)[:, None] == slot_id[None, :]) & placed[None, :]
    ).astype(jnp.bfloat16)
    collect = dispatch.T
    expert_hot = (chosen[:, :, None] == jnp.arange(experts)[None, None, :]).astype(jnp.float32)
    valid = (jnp.arange(slot)[None, :] < lengths[:, None]).astype(jnp.float32)
    keymask = valid[:, None, None, :] > 0.5
    mask3 = valid[:, :, None]
    xfull = tokens.astype(jnp.float32)
    normed1, inverse1 = normalize(xfull)
    act = (normed1 * ln1_gain + ln1_bias).astype(jnp.bfloat16).reshape(-1, width)
    query = project(act, w_query).astype(jnp.bfloat16).reshape(sents, slot, heads, head)
    keyed = project(act, w_key).astype(jnp.bfloat16).reshape(sents, slot, heads, head)
    valued = project(act, w_value).astype(jnp.bfloat16).reshape(sents, slot, heads, head)

    def scores_of(qpart, kpart):
        raw = (
            jnp.einsum("sqhd,skhd->shqk", qpart, kpart, preferred_element_type=jnp.float32) * scale
        )
        return jnp.where(keymask, raw, -1000000000.0)

    scores = scores_of(query, keyed)
    peak = jnp.max(scores, axis=-1, keepdims=True)
    logsum = peak + jnp.log(jnp.sum(jnp.exp(scores - peak), axis=-1, keepdims=True))
    prob_low = jnp.exp(scores - logsum).astype(jnp.bfloat16)
    context = jnp.einsum("shqk,skhd->sqhd", prob_low, valued, preferred_element_type=jnp.float32)
    context = context.astype(jnp.bfloat16).reshape(-1, width)
    attention_block = project(context, w_out).reshape(sents, slot, width)
    hidden_res = xfull + attention_block
    normed2, inverse2 = normalize(hidden_res)
    mixed = (normed2 * ln2_gain + ln2_bias).astype(jnp.bfloat16)
    table_rows = jnp.dot(task_hot.astype(jnp.float32), gate_table, precision=lax.Precision.HIGHEST)
    picked = jnp.sum(expert_hot * table_rows[:, None, :], axis=-1)
    gate_values = jax.nn.softmax(picked, axis=-1)
    grad_total = cotangent.astype(jnp.float32) * mask3
    copies = jnp.broadcast_to(mixed[:, None], (sents, 2, slot, width)).reshape(
        2 * sents, slot * width
    )
    outgoing = (
        project(dispatch, copies).astype(jnp.bfloat16).reshape(experts, capacity, slot, width)
    )
    dycopy = (
        (gate_values[:, :, None, None] * grad_total[:, None])
        .astype(jnp.bfloat16)
        .reshape(2 * sents, slot * width)
    )
    grad_out = (
        project(dispatch, dycopy).astype(jnp.bfloat16).reshape(experts, capacity, slot, width)
    )
    incoming = lax.all_to_all(outgoing, "expert", split_axis=0, concat_axis=0, tiled=True).reshape(
        -1, width
    )
    pre_act, active, produced = expert_forward(incoming, w_in[0], w_back[0])
    returned = lax.all_to_all(
        produced.reshape(experts, capacity, slot, width),
        "expert",
        split_axis=0,
        concat_axis=0,
        tiled=True,
    )
    grad_in = lax.all_to_all(grad_out, "expert", split_axis=0, concat_axis=0, tiled=True).reshape(
        -1, width
    )
    in_local, back_local, dincoming = expert_backward(
        incoming, pre_act, active, grad_in, w_in[0], w_back[0]
    )
    grad_back = lax.all_to_all(
        dincoming.reshape(experts, capacity, slot, width),
        "expert",
        split_axis=0,
        concat_axis=0,
        tiled=True,
    )
    ycopy = project(collect, returned.reshape(experts * capacity, slot * width)).reshape(
        sents, 2, slot, width
    )
    expert_mixture = jnp.sum(gate_values[:, :, None, None] * ycopy, axis=1)
    total = mask3 * (hidden_res + expert_mixture)
    output = total.astype(jnp.bfloat16)
    stats_local = jnp.stack(
        [
            jnp.sum(total * total),
            jnp.sum(mask3 * attention_block * attention_block),
            jnp.sum(mask3 * expert_mixture * expert_mixture),
            jnp.sum(valid),
        ]
    )
    stat_totals = lax.psum(stats_local, ("dp", "expert"))
    gate_dot = jnp.sum(ycopy * grad_total[:, None], axis=(2, 3))
    dpicked = gate_values * (gate_dot - jnp.sum(gate_values * gate_dot, axis=-1, keepdims=True))
    dlogits = jnp.sum(expert_hot * dpicked[:, :, None], axis=1)
    table_grad = jnp.dot(task_hot.T.astype(jnp.float32), dlogits, precision=lax.Precision.HIGHEST)
    dmixed = project(collect, grad_back.reshape(experts * capacity, slot * width)).reshape(
        sents, 2, slot, width
    )
    dmixed = jnp.sum(dmixed, axis=1)
    dres2, gain2_grad, bias2_grad = norm_backward(dmixed, normed2, inverse2, ln2_gain)
    dhidden = grad_total + dres2
    dattn = dhidden.astype(jnp.bfloat16).reshape(-1, width)
    wout_grad = project(context.T, dattn)
    dcontext = project(dattn, w_out.T).astype(jnp.bfloat16).reshape(sents, slot, heads, head)
    again = jnp.exp(scores_of(query, keyed) - logsum)
    dprob = jnp.einsum("sqhd,skhd->shqk", dcontext, valued, preferred_element_type=jnp.float32)
    dscores = (again * (dprob - jnp.sum(dprob * again, axis=-1, keepdims=True))).astype(
        jnp.bfloat16
    )
    dquery = (
        jnp.einsum("shqk,skhd->sqhd", dscores, keyed, preferred_element_type=jnp.float32) * scale
    )
    dkeyed = (
        jnp.einsum("shqk,sqhd->skhd", dscores, query, preferred_element_type=jnp.float32) * scale
    )
    dvalued = jnp.einsum("shqk,sqhd->skhd", prob_low, dcontext, preferred_element_type=jnp.float32)
    dquery = dquery.astype(jnp.bfloat16).reshape(-1, width)
    dkeyed = dkeyed.astype(jnp.bfloat16).reshape(-1, width)
    dvalued = dvalued.astype(jnp.bfloat16).reshape(-1, width)
    wq_grad = project(act.T, dquery)
    wk_grad = project(act.T, dkeyed)
    wv_grad = project(act.T, dvalued)
    dact = project(dquery, w_query.T) + project(dkeyed, w_key.T) + project(dvalued, w_value.T)
    dres1, gain1_grad, bias1_grad = norm_backward(
        dact.reshape(sents, slot, width), normed1, inverse1, ln1_gain
    )
    input_grad = (dhidden + dres1).astype(jnp.bfloat16)
    members = (
        wq_grad,
        wk_grad,
        wv_grad,
        wout_grad,
        gain1_grad,
        bias1_grad,
        gain2_grad,
        bias2_grad,
        table_grad,
    )
    members = members + ()
    summed = lax.psum(members, ("dp", "expert"))
    rms = jnp.sqrt(stat_totals[0:3] / (stat_totals[3] * width))
    in_share, back_share = (
        lax.psum_scatter(
            in_local.astype(jnp.bfloat16), "dp", scatter_dimension=0, tiled=True
        ).astype(jnp.float32),
        lax.psum_scatter(
            back_local.astype(jnp.bfloat16), "dp", scatter_dimension=0, tiled=True
        ).astype(jnp.float32),
    )
    return (
        output,
        input_grad,
        summed[8],
        summed[4],
        summed[5],
        summed[6],
        summed[7],
        summed[0],
        summed[1],
        summed[2],
        summed[3],
        in_share[None],
        back_share[None],
        rms,
    )


def local_plane(
    depth,
    tokens,
    lengths,
    tasks,
    routes,
    gate_table,
    ln1_gain,
    ln1_bias,
    ln2_gain,
    ln2_bias,
    w_query,
    w_key,
    w_value,
    w_out,
    w_in,
    w_back,
    cotangent,
):
    experts = gate_table.shape[1]
    sents, slot, width = tokens.shape
    heads = HEADS
    capacity = max(1, 4 * sents // experts)
    (
        act, query, keyed, valued, context, prob, hidden, mixed, attn_sum, plan, places,
        gate_slots, near, far, core,
    ) = attention_forward(
        tokens, lengths, w_query, w_key, w_value, w_out, ln1_gain, ln1_bias, ln2_gain, ln2_bias,
        tasks, routes.T, gate_table.T, cotangent, heads, capacity,
    )
    dmixed, parts_back, cores_back, in_local, back_local, slot_dots = expert_exchange(
        places, gate_slots, mixed, cotangent, near, far, core, w_in[0], w_back[0], capacity, depth
    )
    input_grad, output, sum_q, sum_k, sum_v, sum_o, in_share, back_share, small = (
        backward_exchange(
            depth, lengths, tokens, cotangent, dmixed, hidden, act, query, keyed, valued,
            context, prob, w_query, w_key, w_value, w_out, ln1_gain, ln2_gain, attn_sum, plan,
            tasks, slot_dots, parts_back, cores_back, in_local, back_local, heads,
        )
    )
    (
        output, input_grad, in_share, back_share, grad_q, grad_k, grad_v, grad_o,
        gain1, bias1, gain2, bias2, table_grad, rms,
    ) = place_outputs(
        output, input_grad, in_share, back_share, sum_q, sum_k, sum_v, sum_o, small,
        experts, gate_table.shape[0],
    )
    return (
        output,
        input_grad,
        table_grad.T,
        gain1.reshape(-1),
        bias1.reshape(-1),
        gain2.reshape(-1),
        bias2.reshape(-1),
        grad_q,
        grad_k,
        grad_v,
        grad_o,
        in_share[None],
        back_share[None],
        rms.reshape(-1),
    )


def solution(mesh):
    in_specs = (
        P(("dp", "expert"), None, None),
        P(("dp", "expert")),
        P(("dp", "expert")),
        P(),
        P(),
        P(),
        P(),
        P(),
        P(),
        P(),
        P(),
        P(),
        P(),
        P("expert", None, None),
        P("expert", None, None),
        P(("dp", "expert"), None, None),
    )
    out_specs = (
        P(("dp", "expert"), None, None),
        P(("dp", "expert"), None, None),
        P(),
        P(),
        P(),
        P(),
        P(),
        P(),
        P(),
        P(),
        P(),
        P("expert", "dp", None),
        P("expert", "dp", None),
        P(),
    )
    plane = dict(mesh.shape)["expert"]
    depth = dict(mesh.shape)["dp"]
    cube = plane == 2 * 2 * 2 and depth > 3
    body = functools.partial(local_plane, depth) if cube else local
    return jax.shard_map(body, mesh=mesh, in_specs=in_specs, out_specs=out_specs, check_vma=False)
```

```python
import functools

import jax
import jax.numpy as jnp
from jax import lax
from jax.experimental import pallas as pl
from jax.experimental.pallas import tpu as pltpu
from jax.sharding import PartitionSpec as P

HEADS = 8


def normalize(value):
    centered = value - jnp.mean(value, axis=-1, keepdims=True)
    variance = jnp.mean(centered * centered, axis=-1, keepdims=True)
    inverse = lax.rsqrt(variance + 1e-05)
    return (centered * inverse, inverse)


def norm_backward(grad, normed, inverse, gain):
    scaled = grad * gain
    inner = scaled - jnp.mean(scaled, axis=-1, keepdims=True)
    inner = inner - normed * jnp.mean(scaled * normed, axis=-1, keepdims=True)
    return (inverse * inner, jnp.sum(grad * normed, axis=(0, 1)), jnp.sum(grad, axis=(0, 1)))


def project(left, right):
    return jnp.dot(left, right, preferred_element_type=jnp.float32)


def expert_forward(incoming, first, second):
    pre_act = project(incoming, first)
    active = jax.nn.gelu(pre_act).astype(jnp.bfloat16)
    produced = project(active, second).astype(jnp.bfloat16)
    return (pre_act, active, produced)


def expert_backward(incoming, pre_act, active, grad_in, first, second):
    dactive = project(grad_in, second.T)
    back_local = project(active.T, grad_in)
    gelu_pull = jax.vjp(jax.nn.gelu, pre_act)[1]
    dpre = gelu_pull(dactive)[0].astype(jnp.bfloat16)
    in_local = project(incoming.T, dpre)
    dincoming = project(dpre, first.T).astype(jnp.bfloat16)
    return (in_local, back_local, dincoming)


BF = jnp.bfloat16
F32 = jnp.float32
VM = pltpu.VMEM


def mm(a, b, ca=1, cb=0):
    return lax.dot_general(a, b, (((ca,), (cb,)), ((), ())), preferred_element_type=F32)


def block_diagonal(group, slot, head):
    shape = (group * slot, group * head)
    rows = lax.broadcasted_iota(jnp.int32, shape, 0) // slot
    cols = lax.broadcasted_iota(jnp.int32, shape, 1) // head
    return rows == cols


def spread(part, mask, group):
    return jnp.where(mask, jnp.concatenate([part] * group, axis=0), jnp.zeros((), part.dtype))


def fold(product, mask, slot, group):
    kept = jnp.where(mask, product, 0.0)
    total = kept[0:slot]
    for one in range(1, group):
        total = total + kept[one * slot : (one + 1) * slot]
    return total


def attend(query, keyed, valued, length, mask, slot, group, scale):
    scores = mm(keyed, spread(query, mask, group), 1, 1) * scale
    place = lax.broadcasted_iota(jnp.int32, scores.shape, 0)
    scores = jnp.where(place < length, scores, -1000000000.0)
    raised = jnp.exp(scores - jnp.max(scores, axis=0, keepdims=True))
    prob = raised / jnp.sum(raised, axis=0, keepdims=True)
    context = fold(mm(prob.astype(BF), valued, 0, 0), mask, slot, group)
    return prob, context


def route_tables(cap, tasks, lengths, routes, gate_table):
    sents = tasks.shape[1]
    experts, ntasks = gate_table.shape
    iota = lambda rows, cols, axis: lax.broadcasted_iota(jnp.int32, (rows, cols), axis)
    hot = (iota(ntasks, sents, 0) == tasks).astype(F32)
    exact = functools.partial(
        lax.dot_general,
        dimension_numbers=(((1,), (0,)), ((), ())),
        precision=lax.Precision.HIGHEST,
        preferred_element_type=F32,
    )
    chosen = exact(routes.astype(F32), hot)
    first, second = chosen[0:1], chosen[1:2]
    expert = iota(experts, sents, 0).astype(F32)
    is_first, is_second = expert == first, expert == second
    hit = jnp.logical_or(is_first, is_second)
    before = (iota(sents, sents, 0) < iota(sents, sents, 1)).astype(BF)
    rank = mm(hit.astype(F32).astype(BF), before)
    place = jnp.where(hit, jnp.where(rank < cap, rank, -1.0), -1.0)
    logits = exact(gate_table, hot)
    one = jnp.sum(jnp.where(is_first, logits, 0.0), axis=0, keepdims=True)
    two = jnp.sum(jnp.where(is_second, logits, 0.0), axis=0, keepdims=True)
    peak = jnp.maximum(one, two)
    one, two = jnp.exp(one - peak), jnp.exp(two - peak)
    gate = jnp.where(is_first, one / (one + two), 0.0)
    gate = gate + jnp.where(is_second, two / (one + two), 0.0)
    lane = iota(experts, 128, 1)
    index = iota(experts, sents, 1).astype(F32)
    table = jnp.zeros((experts, 128), F32)
    gates = jnp.zeros((experts, 128), F32)
    for j in range(cap):
        here = place == float(j)
        pick = lambda value: jnp.sum(jnp.where(here, value, 0.0), axis=1, keepdims=True)
        table = jnp.where(lane == j, pick(index), table)
        table = jnp.where(lane == cap + j, pick(lengths.astype(F32)), table)
        gates = jnp.where(lane == j, pick(gate), gates)
    shift = (iota(sents, 128, 1) == iota(sents, 128, 0) + 2 * cap).astype(BF)
    spots = mm((place + 1.0).astype(BF), shift)
    inside = jnp.logical_and(lane >= 2 * cap, lane < 2 * cap + sents)
    table = jnp.where(inside, spots - 1.0, table)
    return table.astype(jnp.int32), gates, hit.astype(F32), place, gate


def attention_forward_kernel(
    heads, cap, steps, len_ref, x_ref, wq, wk, wv, wo, g1, b1, g2, b2, tasks, lengths, routes,
    gate_table, cot_in,
    act_o, q_o, k_o, v_o, ctx_o, p_o, h_o, m_o, st_o, plan_o, tab_o, gates_o, near_o, far_o,
    core_o, cot, tab_s, gates_s, sends, recvs, local,
):
    count, slot, width = x_ref.shape
    head = width // heads
    group = max(1, min(heads, 256 // head))
    span = group * head
    step = pl.program_id(0)
    scale = head ** -0.5
    mask = block_diagonal(group, slot, head)
    experts = gate_table.shape[0]
    me = lax.axis_index("expert")
    half = cot.shape[0] // 2
    early = near_o.shape[0]
    copies = [
        remote(cot.at[pl.ds(0, early)], near_o, sends, recvs, 0, NEAR),
        remote(cot.at[pl.ds(half, early)], far_o, sends, recvs, 1, FAR),
        remote(cot, core_o, sends, recvs, 2, CORE),
    ]
    for relation in range(1, 8):
        there = plane_peer(relation)
        copies += [
            remote(tab_s.at[there], tab_o.at[me], sends, recvs, 1 + 2 * relation, relation),
            remote(gates_s.at[there], gates_o.at[me], sends, recvs, 2 + 2 * relation, relation),
        ]
    load = pltpu.make_async_copy(cot_in, cot, local.at[2])
    own = [
        pltpu.make_async_copy(tab_s.at[me], tab_o.at[me], local.at[0]),
        pltpu.make_async_copy(gates_s.at[me], gates_o.at[me], local.at[1]),
    ]

    @pl.when(step == 0)
    def _():
        load.start()
        greet()
        table, gates, hit, place, gate = route_tables(
            cap, tasks[...], lengths[...], routes[...], gate_table[...]
        )
        for e in range(experts):
            tab_s[e] = jnp.broadcast_to(table[e : e + 1], (8, 128))
            gates_s[e] = jnp.broadcast_to(gates[e : e + 1], (8, 128))
        plan_o[0:experts] = hit
        plan_o[experts : 2 * experts] = place
        plan_o[2 * experts : 3 * experts] = gate
        st_o[...] = jnp.zeros_like(st_o)

    @pl.when(step == min(1, steps - 1))
    def _():
        await_greetings()
        load.wait()
        for copy in copies + own:
            copy.start()

    x = x_ref[...].astype(F32).reshape(count * slot, width)
    normed, _ = normalize(x)
    act = (normed * g1[...] + b1[...]).astype(BF)
    act_o[...] = act
    q_o[...] = mm(act, wq[...]).astype(BF)
    k_o[...] = mm(act, wk[...]).astype(BF)
    v_o[...] = mm(act, wv[...]).astype(BF)
    for s in range(count):
        length = len_ref[step * count + s]
        rows = slice(s * slot, (s + 1) * slot)
        for part in range(heads // group):
            cols = slice(part * span, (part + 1) * span)
            prob, context = attend(
                q_o[rows, cols], k_o[rows, cols], v_o[rows, cols], length, mask, slot, group, scale
            )
            p_o[s, part] = prob
            ctx_o[rows, cols] = context.astype(BF)
    attn = mm(ctx_o[...], wo[...])
    hidden = x + attn
    h_o[...] = hidden
    normed2, _ = normalize(hidden)
    m_o[...] = (normed2 * g2[...] + b2[...]).astype(BF).reshape(count, slot, width)
    place = lax.broadcasted_iota(jnp.int32, (slot, width), 0)
    total = jnp.zeros((1, width), F32)
    for s in range(count):
        length = len_ref[step * count + s]
        part = attn[s * slot : (s + 1) * slot]
        total = total + jnp.sum(jnp.where(place < length, part * part, 0.0), axis=0, keepdims=True)
    st_o[...] += total

    @pl.when(step == pl.num_programs(0) - 1)
    def _():
        for copy in copies + own:
            copy.wait()


def attention_forward(
    tokens, lengths, wq, wk, wv, wo, g1, b1, g2, b2, tasks, routes, gate_table, cot, heads, cap
):
    sents, slot, width = tokens.shape
    experts = gate_table.shape[0]
    count = 4 if sents % 4 == 0 else 1
    rows = count * slot
    head = width // heads
    group = max(1, min(heads, 256 // head))
    whole = lambda *shape: pl.BlockSpec(shape, lambda i: (0,) * len(shape))
    flat = pl.BlockSpec((rows, width), lambda i: (i, 0))
    cube = pl.BlockSpec((count, slot, width), lambda i: (i, 0, 0))
    probs = pl.BlockSpec((count, heads // group, slot, group * slot), lambda i: (i, 0, 0, 0))
    anywhere = pl.BlockSpec(memory_space=pl.ANY)
    shape = jax.ShapeDtypeStruct
    total = sents * slot
    early = (sents // 4, slot, width)
    return pl.pallas_call(
        functools.partial(attention_forward_kernel, heads, cap, sents // count),
        grid=(sents // count,),
        in_specs=[pl.BlockSpec(memory_space=pltpu.SMEM), cube]
        + [whole(width, width)] * 4
        + [whole(1, width)] * 4
        + [whole(1, sents)] * 2
        + [whole(*routes.shape), whole(*gate_table.shape), anywhere],
        out_specs=[flat] * 5
        + [probs, flat, cube, whole(1, width), whole(3 * experts, sents)]
        + [anywhere] * 5,
        out_shape=[shape((total, width), BF)] * 5
        + [
            shape((sents, heads // group, slot, group * slot), F32),
            shape((total, width), F32),
            shape((sents, slot, width), BF),
            shape((1, width), F32),
            shape((3 * experts, sents), F32),
            shape((experts, 8, 128), jnp.int32),
            shape((experts, 8, 128), F32),
            shape(early, BF),
            shape(early, BF),
            shape(tokens.shape, BF),
        ],
        scratch_shapes=[
            VM(cot.shape, BF),
            VM((experts, 8, 128), jnp.int32),
            VM((experts, 8, 128), F32),
            pltpu.SemaphoreType.DMA((17,)),
            pltpu.SemaphoreType.DMA((17,)),
            pltpu.SemaphoreType.DMA((3,)),
        ],
        compiler_params=pltpu.CompilerParams(
            dimension_semantics=("arbitrary",), vmem_limit_bytes=56 * 2**20,
            collective_id=0, has_side_effects=True,
        ),
        cost_estimate=pl.CostEstimate(
            flops=8 * total * width * width + 4 * total * slot * width,
            bytes_accessed=16 * total * width,
            transcendentals=total * slot * heads,
        ),
    )(
        lengths, tokens, wq, wk, wv, wo, g1[None], b1[None], g2[None], b2[None],
        tasks[None], lengths[None], routes, gate_table, cot,
    )


def row_sum(value, width):
    return jnp.sum(value, axis=0, keepdims=True)


def layer_norm_pull(grad, normed, inverse, gain):
    scaled = grad * gain
    inner = scaled - jnp.mean(scaled, axis=-1, keepdims=True)
    inner = inner - normed * jnp.mean(scaled * normed, axis=-1, keepdims=True)
    return inverse * inner


def attention_pull(dcontext, query, keyed, valued, prob, mask, slot, group, scale):
    low = prob.astype(BF)
    dspread = spread(dcontext, mask, group)
    dprob = mm(valued, dspread, 1, 1)
    inner = jnp.sum(dprob * prob, axis=0, keepdims=True)
    dscores = (prob * (dprob - inner)).astype(BF)
    dquery = fold(mm(dscores, keyed, 0, 0), mask, slot, group) * scale
    dkeyed = mm(dscores, spread(query, mask, group)) * scale
    dvalued = mm(low, dspread)
    return dquery.astype(BF), dkeyed.astype(BF), dvalued.astype(BF)


MESH_ID = pl.DeviceIdType.MESH
CORE, NEAR, FAR = 1, 2, 4


def plane_peer(relation):
    me = lax.axis_index("expert")
    bits = []
    for bit in (CORE, NEAR, FAR):
        value = (me // bit) % 2
        bits.append((1 - value if relation & bit else value) * bit)
    return bits[0] + bits[1] + bits[2]


def remote(src, dst, sends, recvs, index, relation):
    return pltpu.make_async_remote_copy(
        src_ref=src,
        dst_ref=dst,
        send_sem=sends.at[index],
        recv_sem=recvs.at[index],
        device_id=(lax.axis_index("dp"), plane_peer(relation)),
        device_id_type=MESH_ID,
    )


def line_peer(offset, depth):
    return lax.rem(lax.axis_index("dp") + offset, depth)


def along(src, dst, sends, recvs, index, offset, depth):
    return pltpu.make_async_remote_copy(
        src_ref=src,
        dst_ref=dst,
        send_sem=sends.at[index],
        recv_sem=recvs.at[index],
        device_id=(line_peer(offset, depth), lax.axis_index("expert")),
        device_id_type=MESH_ID,
    )


def greet(depth=1):
    barrier = pltpu.get_barrier_semaphore()
    targets = [(lax.axis_index("dp"), plane_peer(relation)) for relation in range(1, 8)]
    for offset in range(1, depth):
        targets.append((line_peer(offset, depth), lax.axis_index("expert")))
    for target in targets:
        pl.semaphore_signal(barrier, inc=1, device_id=target, device_id_type=MESH_ID)


def await_greetings(depth=1):
    pl.semaphore_wait(pltpu.get_barrier_semaphore(), 6 + depth)


def gather_copies(own, held, sends, recvs, base, early=0):
    half = own.shape[0] // 2
    low, high = pl.ds(0, half), pl.ds(half, half)
    near, far = pl.ds(early, half - early), pl.ds(half + early, half - early)
    plan = [
        (own.at[near], held[2].at[near], NEAR),
        (own.at[far], held[4].at[far], FAR),
        (own, held[1], CORE),
        (own.at[high], held[2].at[high], NEAR),
        (own.at[low], held[4].at[low], FAR),
        (held[2].at[low], held[6].at[low], FAR),
        (held[4].at[high], held[6].at[high], NEAR),
        (held[2], held[3], CORE),
        (held[4], held[5], CORE),
        (held[6], held[7], CORE),
    ]
    return [
        remote(src, dst, sends, recvs, base + place, relation)
        for place, (src, dst, relation) in enumerate(plan)
    ]


def return_copies(parts, cores, sides, sends, recvs, base):
    half = parts[0].shape[0] // 2
    low, high = pl.ds(0, half), pl.ds(half, half)
    plan = [
        (parts[1], cores[0], CORE),
        (parts[3], cores[2], CORE),
        (parts[5], cores[4], CORE),
        (parts[7], cores[6], CORE),
        (parts[2].at[low], sides[0], NEAR),
        (parts[6].at[low], sides[1], NEAR),
        (parts[4].at[high], sides[2], FAR),
        (parts[6].at[high], sides[3], FAR),
        (parts[4].at[low], sides[4], FAR),
        (parts[2].at[high], sides[5], NEAR),
    ]
    return [
        remote(src, dst, sends, recvs, base + place, relation)
        for place, (src, dst, relation) in enumerate(plan)
    ]


def add_into(target, start, other, count):
    def one(i, carry):
        target[start + i] = target[start + i] + other[i]
        return carry

    lax.fori_loop(0, count, one, 0, unroll=8)


def split_copies(parts, sides, sends, recvs, base):
    half = parts[0].shape[0] // 2
    piece = half // 2
    hops = []
    for number, (source, first, side, relation) in enumerate(
        [
            (parts[6], 0, sides[1], NEAR),
            (parts[6], half, sides[3], FAR),
            (parts[4], 0, sides[4], FAR),
            (parts[2], half, sides[5], NEAR),
        ]
    ):
        hops.append(
            [
                remote(
                    source.at[pl.ds(first + q * piece, piece)],
                    side.at[pl.ds(q * piece, piece)],
                    sends, recvs, base + 2 * number + q, relation,
                )
                for q in range(2)
            ]
        )
    return hops


def return_finish(parts, sides, back, hops):
    half = parts[0].shape[0] // 2
    piece = half // 2
    for q in range(2):
        here = pl.ds(q * piece, piece)
        hops[0][q].wait_recv()
        add_into(parts[4], q * piece, sides[1].at[here], piece)
        hops[2][q].start()
        hops[1][q].wait_recv()
        add_into(parts[2], half + q * piece, sides[3].at[here], piece)
        hops[3][q].start()
    back[4].wait_recv()
    add_into(parts[0], 0, sides[0], half)
    back[6].wait_recv()
    add_into(parts[0], half, sides[2], half)
    for q in range(2):
        here = pl.ds(q * piece, piece)
        hops[2][q].wait_recv()
        add_into(parts[0], q * piece, sides[4].at[here], piece)
        hops[3][q].wait_recv()
        add_into(parts[0], half + q * piece, sides[5].at[here], piece)
    for copy in back[0:4] + [back[4], back[6]] + [copy for pair in hops for copy in pair]:
        copy.wait_send()


GELU_A = 0.7978845608028654
GELU_B = 0.044715


def expert_steps():
    waves = (((0, 1), (0,)), ((2, 3, 4, 5), (2,)), ((6, 7), ()))
    steps = []
    for taken, closed in waves:
        steps += [("F", r) for r in taken] + [("B", r) for r in taken]
        steps += [("U", r) for r in closed] + [("V", r) for r in closed]
    return steps


def expert_kernel(
    cap, depth, tab, gates, m_in, cot_in, near_in, far_in, core_in, win_in, wback_in,
    dm_o, py_o, cy_o, gin_o, gback_o, dg_o, *scratch
):
    sents, slot, width = m_in.shape
    hidden = win_in.shape[1]
    half = sents // 2
    held_m = dict(zip(range(8), scratch[0:8]))
    held_c = dict(zip(range(8), scratch[8:16]))
    sides = scratch[16:22]
    win, wback = scratch[22:24]
    first_part, xs, dys, zs, dus, ys, dms, stage, dg_s, accb, acci = scratch[24:35]
    line_in, line_back, sends, recvs, local, free = scratch[35:]
    parts = {
        0: first_part, 1: held_c[1], 2: held_m[0], 3: held_c[3],
        4: held_c[0], 5: held_c[5], 6: held_c[6], 7: held_c[7],
    }
    cores = {0: held_m[1], 2: held_m[3], 4: held_m[5], 6: held_m[7]}
    sets = {r: r - 2 if r in (4, 5) else r % 2 for r in range(8)}
    me = lax.axis_index("expert")
    z = lax.axis_index("dp")
    tile = min(512, hidden)
    rows = cap * slot
    early = near_in.shape[0]
    low, high = pl.ds(0, half), pl.ds(half, half)
    loads = [
        pltpu.make_async_copy(src, dst, local.at[2 + place])
        for place, (src, dst) in enumerate(
            [
                (m_in, held_m[0]),
                (cot_in, held_c[0]),
                (win_in, win),
                (wback_in, wback),
                (core_in, held_c[1]),
                (near_in, held_c[2].at[pl.ds(0, early)]),
                (far_in, held_c[4].at[pl.ds(half, early)]),
            ]
        )
    ]
    for load in loads:
        load.start()
    greet(depth)
    to_m = gather_copies(held_m[0], held_m, sends, recvs, 0)
    to_c = gather_copies(held_c[0], held_c, sends, recvs, 10, early)
    back = return_copies(parts, cores, sides, sends, recvs, 20)
    hops = split_copies(parts, sides, sends, recvs, 46)
    gates_back = {
        r: remote(dg_s.at[r], dg_o.at[me], sends, recvs, 30 + r, r) for r in range(1, 8)
    }
    outputs_back = {
        r: remote(stage, cy_o.at[r // 2], sends, recvs, 38 + r // 2, CORE) for r in (1, 3, 5, 7)
    }
    outputs_here = {
        r: pltpu.make_async_copy(stage, py_o.at[r // 2], local.at[0]) for r in (0, 2, 4, 6)
    }

    def line_first(right, array):
        offset = 1 if right else depth - 1
        s = depth - 1 if right else 0
        source, into = ((win, line_in), (wback, line_back))[array]
        share = source.shape[0] // depth
        here = pl.ds(s * share, share)
        index = 42 + 2 * int(right) + array
        return here, along(source.at[here], into, sends, recvs, index, offset, depth)

    def line_open(array):
        for right in (True, False):

            @pl.when(z == (0 if right else depth - 1))
            def _():
                line_first(right, array)[1].start()

    accb[...] = jnp.zeros_like(accb)
    acci[...] = jnp.zeros_like(acci)
    for load in loads[0:2]:
        load.wait()
    await_greetings(depth)
    for index in (0, 1, 2, 3, 4):
        to_m[index].start()
    for index in (0, 1, 3, 4):
        to_c[index].start()
    place = lax.broadcasted_iota(jnp.int32, (slot, width), 0)
    for load in loads[2:4]:
        load.wait()

    def before_forward(r):
        if r == 1:
            to_m[2].wait_recv()
        if r == 2:
            to_m[0].wait_recv()
            to_m[5].start()
            to_m[1].wait_recv()
            to_m[6].start()
            to_m[3].wait_recv()
            to_m[7].start()
            to_m[4].wait_recv()
            to_m[8].start()
        if r == 3:
            to_m[7].wait_recv()
        if r == 4:
            for load in loads[5:7]:
                load.wait()
            to_c[0].wait_recv()
            to_c[5].start()
            to_c[1].wait_recv()
            to_c[6].start()
        if r == 5:
            to_m[8].wait_recv()
        if r == 6:
            to_m[5].wait_recv()
            to_m[6].wait_recv()
            to_m[9].start()
        if r == 7:
            to_m[9].wait_recv()
        source = plane_peer(r)

        def fetch(j, carry):
            xs[sets[r], j] = held_m[r][tab[source, 0, j]]
            return carry

        lax.fori_loop(0, cap, fetch, 0, unroll=True)
        if r % 2 == 1:
            pl.semaphore_signal(
                free.at[r // 2], inc=1, device_id=(z, plane_peer(CORE)), device_id_type=MESH_ID
            )

    def after_forward(r):
        source = plane_peer(r)
        if r > 0 and r % 2 == 1:
            outputs_here[r - 1].wait()
        if r > 0 and r % 2 == 0:
            outputs_back[r - 1].wait_send()

        def give(i, carry):
            index = tab[source, 0, 2 * cap + i]
            there = jnp.maximum(index, 0)
            gate = jnp.where(index >= 0, gates[source, 0, there], 0.0)
            stage[i] = (ys[sets[r], there].astype(F32) * gate).astype(BF)
            return carry

        lax.fori_loop(0, sents, give, 0, unroll=8)
        if r % 2 == 0:
            outputs_here[r].start()
        else:
            outputs_back[r].start()

    def before_backward(r):
        if r == 1:
            loads[4].wait()
        if r == 2:
            to_c[3].wait_recv()
            to_c[7].start()
            to_c[4].wait_recv()
            to_c[8].start()
        if r == 3:
            to_c[7].wait_recv()
        if r == 5:
            to_c[8].wait_recv()
        if r == 6:
            to_c[5].wait_recv()
            to_c[6].wait_recv()
            to_c[9].start()
        if r == 7:
            to_c[9].wait_recv()
        source = plane_peer(r)

        def fetch(j, carry):
            index = tab[source, 0, j]
            length = tab[source, 0, cap + j]
            gate = gates[source, 0, j]
            gt = jnp.where(place < length, held_c[r][index].astype(F32), 0.0)
            dys[sets[r], j] = (gt * gate).astype(BF)
            product = ys[sets[r], j].astype(F32) * gt
            total = jnp.sum(jnp.sum(product, axis=0, keepdims=True), axis=1, keepdims=True)
            if r == 0:
                dg_o[me, pl.ds(j, 1)] = jnp.broadcast_to(total, (1, 128))
            else:
                dg_s[r, pl.ds(j, 1)] = jnp.broadcast_to(total, (1, 128))
            return carry

        lax.fori_loop(0, cap, fetch, 0, unroll=True)
        if r > 0:
            gates_back[r].start()

    def after_backward(r):
        source = plane_peer(r)
        if r == 2:
            for copy in to_m[0:5]:
                copy.wait_send()
        if r == 4:
            for copy in to_c[0:2] + to_c[3:5]:
                copy.wait_send()
        if r == 6:
            to_c[9].wait_send()

        def give(i, carry):
            index = tab[source, 0, 2 * cap + i]
            kept = dms[jnp.maximum(index, 0)]
            parts[r][i] = jnp.where(index >= 0, kept, jnp.zeros_like(kept))
            return carry

        lax.fori_loop(0, sents, give, 0, unroll=8)
        if r % 2 == 1:
            pl.semaphore_wait(free.at[r // 2], 1)
            back[r // 2].start()
        if r == 4:
            join(2)
            back[4].start()

    def join(r):
        back[r // 2].wait_recv()
        add_into(parts[r], 0, cores[r], sents)

    def after_back_grad(r):
        if r == 2:
            join(4)
            back[6].start()

    def after_in_grad(r):
        if r == 2:
            join(0)

    tiles = [slice(f * tile, (f + 1) * tile) for f in range(hidden // tile)]

    def forward(spot):
        x = xs[spot].reshape(rows, width)
        here = pl.ds(pl.multiple_of(spot * rows, rows), rows)
        for cols in tiles:
            u = mm(x, win[:, cols])
            square = u * u
            th = jnp.tanh(u * (GELU_A + GELU_A * GELU_B * square))
            cdf = 0.5 + 0.5 * th
            slope = cdf + (0.5 * u) * (1.0 - th * th) * (GELU_A + 3 * GELU_A * GELU_B * square)
            zs[here, cols] = (u * cdf).astype(BF)
            dus[here, cols] = slope.astype(BF)
        ys[spot] = mm(zs[here, :], wback[...]).astype(BF).reshape(cap, slot, width)

    def backward(spot):
        dy = dys[spot].reshape(rows, width)
        here = pl.ds(pl.multiple_of(spot * rows, rows), rows)
        for cols in tiles:
            dz = mm(dy, wback[cols, :], 1, 1)
            dus[here, cols] = (dz * dus[here, cols].astype(F32)).astype(BF)
        dms[...] = mm(dus[here, :], win[...], 1, 1).astype(BF).reshape(cap, slot, width)

    def back_grad(count):
        dy = dys[0:count].reshape(count * rows, width)
        for cols in tiles:
            yield cols, mm(zs[0 : count * rows, cols], dy, 0, 0)

    def in_grad(count):
        x = xs[0:count].reshape(count * rows, width)
        for cols in tiles:
            yield cols, mm(x, dus[0 : count * rows, cols], 0, 0)

    def back_pair(spot):
        for cols, total in back_grad(2):
            accb[cols, :] += total

    def in_pair(spot):
        for cols, total in in_grad(2):
            acci[:, cols] += total

    steps = expert_steps()
    actions = {
        "F": (before_forward, forward, after_forward),
        "B": (before_backward, backward, after_backward),
        "U": (None, back_pair, after_back_grad),
        "V": (None, in_pair, after_in_grad),
    }

    def spot_of(t, kind):
        spot = jnp.int32(0)
        for number, (other, r) in enumerate(steps):
            if other == kind and sets[r]:
                spot = spot + jnp.where(t == number, sets[r], 0)
        return spot

    def step(t, carry):
        for kind, (pre, work, post) in actions.items():
            mine = [number for number, (other, _) in enumerate(steps) if other == kind]
            spans = [n for n in mine if n - 1 not in mine]
            ends = [n for n in mine if n + 1 not in mine]
            inside = functools.reduce(
                jnp.logical_or,
                [jnp.logical_and(t >= a, t <= b) for a, b in zip(spans, ends)],
            )

            @pl.when(inside)
            def _():
                if pre is not None:
                    for number in mine:
                        pl.when(t == number)(functools.partial(pre, steps[number][1]))
                work(spot_of(t, kind))
                for number in mine:
                    pl.when(t == number)(functools.partial(post, steps[number][1]))

        return carry

    lax.fori_loop(0, len(steps), step, 0)
    for cols, total in back_grad(4):
        wback[cols, :] = (accb[cols, :] + total).astype(BF)
        if cols.start == 0:
            join(6)
            for q in range(2):
                hops[0][q].start()
                hops[1][q].start()
    line_open(1)
    for cols, total in in_grad(4):
        win[:, cols] = (acci[:, cols] + total).astype(BF)
    line_open(0)
    stores = [
        pltpu.make_async_copy(win, gin_o, local.at[4]),
        pltpu.make_async_copy(wback, gback_o, local.at[5]),
    ]
    for store in stores:
        store.start()
    return_finish(parts, sides, back, hops)
    kept = pltpu.make_async_copy(parts[0], dm_o, local.at[2])
    kept.start()
    for store in stores:
        store.wait()
    for right in (True, False):

        @pl.when(z == (1 if right else depth - 2))
        def _():
            again = []
            for array in (1, 0):
                here, copy = line_first(right, array)
                copy.wait_recv()
                source, into = ((win, line_in), (wback, line_back))[array]
                total = source[here, :].astype(F32) + into[...].astype(F32)
                source[here, :] = total.astype(BF)
                output = (gin_o, gback_o)[array]
                again.append(
                    pltpu.make_async_copy(source.at[here], output.at[here], local.at[6 + array])
                )
                again[-1].start()
            for store in again:
                store.wait()

    kept.wait()
    for right in (True, False):

        @pl.when(z == (0 if right else depth - 1))
        def _():
            for array in (0, 1):
                line_first(right, array)[1].wait_send()

    for r in (1, 3, 5, 7):
        outputs_back[r].wait_recv()
    outputs_back[7].wait_send()
    for r in range(1, 8):
        gates_back[r].wait()
    for index in range(5, 10):
        to_m[index].wait_send()
    for index in range(5, 9):
        to_c[index].wait_send()


def expert_exchange(tab, gates, m, cot, near, far, core, win, wback, cap, depth):
    sents, slot, width = m.shape
    hidden = win.shape[1]
    vm = pl.BlockSpec(memory_space=VM)
    sm = pl.BlockSpec(memory_space=pltpu.SMEM)
    anywhere = pl.BlockSpec(memory_space=pl.ANY)
    shape = jax.ShapeDtypeStruct
    cube = (sents, slot, width)
    taken = (cap, slot, width)
    rows = cap * slot
    return pl.pallas_call(
        functools.partial(expert_kernel, cap, depth),
        in_specs=[sm, sm] + [anywhere] * 7,
        out_specs=[anywhere] * 5 + [vm],
        out_shape=[
            shape(cube, BF),
            shape((4,) + cube, BF),
            shape((4,) + cube, BF),
            shape((width, hidden), BF),
            shape((hidden, width), BF),
            shape((8, cap, 128), F32),
        ],
        scratch_shapes=[VM(cube, BF)] * 16
        + [VM((sents // 2, slot, width), BF)] * 6
        + [VM((width, hidden), BF), VM((hidden, width), BF)]
        + [VM(cube, BF)]
        + [VM((4,) + taken, BF)] * 2
        + [VM((4 * rows, hidden), BF)] * 2
        + [VM((4,) + taken, BF), VM(taken, BF), VM(cube, BF)]
        + [VM((8, cap, 128), F32)]
        + [VM((hidden, width), F32), VM((width, hidden), F32)]
        + [VM((width // depth, hidden), BF), VM((hidden // depth, width), BF)]
        + [
            pltpu.SemaphoreType.DMA((54,)),
            pltpu.SemaphoreType.DMA((54,)),
            pltpu.SemaphoreType.DMA((9,)),
            pltpu.SemaphoreType.REGULAR((4,)),
        ],
        compiler_params=pltpu.CompilerParams(
            collective_id=1, has_side_effects=True, vmem_limit_bytes=63 * 2**20
        ),
        cost_estimate=pl.CostEstimate(
            flops=12 * 8 * rows * width * hidden, bytes_accessed=40 * 2**20, transcendentals=0
        ),
    )(tab, gates, m, cot, near, far, core, win, wback)


class Reduction:
    def __init__(self, depth, value, wide, core_r, plane_r, line_s, line_r, final, sems, base):
        self.depth, self.value, self.wide, self.final = depth, value, wide, final
        self.core_r, self.plane_r, self.line_s, self.line_r = core_r, plane_r, line_s, line_r
        sends, recvs = sems
        me = lax.axis_index("expert")
        z = lax.axis_index("dp")
        core = me % 2
        self.half = value.shape[0] // 2
        self.quarter = self.half // 4
        self.share = self.quarter // depth
        self.mine = core * self.half
        self.other = (1 - core) * self.half
        self.block = self.mine + (me // 2) * self.quarter
        self.own = self.block + z * self.share
        self.to_core = remote(wide, core_r, sends, recvs, base, CORE)
        self.to_plane = []
        self.from_plane = []
        for place, relation in enumerate((2, 4, 6)):
            rows = pl.ds((plane_peer(relation) // 2) * self.quarter, self.quarter)
            self.to_plane.append(
                remote(wide.at[rows], plane_r.at[place], sends, recvs, base + 1 + place, relation)
            )
        self.to_line = []
        for offset in range(1, depth):
            rows = pl.ds(line_peer(offset, depth) * self.share, self.share)
            self.to_line.append(
                along(
                    line_s.at[rows], line_r.at[offset - 1], sends, recvs, base + 3 + offset,
                    offset, depth,
                )
            )
        after = base + 3 + depth
        rows = final.at[pl.ds(self.own, self.share)]
        self.back_line = [
            along(rows, rows, sends, recvs, after + offset - 1, offset, depth)
            for offset in range(1, depth)
        ]
        after = after + depth - 1
        rows = final.at[pl.ds(self.block, self.quarter)]
        self.back_plane = [
            remote(rows, rows, sends, recvs, after + place, relation)
            for place, relation in enumerate((2, 4, 6))
        ]
        rows = final.at[pl.ds(self.mine, self.half)]
        self.back_core = remote(rows, rows, sends, recvs, after + 3, CORE)

    @staticmethod
    def semaphores(depth):
        return 2 * depth + 6

    def send_core(self):
        self.wide[...] = self.value[pl.ds(self.other, self.half), :].astype(BF)
        self.to_core.start()

    def send_plane(self):
        self.to_core.wait()
        rows = pl.ds(self.mine, self.half)
        total = self.value[rows, :] + self.core_r[...].astype(F32)
        self.value[rows, :] = total
        self.wide[...] = total.astype(BF)
        for copy in self.to_plane:
            copy.start()

    def send_line(self):
        for copy in self.to_plane:
            copy.wait()
        rows = pl.ds(self.block, self.quarter)
        total = self.value[rows, :]
        for place in range(3):
            total = total + self.plane_r[place].astype(F32)
        self.value[rows, :] = total
        self.line_s[...] = total.astype(BF)
        for copy in self.to_line:
            copy.start()

    def send_back_line(self):
        for copy in self.to_line:
            copy.wait()
        rows = pl.ds(self.own, self.share)
        total = self.value[rows, :]
        for offset in range(1, self.depth):
            total = total + self.line_r[offset - 1].astype(F32)
        self.final[rows, :] = total.astype(BF)
        for copy in self.back_line:
            copy.start()

    def send_back_plane(self):
        for copy in self.back_line:
            copy.wait()
        for copy in self.back_plane:
            copy.start()

    def send_back_core(self):
        for copy in self.back_plane:
            copy.wait()
        self.back_core.start()

    def finish(self):
        self.back_core.wait()


class SmallSum:
    @staticmethod
    def semaphores(depth):
        return 4 + depth

    def __init__(self, depth, value, core_r, plane, line, sems, base):
        sends, recvs = sems
        self.value, self.core_r, self.plane, self.line = value, core_r, plane, line
        self.spot = lax.axis_index("expert") // 2
        self.z = lax.axis_index("dp")
        self.to_core = remote(value, core_r, sends, recvs, base, CORE)
        spot = plane.at[self.spot]
        self.to_plane = [
            remote(spot, spot, sends, recvs, base + 1 + place, relation)
            for place, relation in enumerate((2, 4, 6))
        ]
        spot = line.at[self.z]
        self.to_line = [
            along(spot, spot, sends, recvs, base + 3 + offset, offset, depth)
            for offset in range(1, depth)
        ]

    def send_core(self):
        self.to_core.start()

    def send_plane(self):
        self.to_core.wait()
        self.plane[self.spot] = self.value[...] + self.core_r[...]
        for copy in self.to_plane:
            copy.start()

    def send_line(self):
        for copy in self.to_plane:
            copy.wait()
        total = self.plane[0]
        for place in range(1, 4):
            total = total + self.plane[place]
        self.line[self.z] = total
        for copy in self.to_line:
            copy.start()

    def finish(self, out):
        for copy in self.to_line:
            copy.wait()
        total = self.line[0]
        for place in range(1, self.line.shape[0]):
            total = total + self.line[place]
        out[...] = total


def backward_kernel(
    heads, depth, len_ref, g1, g2, attn_sum, plan, tasks, lengths, dots,
    x_in, cot_in, dm_in, h_in, act_in, q_in, k_in, v_in, ctx_in, p_in,
    wq_in, wk_in, wv_in, wo_in, py, cy, gin, gback,
    ig_out, out_out, gq_o, gk_o, gv_o, go_o, gin_o, gback_o, small_o, *scratch
):
    inputs = (
        x_in, cot_in, dm_in, h_in, act_in, q_in, k_in, v_in, ctx_in, p_in,
        wq_in, wk_in, wv_in, wo_in, gin, gback,
    )
    held = scratch[0:16]
    (
        x_ref, cot_ref, dm_ref, h_ref, act, q, k, v, ctx, p_ref, wq, wk, wv, wo, gin_s, gback_s,
    ) = held
    parts = dict(zip((0, 2, 4, 6), scratch[16:20]))
    cores = dict(zip((0, 2, 4, 6), scratch[20:24]))
    sides = scratch[24:30]
    dh_s, da_s, dctx_s, dq_s, dk_s, dv_s = scratch[30:36]
    red = scratch[36:57]
    line_in, line_back, extra_in, extra_back = scratch[57:61]
    small, small_core, small_plane, small_line = scratch[61:65]
    ig_o, out_o, sends, recvs, local = scratch[65:]
    sems = (sends, recvs)
    sents, slot, width = x_ref.shape
    head = width // heads
    group = max(1, min(heads, 256 // head))
    span = group * head
    scale = head ** -0.5
    count = 4 if sents % 4 == 0 else 1
    rows_per = count * slot
    half = sents // 2
    z = lax.axis_index("dp")

    loads = {
        id(ref): pltpu.make_async_copy(source, ref, local.at[place])
        for place, (source, ref) in enumerate(zip(inputs, held))
    }
    for place, r in enumerate((0, 2, 4, 6)):
        loads[id(parts[r])] = pltpu.make_async_copy(
            py.at[r // 2], parts[r], local.at[16 + place]
        )
        loads[id(cores[r])] = pltpu.make_async_copy(
            cy.at[r // 2], cores[r], local.at[20 + place]
        )

    def begin(*refs):
        for ref in refs:
            loads[id(ref)].start()

    def ready(*refs):
        for ref in refs:
            loads[id(ref)].wait()

    begin(gin_s, gback_s, h_ref, dm_ref, cot_ref, wo, parts[6], cores[6], ctx)
    begin(parts[2], cores[2], parts[4], cores[4], q, k, v, p_ref, act, parts[0], cores[0])
    begin(wq, wk, wv, x_ref)
    greet(depth)
    await_greetings(depth)

    all_parts = {r: parts[r - r % 2] for r in range(8)}
    back = return_copies(all_parts, cores, sides, sends, recvs, 0)

    base = 10
    in_rows = gin_s.shape[0] // depth
    back_rows = gback_s.shape[0] // depth

    def line_piece(s, array, right, last):
        offset = 1 if right else depth - 1
        index = base + (0 if right else 2 * depth) + 2 * s + array
        share, source = ((in_rows, gin_s), (back_rows, gback_s))[array]
        into = (line_in, line_back)[array].at[s]
        if last and not right:
            into = (extra_in, extra_back)[array]
        here = source.at[pl.ds(s * share, share)]
        return along(here, into, sends, recvs, index, offset, depth)

    def add_piece(s, array):
        share, source = ((in_rows, gin_s), (back_rows, gback_s))[array]
        other = (line_in, line_back)[array]
        here = pl.ds(s * share, share)
        source[here, :] = (source[here, :].astype(F32) + other[s].astype(F32)).astype(BF)

    def pieces(right):
        order = range(depth - 1, 0, -1) if right else range(depth - 1)
        return [(s, array) for s in order for array in (0, 1)]

    def start_piece(s, array, right):
        if right:
            line_piece(s, array, True, False).start()
            return
        near = z == s + 1

        @pl.when(near)
        def _():
            line_piece(s, array, False, True).start()

        @pl.when(jnp.logical_not(near))
        def _():
            line_piece(s, array, False, False).start()

    def line_service(t, ahead=0):
        for right in (True, False):
            every = pieces(right)
            edge = 0 if right else depth - 1
            opening = range(2, 3 + ahead) if t == 0 else range(t + ahead + 2, t + ahead + 3)

            @pl.when(z == edge)
            def _():
                for number in opening:
                    if number < len(every):
                        start_piece(*every[number], right)

            for number, (s, array) in enumerate(every):
                away = s if right else depth - 1 - s
                for hops in range(1, away):
                    given = hops == 1 and number < 2
                    if t != (0 if given else number + hops - 1):
                        continue

                    @pl.when(z == (hops if right else depth - 1 - hops))
                    def _():
                        if not given:
                            line_piece(s, array, right, False).wait_recv()
                            add_piece(s, array)
                        start_piece(s, array, right)

    def line_end():
        for s in range(depth):

            @pl.when(z == s)
            def _():
                here = pl.ds(s * in_rows, in_rows)
                there = pl.ds(s * back_rows, back_rows)
                gin_o[...] = gin_s[here, :].astype(F32)
                gback_o[...] = gback_s[there, :].astype(F32)
                if s > 0:
                    for array in (0, 1):
                        line_piece(s, array, True, True).wait_recv()
                    gin_o[...] += line_in[s].astype(F32)
                    gback_o[...] += line_back[s].astype(F32)
                if s < depth - 1:
                    for array in (0, 1):
                        line_piece(s, array, False, True).wait_recv()
                    gin_o[...] += extra_in[...].astype(F32)
                    gback_o[...] += extra_back[...].astype(F32)

        for s in range(depth):
            for array in (0, 1):
                first_right = 1 if s == depth - 1 else 0
                first_left = depth - 2 if s == 0 else depth - 1

                @pl.when(jnp.logical_and(z < s, z >= first_right))
                def _():
                    line_piece(s, array, True, False).wait_send()

                @pl.when(jnp.logical_and(z > s, z <= first_left))
                def _():
                    line_piece(s, array, False, False).wait_send()

    base_red = base + 4 * depth
    per = Reduction.semaphores(depth)
    red_o, red_0, red_1 = [
        Reduction(depth, *red[7 * place : 7 * place + 7], sems, base_red + place * per)
        for place in range(3)
    ]
    sums = SmallSum(
        depth, small, small_core, small_plane, small_line, sems, base_red + 3 * per
    )

    small[...] = jnp.zeros_like(small)
    small[4:5] = attn_sum[...]
    small[7:8, 0:sents] = lengths[...].astype(F32)
    experts = plan.shape[0] // 3
    chunk_place = lax.broadcasted_iota(jnp.int32, (slot, width), 0)

    def masked(ref, c):
        return jnp.concatenate(
            [
                jnp.where(
                    chunk_place < len_ref[c * count + s], ref[c * count + s].astype(F32), 0.0
                )
                for s in range(count)
            ],
            axis=0,
        )

    def flat(ref, c):
        block = ref[pl.ds(c * count, count)]
        return block.astype(F32).reshape(rows_per, width)

    def first(c, carry):
        rows = pl.ds(pl.multiple_of(c * rows_per, rows_per), rows_per)
        normed2, inverse2 = normalize(h_ref[rows, :])
        dm = flat(dm_ref, c)
        dhidden = masked(cot_ref, c) + layer_norm_pull(dm, normed2, inverse2, g2[...])
        small[2:3] += row_sum(dm * normed2, width)
        small[3:4] += row_sum(dm, width)
        dh_s[rows, :] = dhidden
        dattn = dhidden.astype(BF)
        da_s[rows, :] = dattn
        dctx_s[rows, :] = mm(dattn, wo[...], 1, 1).astype(BF)
        return carry

    mask = block_diagonal(group, slot, head)

    def pull(part, into):
        cols = slice(part * span, (part + 1) * span)

        def one(c, carry):
            for s in range(count):
                at = c * count + s
                rows = pl.ds(pl.multiple_of(at * slot, slot), slot)
                dq_s[rows, cols], dk_s[rows, cols], dv_s[rows, cols] = attention_pull(
                    dctx_s[rows, cols], q[rows, cols], k[rows, cols], v[rows, cols],
                    p_ref[at, part], mask, slot, group, scale,
                )
            return carry

        lax.fori_loop(0, sents // count, one, 0)
        into.value[0:width, :] = mm(act[...], dq_s[:, cols], 0, 0)
        into.value[width : 2 * width, :] = mm(act[...], dk_s[:, cols], 0, 0)
        into.value[2 * width : 3 * width, :] = mm(act[...], dv_s[:, cols], 0, 0)
        into.send_core()

    def returned(r):
        ready(parts[r], cores[r])
        add_into(parts[r], 0, cores[r], sents)

    def last(c, carry):
        rows = pl.ds(pl.multiple_of(c * rows_per, rows_per), rows_per)
        dact = (
            mm(dq_s[rows, :], wq[...], 1, 1)
            + mm(dk_s[rows, :], wk[...], 1, 1)
            + mm(dv_s[rows, :], wv[...], 1, 1)
        )
        normed1, inverse1 = normalize(flat(x_ref, c))
        small[0:1] += row_sum(dact * normed1, width)
        small[1:2] += row_sum(dact, width)
        dx = dh_s[rows, :] + layer_norm_pull(dact, normed1, inverse1, g1[...])
        ig_o[pl.ds(c * count, count)] = dx.astype(BF).reshape(count, slot, width)
        return carry

    def outcome(low, side):
        def one(i, carry):
            at = low + i
            valid = chunk_place < len_ref[at]
            moe = jnp.where(valid, parts[0][at].astype(F32) + side[i].astype(F32), 0.0)
            rows = pl.ds(pl.multiple_of(at * slot, slot), slot)
            total = jnp.where(valid, h_ref[rows, :], 0.0) + moe
            out_o[at] = total.astype(BF)
            small[5:6] += row_sum(total * total, width)
            small[6:7] += row_sum(moe * moe, width)
            return carry

        lax.fori_loop(0, half, one, 0)

    def gate_gradient():
        hit = plan[0:experts] > 0.5
        place = plan[experts : 2 * experts]
        gate = plan[2 * experts : 3 * experts]
        taken = jnp.zeros(gate.shape, F32)
        for j in range(dots.shape[1]):
            taken = taken + jnp.where(place == float(j), dots[:, j, 0:sents], 0.0)
        inner = jnp.sum(gate * taken, axis=0, keepdims=True)
        dlogit = jnp.where(hit, gate * (taken - inner), 0.0)
        hot = lax.broadcasted_iota(jnp.int32, (slot, sents), 0) == tasks[...]
        small[8 : 8 + experts, 0:slot] = lax.dot_general(
            dlogit, hot.astype(F32), (((1,), (1,)), ((), ())),
            precision=lax.Precision.HIGHEST, preferred_element_type=F32,
        )

    ready(gin_s, gback_s)
    line_service(0)
    returned(6)
    back[5].start()
    back[7].start()
    ready(h_ref, dm_ref, cot_ref, wo)
    lax.fori_loop(0, sents // count, first, 0)
    ready(ctx)
    red_o.value[...] = mm(ctx[...], da_s[...], 0, 0)
    red_o.send_core()
    returned(2)
    returned(4)
    ready(q, k, v, p_ref, act)
    pull(0, red_0)
    red_o.send_plane()
    line_service(1)
    back[5].wait_recv()
    add_into(parts[4], 0, sides[1], half)
    back[8].start()
    back[7].wait_recv()
    add_into(parts[2], half, sides[3], half)
    back[9].start()
    pull(1, red_1)
    red_0.send_plane()
    back[4].start()
    back[6].start()
    red_o.send_line()
    line_service(2)
    ready(wq, wk, wv, x_ref)
    lax.fori_loop(0, sents // count, last, 0)
    leaving = [
        pltpu.make_async_copy(ig_o, ig_out, local.at[24]),
        pltpu.make_async_copy(out_o, out_out, local.at[25]),
    ]
    leaving[0].start()
    red_1.send_plane()
    red_o.send_back_line()
    gate_gradient()
    returned(0)
    red_0.send_line()
    line_service(3)
    back[4].wait_recv()
    add_into(parts[0], 0, sides[0], half)
    back[6].wait_recv()
    add_into(parts[0], half, sides[2], half)
    red_o.send_back_plane()
    red_0.send_back_line()
    red_1.send_line()
    back[8].wait_recv()
    outcome(0, sides[4])
    back[9].wait_recv()
    outcome(half, sides[5])
    leaving[1].start()
    sums.send_core()
    red_o.send_back_core()
    red_0.send_back_plane()
    red_1.send_back_line()
    sums.send_plane()
    red_1.send_back_plane()
    red_0.send_back_core()
    sums.send_line()
    red_1.send_back_core()
    def leave(source, output):
        copy = pltpu.make_async_copy(source, output, local.at[26 + len(leaving)])
        copy.start()
        leaving.append(copy)

    def share(red, low):
        cols = pl.ds(low, red.final.shape[1])
        for place, ref in enumerate((gq_o, gk_o, gv_o)):
            leave(red.final.at[pl.ds(place * width, width)], ref.at[:, cols])

    red_o.finish()
    leave(red_o.final, go_o)
    red_0.finish()
    share(red_0, 0)
    sums.finish(small_o)
    red_1.finish()
    share(red_1, span)
    line_end()
    for copy in leaving:
        copy.wait()
    for copy in back[4:]:
        copy.wait_send()


def backward_exchange(
    depth, lengths, tokens, cot, dm, hidden, act, q, k, v, ctx, prob, wq, wk, wv, wo, g1, g2,
    attn_sum, plan, tasks, dots, py, cy, gin, gback, heads,
):
    sents, slot, width = tokens.shape
    total = sents * slot
    small = jax.ShapeDtypeStruct((16, width), F32)
    vm = pl.BlockSpec(memory_space=VM)
    anywhere = pl.BlockSpec(memory_space=pl.ANY)
    shape = jax.ShapeDtypeStruct
    cube = (sents, slot, width)
    head = width // heads
    span = max(1, min(heads, 256 // head)) * head
    pieces = [(width, width), (3 * width, span), (3 * width, width - span)]
    red = []
    for rows, cols in pieces:
        red += [
            VM((rows, cols), F32),
            VM((rows // 2, cols), BF),
            VM((rows // 2, cols), BF),
            VM((3, rows // 8, cols), BF),
            VM((rows // 8, cols), BF),
            VM((depth - 1, rows // 8 // depth, cols), BF),
            VM((rows, cols), BF),
        ]
    in_share = (gin.shape[0] // depth, gin.shape[1])
    back_share = (gback.shape[0] // depth, gback.shape[1])
    semaphores = 10 + 4 * depth + 3 * Reduction.semaphores(depth) + SmallSum.semaphores(depth)
    large = (
        tokens, cot, dm, hidden, act, q, k, v, ctx, prob, wq, wk, wv, wo, py, cy, gin, gback,
    )
    return pl.pallas_call(
        functools.partial(backward_kernel, heads, depth),
        in_specs=[pl.BlockSpec(memory_space=pltpu.SMEM)] + [vm] * 7 + [anywhere] * len(large),
        out_specs=[anywhere] * 6 + [vm] * 3,
        out_shape=[shape(cube, BF), shape(cube, BF)]
        + [shape((width, width), BF)] * 4
        + [shape(in_share, F32), shape(back_share, F32), shape(small.shape, F32)],
        scratch_shapes=[VM(ref.shape, ref.dtype) for ref in large[:14] + large[16:]]
        + [VM(cube, BF)] * 8
        + [VM((sents // 2, slot, width), BF)] * 6
        + [VM((total, width), F32)]
        + [VM((total, width), BF)] * 5
        + red
        + [VM((depth,) + in_share, BF), VM((depth,) + back_share, BF)]
        + [VM(in_share, BF), VM(back_share, BF)]
        + [VM(small.shape, F32)] * 2
        + [VM((4,) + small.shape, F32), VM((depth,) + small.shape, F32)]
        + [VM(cube, BF)] * 2
        + [
            pltpu.SemaphoreType.DMA((semaphores,)),
            pltpu.SemaphoreType.DMA((semaphores,)),
            pltpu.SemaphoreType.DMA((35,)),
        ],
        compiler_params=pltpu.CompilerParams(
            collective_id=2, has_side_effects=True, vmem_limit_bytes=63 * 2**20
        ),
        cost_estimate=pl.CostEstimate(
            flops=16 * total * width * width, bytes_accessed=40 * 2**20, transcendentals=0
        ),
    )(
        lengths, g1[None], g2[None], attn_sum, plan, tasks[None], lengths[None], dots, *large
    )


def outputs_kernel(
    out_in, ig_in, gin_in, gback_in, q_in, k_in, v_in, o_in, small,
    out_o, ig_o, gin_o, gback_o, q_o, k_o, v_o, o_o, l1g, l1b, l2g, l2b, table_o, rms_o,
    low, wide, cubes, share_in, share_back, sems,
):
    fetches = [
        pltpu.make_async_copy(src, low.at[place], sems.at[place])
        for place, src in enumerate((q_in, k_in, v_in, o_in))
    ]
    stores = [
        pltpu.make_async_copy(wide.at[place], dst, sems.at[4 + place])
        for place, dst in enumerate((q_o, k_o, v_o, o_o))
    ]
    moves = [
        (pltpu.make_async_copy(src, held, sems.at[8 + place]),
         pltpu.make_async_copy(held, dst, sems.at[12 + place]))
        for place, (src, held, dst) in enumerate(
            [
                (out_in, cubes.at[0], out_o),
                (ig_in, cubes.at[1], ig_o),
                (gin_in, share_in, gin_o),
                (gback_in, share_back, gback_o),
            ]
        )
    ]
    for fetch in fetches:
        fetch.start()
    for enter, _ in moves:
        enter.start()
    width = small.shape[1]
    for row, ref in enumerate((l1g, l1b, l2g, l2b)):
        ref[...] = small[row : row + 1]
    table_o[...] = small[8 : 8 + table_o.shape[0], 0 : table_o.shape[1]]
    sums = jnp.sum(small[4:8], axis=1, keepdims=True)
    ratio = jnp.sqrt(sums / (sums[3:4] * width))
    lane = lax.broadcasted_iota(jnp.int32, (1, 3), 1)
    pair = jnp.where(lane == 1, ratio[0:1], ratio[2:3])
    rms_o[...] = jnp.where(lane == 0, ratio[1:2], pair)
    for place in range(4):
        fetches[place].wait()
        wide[place] = low[place].astype(F32)
        stores[place].start()
        enter, leave = moves[place]
        enter.wait()
        leave.start()
    for store in stores:
        store.wait()
    for _, leave in moves:
        leave.wait()


def place_outputs(out, ig, gin, gback, q, k, v, o, small, experts, ntasks):
    width = small.shape[1]
    vm = pl.BlockSpec(memory_space=VM)
    anywhere = pl.BlockSpec(memory_space=pl.ANY)
    shape = jax.ShapeDtypeStruct
    return pl.pallas_call(
        outputs_kernel,
        in_specs=[anywhere] * 8 + [vm],
        out_specs=[anywhere] * 8 + [vm] * 6,
        out_shape=[shape(a.shape, a.dtype) for a in (out, ig, gin, gback)]
        + [shape(q.shape, F32)] * 4
        + [shape((1, width), F32)] * 4
        + [shape((experts, ntasks), F32), shape((1, 3), F32)],
        scratch_shapes=[
            VM((4,) + q.shape, BF),
            VM((4,) + q.shape, F32),
            VM((2,) + out.shape, BF),
            VM(gin.shape, F32),
            VM(gback.shape, F32),
            pltpu.SemaphoreType.DMA((16,)),
        ],
        compiler_params=pltpu.CompilerParams(vmem_limit_bytes=60 * 2**20),
    )(out, ig, gin, gback, q, k, v, o, small)


def local(
    tokens,
    lengths,
    tasks,
    routes,
    gate_table,
    ln1_gain,
    ln1_bias,
    ln2_gain,
    ln2_bias,
    w_query,
    w_key,
    w_value,
    w_out,
    w_in,
    w_back,
    cotangent,
):
    sents, slot, width = tokens.shape
    heads = HEADS
    head = width // heads
    experts = gate_table.shape[1]
    ntasks = routes.shape[0]
    capacity = max(1, 4 * sents // experts)
    scale = 1.0 / jnp.sqrt(jnp.float32(head))
    task_hot = (tasks[:, None] == jnp.arange(ntasks)[None, :]).astype(jnp.int32)
    chosen = jnp.sum(task_hot[:, :, None] * routes[None, :, :], axis=1)
    flat = chosen.reshape(-1)
    order = jnp.arange(2 * sents)
    earlier = (flat[:, None] == flat[None, :]) & (order[None, :] < order[:, None])
    rank = jnp.sum(earlier.astype(jnp.int32), axis=1)
    slot_id = flat * capacity + rank
    placed = rank < capacity
    dispatch = (
        (jnp.arange(experts * capacity)[:, None] == slot_id[None, :]) & placed[None, :]
    ).astype(jnp.bfloat16)
    collect = dispatch.T
    expert_hot = (chosen[:, :, None] == jnp.arange(experts)[None, None, :]).astype(jnp.float32)
    valid = (jnp.arange(slot)[None, :] < lengths[:, None]).astype(jnp.float32)
    keymask = valid[:, None, None, :] > 0.5
    mask3 = valid[:, :, None]
    xfull = tokens.astype(jnp.float32)
    normed1, inverse1 = normalize(xfull)
    act = (normed1 * ln1_gain + ln1_bias).astype(jnp.bfloat16).reshape(-1, width)
    query = project(act, w_query).astype(jnp.bfloat16).reshape(sents, slot, heads, head)
    keyed = project(act, w_key).astype(jnp.bfloat16).reshape(sents, slot, heads, head)
    valued = project(act, w_value).astype(jnp.bfloat16).reshape(sents, slot, heads, head)

    def scores_of(qpart, kpart):
        raw = (
            jnp.einsum("sqhd,skhd->shqk", qpart, kpart, preferred_element_type=jnp.float32) * scale
        )
        return jnp.where(keymask, raw, -1000000000.0)

    scores = scores_of(query, keyed)
    peak = jnp.max(scores, axis=-1, keepdims=True)
    logsum = peak + jnp.log(jnp.sum(jnp.exp(scores - peak), axis=-1, keepdims=True))
    prob_low = jnp.exp(scores - logsum).astype(jnp.bfloat16)
    context = jnp.einsum("shqk,skhd->sqhd", prob_low, valued, preferred_element_type=jnp.float32)
    context = context.astype(jnp.bfloat16).reshape(-1, width)
    attention_block = project(context, w_out).reshape(sents, slot, width)
    hidden_res = xfull + attention_block
    normed2, inverse2 = normalize(hidden_res)
    mixed = (normed2 * ln2_gain + ln2_bias).astype(jnp.bfloat16)
    table_rows = jnp.dot(task_hot.astype(jnp.float32), gate_table, precision=lax.Precision.HIGHEST)
    picked = jnp.sum(expert_hot * table_rows[:, None, :], axis=-1)
    gate_values = jax.nn.softmax(picked, axis=-1)
    grad_total = cotangent.astype(jnp.float32) * mask3
    copies = jnp.broadcast_to(mixed[:, None], (sents, 2, slot, width)).reshape(
        2 * sents, slot * width
    )
    outgoing = (
        project(dispatch, copies).astype(jnp.bfloat16).reshape(experts, capacity, slot, width)
    )
    dycopy = (
        (gate_values[:, :, None, None] * grad_total[:, None])
        .astype(jnp.bfloat16)
        .reshape(2 * sents, slot * width)
    )
    grad_out = (
        project(dispatch, dycopy).astype(jnp.bfloat16).reshape(experts, capacity, slot, width)
    )
    incoming = lax.all_to_all(outgoing, "expert", split_axis=0, concat_axis=0, tiled=True).reshape(
        -1, width
    )
    pre_act, active, produced = expert_forward(incoming, w_in[0], w_back[0])
    returned = lax.all_to_all(
        produced.reshape(experts, capacity, slot, width),
        "expert",
        split_axis=0,
        concat_axis=0,
        tiled=True,
    )
    grad_in = lax.all_to_all(grad_out, "expert", split_axis=0, concat_axis=0, tiled=True).reshape(
        -1, width
    )
    in_local, back_local, dincoming = expert_backward(
        incoming, pre_act, active, grad_in, w_in[0], w_back[0]
    )
    grad_back = lax.all_to_all(
        dincoming.reshape(experts, capacity, slot, width),
        "expert",
        split_axis=0,
        concat_axis=0,
        tiled=True,
    )
    ycopy = project(collect, returned.reshape(experts * capacity, slot * width)).reshape(
        sents, 2, slot, width
    )
    expert_mixture = jnp.sum(gate_values[:, :, None, None] * ycopy, axis=1)
    total = mask3 * (hidden_res + expert_mixture)
    output = total.astype(jnp.bfloat16)
    stats_local = jnp.stack(
        [
            jnp.sum(total * total),
            jnp.sum(mask3 * attention_block * attention_block),
            jnp.sum(mask3 * expert_mixture * expert_mixture),
            jnp.sum(valid),
        ]
    )
    stat_totals = lax.psum(stats_local, ("dp", "expert"))
    gate_dot = jnp.sum(ycopy * grad_total[:, None], axis=(2, 3))
    dpicked = gate_values * (gate_dot - jnp.sum(gate_values * gate_dot, axis=-1, keepdims=True))
    dlogits = jnp.sum(expert_hot * dpicked[:, :, None], axis=1)
    table_grad = jnp.dot(task_hot.T.astype(jnp.float32), dlogits, precision=lax.Precision.HIGHEST)
    dmixed = project(collect, grad_back.reshape(experts * capacity, slot * width)).reshape(
        sents, 2, slot, width
    )
    dmixed = jnp.sum(dmixed, axis=1)
    dres2, gain2_grad, bias2_grad = norm_backward(dmixed, normed2, inverse2, ln2_gain)
    dhidden = grad_total + dres2
    dattn = dhidden.astype(jnp.bfloat16).reshape(-1, width)
    wout_grad = project(context.T, dattn)
    dcontext = project(dattn, w_out.T).astype(jnp.bfloat16).reshape(sents, slot, heads, head)
    again = jnp.exp(scores_of(query, keyed) - logsum)
    dprob = jnp.einsum("sqhd,skhd->shqk", dcontext, valued, preferred_element_type=jnp.float32)
    dscores = (again * (dprob - jnp.sum(dprob * again, axis=-1, keepdims=True))).astype(
        jnp.bfloat16
    )
    dquery = (
        jnp.einsum("shqk,skhd->sqhd", dscores, keyed, preferred_element_type=jnp.float32) * scale
    )
    dkeyed = (
        jnp.einsum("shqk,sqhd->skhd", dscores, query, preferred_element_type=jnp.float32) * scale
    )
    dvalued = jnp.einsum("shqk,sqhd->skhd", prob_low, dcontext, preferred_element_type=jnp.float32)
    dquery = dquery.astype(jnp.bfloat16).reshape(-1, width)
    dkeyed = dkeyed.astype(jnp.bfloat16).reshape(-1, width)
    dvalued = dvalued.astype(jnp.bfloat16).reshape(-1, width)
    wq_grad = project(act.T, dquery)
    wk_grad = project(act.T, dkeyed)
    wv_grad = project(act.T, dvalued)
    dact = project(dquery, w_query.T) + project(dkeyed, w_key.T) + project(dvalued, w_value.T)
    dres1, gain1_grad, bias1_grad = norm_backward(
        dact.reshape(sents, slot, width), normed1, inverse1, ln1_gain
    )
    input_grad = (dhidden + dres1).astype(jnp.bfloat16)
    members = (
        wq_grad,
        wk_grad,
        wv_grad,
        wout_grad,
        gain1_grad,
        bias1_grad,
        gain2_grad,
        bias2_grad,
        table_grad,
    )
    members = members + ()
    summed = lax.psum(members, ("dp", "expert"))
    rms = jnp.sqrt(stat_totals[0:3] / (stat_totals[3] * width))
    in_share, back_share = (
        lax.psum_scatter(
            in_local.astype(jnp.bfloat16), "dp", scatter_dimension=0, tiled=True
        ).astype(jnp.float32),
        lax.psum_scatter(
            back_local.astype(jnp.bfloat16), "dp", scatter_dimension=0, tiled=True
        ).astype(jnp.float32),
    )
    return (
        output,
        input_grad,
        summed[8],
        summed[4],
        summed[5],
        summed[6],
        summed[7],
        summed[0],
        summed[1],
        summed[2],
        summed[3],
        in_share[None],
        back_share[None],
        rms,
    )


def local_plane(
    depth,
    tokens,
    lengths,
    tasks,
    routes,
    gate_table,
    ln1_gain,
    ln1_bias,
    ln2_gain,
    ln2_bias,
    w_query,
    w_key,
    w_value,
    w_out,
    w_in,
    w_back,
    cotangent,
):
    experts = gate_table.shape[1]
    sents, slot, width = tokens.shape
    heads = HEADS
    capacity = max(1, 4 * sents // experts)
    (
        act, query, keyed, valued, context, prob, hidden, mixed, attn_sum, plan, places,
        gate_slots, near, far, core,
    ) = attention_forward(
        tokens, lengths, w_query, w_key, w_value, w_out, ln1_gain, ln1_bias, ln2_gain, ln2_bias,
        tasks, routes.T, gate_table.T, cotangent, heads, capacity,
    )
    dmixed, parts_back, cores_back, in_local, back_local, slot_dots = expert_exchange(
        places, gate_slots, mixed, cotangent, near, far, core, w_in[0], w_back[0], capacity, depth
    )
    input_grad, output, sum_q, sum_k, sum_v, sum_o, in_share, back_share, small = (
        backward_exchange(
            depth, lengths, tokens, cotangent, dmixed, hidden, act, query, keyed, valued,
            context, prob, w_query, w_key, w_value, w_out, ln1_gain, ln2_gain, attn_sum, plan,
            tasks, slot_dots, parts_back, cores_back, in_local, back_local, heads,
        )
    )
    (
        output, input_grad, in_share, back_share, grad_q, grad_k, grad_v, grad_o,
        gain1, bias1, gain2, bias2, table_grad, rms,
    ) = place_outputs(
        output, input_grad, in_share, back_share, sum_q, sum_k, sum_v, sum_o, small,
        experts, gate_table.shape[0],
    )
    return (
        output,
        input_grad,
        table_grad.T,
        gain1.reshape(-1),
        bias1.reshape(-1),
        gain2.reshape(-1),
        bias2.reshape(-1),
        grad_q,
        grad_k,
        grad_v,
        grad_o,
        in_share[None],
        back_share[None],
        rms.reshape(-1),
    )


def solution(mesh):
    in_specs = (
        P(("dp", "expert"), None, None),
        P(("dp", "expert")),
        P(("dp", "expert")),
        P(),
        P(),
        P(),
        P(),
        P(),
        P(),
        P(),
        P(),
        P(),
        P(),
        P("expert", None, None),
        P("expert", None, None),
        P(("dp", "expert"), None, None),
    )
    out_specs = (
        P(("dp", "expert"), None, None),
        P(("dp", "expert"), None, None),
        P(),
        P(),
        P(),
        P(),
        P(),
        P(),
        P(),
        P(),
        P(),
        P("expert", "dp", None),
        P("expert", "dp", None),
        P(),
    )
    plane = dict(mesh.shape)["expert"]
    depth = dict(mesh.shape)["dp"]
    cube = plane == 2 * 2 * 2 and depth > 3
    body = functools.partial(local_plane, depth) if cube else local
    return jax.shard_map(body, mesh=mesh, in_specs=in_specs, out_specs=out_specs, check_vma=False)
```
